32 devices in a mesh: dp: 4 (over z), op: 8 (over y, x, core).
Axes of the slice: x: 2, y: 2, z: 4, core: 2. Of those that a mesh axis runs over, the one named last changes fastest.
Arguments:
- inputs: bfloat16 [384, 512, 768], P(('dp', 'op')), may hold values from -6 to 6
- candidate: int32 [384, 2], P(('dp', 'op')), may hold values from 0 to 39, as said below
- attn_qkv: bfloat16 [2, 8, 768, 2304], P(None, 'op'), may hold values from -0.21875 to 0.21875
- attn_out: bfloat16 [2, 8, 768, 768], P(None, 'op'), may hold values from -2.5 to 2.5
- ffn_up: bfloat16 [2, 8, 768, 3072], P(None, 'op'), may hold values from -0.21875 to 0.21875
- ffn_down: bfloat16 [2, 8, 3072, 768], P(None, 'op'), may hold values from -0.109375 to 0.109375
- conv_taps: bfloat16 [2, 8, 15, 768], P(None, 'op'), may hold values from -2.5 to 2.5
- conv_point: bfloat16 [2, 8, 3, 768, 768], P(None, 'op'), may hold values from -0.21875 to 0.21875
- norm_gain: bfloat16 [2, 8, 5, 768], P(None, 'op'), may hold values from 0.5 to 1.5
- norm_bias: bfloat16 [2, 8, 5, 768], P(None, 'op'), may hold values from -2.5 to 2.5
- cotangent: bfloat16 [384, 512, 768], P(('dp', 'op')), may hold values from -6 to 6
Outputs:
- outputs: bfloat16 [384, 512, 768], P(('dp', 'op'))
- input_grad: bfloat16 [384, 512, 768], P(('dp', 'op'))
- attn_qkv_grad: float32 [2, 8, 768, 2304], P(None, 'op', 'dp')
- attn_out_grad: float32 [2, 8, 768, 768], P(None, 'op', 'dp')
- ffn_up_grad: float32 [2, 8, 768, 3072], P(None, 'op', 'dp')
- ffn_down_grad: float32 [2, 8, 3072, 768], P(None, 'op', 'dp')
- conv_taps_grad: float32 [2, 8, 15, 768], P(None, 'op', None, 'dp')
- conv_point_grad: float32 [2, 8, 3, 768, 768], P(None, 'op', None, 'dp')
- norm_gain_grad: float32 [2, 8, 5, 768], P(None, 'op', None, 'dp')
- norm_bias_grad: float32 [2, 8, 5, 768], P(None, 'op', None, 'dp')
The draws below stay inside these ranges and needn't reach their ends.
Inputs may be any that keep to these rules, and one draw needn't show every extreme that they name: candidate[n, b] = k * 8 + owner. In each block the 12 sequences of one device go at most 2 to one owner, and some owner gets exactly 2 of them; every owner receives exactly 12 sequences a block from the devices of its dp group, each of its 5 candidates between 1 and 3 of them, one candidate exactly 3.
All inputs are finite; a program needn't handle non-finite values.
Results may differ from the reference program's by a relative error of at most 0.015.
Values may be sent and summed in bfloat16 or wider, within the bound.
No kernel may reach another device: no remote copies, remote signals or barrier semaphores. Data moves between devices by JAX's collectives and lax.ppermute only.
A program may use at most 704 MiB of HBM per device.

```python
import jax
import jax.numpy as jnp
from jax import lax

D = 768
HEADS = 12
HEAD = 64
FF = 3072
L = 512
KINDS = 5
TAPS = 15
BLOCKS = 2
SEQ_DEV = 12
OWN_CAP = 3
OWNERS = 8
GROUPS = 4
SEQS = 384


def route_group(seed_key):
    subkeys = jax.random.split(seed_key, 6)
    src_label = jax.random.permutation(subkeys[0], OWNERS)
    dst_label = jax.random.permutation(subkeys[1], OWNERS)
    offset_perm = jax.random.permutation(subkeys[2], OWNERS)
    seq_ids = jnp.arange(SEQ_DEV)
    offsets = offset_perm[seq_ids % OWNERS]
    senders = jnp.arange(OWNERS)
    target = dst_label[(src_label[senders][:, None] + offsets[None, :]) % OWNERS]
    slot_count = KINDS * OWN_CAP
    slot_ids = jnp.arange(slot_count)
    full_kind = jax.random.randint(subkeys[3], (OWNERS,), 0, KINDS)
    forced = (slot_ids[None, :] // OWN_CAP == full_kind[:, None]) | (slot_ids[None, :] % OWN_CAP == 0)
    ranking = jax.vmap(lambda subkey: jax.random.permutation(subkey, slot_count))(jax.random.split(subkeys[4], OWNERS))
    priority = jnp.where(forced, 0, 1 + ranking)
    ordering = jnp.argsort(priority, axis=1, stable=True)[:, :SEQ_DEV]
    mixing = jax.vmap(lambda subkey: jax.random.permutation(subkey, SEQ_DEV))(jax.random.split(subkeys[5], OWNERS))
    chosen = jnp.take_along_axis(ordering, mixing, axis=1)
    slot_taken = chosen[target, seq_ids[None, :]]
    return (slot_taken // OWN_CAP * OWNERS + target).reshape(-1).astype(jnp.int32)


def draw_candidate(key, part):
    columns = []
    for block_index in range(BLOCKS):
        rows_list = []
        for group_index in range(GROUPS):
            rows_list.append(route_group(jax.random.fold_in(jax.random.fold_in(key, 31 + block_index), group_index)))
        columns.append(jnp.concatenate(rows_list))
    return jnp.stack(columns, axis=1).astype(jnp.int32)


def steps_of(stream_key, dims, cuts, smallest, top_value):
    def one(axis_at, shards_of):
        steps = jax.random.uniform(jax.random.fold_in(jax.random.fold_in(stream_key, 6), axis_at), (shards_of,), jnp.float32, smallest / len(cuts), top_value / len(cuts))
        return jnp.repeat(jnp.exp(steps), dims[axis_at] // shards_of).reshape((-1,) + (1,) * (len(dims) - axis_at - 1))

    level = one(*cuts[0])
    for cut in cuts[1:]:
        level = level * one(*cut)
    return level


def scatter_about(rng, shape, scale, reach, cuts=(), kind=jnp.bfloat16):
    level = steps_of(rng, shape, cuts, -0.22, 0.18) if cuts else 1.0
    result = jax.random.normal(rng, shape, jnp.float32) * scale * level
    return jnp.minimum(jnp.maximum(result, -reach), reach).astype(kind)


def setup_inputs(seed: int = 0) -> dict:
    key_list = jax.random.split(jax.random.key(seed), 12)
    return {
        "inputs": scatter_about(key_list[0], (SEQS, L, D), 1.0, 6.0, ((0, 32),)),
        "candidate": draw_candidate(jax.random.fold_in(key_list[11], 71), 0),
        "attn_qkv": scatter_about(key_list[2], (BLOCKS, OWNERS, D, 3 * D), D ** -0.5, 0.21875, ((1, 8),)),
        "attn_out": scatter_about(key_list[3], (BLOCKS, OWNERS, D, D), (max(D // 128, 1)) ** -0.5, 2.5, ((1, 8),)),
        "ffn_up": scatter_about(key_list[4], (BLOCKS, OWNERS, D, FF), D ** -0.5, 0.21875, ((1, 8),)),
        "ffn_down": scatter_about(key_list[5], (BLOCKS, OWNERS, FF, D), FF ** -0.5, 0.109375, ((1, 8),)),
        "conv_taps": scatter_about(key_list[6], (BLOCKS, OWNERS, TAPS, D), 5 ** -0.5, 2.5, ((1, 8),)),
        "conv_point": scatter_about(key_list[7], (BLOCKS, OWNERS, 3, D, D), D ** -0.5, 0.21875, ((1, 8),)),
        "norm_gain": jnp.clip(1.0 + 0.1 * jax.random.normal(key_list[8], (BLOCKS, OWNERS, KINDS, D), jnp.float32), 0.5, 1.5).astype(jnp.bfloat16),
        "norm_bias": scatter_about(key_list[9], (BLOCKS, OWNERS, KINDS, D), 0.3, 2.5, ((1, 8),)),
        "cotangent": scatter_about(key_list[10], (SEQS, L, D), 1.0, 6.0, ((0, 32),)),
    }


@jax.custom_vjp
def low(v):
    return lax.optimization_barrier(v.astype(jnp.bfloat16)).astype(jnp.float32)

@jax.custom_vjp
def low_back(v):
    return v

def low_keep(v):
    return (low(v), None)

def low_pass(kept, grad):
    return (grad,)

def back_keep(v):
    return (v, None)

def back_low(kept, grad):
    return (low(grad),)
low.defvjp(low_keep, low_pass)
low_back.defvjp(back_keep, back_low)

def matmul(operand_a, operand_b):
    return jnp.matmul(operand_a, operand_b, precision=lax.Precision.HIGHEST)

def layer_norm(summed, gain_row, norm_shift):
    center = summed - lax.optimization_barrier(jnp.mean(summed, axis=-1, keepdims=True))
    spread = lax.optimization_barrier(jnp.mean(center * center, axis=-1, keepdims=True))
    return center * lax.rsqrt(spread + 1e-05) * gain_row + norm_shift

def attend_one(packed_rows):
    model_width = packed_rows.shape[1] // 3
    queries = packed_rows[:, :model_width].reshape(-1, HEADS, HEAD)
    key_rows = packed_rows[:, model_width:2 * model_width].reshape(-1, HEADS, HEAD)
    values = packed_rows[:, 2 * model_width:].reshape(-1, HEADS, HEAD)
    scores = low_back(jnp.einsum('qhe,khe->hqk', queries, key_rows, precision=lax.Precision.HIGHEST) * HEAD ** (-0.5))
    row_max = lax.optimization_barrier(jnp.max(scores, axis=-1, keepdims=True))
    exponent = jnp.exp(scores - row_max)
    attn_probs = exponent / lax.optimization_barrier(jnp.sum(exponent, axis=-1, keepdims=True))
    mixed_heads = jnp.einsum('hqk,khe->qhe', low(attn_probs), values, precision=lax.Precision.HIGHEST)
    return mixed_heads.reshape(-1, model_width)

def attention(block_activation, query_key_value_weight, output_weight):
    packed_rows = low(low_back(matmul(block_activation, query_key_value_weight)))
    attention_result = low(low_back(lax.map(jax.checkpoint(attend_one), packed_rows)))
    return low_back(matmul(attention_result, output_weight))

def separable(block_activation, tap_rows, pointwise_weight):
    tap_count = tap_rows.shape[0]
    half_width = tap_count // 2
    length = block_activation.shape[1]
    padded = jnp.pad(block_activation, ((0, 0), (half_width, half_width), (0, 0)))
    mixed = jnp.zeros(block_activation.shape, jnp.float32)
    for offset in range(tap_count):
        mixed = mixed + padded[:, offset:offset + length] * tap_rows[offset]
    return low_back(matmul(low(mixed), pointwise_weight))

def feed_forward(block_activation, up_weight, down_weight):
    hidden_activation = low_back(matmul(block_activation, up_weight))
    active = low(jax.nn.gelu(hidden_activation, approximate=False))
    return low_back(matmul(active, down_weight))

def owner_block(block_in, params):
    query_key_value_weight, output_weight, up_weight, down_weight, tap_rows, pointwise_weight, norm_gains, norm_shifts = params
    per_kind = block_in.shape[0] // KINDS
    results = []
    for kind_number in range(KINDS):
        block_activation = block_in[kind_number * per_kind:(kind_number + 1) * per_kind]
        if kind_number == 0:
            branch = attention(block_activation, query_key_value_weight, output_weight)
        elif kind_number == KINDS - 1:
            branch = feed_forward(block_activation, up_weight, down_weight)
        else:
            first_row = kind_number * kind_number - 1
            branch = separable(block_activation, tap_rows[first_row:first_row + 2 * kind_number + 1], pointwise_weight[kind_number - 1])
        results.append(layer_norm(block_activation + branch, norm_gains[kind_number], norm_shifts[kind_number]))
    return jnp.concatenate(results, axis=0)

def owner_step(paired):
    return owner_block(paired[0], paired[1])

def route_block(current, column, params):
    owner_of = column % OWNERS
    kind_of = column // OWNERS
    seq_ids = jnp.arange(SEQS, dtype=jnp.int32)
    per_kind = GROUPS * OWN_CAP
    earlier = lax.optimization_barrier(jnp.sum((column[None, :] == column[:, None]) & (seq_ids[None, :] < seq_ids[:, None]), axis=1)).astype(jnp.int32)
    where_at = (kind_of * per_kind + earlier).astype(jnp.int32)
    source_rows = jnp.full((OWNERS, KINDS * per_kind), SEQS, jnp.int32).at[owner_of, where_at].set(seq_ids)
    padded = jnp.concatenate([current, jnp.zeros((1,) + current.shape[1:], jnp.float32)], axis=0)
    results = lax.map(jax.checkpoint(owner_step), (padded[source_rows], params))
    return results[owner_of, where_at]

def forward(current, weights, candidate):
    for block_no in range(BLOCKS):
        params = tuple((stacked[block_no] for stacked in weights))
        current = low(route_block(current, candidate[:, block_no], params))
        if block_no + 1 < BLOCKS:
            current = low_back(current)
    return current

def reference(inputs, candidate, attn_qkv, attn_out, ffn_up, ffn_down, conv_taps, conv_point, norm_gain, norm_bias, cotangent):
    weights = tuple((stacked.astype(jnp.float32) for stacked in (attn_qkv, attn_out, ffn_up, ffn_down, conv_taps, conv_point, norm_gain, norm_bias)))
    outputs, pullback = jax.vjp(lambda state_in, weight_set: forward(state_in, weight_set, candidate), inputs.astype(jnp.float32), weights)
    input_grad, weight_grads = pullback(cotangent.astype(jnp.float32))
    tallies = jnp.stack([jnp.zeros((KINDS * OWNERS,), jnp.float32).at[candidate[:, block_no]].add(1.0).reshape(KINDS, OWNERS) for block_no in range(BLOCKS)])
    per_kind = jnp.transpose(tallies, (0, 2, 1))
    tap_scale = jnp.concatenate([jnp.repeat(per_kind[:, :, kind_number:kind_number + 1], 2 * kind_number + 1, axis=2) for kind_number in range(1, KINDS - 1)], axis=2)
    grad_qkv, grad_out, grad_up, grad_down, grad_taps, grad_point, grad_gain, grad_shift = weight_grads
    return (outputs.astype(jnp.bfloat16), input_grad.astype(jnp.bfloat16), grad_qkv / per_kind[:, :, 0, None, None], grad_out / per_kind[:, :, 0, None, None], grad_up / per_kind[:, :, KINDS - 1, None, None], grad_down / per_kind[:, :, KINDS - 1, None, None], grad_taps / tap_scale[..., None], grad_point / per_kind[:, :, 1:KINDS - 1, None, None], grad_gain / per_kind[..., None], grad_shift / per_kind[..., None])
```

```python
import jax
import jax.numpy as jnp
from jax import lax
from jax.experimental import pallas as pl
from jax.experimental.pallas import tpu as pltpu
from jax.sharding import PartitionSpec as P

HEADS = 12
KINDS = 5
BLOCKS = 2
OWN_CAP = 3
FF_PART = 1024
FF_SUB = 512
LANES = 128
BF16 = jnp.bfloat16
F32 = jnp.float32
VMEM_BYTES = 60 * 2**20


def params_of(axes):
    return pltpu.CompilerParams(
        dimension_semantics=("arbitrary",) * axes, vmem_limit_bytes=VMEM_BYTES
    )


def nn(a, b):
    return lax.dot_general(a, b, (((1,), (0,)), ((), ())), preferred_element_type=F32)


def nt(a, b):
    return lax.dot_general(a, b, (((1,), (1,)), ((), ())), preferred_element_type=F32)


def tn(a, b):
    return lax.dot_general(a, b, (((0,), (0,)), ((), ())), preferred_element_type=F32)


def table_kernel(owners, cap, seqs, cand, me_ref, src, pos, rows, counts, relay_in, relay_out, fill):
    me = me_ref[0]
    slots = owners * cap
    for b in range(BLOCKS):

        def clear_slot(s, _):
            src[b * slots + s] = -1
            return 0

        lax.fori_loop(0, slots, clear_slot, 0)

        def clear_fill(o, _):
            fill[o] = 0
            return 0

        lax.fori_loop(0, owners, clear_fill, 0)
        for k in range(8):
            counts[b * 8 + k] = 0

        def one_home(h, _):
            def one_seq(j, _):
                c = cand[(h * seqs + j) * BLOCKS + b]
                o = lax.rem(c, owners)
                k = lax.div(c, owners)
                stamp = h * (cap + 1)
                before = fill[o]
                r = jnp.minimum(jnp.maximum(before - stamp, 0), cap - 1)
                fill[o] = stamp + r + 1

                @pl.when(h == me)
                def _():
                    src[b * slots + o * cap + r] = j
                    pos[b * seqs + j] = o * cap + r

                @pl.when(o == me)
                def _():
                    n = jnp.minimum(counts[b * 8 + k], OWN_CAP - 1)
                    rows[b * KINDS * OWN_CAP + k * OWN_CAP + n] = h * cap + r
                    counts[b * 8 + k] = n + 1

                return 0

            return lax.fori_loop(0, seqs, one_seq, 0)

        lax.fori_loop(0, owners, one_home, 0)
        for k in range(KINDS):
            base = b * KINDS * OWN_CAP + k * OWN_CAP
            for i in range(1, OWN_CAP):
                rows[base + i] = jnp.where(
                    i < counts[b * 8 + k], rows[base + i], rows[base + i - 1]
                )

        def fill_slot(s, last):
            now = src[b * slots + s]
            now = jnp.where(now < 0, last, now)
            src[b * slots + s] = now
            return now

        lax.fori_loop(0, slots, fill_slot, 0)

    def relays(s, _):
        relay_in[s] = pos[src[slots + s]]
        relay_out[s] = pos[seqs + src[s]]
        return 0

    lax.fori_loop(0, slots, relays, 0)


def make_tables(group, me, owners, cap, seqs):
    slots = owners * cap

    def kernel(*refs):
        table_kernel(owners, cap, seqs, *refs)

    smem = pl.BlockSpec(memory_space=pltpu.SMEM)
    shape = lambda n: jax.ShapeDtypeStruct((n,), jnp.int32)
    return pl.pallas_call(
        kernel,
        in_specs=[smem, smem],
        out_specs=[smem] * 6,
        out_shape=[
            shape(BLOCKS * slots),
            shape(BLOCKS * seqs),
            shape(BLOCKS * KINDS * OWN_CAP),
            shape(BLOCKS * 8),
            shape(slots),
            shape(slots),
        ],
        scratch_shapes=[pltpu.SMEM((max(owners, 8),), jnp.int32)],
        name="tables",
    )(group, me)


def permute_rows(table, source, start, count):
    length, width = source.shape[1:]

    def kernel(table_ref, in_ref, out_ref):
        out_ref[...] = in_ref[...]

    return pl.pallas_call(
        kernel,
        grid_spec=pltpu.PrefetchScalarGridSpec(
            num_scalar_prefetch=1,
            grid=(count,),
            in_specs=[pl.BlockSpec((1, length, width), lambda i, t: (t[start + i], 0, 0))],
            out_specs=pl.BlockSpec((1, length, width), lambda i, t: (i, 0, 0)),
        ),
        out_shape=jax.ShapeDtypeStruct((count, length, width), source.dtype),
        compiler_params=params_of(1),
        cost_estimate=pl.CostEstimate(
            flops=0, transcendentals=0, bytes_accessed=4 * count * length * width
        ),
        name="permute",
    )(table, source)


def norm_forward(summed, gain_row, shift_row):
    center = summed - jnp.mean(summed, axis=-1, keepdims=True)
    spread = jnp.mean(center * center, axis=-1, keepdims=True)
    scale = lax.rsqrt(spread + 1e-05)
    normed = center * scale
    return normed, normed * gain_row + shift_row, scale


def finish_forward(x, branch, gain_row, shift_row, y_ref, zn_ref, rstd_ref):
    normed, result, scale = norm_forward(x.astype(F32) + branch, gain_row, shift_row)
    y_ref[0] = result.astype(BF16)
    zn_ref[0] = normed.astype(BF16)
    rstd_ref[0] = jnp.broadcast_to(scale, rstd_ref.shape[1:])


def norm_backward(dy_ref, zn_ref, rstd_ref, gain_row):
    dy = dy_ref[0].astype(F32)
    normed = zn_ref[0].astype(F32)
    scale = rstd_ref[0][:, :1]
    scaled = dy * gain_row
    first = jnp.mean(scaled, axis=-1, keepdims=True)
    second = jnp.mean(scaled * normed, axis=-1, keepdims=True)
    gain_grad = jnp.sum(dy * normed, axis=0, keepdims=True)
    shift_grad = jnp.sum(dy, axis=0, keepdims=True)
    return (scaled - first - normed * second) * scale, gain_grad, shift_grad


def head_masks(length):
    lane = lax.broadcasted_iota(jnp.int32, (length, LANES), 1)
    low = lane < LANES // 2
    return low


def attention_forward(b, tables, x, weights, norms, y_in):
    rows, counts = tables
    attn_qkv, attn_out = weights
    gains, shifts = norms
    slots, length, width = x.shape
    score_scale = (width // HEADS) ** (-0.5)
    base = b * KINDS * OWN_CAP

    def kernel(rows_ref, counts_ref, x_ref, qkv_w, out_w, gain, shift, *rest):
        y_ref, qkv_ref, o_ref, zn_ref, rstd_ref = rest[-5:]
        i = pl.program_id(0)

        @pl.when(i < counts_ref[b * 8])
        def _():
            xv = x_ref[0]
            for part in range(3):
                cols = slice(part * width, (part + 1) * width)
                qkv_ref[0, :, cols] = nn(xv, qkv_w[:, cols]).astype(BF16)
            low = head_masks(length)
            zero = jnp.zeros((), BF16)
            for pair in range(width // LANES):
                at = pair * LANES
                q2 = qkv_ref[0, :, at : at + LANES] * jnp.asarray(score_scale, BF16)
                k2 = qkv_ref[0, :, width + at : width + at + LANES]
                v2 = qkv_ref[0, :, 2 * width + at : 2 * width + at + LANES]
                mixed = []
                for half in range(2):
                    qm = jnp.where(low if half == 0 else ~low, q2, zero)
                    s = nt(qm, k2)
                    e = jnp.exp(s - jnp.max(s, axis=-1, keepdims=True))
                    total = jnp.sum(e, axis=-1, keepdims=True)
                    mixed.append(nn(e.astype(BF16), v2) / total)
                o_ref[0, :, at : at + LANES] = jnp.where(low, mixed[0], mixed[1]).astype(BF16)
            branch = nn(o_ref[0], out_w[...])
            finish_forward(
                xv, branch, gain[0:1, :], shift[0:1, :], y_ref, zn_ref, rstd_ref
            )

    def at_row(i, r, c):
        return (r[base + i], 0, 0)

    def at_step(i, r, c):
        return (jnp.minimum(i, c[b * 8] - 1), 0, 0)

    seq = (1, length, width)
    in_specs = [
        pl.BlockSpec(seq, at_row),
        pl.BlockSpec(
            (None, None, width, 3 * width), lambda i, r, c: (b, 0, 0, 0), pipeline_mode=pl.Buffered(1)
        ),
        pl.BlockSpec(
            (None, None, width, width), lambda i, r, c: (b, 0, 0, 0), pipeline_mode=pl.Buffered(1)
        ),
        pl.BlockSpec((8, width), lambda i, r, c: (0, 0)),
        pl.BlockSpec((8, width), lambda i, r, c: (0, 0)),
    ]
    args = [rows, counts, x, attn_qkv, attn_out, gains, shifts]
    alias = {}
    if y_in is not None:
        in_specs.append(pl.BlockSpec(memory_space=pl.ANY))
        alias = {len(args): 0}
        args.append(y_in)
    flops = OWN_CAP * length * width * (8 * width + 4 * length)
    return pl.pallas_call(
        kernel,
        grid_spec=pltpu.PrefetchScalarGridSpec(
            num_scalar_prefetch=2,
            grid=(OWN_CAP,),
            in_specs=in_specs,
            out_specs=[
                pl.BlockSpec(seq, at_row),
                pl.BlockSpec((1, length, 3 * width), at_step),
                pl.BlockSpec(seq, at_step),
                pl.BlockSpec(seq, at_step),
                pl.BlockSpec((1, length, LANES), at_step),
            ],
        ),
        out_shape=[
            jax.ShapeDtypeStruct((slots, length, width), BF16),
            jax.ShapeDtypeStruct((OWN_CAP, length, 3 * width), BF16),
            jax.ShapeDtypeStruct((OWN_CAP, length, width), BF16),
            jax.ShapeDtypeStruct((OWN_CAP, length, width), BF16),
            jax.ShapeDtypeStruct((OWN_CAP, length, LANES), F32),
        ],
        input_output_aliases=alias,
        compiler_params=params_of(1),
        cost_estimate=pl.CostEstimate(
            flops=2 * flops, transcendentals=OWN_CAP * HEADS * length * length, bytes_accessed=30 * 2**20
        ),
        name="attention_forward",
    )(*args)


def attention_backward(b, tables, x, dy, kept, weights, gains, dx_in):
    rows, counts = tables
    attn_qkv, attn_out = weights
    qkv, o, zn, rstd = kept
    slots, length, width = x.shape
    score_scale = (width // HEADS) ** (-0.5)
    base = b * KINDS * OWN_CAP

    def kernel(rows_ref, counts_ref, x_ref, dy_ref, qkv_ref, o_ref, zn_ref, rstd_ref, qkv_w, out_w, gain, *rest):
        dx_ref, dqkv_w_ref, dout_w_ref, small_ref, acc_qkv, acc_out, do_scr, dqkv_scr = rest[-8:]
        i = pl.program_id(0)

        @pl.when(i == 0)
        def _():
            acc_qkv[...] = jnp.zeros_like(acc_qkv)
            acc_out[...] = jnp.zeros_like(acc_out)
            small_ref[...] = jnp.zeros_like(small_ref)

        @pl.when(i < counts_ref[b * 8])
        def _():
            dz, gain_grad, shift_grad = norm_backward(dy_ref, zn_ref, rstd_ref, gain[0:1, :])
            small_ref[0:1, :] += gain_grad
            small_ref[1:2, :] += shift_grad
            dh = dz.astype(BF16)
            acc_out[...] += tn(o_ref[0], dh)
            do_scr[...] = nt(dh, out_w[...]).astype(BF16)
            low = head_masks(length)
            zero = jnp.zeros((), BF16)
            for pair in range(width // LANES):
                at = pair * LANES
                q2 = qkv_ref[0, :, at : at + LANES] * jnp.asarray(score_scale, BF16)
                k2 = qkv_ref[0, :, width + at : width + at + LANES]
                v2 = qkv_ref[0, :, 2 * width + at : 2 * width + at + LANES]
                do2 = do_scr[:, at : at + LANES]
                dqs, dks, dvs = [], [], []
                for half in range(2):
                    mask = low if half == 0 else ~low
                    st = nt(jnp.where(mask, k2, zero), q2)
                    e = jnp.exp(st - jnp.max(st, axis=0, keepdims=True))
                    p = e * (1.0 / jnp.sum(e, axis=0, keepdims=True))
                    dvs.append(nn(p.astype(BF16), do2))
                    t = p * nt(jnp.where(mask, v2, zero), do2)
                    ds = (t - p * jnp.sum(t, axis=0, keepdims=True)).astype(BF16)
                    dks.append(nn(ds, q2))
                    dqs.append(tn(ds, k2))
                dqkv_scr[:, at : at + LANES] = (jnp.where(low, dqs[0], dqs[1]) * score_scale).astype(BF16)
                dqkv_scr[:, width + at : width + at + LANES] = jnp.where(low, dks[0], dks[1]).astype(BF16)
                dqkv_scr[:, 2 * width + at : 2 * width + at + LANES] = jnp.where(low, dvs[0], dvs[1]).astype(BF16)
            xv = x_ref[0]
            total = dz
            for part in range(3):
                cols = slice(part * width, (part + 1) * width)
                piece = dqkv_scr[:, cols]
                acc_qkv[:, cols] += tn(xv, piece)
                total = total + nt(piece, qkv_w[:, cols])
            dx_ref[0] = total.astype(BF16)

        @pl.when(i == OWN_CAP - 1)
        def _():
            dqkv_w_ref[...] = acc_qkv[...].astype(BF16)
            dout_w_ref[...] = acc_out[...].astype(BF16)

    def at_row(i, r, c):
        return (r[base + i], 0, 0)

    def at_step(i, r, c):
        return (jnp.minimum(i, c[b * 8] - 1), 0, 0)

    def whole(i, r, c):
        return (0, 0)

    seq = (1, length, width)
    in_specs = [
        pl.BlockSpec(seq, at_row),
        pl.BlockSpec(seq, at_row),
        pl.BlockSpec((1, length, 3 * width), at_step),
        pl.BlockSpec(seq, at_step),
        pl.BlockSpec(seq, at_step),
        pl.BlockSpec((1, length, LANES), at_step),
        pl.BlockSpec(
            (None, None, width, 3 * width), lambda i, r, c: (b, 0, 0, 0), pipeline_mode=pl.Buffered(1)
        ),
        pl.BlockSpec(
            (None, None, width, width), lambda i, r, c: (b, 0, 0, 0), pipeline_mode=pl.Buffered(1)
        ),
        pl.BlockSpec((8, width), whole),
    ]
    args = [rows, counts, x, dy, qkv, o, zn, rstd, attn_qkv, attn_out, gains]
    alias = {}
    if dx_in is not None:
        in_specs.append(pl.BlockSpec(memory_space=pl.ANY))
        alias = {len(args): 0}
        args.append(dx_in)
    flops = 2 * OWN_CAP * length * width * (8 * width + 4 * length)
    return pl.pallas_call(
        kernel,
        grid_spec=pltpu.PrefetchScalarGridSpec(
            num_scalar_prefetch=2,
            grid=(OWN_CAP,),
            in_specs=in_specs,
            out_specs=[
                pl.BlockSpec(seq, at_row),
                pl.BlockSpec((width, 3 * width), whole),
                pl.BlockSpec((width, width), whole),
                pl.BlockSpec((8, width), whole),
            ],
            scratch_shapes=[
                pltpu.VMEM((width, 3 * width), F32),
                pltpu.VMEM((width, width), F32),
                pltpu.VMEM((length, width), BF16),
                pltpu.VMEM((length, 3 * width), BF16),
            ],
        ),
        out_shape=[
            jax.ShapeDtypeStruct((slots, length, width), BF16),
            jax.ShapeDtypeStruct((width, 3 * width), BF16),
            jax.ShapeDtypeStruct((width, width), BF16),
            jax.ShapeDtypeStruct((8, width), F32),
        ],
        input_output_aliases=alias,
        compiler_params=params_of(1),
        cost_estimate=pl.CostEstimate(
            flops=2 * flops, transcendentals=OWN_CAP * HEADS * length * length, bytes_accessed=40 * 2**20
        ),
        name="attention_backward",
    )(*args)


def feed_forward(b, tables, x, weights, norms, y_in):
    rows, counts = tables
    ffn_up, ffn_down = weights
    gains, shifts = norms
    slots, length, width = x.shape
    hidden = ffn_up.shape[-1]
    parts = hidden // FF_PART
    kind = KINDS - 1
    base = b * KINDS * OWN_CAP + kind * OWN_CAP

    def kernel(rows_ref, counts_ref, x_ref, up, down, gain, shift, *rest):
        y_ref, g_ref, slope_ref, zn_ref, rstd_ref, x_scr, h_scr = rest[-7:]
        c, i = pl.program_id(0), pl.program_id(1)

        @pl.when(i < counts_ref[b * 8 + kind])
        def _():
            @pl.when(c == 0)
            def _():
                x_scr[i] = x_ref[0]

            xv = x_scr[i]
            branch = None
            for sub in range(FF_PART // FF_SUB):
                cols = slice(sub * FF_SUB, (sub + 1) * FF_SUB)
                a = nn(xv, up[:, cols])
                phi = 0.5 + 0.5 * lax.erf(a * (0.5**0.5))
                slope = phi + a * (jnp.exp(a * a * -0.5) * 0.3989422804014327)
                g = (a * phi).astype(BF16)
                g_ref[0, :, cols] = g
                slope_ref[0, :, cols] = slope.astype(BF16)
                term = nn(g, down[cols, :])
                branch = term if branch is None else branch + term

            @pl.when(c == 0)
            def _():
                h_scr[i] = branch

            @pl.when(jnp.logical_and(c > 0, c < parts - 1))
            def _():
                h_scr[i] += branch

            @pl.when(c == parts - 1)
            def _():
                finish_forward(
                    xv,
                    h_scr[i] + branch,
                    gain[kind : kind + 1, :],
                    shift[kind : kind + 1, :],
                    y_ref,
                    zn_ref,
                    rstd_ref,
                )

    def in_row(c, i, r, n):
        return (r[base + jnp.where(c == 0, i, OWN_CAP - 1)], 0, 0)

    def out_row(c, i, r, n):
        return (r[base + jnp.where(c == parts - 1, i, 0)], 0, 0)

    def out_step(c, i, r, n):
        return (jnp.where(c == parts - 1, jnp.minimum(i, n[b * 8 + kind] - 1), 0), 0, 0)

    def part_step(c, i, r, n):
        return (jnp.minimum(i, n[b * 8 + kind] - 1), 0, c)

    seq = (1, length, width)
    in_specs = [
        pl.BlockSpec(seq, in_row),
        pl.BlockSpec((None, None, width, FF_PART), lambda c, i, r, n: (b, 0, 0, c)),
        pl.BlockSpec((None, None, FF_PART, width), lambda c, i, r, n: (b, 0, c, 0)),
        pl.BlockSpec((8, width), lambda c, i, r, n: (0, 0)),
        pl.BlockSpec((8, width), lambda c, i, r, n: (0, 0)),
    ]
    args = [rows, counts, x, ffn_up, ffn_down, gains, shifts]
    alias = {}
    if y_in is not None:
        in_specs.append(pl.BlockSpec(memory_space=pl.ANY))
        alias = {len(args): 0}
        args.append(y_in)
    return pl.pallas_call(
        kernel,
        grid_spec=pltpu.PrefetchScalarGridSpec(
            num_scalar_prefetch=2,
            grid=(parts, OWN_CAP),
            in_specs=in_specs,
            out_specs=[
                pl.BlockSpec(seq, out_row),
                pl.BlockSpec((1, length, FF_PART), part_step),
                pl.BlockSpec((1, length, FF_PART), part_step),
                pl.BlockSpec(seq, out_step),
                pl.BlockSpec((1, length, LANES), out_step),
            ],
            scratch_shapes=[
                pltpu.VMEM((OWN_CAP, length, width), BF16),
                pltpu.VMEM((OWN_CAP, length, width), F32),
            ],
        ),
        out_shape=[
            jax.ShapeDtypeStruct((slots, length, width), BF16),
            jax.ShapeDtypeStruct((OWN_CAP, length, hidden), BF16),
            jax.ShapeDtypeStruct((OWN_CAP, length, hidden), BF16),
            jax.ShapeDtypeStruct((OWN_CAP, length, width), BF16),
            jax.ShapeDtypeStruct((OWN_CAP, length, LANES), F32),
        ],
        input_output_aliases=alias,
        compiler_params=params_of(2),
        cost_estimate=pl.CostEstimate(
            flops=4 * OWN_CAP * length * width * hidden,
            transcendentals=2 * OWN_CAP * length * hidden,
            bytes_accessed=40 * 2**20,
        ),
        name="feed_forward",
    )(*args)


def feed_backward(b, tables, x, dy, kept, weights, gains, dx_in):
    rows, counts = tables
    ffn_up, ffn_down = weights
    g, slope, zn, rstd = kept
    slots, length, width = x.shape
    hidden = ffn_up.shape[-1]
    parts = hidden // FF_PART
    kind = KINDS - 1
    base = b * KINDS * OWN_CAP + kind * OWN_CAP

    def kernel(
        rows_ref, counts_ref, x_ref, dy_ref, g_ref, slope_ref, zn_ref, rstd_ref, up, down, gain, *rest
    ):
        dx_ref, dup_ref, ddown_ref, small_ref, x_scr, dh_scr, dx_scr, acc_up, acc_down = rest[-9:]
        c, i = pl.program_id(0), pl.program_id(1)

        @pl.when(jnp.logical_and(c == 0, i == 0))
        def _():
            small_ref[...] = jnp.zeros_like(small_ref)

        @pl.when(i == 0)
        def _():
            acc_up[...] = jnp.zeros_like(acc_up)
            acc_down[...] = jnp.zeros_like(acc_down)

        @pl.when(i < counts_ref[b * 8 + kind])
        def _():
            @pl.when(c == 0)
            def _():
                dz, gain_grad, shift_grad = norm_backward(
                    dy_ref, zn_ref, rstd_ref, gain[kind : kind + 1, :]
                )
                small_ref[0:1, :] += gain_grad
                small_ref[1:2, :] += shift_grad
                x_scr[i] = x_ref[0]
                dh_scr[i] = dz.astype(BF16)
                dx_scr[i] = dz

            xv = x_scr[i]
            dh = dh_scr[i]
            total = None
            for sub in range(FF_PART // FF_SUB):
                cols = slice(sub * FF_SUB, (sub + 1) * FF_SUB)
                dg = nt(dh, down[cols, :])
                da = (dg * slope_ref[0, :, cols].astype(F32)).astype(BF16)
                acc_up[:, cols] += tn(xv, da)
                acc_down[cols, :] += tn(g_ref[0, :, cols], dh)
                term = nt(da, up[:, cols])
                total = term if total is None else total + term

            @pl.when(c < parts - 1)
            def _():
                dx_scr[i] += total

            @pl.when(c == parts - 1)
            def _():
                dx_ref[0] = (dx_scr[i] + total).astype(BF16)

        @pl.when(i == OWN_CAP - 1)
        def _():
            dup_ref[...] = acc_up[...].astype(BF16)
            ddown_ref[...] = acc_down[...].astype(BF16)

    def in_row(c, i, r, n):
        return (r[base + jnp.where(c == 0, i, OWN_CAP - 1)], 0, 0)

    def in_step(c, i, r, n):
        last = n[b * 8 + kind] - 1
        return (jnp.where(c == 0, jnp.minimum(i, last), last), 0, 0)

    def out_row(c, i, r, n):
        return (r[base + jnp.where(c == parts - 1, i, 0)], 0, 0)

    def part_step(c, i, r, n):
        return (jnp.minimum(i, n[b * 8 + kind] - 1), 0, c)

    seq = (1, length, width)
    in_specs = [
        pl.BlockSpec(seq, in_row),
        pl.BlockSpec(seq, in_row),
        pl.BlockSpec((1, length, FF_PART), part_step),
        pl.BlockSpec((1, length, FF_PART), part_step),
        pl.BlockSpec(seq, in_step),
        pl.BlockSpec((1, length, LANES), in_step),
        pl.BlockSpec((None, None, width, FF_PART), lambda c, i, r, n: (b, 0, 0, c)),
        pl.BlockSpec((None, None, FF_PART, width), lambda c, i, r, n: (b, 0, c, 0)),
        pl.BlockSpec((8, width), lambda c, i, r, n: (0, 0)),
    ]
    args = [rows, counts, x, dy, g, slope, zn, rstd, ffn_up, ffn_down, gains]
    alias = {}
    if dx_in is not None:
        in_specs.append(pl.BlockSpec(memory_space=pl.ANY))
        alias = {len(args): 0}
        args.append(dx_in)
    return pl.pallas_call(
        kernel,
        grid_spec=pltpu.PrefetchScalarGridSpec(
            num_scalar_prefetch=2,
            grid=(parts, OWN_CAP),
            in_specs=in_specs,
            out_specs=[
                pl.BlockSpec(seq, out_row),
                pl.BlockSpec((width, FF_PART), lambda c, i, r, n: (0, c)),
                pl.BlockSpec((FF_PART, width), lambda c, i, r, n: (c, 0)),
                pl.BlockSpec((8, width), lambda c, i, r, n: (0, 0)),
            ],
            scratch_shapes=[
                pltpu.VMEM((OWN_CAP, length, width), BF16),
                pltpu.VMEM((OWN_CAP, length, width), BF16),
                pltpu.VMEM((OWN_CAP, length, width), F32),
                pltpu.VMEM((width, FF_PART), F32),
                pltpu.VMEM((FF_PART, width), F32),
            ],
        ),
        out_shape=[
            jax.ShapeDtypeStruct((slots, length, width), BF16),
            jax.ShapeDtypeStruct((width, hidden), BF16),
            jax.ShapeDtypeStruct((hidden, width), BF16),
            jax.ShapeDtypeStruct((8, width), F32),
        ],
        input_output_aliases=alias,
        compiler_params=params_of(2),
        cost_estimate=pl.CostEstimate(
            flops=8 * OWN_CAP * length * width * hidden,
            transcendentals=0,
            bytes_accessed=50 * 2**20,
        ),
        name="feed_backward",
    )(*args)


PAD = 8
ROW_TILE = 128
COL_TILE = 256


def fill_padded(padded, values):
    length = values.shape[0]
    edge = jnp.zeros((PAD, values.shape[1]), F32)
    padded[0:PAD, :] = edge
    padded[PAD + length : PAD + length + PAD, :] = edge
    padded[PAD : PAD + length, :] = values


def conv_forward(b, tables, x, weights, norms, y_in):
    rows, counts = tables
    taps, conv_point = weights
    gains, shifts = norms
    slots, length, width = x.shape
    base = b * KINDS * OWN_CAP + OWN_CAP
    steps = (KINDS - 2) * OWN_CAP

    def kernel(rows_ref, counts_ref, x_ref, point, taps_ref, gain, shift, *rest):
        y_ref, u_ref, zn_ref, rstd_ref, xpad = rest[-5:]
        step = pl.program_id(0)
        which, j = step // OWN_CAP, step % OWN_CAP
        for kind in range(1, KINDS - 1):
            taps_n = 2 * kind + 1
            first = kind * kind - 1

            @pl.when(jnp.logical_and(which == kind - 1, j < counts_ref[b * 8 + kind]))
            def _():
                fill_padded(xpad, x_ref[0].astype(F32))
                for r in range(0, length, ROW_TILE):
                    for col in range(0, width, COL_TILE):
                        cols = slice(col, col + COL_TILE)
                        mixed = None
                        for t in range(taps_n):
                            start = PAD + r + t - kind
                            term = xpad[start : start + ROW_TILE, cols] * taps_ref[first + t : first + t + 1, cols]
                            mixed = term if mixed is None else mixed + term
                        u_ref[0, r : r + ROW_TILE, cols] = mixed.astype(BF16)
                branch = nn(u_ref[0], point[...])
                finish_forward(
                    x_ref[0],
                    branch,
                    gain[kind : kind + 1, :],
                    shift[kind : kind + 1, :],
                    y_ref,
                    zn_ref,
                    rstd_ref,
                )

    def at_row(i, r, c):
        return (r[base + i], 0, 0)

    def at_step(i, r, c):
        which = i // OWN_CAP
        last = c[b * 8 + 1 + which] - 1
        return (which * OWN_CAP + jnp.minimum(i % OWN_CAP, last), 0, 0)

    def whole(i, r, c):
        return (0, 0)

    seq = (1, length, width)
    in_specs = [
        pl.BlockSpec(seq, at_row),
        pl.BlockSpec((None, None, None, width, width), lambda i, r, c: (b, 0, i // OWN_CAP, 0, 0)),
        pl.BlockSpec((16, width), whole),
        pl.BlockSpec((8, width), whole),
        pl.BlockSpec((8, width), whole),
    ]
    args = [rows, counts, x, conv_point, taps, gains, shifts]
    alias = {}
    if y_in is not None:
        in_specs.append(pl.BlockSpec(memory_space=pl.ANY))
        alias = {len(args): 0}
        args.append(y_in)
    return pl.pallas_call(
        kernel,
        grid_spec=pltpu.PrefetchScalarGridSpec(
            num_scalar_prefetch=2,
            grid=(steps,),
            in_specs=in_specs,
            out_specs=[
                pl.BlockSpec(seq, at_row),
                pl.BlockSpec(seq, at_step),
                pl.BlockSpec(seq, at_step),
                pl.BlockSpec((1, length, LANES), at_step),
            ],
            scratch_shapes=[pltpu.VMEM((length + 2 * PAD, width), F32)],
        ),
        out_shape=[
            jax.ShapeDtypeStruct((slots, length, width), BF16),
            jax.ShapeDtypeStruct((steps, length, width), BF16),
            jax.ShapeDtypeStruct((steps, length, width), BF16),
            jax.ShapeDtypeStruct((steps, length, LANES), F32),
        ],
        input_output_aliases=alias,
        compiler_params=params_of(1),
        cost_estimate=pl.CostEstimate(
            flops=2 * steps * length * width * width, transcendentals=0, bytes_accessed=36 * 2**20
        ),
        name="conv_forward",
    )(*args)


def conv_backward(b, tables, x, dy, kept, weights, gains, dx_in):
    rows, counts = tables
    taps, conv_point = weights
    u, zn, rstd = kept
    slots, length, width = x.shape
    base = b * KINDS * OWN_CAP + OWN_CAP
    steps = (KINDS - 2) * OWN_CAP

    def kernel(rows_ref, counts_ref, x_ref, dy_ref, u_ref, zn_ref, rstd_ref, point, taps_ref, gain, *rest):
        dx_ref, dpoint_ref, small_ref, acc, xpad, dupad, dz_scr = rest[-7:]
        step = pl.program_id(0)
        which, j = step // OWN_CAP, step % OWN_CAP

        @pl.when(step == 0)
        def _():
            small_ref[...] = jnp.zeros_like(small_ref)

        @pl.when(j == 0)
        def _():
            acc[...] = jnp.zeros_like(acc)

        for kind in range(1, KINDS - 1):
            taps_n = 2 * kind + 1
            first = kind * kind - 1

            @pl.when(jnp.logical_and(which == kind - 1, j < counts_ref[b * 8 + kind]))
            def _():
                dz, gain_grad, shift_grad = norm_backward(
                    dy_ref, zn_ref, rstd_ref, gain[kind : kind + 1, :]
                )
                small_ref[14 + kind : 15 + kind, :] += gain_grad
                small_ref[17 + kind : 18 + kind, :] += shift_grad
                dz_scr[...] = dz
                dh = dz.astype(BF16)
                acc[...] += tn(u_ref[0], dh)
                fill_padded(xpad, x_ref[0].astype(F32))
                fill_padded(dupad, nt(dh, point[...]))
                for col in range(0, width, COL_TILE):
                    cols = slice(col, col + COL_TILE)
                    sums = [None] * taps_n
                    for r in range(0, length, ROW_TILE):
                        here = dupad[PAD + r : PAD + r + ROW_TILE, cols]
                        total = dz_scr[r : r + ROW_TILE, cols]
                        for t in range(taps_n):
                            back = PAD + r - t + kind
                            total = total + dupad[back : back + ROW_TILE, cols] * taps_ref[first + t : first + t + 1, cols]
                            ahead = PAD + r + t - kind
                            part = jnp.sum(
                                xpad[ahead : ahead + ROW_TILE, cols] * here, axis=0, keepdims=True
                            )
                            sums[t] = part if sums[t] is None else sums[t] + part
                        dx_ref[0, r : r + ROW_TILE, cols] = total.astype(BF16)
                    for t in range(taps_n):
                        small_ref[first + t : first + t + 1, cols] += sums[t]

        @pl.when(j == OWN_CAP - 1)
        def _():
            dpoint_ref[...] = acc[...].astype(BF16)

    def at_row(i, r, c):
        return (r[base + i], 0, 0)

    def at_step(i, r, c):
        which = i // OWN_CAP
        last = c[b * 8 + 1 + which] - 1
        return (which * OWN_CAP + jnp.minimum(i % OWN_CAP, last), 0, 0)

    def whole(i, r, c):
        return (0, 0)

    seq = (1, length, width)
    in_specs = [
        pl.BlockSpec(seq, at_row),
        pl.BlockSpec(seq, at_row),
        pl.BlockSpec(seq, at_step),
        pl.BlockSpec(seq, at_step),
        pl.BlockSpec((1, length, LANES), at_step),
        pl.BlockSpec((None, None, None, width, width), lambda i, r, c: (b, 0, i // OWN_CAP, 0, 0)),
        pl.BlockSpec((16, width), whole),
        pl.BlockSpec((8, width), whole),
    ]
    args = [rows, counts, x, dy, u, zn, rstd, conv_point, taps, gains]
    alias = {}
    if dx_in is not None:
        in_specs.append(pl.BlockSpec(memory_space=pl.ANY))
        alias = {len(args): 0}
        args.append(dx_in)
    return pl.pallas_call(
        kernel,
        grid_spec=pltpu.PrefetchScalarGridSpec(
            num_scalar_prefetch=2,
            grid=(steps,),
            in_specs=in_specs,
            out_specs=[
                pl.BlockSpec(seq, at_row),
                pl.BlockSpec((None, width, width), lambda i, r, c: (i // OWN_CAP, 0, 0)),
                pl.BlockSpec((24, width), whole),
            ],
            scratch_shapes=[
                pltpu.VMEM((width, width), F32),
                pltpu.VMEM((length + 2 * PAD, width), F32),
                pltpu.VMEM((length + 2 * PAD, width), F32),
                pltpu.VMEM((length, width), F32),
            ],
        ),
        out_shape=[
            jax.ShapeDtypeStruct((slots, length, width), BF16),
            jax.ShapeDtypeStruct((KINDS - 2, width, width), BF16),
            jax.ShapeDtypeStruct((24, width), F32),
        ],
        input_output_aliases=alias,
        compiler_params=params_of(1),
        cost_estimate=pl.CostEstimate(
            flops=4 * steps * length * width * width, transcendentals=0, bytes_accessed=50 * 2**20
        ),
        name="conv_backward",
    )(*args)


def owner_forward(b, tables, x, weights, small_weights):
    attn_qkv, attn_out, ffn_up, ffn_down, conv_point = weights
    taps, gains, shifts = small_weights
    norms = (gains, shifts)
    y, g, slope, zn_f, rstd_f = feed_forward(b, tables, x, (ffn_up, ffn_down), norms, None)
    y, qkv, o, zn_a, rstd_a = attention_forward(b, tables, x, (attn_qkv, attn_out), norms, y)
    y, u, zn_c, rstd_c = conv_forward(b, tables, x, (taps, conv_point), norms, y)
    return y, ((g, slope, zn_f, rstd_f), (qkv, o, zn_a, rstd_a), (u, zn_c, rstd_c))


def owner_backward(b, tables, x, dy, kept, weights, small_weights):
    attn_qkv, attn_out, ffn_up, ffn_down, conv_point = weights
    taps, gains, shifts = small_weights
    kept_f, kept_a, kept_c = kept
    dx, dup, ddown, small_f = feed_backward(b, tables, x, dy, kept_f, (ffn_up, ffn_down), gains, None)
    dx, dqkv, dout, small_a = attention_backward(
        b, tables, x, dy, kept_a, (attn_qkv, attn_out), gains, dx
    )
    dx, dpoint, small_c = conv_backward(b, tables, x, dy, kept_c, (taps, conv_point), gains, dx)
    small = jnp.concatenate(
        [
            small_c[:15],
            small_a[0:1],
            small_c[15:18],
            small_f[0:1],
            small_a[1:2],
            small_c[18:21],
            small_f[1:2],
        ]
    )
    return dx, (dup, ddown, dqkv, dout, dpoint, small)


def small_params(b, conv_taps, norm_gain, norm_bias):
    taps = jnp.pad(conv_taps[b, 0].astype(F32), ((0, 1), (0, 0)))
    gains = jnp.pad(norm_gain[b, 0].astype(F32), ((0, 3), (0, 0)))
    shifts = jnp.pad(norm_bias[b, 0].astype(F32), ((0, 3), (0, 0)))
    return taps, gains, shifts


def exchange(rows):
    return lax.all_to_all(rows, "op", split_axis=0, concat_axis=0, tiled=True)


def per_device(
    inputs,
    candidate,
    attn_qkv,
    attn_out,
    ffn_up,
    ffn_down,
    conv_taps,
    conv_point,
    norm_gain,
    norm_bias,
    cotangent,
):
    owners = lax.axis_size("op")
    groups = lax.axis_size("dp")
    seqs = inputs.shape[0]
    width = inputs.shape[-1]
    cap = -(-seqs // owners)
    slots = owners * cap
    weights = (attn_qkv, attn_out, ffn_up, ffn_down, conv_point)
    smalls = [small_params(b, conv_taps, norm_gain, norm_bias) for b in range(BLOCKS)]
    me = lax.axis_index("op")
    everyone = lax.all_gather(candidate, ("dp", "op"), axis=0, tiled=True)
    group = lax.dynamic_slice_in_dim(
        everyone, lax.axis_index("dp") * (owners * seqs), owners * seqs, axis=0
    )
    own = jnp.arange(KINDS, dtype=jnp.int32) * owners + me
    totals = jnp.sum((everyone[:, :, None] == own).astype(F32), axis=0)
    src, pos, rows, counts, relay_in, relay_out = make_tables(
        group.reshape(-1), me.astype(jnp.int32)[None], owners, cap, seqs
    )
    tables = (rows, counts)

    x0 = exchange(permute_rows(src, inputs, 0, slots))
    dy1 = exchange(permute_rows(src, cotangent, slots, slots))
    y0, kept0 = owner_forward(0, tables, x0, weights, smalls[0])
    x1 = exchange(permute_rows(relay_in, exchange(y0), 0, slots))
    y1, kept1 = owner_forward(1, tables, x1, weights, smalls[1])
    outputs = permute_rows(pos, exchange(y1), seqs, seqs)
    dx1, grads1 = owner_backward(1, tables, x1, dy1, kept1, weights, smalls[1])
    dy0 = exchange(permute_rows(relay_out, exchange(dx1), 0, slots))
    dx0, grads0 = owner_backward(0, tables, x0, dy0, kept0, weights, smalls[0])
    input_grad = permute_rows(pos, exchange(dx0), 0, seqs)

    def scatter(grad, dim):
        return lax.psum_scatter(grad, "dp", scatter_dimension=dim, tiled=True).astype(F32)

    finished = [None, None]
    for b, (dup, ddown, dqkv, dout, dpoint, small) in ((1, grads1), (0, grads0)):
        total = totals[b]
        small = small.reshape(25, groups, width // groups).transpose(1, 0, 2).astype(BF16)
        small = lax.psum_scatter(small, "dp", scatter_dimension=0, tiled=True)[0].astype(F32)
        tap_total = jnp.repeat(
            total[1 : KINDS - 1], jnp.array([3, 5, 7]), total_repeat_length=15
        )
        finished[b] = (
            scatter(dqkv, 0) / total[0],
            scatter(dout, 0) / total[0],
            scatter(dup, 0) / total[KINDS - 1],
            scatter(ddown, 0) / total[KINDS - 1],
            small[:15] / tap_total[:, None],
            scatter(dpoint, 1) / total[1 : KINDS - 1, None, None],
            small[15:20] / total[:, None],
            small[20:25] / total[:, None],
        )
    grads = tuple(
        jnp.stack([finished[0][n], finished[1][n]])[:, None] for n in range(8)
    )
    return (outputs, input_grad) + grads


def solution(mesh):
    placed = (
        P(("dp", "op"), None, None),
        P(("dp", "op"), None),
        P(None, "op", None, None),
        P(None, "op", None, None),
        P(None, "op", None, None),
        P(None, "op", None, None),
        P(None, "op", None, None),
        P(None, "op", None, None, None),
        P(None, "op", None, None),
        P(None, "op", None, None),
        P(("dp", "op"), None, None),
    )
    return jax.shard_map(
        per_device,
        mesh=mesh,
        in_specs=placed,
        out_specs=(
            P(("dp", "op"), None, None),
            P(("dp", "op"), None, None),
            P(None, "op", "dp", None),
            P(None, "op", "dp", None),
            P(None, "op", "dp", None),
            P(None, "op", "dp", None),
            P(None, "op", None, "dp"),
            P(None, "op", None, "dp", None),
            P(None, "op", None, "dp"),
            P(None, "op", None, "dp"),
        ),
        check_vma=False,
    )
```

```python
import jax
import jax.numpy as jnp
from jax import lax
from jax.experimental import pallas as pl
from jax.experimental.pallas import tpu as pltpu
from jax.sharding import PartitionSpec as P

HEADS = 12
KINDS = 5
BLOCKS = 2
OWN_CAP = 3
HALVES = 2
SLOTS = KINDS * OWN_CAP
FF_PART = 768
FF_SUB = 256
LANES = 128
SMALL_ROWS = 16
BF16 = jnp.bfloat16
F32 = jnp.float32
VMEM_BYTES = 60 * 2**20


def params_of(axes):
    return pltpu.CompilerParams(
        dimension_semantics=("arbitrary",) * axes, vmem_limit_bytes=VMEM_BYTES
    )


def nn(a, b):
    return lax.dot_general(a, b, (((1,), (0,)), ((), ())), preferred_element_type=F32)


def nt(a, b):
    return lax.dot_general(a, b, (((1,), (1,)), ((), ())), preferred_element_type=F32)


def tn(a, b):
    return lax.dot_general(a, b, (((0,), (0,)), ((), ())), preferred_element_type=F32)


def home_kernel(owners, seqs, cand, send, relay, tags, color, partner, first, tally):
    for b in range(BLOCKS):

        def clear_owner(o, _):
            first[b * owners + o] = -1
            for half in range(HALVES):
                send[(b * HALVES + half) * owners + o] = -1
                relay[(b * HALVES + half) * owners + o] = -1
                tags[o * BLOCKS * HALVES + b * HALVES + half] = KINDS
            return 0

        lax.fori_loop(0, owners, clear_owner, 0)
    for half in range(HALVES):
        tally[half] = 0

    def pair_up(j, _):
        color[j] = -1
        for b in range(BLOCKS):
            o = b * owners + lax.rem(cand[j * BLOCKS + b], owners)
            other = first[o]
            partner[b * seqs + j] = other
            first[o] = j

            @pl.when(other >= 0)
            def _():
                partner[b * seqs + other] = j

        return 0

    lax.fori_loop(0, seqs, pair_up, 0)

    def give(j, shade):
        color[j] = shade
        tally[shade] = tally[shade] + 1

    def paint(j, _):
        @pl.when(color[j] < 0)
        def _():
            shade = jnp.where(tally[0] > tally[1], 1, 0).astype(jnp.int32)
            give(j, shade)
            for side in range(2):

                def more(state):
                    return state[0] >= 0

                def walk(state):
                    now, use, tone = state
                    after = partner[use * seqs + now]
                    free = jnp.logical_and(after >= 0, color[jnp.maximum(after, 0)] < 0)

                    @pl.when(free)
                    def _():
                        give(after, 1 - tone)

                    return (jnp.where(free, after, -1), 1 - use, 1 - tone)

                lax.while_loop(more, walk, (j, jnp.int32(side), shade))

        return 0

    lax.fori_loop(0, seqs, paint, 0)

    def place(j, _):
        half = color[j]
        spots = []
        for b in range(BLOCKS):
            c = cand[j * BLOCKS + b]
            o = lax.rem(c, owners)
            spots.append(o)
            send[(b * HALVES + half) * owners + o] = j
            tags[o * BLOCKS * HALVES + b * HALVES + half] = lax.div(c, owners)
        relay[half * owners + spots[1]] = spots[0]
        relay[(HALVES + half) * owners + spots[0]] = spots[1]
        return 0

    lax.fori_loop(0, seqs, place, 0)


SMEM_SPEC = pl.BlockSpec(memory_space=pltpu.SMEM)
ANY_SPEC = pl.BlockSpec(memory_space=pl.ANY)


def int_shape(n):
    return jax.ShapeDtypeStruct((n,), jnp.int32)


def home_tables(cand, owners, seqs):
    def kernel(*refs):
        home_kernel(owners, seqs, *refs)

    size = BLOCKS * HALVES * owners
    return pl.pallas_call(
        kernel,
        in_specs=[SMEM_SPEC],
        out_specs=[SMEM_SPEC] * 3,
        out_shape=[int_shape(size)] * 3,
        scratch_shapes=[
            pltpu.SMEM((seqs,), jnp.int32),
            pltpu.SMEM((BLOCKS * seqs,), jnp.int32),
            pltpu.SMEM((BLOCKS * owners,), jnp.int32),
            pltpu.SMEM((HALVES,), jnp.int32),
        ],
        name="home_tables",
    )(cand)


def owner_kernel(owners, tags, rows, counts):
    for b in range(BLOCKS):
        for half in range(HALVES):
            part = b * HALVES + half
            for k in range(8):
                counts[part * 8 + k] = 0

            def arrive(h, free):
                k = tags[h * BLOCKS * HALVES + part]
                there = k < KINDS

                @pl.when(there)
                def _():
                    n = jnp.minimum(counts[part * 8 + k], OWN_CAP - 1)
                    rows[part * SLOTS + k * OWN_CAP + n] = h
                    counts[part * 8 + k] = n + 1

                return jnp.where(there, free, h)

            free = lax.fori_loop(0, owners, arrive, jnp.int32(0))

            def spare(k, otherwise):
                return jnp.where(
                    counts[part * 8 + k] > 0, rows[part * SLOTS + k * OWN_CAP], otherwise
                )

            conv_spare = free
            for k in reversed(range(1, KINDS - 1)):
                conv_spare = spare(k, conv_spare)
            attn_spare = spare(0, conv_spare)
            feed_spare = spare(KINDS - 1, attn_spare)
            last = conv_spare
            for k, start in ((1, None), (2, None), (3, None), (0, attn_spare), (KINDS - 1, feed_spare)):
                last = last if start is None else start
                for i in range(OWN_CAP):
                    at = part * SLOTS + k * OWN_CAP + i
                    last = jnp.where(i < counts[part * 8 + k], rows[at], last)
                    rows[at] = last


def owner_tables(tags, owners):
    def kernel(*refs):
        owner_kernel(owners, *refs)

    return pl.pallas_call(
        kernel,
        in_specs=[SMEM_SPEC],
        out_specs=[SMEM_SPEC] * 2,
        out_shape=[int_shape(BLOCKS * HALVES * SLOTS), int_shape(BLOCKS * HALVES * 8)],
        name="owner_tables",
    )(tags)


def move_rows(table, starts, sources, count, scatter, name, wait_for=()):
    length, width = sources[0].shape[1:]
    each = table.shape[0] // (BLOCKS * HALVES)
    total = each * len(sources)

    def kernel(table_ref, *refs):
        ins = refs[: len(sources)]
        out_ref, buf, sem_in, sem_out = refs[-4:]

        def load(part, s):
            idx = table_ref[starts[part] + s]
            at = s if scatter else idx
            to = part * each + s
            return pltpu.make_async_copy(ins[part].at[at], buf.at[to], sem_in.at[to])

        def store(part, s):
            idx = table_ref[starts[part] + s]
            at = part * each + s
            to = idx if scatter else at
            return pltpu.make_async_copy(buf.at[at], out_ref.at[to], sem_out.at[at])

        todo = [(part, s) for part in range(len(sources)) for s in range(each)]
        for part, s in todo:

            @pl.when(table_ref[starts[part] + s] >= 0)
            def _():
                load(part, s).start()

        for part, s in todo:

            @pl.when(table_ref[starts[part] + s] >= 0)
            def _():
                load(part, s).wait()
                store(part, s).start()

        for part, s in todo:

            @pl.when(table_ref[starts[part] + s] >= 0)
            def _():
                store(part, s).wait()

    return pl.pallas_call(
        kernel,
        grid_spec=pltpu.PrefetchScalarGridSpec(
            num_scalar_prefetch=1,
            grid=(1,),
            in_specs=[ANY_SPEC] * (len(sources) + len(wait_for)),
            out_specs=ANY_SPEC,
            scratch_shapes=[
                pltpu.VMEM((total, length, width), BF16),
                pltpu.SemaphoreType.DMA((total,)),
                pltpu.SemaphoreType.DMA((total,)),
            ],
        ),
        out_shape=jax.ShapeDtypeStruct((count, length, width), BF16),
        compiler_params=params_of(1),
        cost_estimate=pl.CostEstimate(
            flops=0, transcendentals=0, bytes_accessed=4 * total * length * width
        ),
        name=name,
    )(table, *sources, *wait_for)


def after(value, earlier):
    def kernel(*refs):
        return

    return pl.pallas_call(
        kernel,
        in_specs=[ANY_SPEC] * (1 + len(earlier)),
        out_specs=ANY_SPEC,
        out_shape=jax.ShapeDtypeStruct(value.shape, value.dtype),
        input_output_aliases={0: 0},
        name="after",
    )(value, *earlier)


def norm_forward(summed, gain_row, shift_row):
    center = summed - jnp.mean(summed, axis=-1, keepdims=True)
    spread = jnp.mean(center * center, axis=-1, keepdims=True)
    scale = lax.rsqrt(spread + 1e-05)
    normed = center * scale
    return normed, normed * gain_row + shift_row, scale


def finish_forward(x, branch, gain_row, shift_row, y_ref, zn_ref, rstd_ref):
    normed, result, scale = norm_forward(x.astype(F32) + branch, gain_row, shift_row)
    y_ref[0] = result.astype(BF16)
    zn_ref[0] = normed.astype(BF16)
    rstd_ref[0] = jnp.broadcast_to(scale, rstd_ref.shape[1:])


def norm_backward(dy_ref, zn_ref, rstd_ref, gain_row):
    dy = dy_ref[0].astype(F32)
    normed = zn_ref[0].astype(F32)
    scale = rstd_ref[0][:, :1]
    scaled = dy * gain_row
    first = jnp.mean(scaled, axis=-1, keepdims=True)
    second = jnp.mean(scaled * normed, axis=-1, keepdims=True)
    gain_grad = jnp.sum(dy * normed, axis=0, keepdims=True)
    shift_grad = jnp.sum(dy, axis=0, keepdims=True)
    return (scaled - first - normed * second) * scale, gain_grad, shift_grad


def head_masks(length):
    lane = lax.broadcasted_iota(jnp.int32, (length, LANES), 1)
    low = lane < LANES // 2
    return low


def attention_forward(part, tables, x, weights, norms, y_in):
    rows, counts = tables
    b = part // HALVES
    attn_qkv, attn_out = weights
    gains, shifts = norms
    slots, length, width = x.shape
    score_scale = (width // HEADS) ** (-0.5)
    base = part * SLOTS

    def kernel(rows_ref, counts_ref, x_ref, qkv_w, out_w, gain, shift, *rest):
        y_ref, qkv_ref, o_ref, zn_ref, rstd_ref = rest[-5:]
        i = pl.program_id(0)

        @pl.when(i < counts_ref[part * 8])
        def _():
            xv = x_ref[0]
            for third in range(3):
                cols = slice(third * width, (third + 1) * width)
                qkv_ref[0, :, cols] = nn(xv, qkv_w[:, cols]).astype(BF16)
            low = head_masks(length)
            zero = jnp.zeros((), BF16)
            for pair in range(width // LANES):
                at = pair * LANES
                q2 = qkv_ref[0, :, at : at + LANES] * jnp.asarray(score_scale, BF16)
                k2 = qkv_ref[0, :, width + at : width + at + LANES]
                v2 = qkv_ref[0, :, 2 * width + at : 2 * width + at + LANES]
                mixed = []
                for half in range(2):
                    qm = jnp.where(low if half == 0 else ~low, q2, zero)
                    s = nt(qm, k2)
                    e = jnp.exp(s - jnp.max(s, axis=-1, keepdims=True))
                    total = jnp.sum(e, axis=-1, keepdims=True)
                    mixed.append(nn(e.astype(BF16), v2) / total)
                o_ref[0, :, at : at + LANES] = jnp.where(low, mixed[0], mixed[1]).astype(BF16)
            branch = nn(o_ref[0], out_w[...])
            finish_forward(
                xv, branch, gain[0:1, :], shift[0:1, :], y_ref, zn_ref, rstd_ref
            )

    def at_row(i, r, c):
        return (r[base + i], 0, 0)

    def at_step(i, r, c):
        return (jnp.maximum(jnp.minimum(i, c[part * 8] - 1), 0), 0, 0)

    seq = (1, length, width)
    in_specs = [
        pl.BlockSpec(seq, at_row),
        pl.BlockSpec(
            (None, None, width, 3 * width), lambda i, r, c: (b, 0, 0, 0), pipeline_mode=pl.Buffered(1)
        ),
        pl.BlockSpec(
            (None, None, width, width), lambda i, r, c: (b, 0, 0, 0), pipeline_mode=pl.Buffered(1)
        ),
        pl.BlockSpec((8, width), lambda i, r, c: (0, 0)),
        pl.BlockSpec((8, width), lambda i, r, c: (0, 0)),
    ]
    args = [rows, counts, x, attn_qkv, attn_out, gains, shifts]
    alias = {}
    if y_in is not None:
        in_specs.append(pl.BlockSpec(memory_space=pl.ANY))
        alias = {len(args): 0}
        args.append(y_in)
    flops = OWN_CAP * length * width * (8 * width + 4 * length)
    return pl.pallas_call(
        kernel,
        grid_spec=pltpu.PrefetchScalarGridSpec(
            num_scalar_prefetch=2,
            grid=(OWN_CAP,),
            in_specs=in_specs,
            out_specs=[
                pl.BlockSpec(seq, at_row),
                pl.BlockSpec((1, length, 3 * width), at_step),
                pl.BlockSpec(seq, at_step),
                pl.BlockSpec(seq, at_step),
                pl.BlockSpec((1, length, LANES), at_step),
            ],
        ),
        out_shape=[
            jax.ShapeDtypeStruct((slots, length, width), BF16),
            jax.ShapeDtypeStruct((OWN_CAP, length, 3 * width), BF16),
            jax.ShapeDtypeStruct((OWN_CAP, length, width), BF16),
            jax.ShapeDtypeStruct((OWN_CAP, length, width), BF16),
            jax.ShapeDtypeStruct((OWN_CAP, length, LANES), F32),
        ],
        input_output_aliases=alias,
        compiler_params=params_of(1),
        cost_estimate=pl.CostEstimate(
            flops=2 * flops, transcendentals=OWN_CAP * HEADS * length * length, bytes_accessed=30 * 2**20
        ),
        name="attention_forward",
    )(*args)


def attention_backward(part, tables, x, dy, kept, weights, gains, dx_in, sums, packed):
    rows, counts = tables
    b = part // HALVES
    attn_qkv, attn_out = weights
    qkv, o, zn, rstd = kept
    slots, length, width = x.shape
    score_scale = (width // HEADS) ** (-0.5)
    base = part * SLOTS
    first = sums is None
    n_out = 4 if first else 3

    def kernel(rows_ref, counts_ref, x_ref, dy_ref, qkv_ref, o_ref, zn_ref, rstd_ref, qkv_w, out_w, gain, *rest):
        ins = rest[: len(rest) - n_out - 7]
        outs = rest[len(ins) : len(ins) + n_out]
        acc_qkv, acc_out, do_scr, dqkv_scr, dh_scr, dz_scr, sems = rest[-7:]
        dx_ref, small_ref = outs[0], outs[1]
        i = pl.program_id(0)
        here = i < counts_ref[part * 8]

        def copies():
            if first:
                pairs = ((acc_qkv, outs[2]), (acc_out, outs[3]))
            else:
                pairs = ((ins[0], acc_qkv), (ins[1], acc_out))
            return [
                pltpu.make_async_copy(source, target, sems.at[n])
                for n, (source, target) in enumerate(pairs)
            ]

        @pl.when(i == 0)
        def _():
            small_ref[...] = jnp.zeros_like(small_ref)
            if first:
                acc_qkv[...] = jnp.zeros_like(acc_qkv)
                acc_out[...] = jnp.zeros_like(acc_out)
            else:
                for copy in copies():
                    copy.start()

        @pl.when(here)
        def _():
            dz, gain_grad, shift_grad = norm_backward(dy_ref, zn_ref, rstd_ref, gain[0:1, :])
            small_ref[0:1, :] += gain_grad
            small_ref[1:2, :] += shift_grad
            dz_scr[...] = dz
            dh = dz.astype(BF16)
            dh_scr[...] = dh
            do_scr[...] = nt(dh, out_w[...]).astype(BF16)
            low = head_masks(length)
            zero = jnp.zeros((), BF16)
            for pair in range(width // LANES):
                at = pair * LANES
                q2 = qkv_ref[0, :, at : at + LANES] * jnp.asarray(score_scale, BF16)
                k2 = qkv_ref[0, :, width + at : width + at + LANES]
                v2 = qkv_ref[0, :, 2 * width + at : 2 * width + at + LANES]
                do2 = do_scr[:, at : at + LANES]
                dqs, dks, dvs = [], [], []
                for half in range(2):
                    mask = low if half == 0 else ~low
                    st = nt(jnp.where(mask, k2, zero), q2)
                    e = jnp.exp(st - jnp.max(st, axis=0, keepdims=True))
                    p = e * (1.0 / jnp.sum(e, axis=0, keepdims=True))
                    dvs.append(nn(p.astype(BF16), do2))
                    t = p * nt(jnp.where(mask, v2, zero), do2)
                    ds = (t - p * jnp.sum(t, axis=0, keepdims=True)).astype(BF16)
                    dks.append(nn(ds, q2))
                    dqs.append(tn(ds, k2))
                dqkv_scr[:, at : at + LANES] = (jnp.where(low, dqs[0], dqs[1]) * score_scale).astype(BF16)
                dqkv_scr[:, width + at : width + at + LANES] = jnp.where(low, dks[0], dks[1]).astype(BF16)
                dqkv_scr[:, 2 * width + at : 2 * width + at + LANES] = jnp.where(low, dvs[0], dvs[1]).astype(BF16)
            total = dz_scr[...]
            for third in range(3):
                cols = slice(third * width, (third + 1) * width)
                total = total + nt(dqkv_scr[:, cols], qkv_w[:, cols])
            dx_ref[0] = total.astype(BF16)

        if not first:

            @pl.when(i == 0)
            def _():
                for copy in copies():
                    copy.wait()

        @pl.when(here)
        def _():
            xv = x_ref[0]
            for third in range(3):
                cols = slice(third * width, (third + 1) * width)
                acc_qkv[:, cols] += tn(xv, dqkv_scr[:, cols])
            acc_out[...] += tn(o_ref[0], dh_scr[...])

        @pl.when(i == OWN_CAP - 1)
        def _():
            if first:
                for copy in copies():
                    copy.start()
                for copy in copies():
                    copy.wait()
            else:
                packed_ref = outs[2]
                groups, tall = packed_ref.shape[0], packed_ref.shape[1] // 4
                for third in range(3):
                    piece = acc_qkv[:, third * width : (third + 1) * width].astype(BF16)
                    packed_ref[:, third * tall : (third + 1) * tall, :] = piece.reshape(
                        groups, tall, width
                    )
                packed_ref[:, 3 * tall : 4 * tall, :] = (
                    acc_out[...].astype(BF16).reshape(groups, tall, width)
                )

    def at_row(i, r, c):
        return (r[base + i], 0, 0)

    def at_step(i, r, c):
        return (jnp.maximum(jnp.minimum(i, c[part * 8] - 1), 0), 0, 0)

    def whole(i, r, c):
        return (0, 0)

    seq = (1, length, width)
    in_specs = [
        pl.BlockSpec(seq, at_row),
        pl.BlockSpec(seq, at_row),
        pl.BlockSpec((1, length, 3 * width), at_step),
        pl.BlockSpec(seq, at_step),
        pl.BlockSpec(seq, at_step),
        pl.BlockSpec((1, length, LANES), at_step),
        pl.BlockSpec(
            (None, None, width, 3 * width), lambda i, r, c: (b, 0, 0, 0), pipeline_mode=pl.Buffered(1)
        ),
        pl.BlockSpec(
            (None, None, width, width), lambda i, r, c: (b, 0, 0, 0), pipeline_mode=pl.Buffered(1)
        ),
        pl.BlockSpec((8, width), whole),
    ]
    args = [rows, counts, x, dy, qkv, o, zn, rstd, attn_qkv, attn_out, gains]
    out_specs = [pl.BlockSpec(seq, at_row), pl.BlockSpec((8, width), whole)]
    out_shape = [
        jax.ShapeDtypeStruct((slots, length, width), BF16),
        jax.ShapeDtypeStruct((8, width), F32),
    ]
    if first:
        out_specs += [ANY_SPEC, ANY_SPEC]
        out_shape += [
            jax.ShapeDtypeStruct((width, 3 * width), F32),
            jax.ShapeDtypeStruct((width, width), F32),
        ]
    else:
        groups, total_rows = packed
        out_specs.append(
            pl.BlockSpec((groups, 4 * width // groups, width), lambda i, r, c: (0, 0, 0))
        )
        out_shape.append(jax.ShapeDtypeStruct((groups, total_rows, width), BF16))
        in_specs += [ANY_SPEC, ANY_SPEC]
        args += list(sums)
    in_specs.append(ANY_SPEC)
    alias = {len(args): 0}
    args.append(dx_in)
    flops = 2 * OWN_CAP * length * width * (8 * width + 4 * length)
    return pl.pallas_call(
        kernel,
        grid_spec=pltpu.PrefetchScalarGridSpec(
            num_scalar_prefetch=2,
            grid=(OWN_CAP,),
            in_specs=in_specs,
            out_specs=out_specs,
            scratch_shapes=[
                pltpu.VMEM((width, 3 * width), F32),
                pltpu.VMEM((width, width), F32),
                pltpu.VMEM((length, width), BF16),
                pltpu.VMEM((length, 3 * width), BF16),
                pltpu.VMEM((length, width), BF16),
                pltpu.VMEM((length, width), F32),
                pltpu.SemaphoreType.DMA((2,)),
            ],
        ),
        out_shape=out_shape,
        input_output_aliases=alias,
        compiler_params=params_of(1),
        cost_estimate=pl.CostEstimate(
            flops=flops, transcendentals=OWN_CAP * HEADS * length * length // 2, bytes_accessed=40 * 2**20
        ),
        name="attention_backward",
    )(*args)


def feed_forward(part, tables, x, weights, norms, y_in):
    rows, counts = tables
    b = part // HALVES
    ffn_up, ffn_down = weights
    gains, shifts = norms
    slots, length, width = x.shape
    hidden = ffn_up.shape[-1]
    parts = hidden // FF_PART
    kind = KINDS - 1
    base = part * SLOTS + kind * OWN_CAP

    def kernel(rows_ref, counts_ref, x_ref, up, down, gain, shift, *rest):
        y_ref, g_ref, slope_ref, zn_ref, rstd_ref, x_scr, h_scr = rest[-7:]
        c, i = pl.program_id(0), pl.program_id(1)

        @pl.when(i < counts_ref[part * 8 + kind])
        def _():
            @pl.when(c == 0)
            def _():
                x_scr[i] = x_ref[0]

            xv = x_scr[i]
            for sub in range(FF_PART // FF_SUB):
                cols = slice(sub * FF_SUB, (sub + 1) * FF_SUB)
                a = nn(xv, up[:, cols])
                phi = 0.5 + 0.5 * lax.erf(a * (0.5**0.5))
                slope = phi + a * (jnp.exp(a * a * -0.5) * 0.3989422804014327)
                g = (a * phi).astype(BF16)
                g_ref[0, :, cols] = g
                slope_ref[0, :, cols] = slope.astype(BF16)
            branch = nn(g_ref[0], down[...])

            @pl.when(c == 0)
            def _():
                h_scr[i] = branch

            @pl.when(jnp.logical_and(c > 0, c < parts - 1))
            def _():
                h_scr[i] += branch

            @pl.when(c == parts - 1)
            def _():
                finish_forward(
                    xv,
                    h_scr[i] + branch,
                    gain[kind : kind + 1, :],
                    shift[kind : kind + 1, :],
                    y_ref,
                    zn_ref,
                    rstd_ref,
                )

    def in_row(c, i, r, n):
        return (r[base + jnp.where(c == 0, i, OWN_CAP - 1)], 0, 0)

    def out_row(c, i, r, n):
        return (r[base + jnp.where(c == parts - 1, i, 0)], 0, 0)

    def out_step(c, i, r, n):
        return (jnp.where(c == parts - 1, jnp.maximum(jnp.minimum(i, n[part * 8 + kind] - 1), 0), 0), 0, 0)

    def part_step(c, i, r, n):
        return (jnp.maximum(jnp.minimum(i, n[part * 8 + kind] - 1), 0), 0, c)

    seq = (1, length, width)
    in_specs = [
        pl.BlockSpec(seq, in_row),
        pl.BlockSpec((None, None, width, FF_PART), lambda c, i, r, n: (b, 0, 0, c)),
        pl.BlockSpec((None, None, FF_PART, width), lambda c, i, r, n: (b, 0, c, 0)),
        pl.BlockSpec((8, width), lambda c, i, r, n: (0, 0)),
        pl.BlockSpec((8, width), lambda c, i, r, n: (0, 0)),
    ]
    args = [rows, counts, x, ffn_up, ffn_down, gains, shifts]
    alias = {}
    if y_in is not None:
        in_specs.append(pl.BlockSpec(memory_space=pl.ANY))
        alias = {len(args): 0}
        args.append(y_in)
    return pl.pallas_call(
        kernel,
        grid_spec=pltpu.PrefetchScalarGridSpec(
            num_scalar_prefetch=2,
            grid=(parts, OWN_CAP),
            in_specs=in_specs,
            out_specs=[
                pl.BlockSpec(seq, out_row),
                pl.BlockSpec((1, length, FF_PART), part_step),
                pl.BlockSpec((1, length, FF_PART), part_step),
                pl.BlockSpec(seq, out_step),
                pl.BlockSpec((1, length, LANES), out_step),
            ],
            scratch_shapes=[
                pltpu.VMEM((OWN_CAP, length, width), BF16),
                pltpu.VMEM((OWN_CAP, length, width), F32),
            ],
        ),
        out_shape=[
            jax.ShapeDtypeStruct((slots, length, width), BF16),
            jax.ShapeDtypeStruct((OWN_CAP, length, hidden), BF16),
            jax.ShapeDtypeStruct((OWN_CAP, length, hidden), BF16),
            jax.ShapeDtypeStruct((OWN_CAP, length, width), BF16),
            jax.ShapeDtypeStruct((OWN_CAP, length, LANES), F32),
        ],
        input_output_aliases=alias,
        compiler_params=params_of(2),
        cost_estimate=pl.CostEstimate(
            flops=4 * OWN_CAP * length * width * hidden,
            transcendentals=2 * OWN_CAP * length * hidden,
            bytes_accessed=40 * 2**20,
        ),
        name="feed_forward",
    )(*args)


def feed_backward(part, tables, x, dy, kept, weights, gains, sums, packed):
    rows, counts = tables
    b = part // HALVES
    ffn_up, ffn_down = weights
    g, slope, zn, rstd = kept
    slots, length, width = x.shape
    hidden = ffn_up.shape[-1]
    parts = hidden // FF_PART
    kind = KINDS - 1
    base = part * SLOTS + kind * OWN_CAP
    first = sums is None
    groups = packed[0]
    tall = width // groups
    deep = hidden // groups

    def kernel(
        rows_ref, counts_ref, x_ref, dy_ref, g_ref, slope_ref, zn_ref, rstd_ref, up, down, gain, *rest
    ):
        if first:
            dx_ref, small_ref, acc_up, acc_down = rest[:4]
        else:
            sum_up, sum_down, dx_ref, small_ref, packed_ref = rest[:5]
            acc_up, acc_down, low_up, low_down, sems = rest[-5:]
        x_scr, dh_scr, dx_scr, da_scr = rest[-4:] if first else rest[-9:-5]
        c, i = pl.program_id(0), pl.program_id(1)

        @pl.when(jnp.logical_and(c == 0, i == 0))
        def _():
            small_ref[...] = jnp.zeros_like(small_ref)

        @pl.when(i == 0)
        def _():
            if first:
                acc_up[...] = jnp.zeros_like(acc_up)
                acc_down[...] = jnp.zeros_like(acc_down)
            else:
                acc_up[...] = sum_up[...]
                acc_down[...] = sum_down[...]

        @pl.when(i < counts_ref[part * 8 + kind])
        def _():
            @pl.when(c == 0)
            def _():
                dz, gain_grad, shift_grad = norm_backward(
                    dy_ref, zn_ref, rstd_ref, gain[kind : kind + 1, :]
                )
                small_ref[0:1, :] += gain_grad
                small_ref[1:2, :] += shift_grad
                x_scr[i] = x_ref[0]
                dh_scr[i] = dz.astype(BF16)
                dx_scr[i] = dz

            dh = dh_scr[i]
            for sub in range(FF_PART // FF_SUB):
                cols = slice(sub * FF_SUB, (sub + 1) * FF_SUB)
                dg = nt(dh, down[cols, :])
                da_scr[:, cols] = (dg * slope_ref[0, :, cols].astype(F32)).astype(BF16)
            acc_down[...] += tn(g_ref[0], dh)
            acc_up[...] += tn(x_scr[i], da_scr[...])
            total = dx_scr[i] + nt(da_scr[...], up[...])

            @pl.when(c < parts - 1)
            def _():
                dx_scr[i] = total

            @pl.when(c == parts - 1)
            def _():
                dx_ref[0] = total.astype(BF16)

        if not first:

            @pl.when(i == OWN_CAP - 1)
            def _():
                low_up[...] = acc_up[...].astype(BF16)
                low_down[...] = acc_down[...].astype(BF16)
                copies = [
                    pltpu.make_async_copy(
                        low_up.at[pl.ds(z * tall, tall)],
                        packed_ref.at[z, pl.ds(c * tall, tall)],
                        sems.at[z],
                    )
                    for z in range(groups)
                ]
                shares = FF_PART // deep
                copies += [
                    pltpu.make_async_copy(
                        low_down.at[pl.ds(m * deep, deep)],
                        packed_ref.at[c * shares + m, pl.ds(parts * tall, deep)],
                        sems.at[groups + m],
                    )
                    for m in range(shares)
                ]
                for copy in copies:
                    copy.start()
                for copy in copies:
                    copy.wait()

    def in_row(c, i, r, n):
        return (r[base + jnp.where(c == 0, i, OWN_CAP - 1)], 0, 0)

    def in_step(c, i, r, n):
        last = jnp.maximum(n[part * 8 + kind] - 1, 0)
        return (jnp.where(c == 0, jnp.minimum(i, last), last), 0, 0)

    def out_row(c, i, r, n):
        return (r[base + jnp.where(c == parts - 1, i, 0)], 0, 0)

    def part_step(c, i, r, n):
        return (jnp.maximum(jnp.minimum(i, n[part * 8 + kind] - 1), 0), 0, c)

    seq = (1, length, width)
    in_specs = [
        pl.BlockSpec(seq, in_row),
        pl.BlockSpec(seq, in_row),
        pl.BlockSpec((1, length, FF_PART), part_step),
        pl.BlockSpec((1, length, FF_PART), part_step),
        pl.BlockSpec(seq, in_step),
        pl.BlockSpec((1, length, LANES), in_step),
        pl.BlockSpec((None, None, width, FF_PART), lambda c, i, r, n: (b, 0, 0, c)),
        pl.BlockSpec((None, None, FF_PART, width), lambda c, i, r, n: (b, 0, c, 0)),
        pl.BlockSpec((8, width), lambda c, i, r, n: (0, 0)),
    ]
    args = [rows, counts, x, dy, g, slope, zn, rstd, ffn_up, ffn_down, gains]
    up_spec = pl.BlockSpec((width, FF_PART), lambda c, i, r, n: (0, c))
    down_spec = pl.BlockSpec((FF_PART, width), lambda c, i, r, n: (c, 0))
    out_specs = [pl.BlockSpec(seq, out_row), pl.BlockSpec((8, width), lambda c, i, r, n: (0, 0))]
    out_shape = [
        jax.ShapeDtypeStruct((slots, length, width), BF16),
        jax.ShapeDtypeStruct((8, width), F32),
    ]
    scratch = [
        pltpu.VMEM((OWN_CAP, length, width), BF16),
        pltpu.VMEM((OWN_CAP, length, width), BF16),
        pltpu.VMEM((OWN_CAP, length, width), F32),
        pltpu.VMEM((length, FF_PART), BF16),
    ]
    if first:
        out_specs += [up_spec, down_spec]
        out_shape += [
            jax.ShapeDtypeStruct((width, hidden), F32),
            jax.ShapeDtypeStruct((hidden, width), F32),
        ]
    else:
        in_specs += [up_spec, down_spec]
        args += list(sums)
        out_specs.append(ANY_SPEC)
        out_shape.append(jax.ShapeDtypeStruct((groups, parts * tall + deep, width), BF16))
        scratch += [
            pltpu.VMEM((width, FF_PART), F32),
            pltpu.VMEM((FF_PART, width), F32),
            pltpu.VMEM((width, FF_PART), BF16),
            pltpu.VMEM((FF_PART, width), BF16),
            pltpu.SemaphoreType.DMA((groups + FF_PART // deep,)),
        ]
    return pl.pallas_call(
        kernel,
        grid_spec=pltpu.PrefetchScalarGridSpec(
            num_scalar_prefetch=2,
            grid=(parts, OWN_CAP),
            in_specs=in_specs,
            out_specs=out_specs,
            scratch_shapes=scratch,
        ),
        out_shape=out_shape,
        compiler_params=params_of(2),
        cost_estimate=pl.CostEstimate(
            flops=4 * OWN_CAP * length * width * hidden,
            transcendentals=0,
            bytes_accessed=50 * 2**20,
        ),
        name="feed_backward",
    )(*args)


PAD = 8
ROW_TILE = 128
COL_TILE = 256


def fill_padded(padded, values):
    length = values.shape[0]
    edge = jnp.zeros((PAD, values.shape[1]), F32)
    padded[0:PAD, :] = edge
    padded[PAD + length : PAD + length + PAD, :] = edge
    padded[PAD : PAD + length, :] = values


def conv_forward(part, tables, x, weights, norms, y_in):
    rows, counts = tables
    b = part // HALVES
    taps, conv_point = weights
    gains, shifts = norms
    slots, length, width = x.shape
    base = part * SLOTS + OWN_CAP
    steps = (KINDS - 2) * OWN_CAP

    def kernel(rows_ref, counts_ref, x_ref, point, taps_ref, gain, shift, *rest):
        y_ref, u_ref, zn_ref, rstd_ref, xpad = rest[-5:]
        step = pl.program_id(0)
        which, j = step // OWN_CAP, step % OWN_CAP
        for kind in range(1, KINDS - 1):
            taps_n = 2 * kind + 1
            first = kind * kind - 1

            @pl.when(jnp.logical_and(which == kind - 1, j < counts_ref[part * 8 + kind]))
            def _():
                fill_padded(xpad, x_ref[0].astype(F32))
                for r in range(0, length, ROW_TILE):
                    for col in range(0, width, COL_TILE):
                        cols = slice(col, col + COL_TILE)
                        mixed = None
                        for t in range(taps_n):
                            start = PAD + r + t - kind
                            term = xpad[start : start + ROW_TILE, cols] * taps_ref[first + t : first + t + 1, cols]
                            mixed = term if mixed is None else mixed + term
                        u_ref[0, r : r + ROW_TILE, cols] = mixed.astype(BF16)
                branch = nn(u_ref[0], point[...])
                finish_forward(
                    x_ref[0],
                    branch,
                    gain[kind : kind + 1, :],
                    shift[kind : kind + 1, :],
                    y_ref,
                    zn_ref,
                    rstd_ref,
                )

    def at_row(i, r, c):
        return (r[base + i], 0, 0)

    def at_step(i, r, c):
        which = i // OWN_CAP
        last = c[part * 8 + 1 + which] - 1
        return (which * OWN_CAP + jnp.maximum(jnp.minimum(i % OWN_CAP, last), 0), 0, 0)

    def whole(i, r, c):
        return (0, 0)

    seq = (1, length, width)
    in_specs = [
        pl.BlockSpec(seq, at_row),
        pl.BlockSpec((None, None, None, width, width), lambda i, r, c: (b, 0, i // OWN_CAP, 0, 0)),
        pl.BlockSpec((16, width), whole),
        pl.BlockSpec((8, width), whole),
        pl.BlockSpec((8, width), whole),
    ]
    args = [rows, counts, x, conv_point, taps, gains, shifts]
    alias = {}
    if y_in is not None:
        in_specs.append(pl.BlockSpec(memory_space=pl.ANY))
        alias = {len(args): 0}
        args.append(y_in)
    return pl.pallas_call(
        kernel,
        grid_spec=pltpu.PrefetchScalarGridSpec(
            num_scalar_prefetch=2,
            grid=(steps,),
            in_specs=in_specs,
            out_specs=[
                pl.BlockSpec(seq, at_row),
                pl.BlockSpec(seq, at_step),
                pl.BlockSpec(seq, at_step),
                pl.BlockSpec((1, length, LANES), at_step),
            ],
            scratch_shapes=[pltpu.VMEM((length + 2 * PAD, width), F32)],
        ),
        out_shape=[
            jax.ShapeDtypeStruct((slots, length, width), BF16),
            jax.ShapeDtypeStruct((steps, length, width), BF16),
            jax.ShapeDtypeStruct((steps, length, width), BF16),
            jax.ShapeDtypeStruct((steps, length, LANES), F32),
        ],
        input_output_aliases=alias,
        compiler_params=params_of(1),
        cost_estimate=pl.CostEstimate(
            flops=2 * steps * length * width * width, transcendentals=0, bytes_accessed=36 * 2**20
        ),
        name="conv_forward",
    )(*args)


def conv_backward(part, tables, x, dy, kept, weights, gains, dx_in, sums, packed):
    rows, counts = tables
    b = part // HALVES
    taps, conv_point = weights
    u, zn, rstd = kept
    slots, length, width = x.shape
    base = part * SLOTS + OWN_CAP
    steps = (KINDS - 2) * OWN_CAP
    first_half = sums is None
    groups = packed[0]

    def kernel(rows_ref, counts_ref, x_ref, dy_ref, u_ref, zn_ref, rstd_ref, point, taps_ref, gain, *rest):
        if first_half:
            dx_ref, small_ref, acc, xpad, dupad, dz_scr = rest[-6:]
        else:
            sum_ref = rest[0]
            dx_ref, small_ref, packed_ref, xpad, dupad, dz_scr, acc = rest[-7:]
        step = pl.program_id(0)
        which, j = step // OWN_CAP, step % OWN_CAP

        @pl.when(step == 0)
        def _():
            small_ref[...] = jnp.zeros_like(small_ref)

        @pl.when(j == 0)
        def _():
            acc[...] = jnp.zeros_like(acc) if first_half else sum_ref[...]

        for kind in range(1, KINDS - 1):
            taps_n = 2 * kind + 1
            first = kind * kind - 1

            @pl.when(jnp.logical_and(which == kind - 1, j < counts_ref[part * 8 + kind]))
            def _():
                dz, gain_grad, shift_grad = norm_backward(
                    dy_ref, zn_ref, rstd_ref, gain[kind : kind + 1, :]
                )
                small_ref[14 + kind : 15 + kind, :] += gain_grad
                small_ref[17 + kind : 18 + kind, :] += shift_grad
                dz_scr[...] = dz
                dh = dz.astype(BF16)
                acc[...] += tn(u_ref[0], dh)
                fill_padded(xpad, x_ref[0].astype(F32))
                fill_padded(dupad, nt(dh, point[...]))
                for col in range(0, width, COL_TILE):
                    cols = slice(col, col + COL_TILE)
                    sums = [None] * taps_n
                    for r in range(0, length, ROW_TILE):
                        here = dupad[PAD + r : PAD + r + ROW_TILE, cols]
                        total = dz_scr[r : r + ROW_TILE, cols]
                        for t in range(taps_n):
                            back = PAD + r - t + kind
                            total = total + dupad[back : back + ROW_TILE, cols] * taps_ref[first + t : first + t + 1, cols]
                            ahead = PAD + r + t - kind
                            part = jnp.sum(
                                xpad[ahead : ahead + ROW_TILE, cols] * here, axis=0, keepdims=True
                            )
                            sums[t] = part if sums[t] is None else sums[t] + part
                        dx_ref[0, r : r + ROW_TILE, cols] = total.astype(BF16)
                    for t in range(taps_n):
                        small_ref[first + t : first + t + 1, cols] += sums[t]

        if not first_half:

            @pl.when(j == OWN_CAP - 1)
            def _():
                packed_ref[...] = acc[...].astype(BF16).reshape(packed_ref.shape)

    def at_row(i, r, c):
        return (r[base + i], 0, 0)

    def at_step(i, r, c):
        which = i // OWN_CAP
        last = c[part * 8 + 1 + which] - 1
        return (which * OWN_CAP + jnp.maximum(jnp.minimum(i % OWN_CAP, last), 0), 0, 0)

    def whole(i, r, c):
        return (0, 0)

    seq = (1, length, width)
    in_specs = [
        pl.BlockSpec(seq, at_row),
        pl.BlockSpec(seq, at_row),
        pl.BlockSpec(seq, at_step),
        pl.BlockSpec(seq, at_step),
        pl.BlockSpec((1, length, LANES), at_step),
        pl.BlockSpec((None, None, None, width, width), lambda i, r, c: (b, 0, i // OWN_CAP, 0, 0)),
        pl.BlockSpec((16, width), whole),
        pl.BlockSpec((8, width), whole),
    ]
    args = [rows, counts, x, dy, u, zn, rstd, conv_point, taps, gains]
    sum_spec = pl.BlockSpec((None, width, width), lambda i, r, c: (i // OWN_CAP, 0, 0))
    out_specs = [pl.BlockSpec(seq, at_row), pl.BlockSpec((24, width), whole)]
    out_shape = [
        jax.ShapeDtypeStruct((slots, length, width), BF16),
        jax.ShapeDtypeStruct((24, width), F32),
    ]
    scratch = [
        pltpu.VMEM((length + 2 * PAD, width), F32),
        pltpu.VMEM((length + 2 * PAD, width), F32),
        pltpu.VMEM((length, width), F32),
    ]
    alias = {}
    if first_half:
        out_specs.append(sum_spec)
        out_shape.append(jax.ShapeDtypeStruct((KINDS - 2, width, width), F32))
    else:
        in_specs.append(sum_spec)
        args.append(sums)
        out_specs.append(
            pl.BlockSpec((groups, width // groups, width), lambda i, r, c: (0, 4 + i // OWN_CAP, 0))
        )
        out_shape.append(jax.ShapeDtypeStruct(packed[1].shape, BF16))
        in_specs.append(ANY_SPEC)
        alias = {len(args): 2}
        args.append(packed[1])
        scratch.append(pltpu.VMEM((width, width), F32))
    in_specs.append(ANY_SPEC)
    alias = {**alias, len(args): 0}
    args.append(dx_in)
    return pl.pallas_call(
        kernel,
        grid_spec=pltpu.PrefetchScalarGridSpec(
            num_scalar_prefetch=2,
            grid=(steps,),
            in_specs=in_specs,
            out_specs=out_specs,
            scratch_shapes=scratch,
        ),
        out_shape=out_shape,
        input_output_aliases=alias,
        compiler_params=params_of(1),
        cost_estimate=pl.CostEstimate(
            flops=3 * steps * length * width * width, transcendentals=0, bytes_accessed=50 * 2**20
        ),
        name="conv_backward",
    )(*args)


def owner_forward(part, tables, x, weights, small_weights):
    attn_qkv, attn_out, ffn_up, ffn_down, conv_point = weights
    taps, gains, shifts = small_weights
    norms = (gains, shifts)
    y, g, slope, zn_f, rstd_f = feed_forward(part, tables, x, (ffn_up, ffn_down), norms, None)
    y, qkv, o, zn_a, rstd_a = attention_forward(part, tables, x, (attn_qkv, attn_out), norms, y)
    y, u, zn_c, rstd_c = conv_forward(part, tables, x, (taps, conv_point), norms, y)
    return y, ((g, slope, zn_f, rstd_f), (qkv, o, zn_a, rstd_a), (u, zn_c, rstd_c))


def join_small(small_f, small_a, small_c):
    return jnp.concatenate(
        [
            small_c[:15],
            small_a[0:1],
            small_c[15:18],
            small_f[0:1],
            small_a[1:2],
            small_c[18:21],
            small_f[1:2],
        ]
    )


def owner_backward(b, tables, x, dy, kept, weights, small_weights, groups):
    attn_qkv, attn_out, ffn_up, ffn_down, conv_point = weights
    taps, gains, shifts = small_weights
    width = x[0].shape[-1]
    rest_rows = 7 * width // groups + SMALL_ROWS
    dx, smalls = [None, None], [None, None]
    sums = None
    for half in range(HALVES):
        part = b * HALVES + half
        kept_f, kept_a, kept_c = kept[half]
        xh, dyh = x[half], dy[half]
        first = half == 0
        if first:
            d, small_f, *sum_f = feed_backward(
                part, tables, xh, dyh, kept_f, (ffn_up, ffn_down), gains, None, (groups,)
            )
            d, small_a, *sum_a = attention_backward(
                part, tables, xh, dyh, kept_a, (attn_qkv, attn_out), gains, d, None, None
            )
            d, small_c, sum_c = conv_backward(
                part, tables, xh, dyh, kept_c, (taps, conv_point), gains, d, None, (groups,)
            )
        else:
            d, small_f, feed_pack = feed_backward(
                part, tables, xh, dyh, kept_f, (ffn_up, ffn_down), gains, sum_f, (groups,)
            )
            d, small_a, rest_pack = attention_backward(
                part, tables, xh, dyh, kept_a, (attn_qkv, attn_out), gains, d, sum_a, (groups, rest_rows)
            )
            d, small_c, rest_pack = conv_backward(
                part, tables, xh, dyh, kept_c, (taps, conv_point), gains, d, sum_c, (groups, rest_pack)
            )
        dx[half] = d
        smalls[half] = join_small(small_f, small_a, small_c)
    counts = tables[1].reshape(BLOCKS, HALVES, 8)[b].sum(axis=0).astype(BF16)
    small = (smalls[0] + smalls[1]).reshape(25, groups, width // groups)
    small = small.transpose(1, 0, 2).reshape(groups, -1).astype(BF16)
    small = jnp.pad(small, ((0, 0), (0, (SMALL_ROWS - 1) * width - small.shape[1])))
    last = jnp.pad(jnp.broadcast_to(counts, (groups, 8)), ((0, 0), (0, width - 8)))
    small = jnp.concatenate([small, last], axis=1).reshape(groups, SMALL_ROWS, width)
    rest_pack = lax.dynamic_update_slice(rest_pack, small, (0, rest_rows - SMALL_ROWS, 0))
    return dx, feed_pack, rest_pack


def small_params(b, conv_taps, norm_gain, norm_bias):
    taps = jnp.pad(conv_taps[b, 0].astype(F32), ((0, 1), (0, 0)))
    gains = jnp.pad(norm_gain[b, 0].astype(F32), ((0, 3), (0, 0)))
    shifts = jnp.pad(norm_bias[b, 0].astype(F32), ((0, 3), (0, 0)))
    return taps, gains, shifts


def exchange(rows):
    return lax.all_to_all(rows, "op", split_axis=0, concat_axis=0, tiled=True)


def per_device(
    inputs,
    candidate,
    attn_qkv,
    attn_out,
    ffn_up,
    ffn_down,
    conv_taps,
    conv_point,
    norm_gain,
    norm_bias,
    cotangent,
):
    owners = lax.axis_size("op")
    groups = lax.axis_size("dp")
    seqs = inputs.shape[0]
    width = inputs.shape[-1]
    hidden = ffn_up.shape[-1]
    weights = (attn_qkv, attn_out, ffn_up, ffn_down, conv_point)
    smalls = [small_params(b, conv_taps, norm_gain, norm_bias) for b in range(BLOCKS)]
    send, relay, tags = home_tables(candidate.reshape(-1), owners, seqs)
    arrived = exchange(tags.reshape(owners, BLOCKS * HALVES))
    tables = owner_tables(arrived.reshape(-1), owners)
    both = range(HALVES)

    def start(b, half):
        return (b * HALVES + half) * owners

    x0 = [
        exchange(move_rows(send, [start(0, h)], [inputs], owners, False, "send_inputs"))
        for h in both
    ]
    y0, kept0 = zip(*[owner_forward(h, tables, x0[h], weights, smalls[0]) for h in both])
    x1 = []
    for h in both:
        back = exchange(y0[h])
        x1.append(exchange(move_rows(relay, [start(0, h)], [back], owners, False, "relay_x")))
    dy1 = [
        exchange(
            move_rows(
                send, [start(1, h)], [cotangent], owners, False, "send_cotangent", (x1[0],)
            )
        )
        for h in both
    ]
    y1, kept1 = zip(
        *[owner_forward(HALVES + h, tables, x1[h], weights, smalls[1]) for h in both]
    )
    dx1, feed1, rest1 = owner_backward(1, tables, x1, dy1, kept1, weights, smalls[1], groups)
    dy0 = []
    for h in both:
        back = exchange(dx1[h])
        dy0.append(exchange(move_rows(relay, [start(1, h)], [back], owners, False, "relay_dx")))
    dx0, feed0, rest0 = owner_backward(0, tables, x0, dy0, kept0, weights, smalls[0], groups)
    starts = [start(1, h) for h in both]
    y_home = [exchange(after(y1[h], (dy0[1],))) for h in both]
    outputs = move_rows(send, starts, y_home, seqs, True, "outputs")
    starts = [start(0, h) for h in both]
    dx_home = [exchange(dx0[h]) for h in both]
    input_grad = move_rows(send, starts, dx_home, seqs, True, "input_grad")

    tall, deep, parts = width // groups, hidden // groups, hidden // FF_PART
    finished, earlier = [None, None], None
    for b, feed, rest in ((1, feed1, rest1), (0, feed0, rest0)):
        if earlier is not None:
            feed = after(feed, (earlier,))
        feed = lax.psum_scatter(feed, "dp", scatter_dimension=0, tiled=False)
        rest = after(rest, (feed,))
        earlier = lax.psum_scatter(rest, "dp", scatter_dimension=0, tiled=False)
        feed, rest = feed.astype(F32), earlier.astype(F32)
        total = rest[-1, :KINDS]
        small = rest[7 * tall : -1].reshape(-1)[: 25 * tall].reshape(25, tall)
        up = feed[: parts * tall].reshape(parts, tall, FF_PART).transpose(1, 0, 2)
        qkv = rest[: 3 * tall].reshape(3, tall, width).transpose(1, 0, 2)
        point = rest[4 * tall : 7 * tall].reshape(KINDS - 2, tall, width)
        tap_total = jnp.concatenate(
            [jnp.broadcast_to(total[k], (2 * k + 1,)) for k in range(1, KINDS - 1)]
        )
        finished[b] = (
            qkv.reshape(tall, 3 * width) / total[0],
            rest[3 * tall : 4 * tall] / total[0],
            up.reshape(tall, hidden) / total[KINDS - 1],
            feed[parts * tall :] / total[KINDS - 1],
            small[:15] / tap_total[:, None],
            point / total[1 : KINDS - 1, None, None],
            small[15:20] / total[:, None],
            small[20:25] / total[:, None],
        )
    grads = tuple(
        jnp.stack([finished[0][n], finished[1][n]])[:, None] for n in range(8)
    )
    return (outputs, input_grad) + grads


def solution(mesh):
    placed = (
        P(("dp", "op"), None, None),
        P(("dp", "op"), None),
        P(None, "op", None, None),
        P(None, "op", None, None),
        P(None, "op", None, None),
        P(None, "op", None, None),
        P(None, "op", None, None),
        P(None, "op", None, None, None),
        P(None, "op", None, None),
        P(None, "op", None, None),
        P(("dp", "op"), None, None),
    )
    return jax.shard_map(
        per_device,
        mesh=mesh,
        in_specs=placed,
        out_specs=(
            P(("dp", "op"), None, None),
            P(("dp", "op"), None, None),
            P(None, "op", "dp", None),
            P(None, "op", "dp", None),
            P(None, "op", "dp", None),
            P(None, "op", "dp", None),
            P(None, "op", None, "dp"),
            P(None, "op", None, "dp", None),
            P(None, "op", None, "dp"),
            P(None, "op", None, "dp"),
        ),
        check_vma=False,
    )
```

```python
import jax
import jax.numpy as jnp
from jax import lax
from jax.experimental import pallas as pl
from jax.experimental.pallas import tpu as pltpu
from jax.sharding import PartitionSpec as P

HEADS = 12
KINDS = 5
BLOCKS = 2
OWN_CAP = 3
HALVES = 2
SLOTS = KINDS * OWN_CAP
FF_PART = 768
FF_SUB = 256
LANES = 128
SMALL_ROWS = 32
COUNT_ROWS = 16
BF16 = jnp.bfloat16
F32 = jnp.float32
VMEM_BYTES = 60 * 2**20


def params_of(axes):
    return pltpu.CompilerParams(
        dimension_semantics=("arbitrary",) * axes, vmem_limit_bytes=VMEM_BYTES
    )


def nn(a, b):
    return lax.dot_general(a, b, (((1,), (0,)), ((), ())), preferred_element_type=F32)


def nt(a, b):
    return lax.dot_general(a, b, (((1,), (1,)), ((), ())), preferred_element_type=F32)


def tn(a, b):
    return lax.dot_general(a, b, (((0,), (0,)), ((), ())), preferred_element_type=F32)


def home_kernel(owners, seqs, cand, send, relay, tags, color, partner, first, tally):
    for b in range(BLOCKS):

        def clear_owner(o, _):
            first[b * owners + o] = -1
            for half in range(HALVES):
                send[(b * HALVES + half) * owners + o] = -1
                relay[(b * HALVES + half) * owners + o] = -1
                tags[o * BLOCKS * HALVES + b * HALVES + half] = KINDS
            return 0

        lax.fori_loop(0, owners, clear_owner, 0)
    for half in range(HALVES):
        tally[half] = 0

    def pair_up(j, _):
        color[j] = -1
        for b in range(BLOCKS):
            o = b * owners + lax.rem(cand[j * BLOCKS + b], owners)
            other = first[o]
            partner[b * seqs + j] = other
            first[o] = j

            @pl.when(other >= 0)
            def _():
                partner[b * seqs + other] = j

        return 0

    lax.fori_loop(0, seqs, pair_up, 0)

    def give(j, shade):
        color[j] = shade
        tally[shade] = tally[shade] + 1

    def paint(j, _):
        @pl.when(color[j] < 0)
        def _():
            shade = jnp.where(tally[0] > tally[1], 1, 0).astype(jnp.int32)
            give(j, shade)
            for side in range(2):

                def more(state):
                    return state[0] >= 0

                def walk(state):
                    now, use, tone = state
                    after = partner[use * seqs + now]
                    free = jnp.logical_and(after >= 0, color[jnp.maximum(after, 0)] < 0)

                    @pl.when(free)
                    def _():
                        give(after, 1 - tone)

                    return (jnp.where(free, after, -1), 1 - use, 1 - tone)

                lax.while_loop(more, walk, (j, jnp.int32(side), shade))

        return 0

    lax.fori_loop(0, seqs, paint, 0)

    def place(j, _):
        half = color[j]
        spots = []
        for b in range(BLOCKS):
            c = cand[j * BLOCKS + b]
            o = lax.rem(c, owners)
            spots.append(o)
            send[(b * HALVES + half) * owners + o] = j
            tags[o * BLOCKS * HALVES + b * HALVES + half] = lax.div(c, owners)
        relay[half * owners + spots[1]] = spots[0]
        relay[(HALVES + half) * owners + spots[0]] = spots[1]
        return 0

    lax.fori_loop(0, seqs, place, 0)


SMEM_SPEC = pl.BlockSpec(memory_space=pltpu.SMEM)
ANY_SPEC = pl.BlockSpec(memory_space=pl.ANY)


def int_shape(n):
    return jax.ShapeDtypeStruct((n,), jnp.int32)


def home_tables(cand, owners, seqs):
    def kernel(*refs):
        home_kernel(owners, seqs, *refs)

    size = BLOCKS * HALVES * owners
    return pl.pallas_call(
        kernel,
        in_specs=[SMEM_SPEC],
        out_specs=[SMEM_SPEC] * 3,
        out_shape=[int_shape(size)] * 3,
        scratch_shapes=[
            pltpu.SMEM((seqs,), jnp.int32),
            pltpu.SMEM((BLOCKS * seqs,), jnp.int32),
            pltpu.SMEM((BLOCKS * owners,), jnp.int32),
            pltpu.SMEM((HALVES,), jnp.int32),
        ],
        name="home_tables",
    )(cand)


def owner_kernel(owners, tags, rows, counts):
    for b in range(BLOCKS):
        for half in range(HALVES):
            part = b * HALVES + half
            for k in range(8):
                counts[part * 8 + k] = 0

            def arrive(h, free):
                k = tags[h * BLOCKS * HALVES + part]
                there = k < KINDS

                @pl.when(there)
                def _():
                    n = jnp.minimum(counts[part * 8 + k], OWN_CAP - 1)
                    rows[part * SLOTS + k * OWN_CAP + n] = h
                    counts[part * 8 + k] = n + 1

                return jnp.where(there, free, h)

            free = lax.fori_loop(0, owners, arrive, jnp.int32(0))

            def spare(k, otherwise):
                return jnp.where(
                    counts[part * 8 + k] > 0, rows[part * SLOTS + k * OWN_CAP], otherwise
                )

            conv_spare = free
            for k in reversed(range(1, KINDS - 1)):
                conv_spare = spare(k, conv_spare)
            attn_spare = spare(0, conv_spare)
            feed_spare = spare(KINDS - 1, attn_spare)
            last = conv_spare
            for k, start in ((1, None), (2, None), (3, None), (0, attn_spare), (KINDS - 1, feed_spare)):
                last = last if start is None else start
                for i in range(OWN_CAP):
                    at = part * SLOTS + k * OWN_CAP + i
                    last = jnp.where(i < counts[part * 8 + k], rows[at], last)
                    rows[at] = last


def owner_tables(tags, owners):
    def kernel(*refs):
        owner_kernel(owners, *refs)

    return pl.pallas_call(
        kernel,
        in_specs=[SMEM_SPEC],
        out_specs=[SMEM_SPEC] * 2,
        out_shape=[int_shape(BLOCKS * HALVES * SLOTS), int_shape(BLOCKS * HALVES * 8)],
        name="owner_tables",
    )(tags)


def move_rows(table, starts, sources, count, scatter, name, wait_for=()):
    length, width = sources[0].shape[1:]
    each = table.shape[0] // (BLOCKS * HALVES)
    total = each * len(sources)

    def kernel(table_ref, *refs):
        ins = refs[: len(sources)]
        out_ref, buf, sem_in, sem_out = refs[-4:]

        def load(part, s):
            idx = table_ref[starts[part] + s]
            at = s if scatter else idx
            to = part * each + s
            return pltpu.make_async_copy(ins[part].at[at], buf.at[to], sem_in.at[to])

        def store(part, s):
            idx = table_ref[starts[part] + s]
            at = part * each + s
            to = idx if scatter else at
            return pltpu.make_async_copy(buf.at[at], out_ref.at[to], sem_out.at[at])

        todo = [(part, s) for part in range(len(sources)) for s in range(each)]
        for part, s in todo:

            @pl.when(table_ref[starts[part] + s] >= 0)
            def _():
                load(part, s).start()

        for part, s in todo:

            @pl.when(table_ref[starts[part] + s] >= 0)
            def _():
                load(part, s).wait()
                store(part, s).start()

        for part, s in todo:

            @pl.when(table_ref[starts[part] + s] >= 0)
            def _():
                store(part, s).wait()

    return pl.pallas_call(
        kernel,
        grid_spec=pltpu.PrefetchScalarGridSpec(
            num_scalar_prefetch=1,
            grid=(1,),
            in_specs=[ANY_SPEC] * (len(sources) + len(wait_for)),
            out_specs=ANY_SPEC,
            scratch_shapes=[
                pltpu.VMEM((total, length, width), BF16),
                pltpu.SemaphoreType.DMA((total,)),
                pltpu.SemaphoreType.DMA((total,)),
            ],
        ),
        out_shape=jax.ShapeDtypeStruct((count, length, width), BF16),
        compiler_params=params_of(1),
        cost_estimate=pl.CostEstimate(
            flops=0, transcendentals=0, bytes_accessed=4 * total * length * width
        ),
        name=name,
    )(table, *sources, *wait_for)


def after(value, earlier):
    def kernel(*refs):
        return

    return pl.pallas_call(
        kernel,
        in_specs=[ANY_SPEC] * (1 + len(earlier)),
        out_specs=ANY_SPEC,
        out_shape=jax.ShapeDtypeStruct(value.shape, value.dtype),
        input_output_aliases={0: 0},
        name="after",
    )(value, *earlier)


def norm_forward(summed, gain_row, shift_row):
    center = summed - jnp.mean(summed, axis=-1, keepdims=True)
    spread = jnp.mean(center * center, axis=-1, keepdims=True)
    scale = lax.rsqrt(spread + 1e-05)
    normed = center * scale
    return normed, normed * gain_row + shift_row, scale


def finish_forward(x, branch, gain_row, shift_row, y_ref, zn_ref, rstd_ref):
    normed, result, scale = norm_forward(x.astype(F32) + branch, gain_row, shift_row)
    y_ref[0] = result.astype(BF16)
    zn_ref[0] = normed.astype(BF16)
    rstd_ref[0] = jnp.broadcast_to(scale, rstd_ref.shape[1:])


def norm_backward(dy_ref, zn_ref, rstd_ref, gain_row):
    dy = dy_ref[0].astype(F32)
    normed = zn_ref[0].astype(F32)
    scale = rstd_ref[0][:, :1]
    scaled = dy * gain_row
    first = jnp.mean(scaled, axis=-1, keepdims=True)
    second = jnp.mean(scaled * normed, axis=-1, keepdims=True)
    gain_grad = jnp.sum(dy * normed, axis=0, keepdims=True)
    shift_grad = jnp.sum(dy, axis=0, keepdims=True)
    return (scaled - first - normed * second) * scale, gain_grad, shift_grad


def head_masks(length):
    lane = lax.broadcasted_iota(jnp.int32, (length, LANES), 1)
    low = lane < LANES // 2
    return low


def attention_forward(part, tables, x, weights, norms, y_in):
    rows, counts = tables
    b = part // HALVES
    attn_qkv, attn_out = weights
    gains, shifts = norms
    slots, length, width = x.shape
    score_scale = (width // HEADS) ** (-0.5)
    base = part * SLOTS

    def kernel(rows_ref, counts_ref, x_ref, qkv_w, out_w, gain, shift, *rest):
        y_ref, qkv_ref, o_ref, zn_ref, rstd_ref = rest[-5:]
        i = pl.program_id(0)

        @pl.when(i < counts_ref[part * 8])
        def _():
            xv = x_ref[0]
            for third in range(3):
                cols = slice(third * width, (third + 1) * width)
                qkv_ref[0, :, cols] = nn(xv, qkv_w[:, cols]).astype(BF16)
            low = head_masks(length)
            zero = jnp.zeros((), BF16)
            for pair in range(width // LANES):
                at = pair * LANES
                q2 = qkv_ref[0, :, at : at + LANES] * jnp.asarray(score_scale, BF16)
                k2 = qkv_ref[0, :, width + at : width + at + LANES]
                v2 = qkv_ref[0, :, 2 * width + at : 2 * width + at + LANES]
                mixed = []
                for half in range(2):
                    qm = jnp.where(low if half == 0 else ~low, q2, zero)
                    s = nt(qm, k2)
                    e = jnp.exp(s - jnp.max(s, axis=-1, keepdims=True))
                    total = jnp.sum(e, axis=-1, keepdims=True)
                    mixed.append(nn(e.astype(BF16), v2) / total)
                o_ref[0, :, at : at + LANES] = jnp.where(low, mixed[0], mixed[1]).astype(BF16)
            branch = nn(o_ref[0], out_w[...])
            finish_forward(
                xv, branch, gain[0:1, :], shift[0:1, :], y_ref, zn_ref, rstd_ref
            )

    def at_row(i, r, c):
        return (r[base + i], 0, 0)

    def at_step(i, r, c):
        return (jnp.maximum(jnp.minimum(i, c[part * 8] - 1), 0), 0, 0)

    seq = (1, length, width)
    in_specs = [
        pl.BlockSpec(seq, at_row),
        pl.BlockSpec(
            (None, None, width, 3 * width), lambda i, r, c: (b, 0, 0, 0), pipeline_mode=pl.Buffered(1)
        ),
        pl.BlockSpec(
            (None, None, width, width), lambda i, r, c: (b, 0, 0, 0), pipeline_mode=pl.Buffered(1)
        ),
        pl.BlockSpec((8, width), lambda i, r, c: (0, 0)),
        pl.BlockSpec((8, width), lambda i, r, c: (0, 0)),
    ]
    args = [rows, counts, x, attn_qkv, attn_out, gains, shifts]
    alias = {}
    if y_in is not None:
        in_specs.append(pl.BlockSpec(memory_space=pl.ANY))
        alias = {len(args): 0}
        args.append(y_in)
    flops = OWN_CAP * length * width * (8 * width + 4 * length)
    return pl.pallas_call(
        kernel,
        grid_spec=pltpu.PrefetchScalarGridSpec(
            num_scalar_prefetch=2,
            grid=(OWN_CAP,),
            in_specs=in_specs,
            out_specs=[
                pl.BlockSpec(seq, at_row),
                pl.BlockSpec((1, length, 3 * width), at_step),
                pl.BlockSpec(seq, at_step),
                pl.BlockSpec(seq, at_step),
                pl.BlockSpec((1, length, LANES), at_step),
            ],
        ),
        out_shape=[
            jax.ShapeDtypeStruct((slots, length, width), BF16),
            jax.ShapeDtypeStruct((OWN_CAP, length, 3 * width), BF16),
            jax.ShapeDtypeStruct((OWN_CAP, length, width), BF16),
            jax.ShapeDtypeStruct((OWN_CAP, length, width), BF16),
            jax.ShapeDtypeStruct((OWN_CAP, length, LANES), F32),
        ],
        input_output_aliases=alias,
        compiler_params=params_of(1),
        cost_estimate=pl.CostEstimate(
            flops=2 * flops, transcendentals=OWN_CAP * HEADS * length * length, bytes_accessed=30 * 2**20
        ),
        name="attention_forward",
    )(*args)


def attention_backward(part, tables, x, dy, kept, weights, gains, dx_in, sums, packed):
    rows, counts = tables
    b = part // HALVES
    attn_qkv, attn_out = weights
    qkv, o, zn, rstd = kept
    slots, length, width = x.shape
    score_scale = (width // HEADS) ** (-0.5)
    base = part * SLOTS
    first = sums is None
    n_out = 4 if first else 3

    def kernel(rows_ref, counts_ref, x_ref, dy_ref, qkv_ref, o_ref, zn_ref, rstd_ref, qkv_w, out_w, gain, *rest):
        ins = rest[: len(rest) - n_out - 7]
        outs = rest[len(ins) : len(ins) + n_out]
        acc_qkv, acc_out, do_scr, dqkv_scr, dh_scr, dz_scr, sems = rest[-7:]
        dx_ref, small_ref = outs[0], outs[1]
        i = pl.program_id(0)
        here = i < counts_ref[part * 8]

        def copies():
            if first:
                pairs = ((acc_qkv, outs[2]), (acc_out, outs[3]))
            else:
                pairs = ((ins[0], acc_qkv), (ins[1], acc_out))
            return [
                pltpu.make_async_copy(source, target, sems.at[n])
                for n, (source, target) in enumerate(pairs)
            ]

        @pl.when(i == 0)
        def _():
            small_ref[...] = jnp.zeros_like(small_ref)
            if first:
                acc_qkv[...] = jnp.zeros_like(acc_qkv)
                acc_out[...] = jnp.zeros_like(acc_out)
            else:
                for copy in copies():
                    copy.start()

        @pl.when(here)
        def _():
            dz, gain_grad, shift_grad = norm_backward(dy_ref, zn_ref, rstd_ref, gain[0:1, :])
            small_ref[0:1, :] += gain_grad
            small_ref[1:2, :] += shift_grad
            dz_scr[...] = dz
            dh = dz.astype(BF16)
            dh_scr[...] = dh
            do_scr[...] = nt(dh, out_w[...]).astype(BF16)
            low = head_masks(length)
            zero = jnp.zeros((), BF16)
            for pair in range(width // LANES):
                at = pair * LANES
                q2 = qkv_ref[0, :, at : at + LANES] * jnp.asarray(score_scale, BF16)
                k2 = qkv_ref[0, :, width + at : width + at + LANES]
                v2 = qkv_ref[0, :, 2 * width + at : 2 * width + at + LANES]
                do2 = do_scr[:, at : at + LANES]
                dqs, dks, dvs = [], [], []
                for half in range(2):
                    mask = low if half == 0 else ~low
                    st = nt(jnp.where(mask, k2, zero), q2)
                    e = jnp.exp(st - jnp.max(st, axis=0, keepdims=True))
                    p = e * (1.0 / jnp.sum(e, axis=0, keepdims=True))
                    dvs.append(nn(p.astype(BF16), do2))
                    t = p * nt(jnp.where(mask, v2, zero), do2)
                    ds = (t - p * jnp.sum(t, axis=0, keepdims=True)).astype(BF16)
                    dks.append(nn(ds, q2))
                    dqs.append(tn(ds, k2))
                dqkv_scr[:, at : at + LANES] = (jnp.where(low, dqs[0], dqs[1]) * score_scale).astype(BF16)
                dqkv_scr[:, width + at : width + at + LANES] = jnp.where(low, dks[0], dks[1]).astype(BF16)
                dqkv_scr[:, 2 * width + at : 2 * width + at + LANES] = jnp.where(low, dvs[0], dvs[1]).astype(BF16)
            total = dz_scr[...]
            for third in range(3):
                cols = slice(third * width, (third + 1) * width)
                total = total + nt(dqkv_scr[:, cols], qkv_w[:, cols])
            dx_ref[0] = total.astype(BF16)

        if not first:

            @pl.when(i == 0)
            def _():
                for copy in copies():
                    copy.wait()

        @pl.when(here)
        def _():
            xv = x_ref[0]
            for third in range(3):
                cols = slice(third * width, (third + 1) * width)
                acc_qkv[:, cols] += tn(xv, dqkv_scr[:, cols])
            acc_out[...] += tn(o_ref[0], dh_scr[...])

        @pl.when(i == OWN_CAP - 1)
        def _():
            if first:
                for copy in copies():
                    copy.start()
                for copy in copies():
                    copy.wait()
            else:
                packed_ref = outs[2]
                groups, tall = packed_ref.shape[0], packed_ref.shape[1] // 4
                for third in range(3):
                    piece = acc_qkv[:, third * width : (third + 1) * width].astype(BF16)
                    packed_ref[:, third * tall : (third + 1) * tall, :] = piece.reshape(
                        groups, tall, width
                    )
                packed_ref[:, 3 * tall : 4 * tall, :] = (
                    acc_out[...].astype(BF16).reshape(groups, tall, width)
                )

    def at_row(i, r, c):
        return (r[base + i], 0, 0)

    def at_step(i, r, c):
        return (jnp.maximum(jnp.minimum(i, c[part * 8] - 1), 0), 0, 0)

    def whole(i, r, c):
        return (0, 0)

    seq = (1, length, width)
    in_specs = [
        pl.BlockSpec(seq, at_row),
        pl.BlockSpec(seq, at_row),
        pl.BlockSpec((1, length, 3 * width), at_step),
        pl.BlockSpec(seq, at_step),
        pl.BlockSpec(seq, at_step),
        pl.BlockSpec((1, length, LANES), at_step),
        pl.BlockSpec(
            (None, None, width, 3 * width), lambda i, r, c: (b, 0, 0, 0), pipeline_mode=pl.Buffered(1)
        ),
        pl.BlockSpec(
            (None, None, width, width), lambda i, r, c: (b, 0, 0, 0), pipeline_mode=pl.Buffered(1)
        ),
        pl.BlockSpec((8, width), whole),
    ]
    args = [rows, counts, x, dy, qkv, o, zn, rstd, attn_qkv, attn_out, gains]
    out_specs = [pl.BlockSpec(seq, at_row), pl.BlockSpec((8, width), whole)]
    out_shape = [
        jax.ShapeDtypeStruct((slots, length, width), BF16),
        jax.ShapeDtypeStruct((8, width), F32),
    ]
    if first:
        out_specs += [ANY_SPEC, ANY_SPEC]
        out_shape += [
            jax.ShapeDtypeStruct((width, 3 * width), F32),
            jax.ShapeDtypeStruct((width, width), F32),
        ]
    else:
        groups, total_rows = packed
        out_specs.append(
            pl.BlockSpec((groups, 4 * width // groups, width), lambda i, r, c: (0, 0, 0))
        )
        out_shape.append(jax.ShapeDtypeStruct((groups, total_rows, width), BF16))
        in_specs += [ANY_SPEC, ANY_SPEC]
        args += list(sums)
    in_specs.append(ANY_SPEC)
    alias = {len(args): 0}
    args.append(dx_in)
    flops = 2 * OWN_CAP * length * width * (8 * width + 4 * length)
    return pl.pallas_call(
        kernel,
        grid_spec=pltpu.PrefetchScalarGridSpec(
            num_scalar_prefetch=2,
            grid=(OWN_CAP,),
            in_specs=in_specs,
            out_specs=out_specs,
            scratch_shapes=[
                pltpu.VMEM((width, 3 * width), F32),
                pltpu.VMEM((width, width), F32),
                pltpu.VMEM((length, width), BF16),
                pltpu.VMEM((length, 3 * width), BF16),
                pltpu.VMEM((length, width), BF16),
                pltpu.VMEM((length, width), F32),
                pltpu.SemaphoreType.DMA((2,)),
            ],
        ),
        out_shape=out_shape,
        input_output_aliases=alias,
        compiler_params=params_of(1),
        cost_estimate=pl.CostEstimate(
            flops=flops, transcendentals=OWN_CAP * HEADS * length * length // 2, bytes_accessed=40 * 2**20
        ),
        name="attention_backward",
    )(*args)


def feed_forward(part, tables, x, weights, norms, y_in):
    rows, counts = tables
    b = part // HALVES
    ffn_up, ffn_down = weights
    gains, shifts = norms
    slots, length, width = x.shape
    hidden = ffn_up.shape[-1]
    parts = hidden // FF_PART
    kind = KINDS - 1
    base = part * SLOTS + kind * OWN_CAP

    def kernel(rows_ref, counts_ref, x_ref, up, down, gain, shift, *rest):
        y_ref, g_ref, slope_ref, zn_ref, rstd_ref, x_scr, h_scr = rest[-7:]
        c, i = pl.program_id(0), pl.program_id(1)

        @pl.when(i < counts_ref[part * 8 + kind])
        def _():
            @pl.when(c == 0)
            def _():
                x_scr[i] = x_ref[0]

            xv = x_scr[i]
            for sub in range(FF_PART // FF_SUB):
                cols = slice(sub * FF_SUB, (sub + 1) * FF_SUB)
                a = nn(xv, up[:, cols])
                phi = 0.5 + 0.5 * lax.erf(a * (0.5**0.5))
                slope = phi + a * (jnp.exp(a * a * -0.5) * 0.3989422804014327)
                g = (a * phi).astype(BF16)
                g_ref[0, :, cols] = g
                slope_ref[0, :, cols] = slope.astype(BF16)
            branch = nn(g_ref[0], down[...])

            @pl.when(c == 0)
            def _():
                h_scr[i] = branch

            @pl.when(jnp.logical_and(c > 0, c < parts - 1))
            def _():
                h_scr[i] += branch

            @pl.when(c == parts - 1)
            def _():
                finish_forward(
                    xv,
                    h_scr[i] + branch,
                    gain[kind : kind + 1, :],
                    shift[kind : kind + 1, :],
                    y_ref,
                    zn_ref,
                    rstd_ref,
                )

    def in_row(c, i, r, n):
        return (r[base + jnp.where(c == 0, i, OWN_CAP - 1)], 0, 0)

    def out_row(c, i, r, n):
        return (r[base + jnp.where(c == parts - 1, i, 0)], 0, 0)

    def out_step(c, i, r, n):
        return (jnp.where(c == parts - 1, jnp.maximum(jnp.minimum(i, n[part * 8 + kind] - 1), 0), 0), 0, 0)

    def part_step(c, i, r, n):
        return (jnp.maximum(jnp.minimum(i, n[part * 8 + kind] - 1), 0), 0, c)

    seq = (1, length, width)
    in_specs = [
        pl.BlockSpec(seq, in_row),
        pl.BlockSpec((None, None, width, FF_PART), lambda c, i, r, n: (b, 0, 0, c)),
        pl.BlockSpec((None, None, FF_PART, width), lambda c, i, r, n: (b, 0, c, 0)),
        pl.BlockSpec((8, width), lambda c, i, r, n: (0, 0)),
        pl.BlockSpec((8, width), lambda c, i, r, n: (0, 0)),
    ]
    args = [rows, counts, x, ffn_up, ffn_down, gains, shifts]
    alias = {}
    if y_in is not None:
        in_specs.append(pl.BlockSpec(memory_space=pl.ANY))
        alias = {len(args): 0}
        args.append(y_in)
    return pl.pallas_call(
        kernel,
        grid_spec=pltpu.PrefetchScalarGridSpec(
            num_scalar_prefetch=2,
            grid=(parts, OWN_CAP),
            in_specs=in_specs,
            out_specs=[
                pl.BlockSpec(seq, out_row),
                pl.BlockSpec((1, length, FF_PART), part_step),
                pl.BlockSpec((1, length, FF_PART), part_step),
                pl.BlockSpec(seq, out_step),
                pl.BlockSpec((1, length, LANES), out_step),
            ],
            scratch_shapes=[
                pltpu.VMEM((OWN_CAP, length, width), BF16),
                pltpu.VMEM((OWN_CAP, length, width), F32),
            ],
        ),
        out_shape=[
            jax.ShapeDtypeStruct((slots, length, width), BF16),
            jax.ShapeDtypeStruct((OWN_CAP, length, hidden), BF16),
            jax.ShapeDtypeStruct((OWN_CAP, length, hidden), BF16),
            jax.ShapeDtypeStruct((OWN_CAP, length, width), BF16),
            jax.ShapeDtypeStruct((OWN_CAP, length, LANES), F32),
        ],
        input_output_aliases=alias,
        compiler_params=params_of(2),
        cost_estimate=pl.CostEstimate(
            flops=4 * OWN_CAP * length * width * hidden,
            transcendentals=2 * OWN_CAP * length * hidden,
            bytes_accessed=40 * 2**20,
        ),
        name="feed_forward",
    )(*args)


def feed_backward(part, tables, x, dy, kept, weights, gains, sums, packed):
    rows, counts = tables
    b = part // HALVES
    ffn_up, ffn_down = weights
    g, slope, zn, rstd = kept
    slots, length, width = x.shape
    hidden = ffn_up.shape[-1]
    parts = hidden // FF_PART
    kind = KINDS - 1
    base = part * SLOTS + kind * OWN_CAP
    first = sums is None
    groups = packed[0]
    tall = width // groups
    deep = hidden // groups

    def kernel(
        rows_ref, counts_ref, x_ref, dy_ref, g_ref, slope_ref, zn_ref, rstd_ref, up, down, gain, *rest
    ):
        if first:
            dx_ref, small_ref, acc_up, acc_down = rest[:4]
        else:
            sum_up, sum_down, dx_ref, small_ref, packed_ref = rest[:5]
            acc_up, acc_down, low_up, low_down, tally, sems = rest[-6:]
        x_scr, dh_scr, dx_scr, da_scr = rest[-4:] if first else rest[-10:-6]
        c, i = pl.program_id(0), pl.program_id(1)

        @pl.when(jnp.logical_and(c == 0, i == 0))
        def _():
            small_ref[...] = jnp.zeros_like(small_ref)

        @pl.when(i == 0)
        def _():
            if first:
                acc_up[...] = jnp.zeros_like(acc_up)
                acc_down[...] = jnp.zeros_like(acc_down)
            else:
                acc_up[...] = sum_up[...]
                acc_down[...] = sum_down[...]

        @pl.when(i < counts_ref[part * 8 + kind])
        def _():
            @pl.when(c == 0)
            def _():
                dz, gain_grad, shift_grad = norm_backward(
                    dy_ref, zn_ref, rstd_ref, gain[kind : kind + 1, :]
                )
                small_ref[0:1, :] += gain_grad
                small_ref[1:2, :] += shift_grad
                x_scr[i] = x_ref[0]
                dh_scr[i] = dz.astype(BF16)
                dx_scr[i] = dz

            dh = dh_scr[i]
            for sub in range(FF_PART // FF_SUB):
                cols = slice(sub * FF_SUB, (sub + 1) * FF_SUB)
                dg = nt(dh, down[cols, :])
                da_scr[:, cols] = (dg * slope_ref[0, :, cols].astype(F32)).astype(BF16)
            acc_down[...] += tn(g_ref[0], dh)
            acc_up[...] += tn(x_scr[i], da_scr[...])
            total = dx_scr[i] + nt(da_scr[...], up[...])

            @pl.when(c < parts - 1)
            def _():
                dx_scr[i] = total

            @pl.when(c == parts - 1)
            def _():
                dx_ref[0] = total.astype(BF16)

        if not first:

            @pl.when(i == OWN_CAP - 1)
            def _():
                low_up[...] = acc_up[...].astype(BF16)
                low_down[...] = acc_down[...].astype(BF16)
                copies = [
                    pltpu.make_async_copy(
                        low_up.at[pl.ds(z * tall, tall)],
                        packed_ref.at[z, pl.ds(c * tall, tall)],
                        sems.at[z],
                    )
                    for z in range(groups)
                ]
                shares = FF_PART // deep
                lane = lax.broadcasted_iota(jnp.int32, (COUNT_ROWS, width), 1)
                counted = jnp.zeros((COUNT_ROWS, width), F32)
                for k in range(KINDS):
                    there = sum(counts_ref[(b * HALVES + half) * 8 + k] for half in range(HALVES))
                    counted = jnp.where(lane == k, there.astype(F32), counted)
                tally[...] = counted.astype(BF16)
                copies += [
                    pltpu.make_async_copy(
                        tally,
                        packed_ref.at[z, pl.ds(parts * tall + deep, COUNT_ROWS)],
                        sems.at[groups + shares + z],
                    )
                    for z in range(groups)
                ]
                copies += [
                    pltpu.make_async_copy(
                        low_down.at[pl.ds(m * deep, deep)],
                        packed_ref.at[c * shares + m, pl.ds(parts * tall, deep)],
                        sems.at[groups + m],
                    )
                    for m in range(shares)
                ]
                for copy in copies:
                    copy.start()
                for copy in copies:
                    copy.wait()

    def in_row(c, i, r, n):
        return (r[base + jnp.where(c == 0, i, OWN_CAP - 1)], 0, 0)

    def in_step(c, i, r, n):
        last = jnp.maximum(n[part * 8 + kind] - 1, 0)
        return (jnp.where(c == 0, jnp.minimum(i, last), last), 0, 0)

    def out_row(c, i, r, n):
        return (r[base + jnp.where(c == parts - 1, i, 0)], 0, 0)

    def part_step(c, i, r, n):
        return (jnp.maximum(jnp.minimum(i, n[part * 8 + kind] - 1), 0), 0, c)

    seq = (1, length, width)
    in_specs = [
        pl.BlockSpec(seq, in_row),
        pl.BlockSpec(seq, in_row),
        pl.BlockSpec((1, length, FF_PART), part_step),
        pl.BlockSpec((1, length, FF_PART), part_step),
        pl.BlockSpec(seq, in_step),
        pl.BlockSpec((1, length, LANES), in_step),
        pl.BlockSpec((None, None, width, FF_PART), lambda c, i, r, n: (b, 0, 0, c)),
        pl.BlockSpec((None, None, FF_PART, width), lambda c, i, r, n: (b, 0, c, 0)),
        pl.BlockSpec((8, width), lambda c, i, r, n: (0, 0)),
    ]
    args = [rows, counts, x, dy, g, slope, zn, rstd, ffn_up, ffn_down, gains]
    up_spec = pl.BlockSpec((width, FF_PART), lambda c, i, r, n: (0, c))
    down_spec = pl.BlockSpec((FF_PART, width), lambda c, i, r, n: (c, 0))
    out_specs = [pl.BlockSpec(seq, out_row), pl.BlockSpec((8, width), lambda c, i, r, n: (0, 0))]
    out_shape = [
        jax.ShapeDtypeStruct((slots, length, width), BF16),
        jax.ShapeDtypeStruct((8, width), F32),
    ]
    scratch = [
        pltpu.VMEM((OWN_CAP, length, width), BF16),
        pltpu.VMEM((OWN_CAP, length, width), BF16),
        pltpu.VMEM((OWN_CAP, length, width), F32),
        pltpu.VMEM((length, FF_PART), BF16),
    ]
    if first:
        out_specs += [up_spec, down_spec]
        out_shape += [
            jax.ShapeDtypeStruct((width, hidden), F32),
            jax.ShapeDtypeStruct((hidden, width), F32),
        ]
    else:
        in_specs += [up_spec, down_spec]
        args += list(sums)
        out_specs.append(ANY_SPEC)
        out_shape.append(
            jax.ShapeDtypeStruct((groups, parts * tall + deep + COUNT_ROWS, width), BF16)
        )
        scratch += [
            pltpu.VMEM((width, FF_PART), F32),
            pltpu.VMEM((FF_PART, width), F32),
            pltpu.VMEM((width, FF_PART), BF16),
            pltpu.VMEM((FF_PART, width), BF16),
            pltpu.VMEM((COUNT_ROWS, width), BF16),
            pltpu.SemaphoreType.DMA((2 * groups + FF_PART // deep,)),
        ]
    return pl.pallas_call(
        kernel,
        grid_spec=pltpu.PrefetchScalarGridSpec(
            num_scalar_prefetch=2,
            grid=(parts, OWN_CAP),
            in_specs=in_specs,
            out_specs=out_specs,
            scratch_shapes=scratch,
        ),
        out_shape=out_shape,
        compiler_params=params_of(2),
        cost_estimate=pl.CostEstimate(
            flops=4 * OWN_CAP * length * width * hidden,
            transcendentals=0,
            bytes_accessed=50 * 2**20,
        ),
        name="feed_backward",
    )(*args)


PAD = 8
ROW_TILE = 128
COL_TILE = 256


def fill_padded(padded, values):
    length = values.shape[0]
    edge = jnp.zeros((PAD, values.shape[1]), F32)
    padded[0:PAD, :] = edge
    padded[PAD + length : PAD + length + PAD, :] = edge
    padded[PAD : PAD + length, :] = values


def conv_forward(part, tables, x, weights, norms, y_in):
    rows, counts = tables
    b = part // HALVES
    taps, conv_point = weights
    gains, shifts = norms
    slots, length, width = x.shape
    base = part * SLOTS + OWN_CAP
    steps = (KINDS - 2) * OWN_CAP

    def kernel(rows_ref, counts_ref, x_ref, point, taps_ref, gain, shift, *rest):
        y_ref, u_ref, zn_ref, rstd_ref, xpad = rest[-5:]
        step = pl.program_id(0)
        which, j = step // OWN_CAP, step % OWN_CAP
        for kind in range(1, KINDS - 1):
            taps_n = 2 * kind + 1
            first = kind * kind - 1

            @pl.when(jnp.logical_and(which == kind - 1, j < counts_ref[part * 8 + kind]))
            def _():
                fill_padded(xpad, x_ref[0].astype(F32))
                for r in range(0, length, ROW_TILE):
                    for col in range(0, width, COL_TILE):
                        cols = slice(col, col + COL_TILE)
                        mixed = None
                        for t in range(taps_n):
                            start = PAD + r + t - kind
                            term = xpad[start : start + ROW_TILE, cols] * taps_ref[first + t : first + t + 1, cols]
                            mixed = term if mixed is None else mixed + term
                        u_ref[0, r : r + ROW_TILE, cols] = mixed.astype(BF16)
                branch = nn(u_ref[0], point[...])
                finish_forward(
                    x_ref[0],
                    branch,
                    gain[kind : kind + 1, :],
                    shift[kind : kind + 1, :],
                    y_ref,
                    zn_ref,
                    rstd_ref,
                )

    def at_row(i, r, c):
        return (r[base + i], 0, 0)

    def at_step(i, r, c):
        which = i // OWN_CAP
        last = c[part * 8 + 1 + which] - 1
        return (which * OWN_CAP + jnp.maximum(jnp.minimum(i % OWN_CAP, last), 0), 0, 0)

    def whole(i, r, c):
        return (0, 0)

    seq = (1, length, width)
    in_specs = [
        pl.BlockSpec(seq, at_row),
        pl.BlockSpec((None, None, None, width, width), lambda i, r, c: (b, 0, i // OWN_CAP, 0, 0)),
        pl.BlockSpec((16, width), whole),
        pl.BlockSpec((8, width), whole),
        pl.BlockSpec((8, width), whole),
    ]
    args = [rows, counts, x, conv_point, taps, gains, shifts]
    alias = {}
    if y_in is not None:
        in_specs.append(pl.BlockSpec(memory_space=pl.ANY))
        alias = {len(args): 0}
        args.append(y_in)
    return pl.pallas_call(
        kernel,
        grid_spec=pltpu.PrefetchScalarGridSpec(
            num_scalar_prefetch=2,
            grid=(steps,),
            in_specs=in_specs,
            out_specs=[
                pl.BlockSpec(seq, at_row),
                pl.BlockSpec(seq, at_step),
                pl.BlockSpec(seq, at_step),
                pl.BlockSpec((1, length, LANES), at_step),
            ],
            scratch_shapes=[pltpu.VMEM((length + 2 * PAD, width), F32)],
        ),
        out_shape=[
            jax.ShapeDtypeStruct((slots, length, width), BF16),
            jax.ShapeDtypeStruct((steps, length, width), BF16),
            jax.ShapeDtypeStruct((steps, length, width), BF16),
            jax.ShapeDtypeStruct((steps, length, LANES), F32),
        ],
        input_output_aliases=alias,
        compiler_params=params_of(1),
        cost_estimate=pl.CostEstimate(
            flops=2 * steps * length * width * width, transcendentals=0, bytes_accessed=36 * 2**20
        ),
        name="conv_forward",
    )(*args)


def conv_backward(part, tables, x, dy, kept, weights, gains, dx_in, sums, packed):
    rows, counts = tables
    b = part // HALVES
    taps, conv_point = weights
    u, zn, rstd = kept
    slots, length, width = x.shape
    base = part * SLOTS + OWN_CAP
    steps = (KINDS - 2) * OWN_CAP
    first_half = sums is None
    groups = packed[0]

    def kernel(rows_ref, counts_ref, x_ref, dy_ref, u_ref, zn_ref, rstd_ref, point, taps_ref, gain, *rest):
        if first_half:
            dx_ref, small_ref, acc, xpad, dupad, dz_scr = rest[-6:]
        else:
            sum_ref = rest[0]
            dx_ref, small_ref, packed_ref, xpad, dupad, dz_scr, acc = rest[-7:]
        step = pl.program_id(0)
        which, j = step // OWN_CAP, step % OWN_CAP

        @pl.when(step == 0)
        def _():
            small_ref[...] = jnp.zeros_like(small_ref)

        @pl.when(j == 0)
        def _():
            acc[...] = jnp.zeros_like(acc) if first_half else sum_ref[...]

        for kind in range(1, KINDS - 1):
            taps_n = 2 * kind + 1
            first = kind * kind - 1

            @pl.when(jnp.logical_and(which == kind - 1, j < counts_ref[part * 8 + kind]))
            def _():
                dz, gain_grad, shift_grad = norm_backward(
                    dy_ref, zn_ref, rstd_ref, gain[kind : kind + 1, :]
                )
                small_ref[14 + kind : 15 + kind, :] += gain_grad
                small_ref[17 + kind : 18 + kind, :] += shift_grad
                dz_scr[...] = dz
                dh = dz.astype(BF16)
                acc[...] += tn(u_ref[0], dh)
                fill_padded(xpad, x_ref[0].astype(F32))
                fill_padded(dupad, nt(dh, point[...]))
                for col in range(0, width, COL_TILE):
                    cols = slice(col, col + COL_TILE)
                    sums = [None] * taps_n
                    for r in range(0, length, ROW_TILE):
                        here = dupad[PAD + r : PAD + r + ROW_TILE, cols]
                        total = dz_scr[r : r + ROW_TILE, cols]
                        for t in range(taps_n):
                            back = PAD + r - t + kind
                            total = total + dupad[back : back + ROW_TILE, cols] * taps_ref[first + t : first + t + 1, cols]
                            ahead = PAD + r + t - kind
                            part = jnp.sum(
                                xpad[ahead : ahead + ROW_TILE, cols] * here, axis=0, keepdims=True
                            )
                            sums[t] = part if sums[t] is None else sums[t] + part
                        dx_ref[0, r : r + ROW_TILE, cols] = total.astype(BF16)
                    for t in range(taps_n):
                        small_ref[first + t : first + t + 1, cols] += sums[t]

        if not first_half:

            @pl.when(j == OWN_CAP - 1)
            def _():
                packed_ref[...] = acc[...].astype(BF16).reshape(packed_ref.shape)

    def at_row(i, r, c):
        return (r[base + i], 0, 0)

    def at_step(i, r, c):
        which = i // OWN_CAP
        last = c[part * 8 + 1 + which] - 1
        return (which * OWN_CAP + jnp.maximum(jnp.minimum(i % OWN_CAP, last), 0), 0, 0)

    def whole(i, r, c):
        return (0, 0)

    seq = (1, length, width)
    in_specs = [
        pl.BlockSpec(seq, at_row),
        pl.BlockSpec(seq, at_row),
        pl.BlockSpec(seq, at_step),
        pl.BlockSpec(seq, at_step),
        pl.BlockSpec((1, length, LANES), at_step),
        pl.BlockSpec((None, None, None, width, width), lambda i, r, c: (b, 0, i // OWN_CAP, 0, 0)),
        pl.BlockSpec((16, width), whole),
        pl.BlockSpec((8, width), whole),
    ]
    args = [rows, counts, x, dy, u, zn, rstd, conv_point, taps, gains]
    sum_spec = pl.BlockSpec((None, width, width), lambda i, r, c: (i // OWN_CAP, 0, 0))
    out_specs = [pl.BlockSpec(seq, at_row), pl.BlockSpec((24, width), whole)]
    out_shape = [
        jax.ShapeDtypeStruct((slots, length, width), BF16),
        jax.ShapeDtypeStruct((24, width), F32),
    ]
    scratch = [
        pltpu.VMEM((length + 2 * PAD, width), F32),
        pltpu.VMEM((length + 2 * PAD, width), F32),
        pltpu.VMEM((length, width), F32),
    ]
    alias = {}
    if first_half:
        out_specs.append(sum_spec)
        out_shape.append(jax.ShapeDtypeStruct((KINDS - 2, width, width), F32))
    else:
        in_specs.append(sum_spec)
        args.append(sums)
        out_specs.append(
            pl.BlockSpec((groups, width // groups, width), lambda i, r, c: (0, 4 + i // OWN_CAP, 0))
        )
        out_shape.append(jax.ShapeDtypeStruct(packed[1].shape, BF16))
        in_specs.append(ANY_SPEC)
        alias = {len(args): 2}
        args.append(packed[1])
        scratch.append(pltpu.VMEM((width, width), F32))
    in_specs.append(ANY_SPEC)
    alias = {**alias, len(args): 0}
    args.append(dx_in)
    return pl.pallas_call(
        kernel,
        grid_spec=pltpu.PrefetchScalarGridSpec(
            num_scalar_prefetch=2,
            grid=(steps,),
            in_specs=in_specs,
            out_specs=out_specs,
            scratch_shapes=scratch,
        ),
        out_shape=out_shape,
        input_output_aliases=alias,
        compiler_params=params_of(1),
        cost_estimate=pl.CostEstimate(
            flops=3 * steps * length * width * width, transcendentals=0, bytes_accessed=50 * 2**20
        ),
        name="conv_backward",
    )(*args)


def owner_forward(part, tables, x, weights, small_weights):
    attn_qkv, attn_out, ffn_up, ffn_down, conv_point = weights
    taps, gains, shifts = small_weights
    norms = (gains, shifts)
    y, g, slope, zn_f, rstd_f = feed_forward(part, tables, x, (ffn_up, ffn_down), norms, None)
    y, qkv, o, zn_a, rstd_a = attention_forward(part, tables, x, (attn_qkv, attn_out), norms, y)
    y, u, zn_c, rstd_c = conv_forward(part, tables, x, (taps, conv_point), norms, y)
    return y, ((g, slope, zn_f, rstd_f), (qkv, o, zn_a, rstd_a), (u, zn_c, rstd_c))


def join_small(small_f, small_a, small_c):
    return jnp.concatenate(
        [
            small_c[:15],
            small_a[0:1],
            small_c[15:18],
            small_f[0:1],
            small_a[1:2],
            small_c[18:21],
            small_f[1:2],
        ]
    )


def owner_backward(b, tables, x, dy, kept, weights, small_weights, groups):
    attn_qkv, attn_out, ffn_up, ffn_down, conv_point = weights
    taps, gains, shifts = small_weights
    width = x[0].shape[-1]
    rest_rows = 7 * width // groups + SMALL_ROWS
    dx, smalls = [None, None], [None, None]
    sums = None
    for half in range(HALVES):
        part = b * HALVES + half
        kept_f, kept_a, kept_c = kept[half]
        xh, dyh = x[half], dy[half]
        first = half == 0
        if first:
            d, small_f, *sum_f = feed_backward(
                part, tables, xh, dyh, kept_f, (ffn_up, ffn_down), gains, None, (groups,)
            )
            d, small_a, *sum_a = attention_backward(
                part, tables, xh, dyh, kept_a, (attn_qkv, attn_out), gains, d, None, None
            )
            d, small_c, sum_c = conv_backward(
                part, tables, xh, dyh, kept_c, (taps, conv_point), gains, d, None, (groups,)
            )
        else:
            d, small_f, feed_pack = feed_backward(
                part, tables, xh, dyh, kept_f, (ffn_up, ffn_down), gains, sum_f, (groups,)
            )
            d, small_a, rest_pack = attention_backward(
                part, tables, xh, dyh, kept_a, (attn_qkv, attn_out), gains, d, sum_a, (groups, rest_rows)
            )
            d, small_c, rest_pack = conv_backward(
                part, tables, xh, dyh, kept_c, (taps, conv_point), gains, d, sum_c, (groups, rest_pack)
            )
        dx[half] = d
        smalls[half] = join_small(small_f, small_a, small_c)
    small = (smalls[0] + smalls[1]).astype(BF16).reshape(25, groups, width // groups)
    small = small.transpose(1, 0, 2)
    small = jnp.pad(small, ((0, 0), (0, SMALL_ROWS - 25), (0, width - width // groups)))
    rest_pack = lax.dynamic_update_slice(rest_pack, small, (0, rest_rows - SMALL_ROWS, 0))
    return dx, feed_pack, rest_pack


def finish_feed(b, feed, up_out, down_out, shapes):
    parts = shapes[0].shape[-1] // FF_PART
    tall, width = shapes[0].shape[2], FF_PART
    count_block = 2 * parts * tall // COUNT_ROWS

    def kernel(up_ref, down_ref, count_ref, *rest):
        up_to, down_to = rest[-2:]
        scale = 1.0 / count_ref[0:1, KINDS - 1 : KINDS].astype(F32)
        up_to[...] = up_ref[...].astype(F32) * scale
        down_to[...] = down_ref[...].astype(F32) * scale

    old = [] if up_out is None else [up_out, down_out]
    return pl.pallas_call(
        kernel,
        grid=(parts,),
        in_specs=[
            pl.BlockSpec((tall, width), lambda c: (c, 0)),
            pl.BlockSpec((tall, width), lambda c: (parts + c, 0)),
            pl.BlockSpec((COUNT_ROWS, width), lambda c: (count_block, 0)),
        ]
        + [ANY_SPEC] * len(old),
        out_specs=[
            pl.BlockSpec((None, None, tall, width), lambda c: (b, 0, 0, c)),
            pl.BlockSpec((None, None, tall, width), lambda c: (b, 0, c, 0)),
        ],
        out_shape=list(shapes),
        input_output_aliases={3 + n: n for n in range(len(old))},
        compiler_params=params_of(1),
        cost_estimate=pl.CostEstimate(flops=0, transcendentals=0, bytes_accessed=8 * 2**20),
        name="finish_feed",
    )(feed, feed, feed, *old)


def finish_rest(b, rest, feed, old, shapes):
    tall, width = shapes[1].shape[2:]
    count_block = (feed.shape[0] - COUNT_ROWS) // COUNT_ROWS
    small_block = 7 * tall // SMALL_ROWS

    def kernel(rest_ref, small_ref, count_ref, *refs):
        qkv_to, out_to, taps_to, point_to, gain_to, shift_to = refs[-6:]
        i = pl.program_id(0)
        scales = 1.0 / count_ref[0:1, 0:8].astype(F32)
        values = rest_ref[...].astype(F32)

        @pl.when(i < 3)
        def _():
            qkv_to[...] = values * scales[:, 0:1]

        @pl.when(i == 3)
        def _():
            out_to[...] = values * scales[:, 0:1]
            small = small_ref[...].astype(F32)
            row = lax.broadcasted_iota(jnp.int32, small.shape, 0)
            which = jnp.where(row < 3, 1, jnp.where(row < 8, 2, jnp.where(row < 15, 3, 0)))
            which = jnp.where(row >= 15, row - 15, which)
            which = jnp.where(row >= 20, row - 20, which)
            scale = jnp.zeros_like(small)
            for k in range(KINDS):
                scale = jnp.where(which == k, scales[:, k : k + 1], scale)
            small = small * scale
            taps_to[...] = small[:15, :tall]
            gain_to[...] = small[15:20, :tall]
            shift_to[...] = small[20:25, :tall]

        for k in range(1, KINDS - 1):

            @pl.when(i == 3 + k)
            def _():
                point_to[...] = values * scales[:, k : k + 1]

    old = list(old)
    return pl.pallas_call(
        kernel,
        grid=(7,),
        in_specs=[
            pl.BlockSpec((tall, width), lambda i: (i, 0)),
            pl.BlockSpec((SMALL_ROWS, width), lambda i: (small_block, 0)),
            pl.BlockSpec((COUNT_ROWS, width), lambda i: (count_block, 0)),
        ]
        + [ANY_SPEC] * len(old),
        out_specs=[
            pl.BlockSpec((None, None, tall, width), lambda i: (b, 0, 0, jnp.minimum(i, 2))),
            pl.BlockSpec((None, None, tall, width), lambda i: (b, 0, 0, 0)),
            pl.BlockSpec((None, None, 15, tall), lambda i: (b, 0, 0, 0)),
            pl.BlockSpec(
                (None, None, None, tall, width), lambda i: (b, 0, jnp.maximum(i - 4, 0), 0, 0)
            ),
            pl.BlockSpec((None, None, KINDS, tall), lambda i: (b, 0, 0, 0)),
            pl.BlockSpec((None, None, KINDS, tall), lambda i: (b, 0, 0, 0)),
        ],
        out_shape=list(shapes),
        input_output_aliases={3 + n: n for n in range(len(old))},
        compiler_params=params_of(1),
        cost_estimate=pl.CostEstimate(flops=0, transcendentals=0, bytes_accessed=8 * 2**20),
        name="finish_rest",
    )(rest, rest, feed, *old)


def small_params(b, conv_taps, norm_gain, norm_bias):
    taps = jnp.pad(conv_taps[b, 0].astype(F32), ((0, 1), (0, 0)))
    gains = jnp.pad(norm_gain[b, 0].astype(F32), ((0, 3), (0, 0)))
    shifts = jnp.pad(norm_bias[b, 0].astype(F32), ((0, 3), (0, 0)))
    return taps, gains, shifts


def exchange(rows):
    return lax.all_to_all(rows, "op", split_axis=0, concat_axis=0, tiled=True)


def per_device(
    inputs,
    candidate,
    attn_qkv,
    attn_out,
    ffn_up,
    ffn_down,
    conv_taps,
    conv_point,
    norm_gain,
    norm_bias,
    cotangent,
):
    owners = lax.axis_size("op")
    groups = lax.axis_size("dp")
    seqs = inputs.shape[0]
    width = inputs.shape[-1]
    hidden = ffn_up.shape[-1]
    weights = (attn_qkv, attn_out, ffn_up, ffn_down, conv_point)
    smalls = [small_params(b, conv_taps, norm_gain, norm_bias) for b in range(BLOCKS)]
    send, relay, tags = home_tables(candidate.reshape(-1), owners, seqs)
    arrived = exchange(tags.reshape(owners, BLOCKS * HALVES))
    tables = owner_tables(arrived.reshape(-1), owners)
    both = range(HALVES)

    def start(b, half):
        return (b * HALVES + half) * owners

    x0 = [
        exchange(move_rows(send, [start(0, h)], [inputs], owners, False, "send_inputs"))
        for h in both
    ]
    y0, kept0 = zip(*[owner_forward(h, tables, x0[h], weights, smalls[0]) for h in both])
    x1 = []
    for h in both:
        back = exchange(y0[h])
        x1.append(exchange(move_rows(relay, [start(0, h)], [back], owners, False, "relay_x")))
    y1, kept1 = zip(
        *[owner_forward(HALVES + h, tables, x1[h], weights, smalls[1]) for h in both]
    )
    dy1 = [
        exchange(
            move_rows(
                send, [start(1, h)], [cotangent], owners, False, "send_cotangent", (y1[h],)
            )
        )
        for h in both
    ]
    dx1, feed1, rest1 = owner_backward(1, tables, x1, dy1, kept1, weights, smalls[1], groups)
    dy0 = []
    for h in both:
        back = exchange(dx1[h])
        dy0.append(exchange(move_rows(relay, [start(1, h)], [back], owners, False, "relay_dx")))
    dx0, feed0, rest0 = owner_backward(0, tables, x0, dy0, kept0, weights, smalls[0], groups)
    starts = [start(1, h) for h in both]
    y_home = [exchange(after(y1[h], (dy0[1],))) for h in both]
    outputs = move_rows(send, starts, y_home, seqs, True, "outputs")
    starts = [start(0, h) for h in both]
    dx_home = [exchange(dx0[h]) for h in both]
    input_grad = move_rows(send, starts, dx_home, seqs, True, "input_grad")

    tall, deep = width // groups, hidden // groups
    grad = lambda *dims: jax.ShapeDtypeStruct((BLOCKS, 1) + dims, F32)
    feed_shapes = (grad(tall, hidden), grad(deep, width))
    rest_shapes = (
        grad(tall, 3 * width),
        grad(tall, width),
        grad(15, tall),
        grad(KINDS - 2, tall, width),
        grad(KINDS, tall),
        grad(KINDS, tall),
    )
    earlier, feeds, rests = None, (None, None), ()
    for b, feed, rest in ((1, feed1, rest1), (0, feed0, rest0)):
        if earlier is not None:
            feed = after(feed, (earlier,))
        feed = lax.psum_scatter(feed, "dp", scatter_dimension=0, tiled=False)
        rest = after(rest, (feed,) if b else (feed, y_home[0], dx_home[0]))
        earlier = lax.psum_scatter(rest, "dp", scatter_dimension=0, tiled=False)
        feeds = finish_feed(b, feed, *feeds, feed_shapes)
        rests = finish_rest(b, earlier, feed, rests, rest_shapes)
    qkv, out, taps, point, gain, shift = rests
    grads = (qkv, out, *feeds, taps, point, gain, shift)
    return (outputs, input_grad) + grads


def solution(mesh):
    placed = (
        P(("dp", "op"), None, None),
        P(("dp", "op"), None),
        P(None, "op", None, None),
        P(None, "op", None, None),
        P(None, "op", None, None),
        P(None, "op", None, None),
        P(None, "op", None, None),
        P(None, "op", None, None, None),
        P(None, "op", None, None),
        P(None, "op", None, None),
        P(("dp", "op"), None, None),
    )
    return jax.shard_map(
        per_device,
        mesh=mesh,
        in_specs=placed,
        out_specs=(
            P(("dp", "op"), None, None),
            P(("dp", "op"), None, None),
            P(None, "op", "dp", None),
            P(None, "op", "dp", None),
            P(None, "op", "dp", None),
            P(None, "op", "dp", None),
            P(None, "op", None, "dp"),
            P(None, "op", None, "dp", None),
            P(None, "op", None, "dp"),
            P(None, "op", None, "dp"),
        ),
        check_vma=False,
    )
```

```python
import jax
import jax.numpy as jnp
from jax import lax
from jax.experimental import pallas as pl
from jax.experimental.pallas import tpu as pltpu
from jax.sharding import PartitionSpec as P

HEADS = 12
KINDS = 5
BLOCKS = 2
OWN_CAP = 3
HALVES = 2
SLOTS = KINDS * OWN_CAP
FF_PART = 768
FF_SUB = 256
LANES = 128
SMALL_ROWS = 32
COUNT_ROWS = 16
BF16 = jnp.bfloat16
F32 = jnp.float32
VMEM_BYTES = 60 * 2**20


def params_of(axes):
    return pltpu.CompilerParams(
        dimension_semantics=("arbitrary",) * axes, vmem_limit_bytes=VMEM_BYTES
    )


def nn(a, b):
    return lax.dot_general(a, b, (((1,), (0,)), ((), ())), preferred_element_type=F32)


def nt(a, b):
    return lax.dot_general(a, b, (((1,), (1,)), ((), ())), preferred_element_type=F32)


def tn(a, b):
    return lax.dot_general(a, b, (((0,), (0,)), ((), ())), preferred_element_type=F32)


def home_kernel(owners, seqs, cand, send, relay, tags, color, partner, first, tally):
    for b in range(BLOCKS):

        def clear_owner(o, _):
            first[b * owners + o] = -1
            for half in range(HALVES):
                send[(b * HALVES + half) * owners + o] = -1
                relay[(b * HALVES + half) * owners + o] = -1
                tags[o * BLOCKS * HALVES + b * HALVES + half] = KINDS
            return 0

        lax.fori_loop(0, owners, clear_owner, 0)
    for half in range(HALVES):
        tally[half] = 0

    def pair_up(j, _):
        color[j] = -1
        for b in range(BLOCKS):
            o = b * owners + lax.rem(cand[j * BLOCKS + b], owners)
            other = first[o]
            partner[b * seqs + j] = other
            first[o] = j

            @pl.when(other >= 0)
            def _():
                partner[b * seqs + other] = j

        return 0

    lax.fori_loop(0, seqs, pair_up, 0)

    def give(j, shade):
        color[j] = shade
        tally[shade] = tally[shade] + 1

    def paint(j, _):
        @pl.when(color[j] < 0)
        def _():
            shade = jnp.where(tally[0] > tally[1], 1, 0).astype(jnp.int32)
            give(j, shade)
            for side in range(2):

                def more(state):
                    return state[0] >= 0

                def walk(state):
                    now, use, tone = state
                    after = partner[use * seqs + now]
                    free = jnp.logical_and(after >= 0, color[jnp.maximum(after, 0)] < 0)

                    @pl.when(free)
                    def _():
                        give(after, 1 - tone)

                    return (jnp.where(free, after, -1), 1 - use, 1 - tone)

                lax.while_loop(more, walk, (j, jnp.int32(side), shade))

        return 0

    lax.fori_loop(0, seqs, paint, 0)

    def place(j, _):
        half = color[j]
        spots = []
        for b in range(BLOCKS):
            c = cand[j * BLOCKS + b]
            o = lax.rem(c, owners)
            spots.append(o)
            send[(b * HALVES + half) * owners + o] = j
            tags[o * BLOCKS * HALVES + b * HALVES + half] = lax.div(c, owners)
        relay[half * owners + spots[1]] = spots[0]
        relay[(HALVES + half) * owners + spots[0]] = spots[1]
        return 0

    lax.fori_loop(0, seqs, place, 0)


SMEM_SPEC = pl.BlockSpec(memory_space=pltpu.SMEM)
ANY_SPEC = pl.BlockSpec(memory_space=pl.ANY)


def int_shape(n):
    return jax.ShapeDtypeStruct((n,), jnp.int32)


def home_tables(cand, owners, seqs):
    def kernel(*refs):
        home_kernel(owners, seqs, *refs)

    size = BLOCKS * HALVES * owners
    return pl.pallas_call(
        kernel,
        in_specs=[SMEM_SPEC],
        out_specs=[SMEM_SPEC] * 3,
        out_shape=[int_shape(size)] * 3,
        scratch_shapes=[
            pltpu.SMEM((seqs,), jnp.int32),
            pltpu.SMEM((BLOCKS * seqs,), jnp.int32),
            pltpu.SMEM((BLOCKS * owners,), jnp.int32),
            pltpu.SMEM((HALVES,), jnp.int32),
        ],
        name="home_tables",
    )(cand)


def owner_kernel(owners, tags, rows, counts):
    for b in range(BLOCKS):
        for half in range(HALVES):
            part = b * HALVES + half
            for k in range(8):
                counts[part * 8 + k] = 0

            def arrive(h, free):
                k = tags[h * BLOCKS * HALVES + part]
                there = k < KINDS

                @pl.when(there)
                def _():
                    n = jnp.minimum(counts[part * 8 + k], OWN_CAP - 1)
                    rows[part * SLOTS + k * OWN_CAP + n] = h
                    counts[part * 8 + k] = n + 1

                return jnp.where(there, free, h)

            free = lax.fori_loop(0, owners, arrive, jnp.int32(0))

            def spare(k, otherwise):
                return jnp.where(
                    counts[part * 8 + k] > 0, rows[part * SLOTS + k * OWN_CAP], otherwise
                )

            conv_spare = free
            for k in reversed(range(1, KINDS - 1)):
                conv_spare = spare(k, conv_spare)
            attn_spare = spare(0, conv_spare)
            feed_spare = spare(KINDS - 1, attn_spare)
            last = conv_spare
            for k, start in ((1, None), (2, None), (3, None), (0, attn_spare), (KINDS - 1, feed_spare)):
                last = last if start is None else start
                for i in range(OWN_CAP):
                    at = part * SLOTS + k * OWN_CAP + i
                    last = jnp.where(i < counts[part * 8 + k], rows[at], last)
                    rows[at] = last


def owner_tables(tags, owners):
    def kernel(*refs):
        owner_kernel(owners, *refs)

    return pl.pallas_call(
        kernel,
        in_specs=[SMEM_SPEC],
        out_specs=[SMEM_SPEC] * 2,
        out_shape=[int_shape(BLOCKS * HALVES * SLOTS), int_shape(BLOCKS * HALVES * 8)],
        name="owner_tables",
    )(tags)


def move_rows(table, starts, sources, count, scatter, name, wait_for=()):
    length, width = sources[0].shape[1:]
    each = table.shape[0] // (BLOCKS * HALVES)
    total = each * len(sources)

    def kernel(table_ref, *refs):
        ins = refs[: len(sources)]
        out_ref, buf, sem_in, sem_out = refs[-4:]

        def load(part, s):
            idx = table_ref[starts[part] + s]
            at = s if scatter else idx
            to = part * each + s
            return pltpu.make_async_copy(ins[part].at[at], buf.at[to], sem_in.at[to])

        def store(part, s):
            idx = table_ref[starts[part] + s]
            at = part * each + s
            to = idx if scatter else at
            return pltpu.make_async_copy(buf.at[at], out_ref.at[to], sem_out.at[at])

        todo = [(part, s) for part in range(len(sources)) for s in range(each)]
        for part, s in todo:

            @pl.when(table_ref[starts[part] + s] >= 0)
            def _():
                load(part, s).start()

        for part, s in todo:

            @pl.when(table_ref[starts[part] + s] >= 0)
            def _():
                load(part, s).wait()
                store(part, s).start()

        for part, s in todo:

            @pl.when(table_ref[starts[part] + s] >= 0)
            def _():
                store(part, s).wait()

    return pl.pallas_call(
        kernel,
        grid_spec=pltpu.PrefetchScalarGridSpec(
            num_scalar_prefetch=1,
            grid=(1,),
            in_specs=[ANY_SPEC] * (len(sources) + len(wait_for)),
            out_specs=ANY_SPEC,
            scratch_shapes=[
                pltpu.VMEM((total, length, width), BF16),
                pltpu.SemaphoreType.DMA((total,)),
                pltpu.SemaphoreType.DMA((total,)),
            ],
        ),
        out_shape=jax.ShapeDtypeStruct((count, length, width), BF16),
        compiler_params=params_of(1),
        cost_estimate=pl.CostEstimate(
            flops=0, transcendentals=0, bytes_accessed=4 * total * length * width
        ),
        name=name,
    )(table, *sources, *wait_for)


def after(value, earlier):
    def kernel(*refs):
        return

    return pl.pallas_call(
        kernel,
        in_specs=[ANY_SPEC] * (1 + len(earlier)),
        out_specs=ANY_SPEC,
        out_shape=jax.ShapeDtypeStruct(value.shape, value.dtype),
        input_output_aliases={0: 0},
        name="after",
    )(value, *earlier)


def norm_forward(summed, gain_row, shift_row):
    center = summed - jnp.mean(summed, axis=-1, keepdims=True)
    spread = jnp.mean(center * center, axis=-1, keepdims=True)
    scale = lax.rsqrt(spread + 1e-05)
    normed = center * scale
    return normed, normed * gain_row + shift_row, scale


def finish_forward(x, branch, gain_row, shift_row, y_ref, zn_ref, rstd_ref):
    normed, result, scale = norm_forward(x.astype(F32) + branch, gain_row, shift_row)
    y_ref[0] = result.astype(BF16)
    zn_ref[0] = normed.astype(BF16)
    rstd_ref[0] = jnp.broadcast_to(scale, rstd_ref.shape[1:])


def norm_backward(dy, zn_ref, rstd_ref, gain_row):
    dy = dy.astype(F32)
    normed = zn_ref[0].astype(F32)
    scale = rstd_ref[0][:, :1]
    scaled = dy * gain_row
    first = jnp.mean(scaled, axis=-1, keepdims=True)
    second = jnp.mean(scaled * normed, axis=-1, keepdims=True)
    gain_grad = jnp.sum(dy * normed, axis=0, keepdims=True)
    shift_grad = jnp.sum(dy, axis=0, keepdims=True)
    return (scaled - first - normed * second) * scale, gain_grad, shift_grad


def head_masks(length):
    lane = lax.broadcasted_iota(jnp.int32, (length, LANES), 1)
    low = lane < LANES // 2
    return low


def attention_forward(part, tables, x, weights, norms, y_in):
    rows, counts = tables
    b = part // HALVES
    attn_qkv, attn_out = weights
    gains, shifts = norms
    slots, length, width = x.shape
    score_scale = (width // HEADS) ** (-0.5)
    base = part * SLOTS

    def kernel(rows_ref, counts_ref, x_ref, qkv_w, out_w, gain, shift, *rest):
        y_ref, qkv_ref, o_ref, zn_ref, rstd_ref = rest[-5:]
        i = pl.program_id(0)

        @pl.when(i < counts_ref[part * 8])
        def _():
            xv = x_ref[0]
            for third in range(3):
                cols = slice(third * width, (third + 1) * width)
                qkv_ref[0, :, cols] = nn(xv, qkv_w[:, cols]).astype(BF16)
            low = head_masks(length)
            zero = jnp.zeros((), BF16)
            for pair in range(width // LANES):
                at = pair * LANES
                q2 = qkv_ref[0, :, at : at + LANES] * jnp.asarray(score_scale, BF16)
                k2 = qkv_ref[0, :, width + at : width + at + LANES]
                v2 = qkv_ref[0, :, 2 * width + at : 2 * width + at + LANES]
                mixed = []
                for half in range(2):
                    qm = jnp.where(low if half == 0 else ~low, q2, zero)
                    s = nt(qm, k2)
                    e = jnp.exp(s - jnp.max(s, axis=-1, keepdims=True))
                    total = jnp.sum(e, axis=-1, keepdims=True)
                    mixed.append(nn(e.astype(BF16), v2) / total)
                o_ref[0, :, at : at + LANES] = jnp.where(low, mixed[0], mixed[1]).astype(BF16)
            branch = nn(o_ref[0], out_w[...])
            finish_forward(
                xv, branch, gain[0:1, :], shift[0:1, :], y_ref, zn_ref, rstd_ref
            )

    def at_row(i, r, c):
        return (r[base + i], 0, 0)

    def at_step(i, r, c):
        return (jnp.maximum(jnp.minimum(i, c[part * 8] - 1), 0), 0, 0)

    seq = (1, length, width)
    in_specs = [
        pl.BlockSpec(seq, at_row),
        pl.BlockSpec(
            (None, None, width, 3 * width), lambda i, r, c: (b, 0, 0, 0), pipeline_mode=pl.Buffered(1)
        ),
        pl.BlockSpec(
            (None, None, width, width), lambda i, r, c: (b, 0, 0, 0), pipeline_mode=pl.Buffered(1)
        ),
        pl.BlockSpec((8, width), lambda i, r, c: (0, 0)),
        pl.BlockSpec((8, width), lambda i, r, c: (0, 0)),
    ]
    args = [rows, counts, x, attn_qkv, attn_out, gains, shifts]
    alias = {}
    if y_in is not None:
        in_specs.append(pl.BlockSpec(memory_space=pl.ANY))
        alias = {len(args): 0}
        args.append(y_in)
    flops = OWN_CAP * length * width * (8 * width + 4 * length)
    return pl.pallas_call(
        kernel,
        grid_spec=pltpu.PrefetchScalarGridSpec(
            num_scalar_prefetch=2,
            grid=(OWN_CAP,),
            in_specs=in_specs,
            out_specs=[
                pl.BlockSpec(seq, at_row),
                pl.BlockSpec((1, length, 3 * width), at_step),
                pl.BlockSpec(seq, at_step),
                pl.BlockSpec(seq, at_step),
                pl.BlockSpec((1, length, LANES), at_step),
            ],
        ),
        out_shape=[
            jax.ShapeDtypeStruct((slots, length, width), BF16),
            jax.ShapeDtypeStruct((OWN_CAP, length, 3 * width), BF16),
            jax.ShapeDtypeStruct((OWN_CAP, length, width), BF16),
            jax.ShapeDtypeStruct((OWN_CAP, length, width), BF16),
            jax.ShapeDtypeStruct((OWN_CAP, length, LANES), F32),
        ],
        input_output_aliases=alias,
        compiler_params=params_of(1),
        cost_estimate=pl.CostEstimate(
            flops=2 * flops, transcendentals=OWN_CAP * HEADS * length * length, bytes_accessed=30 * 2**20
        ),
        name="attention_forward",
    )(*args)


def attention_backward(part, tables, x, dy, kept, weights, gains, dx_in, sums, packed):
    rows, counts = tables
    b = part // HALVES
    attn_qkv, attn_out = weights
    qkv, o, zn, rstd = kept
    slots, length, width = x.shape
    score_scale = (width // HEADS) ** (-0.5)
    base = part * SLOTS
    first = sums is None
    n_out = 4 if first else 3

    def kernel(rows_ref, counts_ref, x_ref, dy_ref, qkv_ref, o_ref, zn_ref, rstd_ref, qkv_w, out_w, gain, *rest):
        ins = rest[: len(rest) - n_out - 7]
        outs = rest[len(ins) : len(ins) + n_out]
        acc_qkv, acc_out, do_scr, dqkv_scr, dh_scr, dz_scr, sems = rest[-7:]
        dx_ref, small_ref = outs[0], outs[1]
        i = pl.program_id(0)
        here = i < counts_ref[part * 8]

        def copies():
            if first:
                pairs = ((acc_qkv, outs[2]), (acc_out, outs[3]))
            else:
                pairs = ((ins[0], acc_qkv), (ins[1], acc_out))
            return [
                pltpu.make_async_copy(source, target, sems.at[n])
                for n, (source, target) in enumerate(pairs)
            ]

        @pl.when(i == 0)
        def _():
            small_ref[...] = jnp.zeros_like(small_ref)
            if first:
                acc_qkv[...] = jnp.zeros_like(acc_qkv)
                acc_out[...] = jnp.zeros_like(acc_out)
            else:
                for copy in copies():
                    copy.start()

        @pl.when(here)
        def _():
            dz, gain_grad, shift_grad = norm_backward(dy_ref[0], zn_ref, rstd_ref, gain[0:1, :])
            small_ref[0:1, :] += gain_grad
            small_ref[1:2, :] += shift_grad
            dz_scr[...] = dz
            dh = dz.astype(BF16)
            dh_scr[...] = dh
            do_scr[...] = nt(dh, out_w[...]).astype(BF16)
            low = head_masks(length)
            zero = jnp.zeros((), BF16)
            for pair in range(width // LANES):
                at = pair * LANES
                q2 = qkv_ref[0, :, at : at + LANES] * jnp.asarray(score_scale, BF16)
                k2 = qkv_ref[0, :, width + at : width + at + LANES]
                v2 = qkv_ref[0, :, 2 * width + at : 2 * width + at + LANES]
                do2 = do_scr[:, at : at + LANES]
                dqs, dks, dvs = [], [], []
                for half in range(2):
                    mask = low if half == 0 else ~low
                    st = nt(jnp.where(mask, k2, zero), q2)
                    e = jnp.exp(st - jnp.max(st, axis=0, keepdims=True))
                    p = e * (1.0 / jnp.sum(e, axis=0, keepdims=True))
                    dvs.append(nn(p.astype(BF16), do2))
                    t = p * nt(jnp.where(mask, v2, zero), do2)
                    ds = (t - p * jnp.sum(t, axis=0, keepdims=True)).astype(BF16)
                    dks.append(nn(ds, q2))
                    dqs.append(tn(ds, k2))
                dqkv_scr[:, at : at + LANES] = (jnp.where(low, dqs[0], dqs[1]) * score_scale).astype(BF16)
                dqkv_scr[:, width + at : width + at + LANES] = jnp.where(low, dks[0], dks[1]).astype(BF16)
                dqkv_scr[:, 2 * width + at : 2 * width + at + LANES] = jnp.where(low, dvs[0], dvs[1]).astype(BF16)
            total = dz_scr[...]
            for third in range(3):
                cols = slice(third * width, (third + 1) * width)
                total = total + nt(dqkv_scr[:, cols], qkv_w[:, cols])
            dx_ref[0] = total.astype(BF16)

        if not first:

            @pl.when(i == 0)
            def _():
                for copy in copies():
                    copy.wait()

        @pl.when(here)
        def _():
            xv = x_ref[0]
            for third in range(3):
                cols = slice(third * width, (third + 1) * width)
                acc_qkv[:, cols] += tn(xv, dqkv_scr[:, cols])
            acc_out[...] += tn(o_ref[0], dh_scr[...])

        @pl.when(i == OWN_CAP - 1)
        def _():
            if first:
                for copy in copies():
                    copy.start()
                for copy in copies():
                    copy.wait()
            else:
                packed_ref = outs[2]
                groups, tall = packed_ref.shape[0], packed_ref.shape[1] // 4
                for third in range(3):
                    piece = acc_qkv[:, third * width : (third + 1) * width].astype(BF16)
                    packed_ref[:, third * tall : (third + 1) * tall, :] = piece.reshape(
                        groups, tall, width
                    )
                packed_ref[:, 3 * tall : 4 * tall, :] = (
                    acc_out[...].astype(BF16).reshape(groups, tall, width)
                )

    def at_row(i, r, c):
        return (r[base + i], 0, 0)

    def at_step(i, r, c):
        return (jnp.maximum(jnp.minimum(i, c[part * 8] - 1), 0), 0, 0)

    def whole(i, r, c):
        return (0, 0)

    seq = (1, length, width)
    in_specs = [
        pl.BlockSpec(seq, at_row),
        pl.BlockSpec(seq, at_row),
        pl.BlockSpec((1, length, 3 * width), at_step),
        pl.BlockSpec(seq, at_step),
        pl.BlockSpec(seq, at_step),
        pl.BlockSpec((1, length, LANES), at_step),
        pl.BlockSpec(
            (None, None, width, 3 * width), lambda i, r, c: (b, 0, 0, 0), pipeline_mode=pl.Buffered(1)
        ),
        pl.BlockSpec(
            (None, None, width, width), lambda i, r, c: (b, 0, 0, 0), pipeline_mode=pl.Buffered(1)
        ),
        pl.BlockSpec((8, width), whole),
    ]
    args = [rows, counts, x, dy, qkv, o, zn, rstd, attn_qkv, attn_out, gains]
    out_specs = [pl.BlockSpec(seq, at_row), pl.BlockSpec((8, width), whole)]
    out_shape = [
        jax.ShapeDtypeStruct((slots, length, width), BF16),
        jax.ShapeDtypeStruct((8, width), F32),
    ]
    if first:
        out_specs += [ANY_SPEC, ANY_SPEC]
        out_shape += [
            jax.ShapeDtypeStruct((width, 3 * width), F32),
            jax.ShapeDtypeStruct((width, width), F32),
        ]
    else:
        groups, total_rows = packed
        out_specs.append(
            pl.BlockSpec((groups, 4 * width // groups, width), lambda i, r, c: (0, 0, 0))
        )
        out_shape.append(jax.ShapeDtypeStruct((groups, total_rows, width), BF16))
        in_specs += [ANY_SPEC, ANY_SPEC]
        args += list(sums)
    alias = {}
    if dx_in is not None:
        in_specs.append(ANY_SPEC)
        alias = {len(args): 0}
        args.append(dx_in)
    flops = 2 * OWN_CAP * length * width * (8 * width + 4 * length)
    return pl.pallas_call(
        kernel,
        grid_spec=pltpu.PrefetchScalarGridSpec(
            num_scalar_prefetch=2,
            grid=(OWN_CAP,),
            in_specs=in_specs,
            out_specs=out_specs,
            scratch_shapes=[
                pltpu.VMEM((width, 3 * width), F32),
                pltpu.VMEM((width, width), F32),
                pltpu.VMEM((length, width), BF16),
                pltpu.VMEM((length, 3 * width), BF16),
                pltpu.VMEM((length, width), BF16),
                pltpu.VMEM((length, width), F32),
                pltpu.SemaphoreType.DMA((2,)),
            ],
        ),
        out_shape=out_shape,
        input_output_aliases=alias,
        compiler_params=params_of(1),
        cost_estimate=pl.CostEstimate(
            flops=flops, transcendentals=OWN_CAP * HEADS * length * length // 2, bytes_accessed=40 * 2**20
        ),
        name="attention_backward",
    )(*args)


def feed_forward(part, tables, x, weights, norms, earlier):
    rows, counts = tables
    b = part // HALVES
    ffn_up, ffn_down = weights
    gains, shifts = norms
    slots, length, width = x.shape
    hidden = ffn_up.shape[-1]
    parts = hidden // FF_PART
    kind = KINDS - 1
    base = part * SLOTS + kind * OWN_CAP

    def kernel(rows_ref, counts_ref, x_ref, up, down, gain, shift, *rest):
        y_ref, g_ref, slope_ref, zn_ref, rstd_ref, x_scr, h_scr = rest[-7:]
        c, i = pl.program_id(0), pl.program_id(1)

        @pl.when(i < counts_ref[part * 8 + kind])
        def _():
            @pl.when(c == 0)
            def _():
                x_scr[i] = x_ref[0]

            xv = x_scr[i]
            for sub in range(FF_PART // FF_SUB):
                cols = slice(sub * FF_SUB, (sub + 1) * FF_SUB)
                a = nn(xv, up[:, cols])
                phi = 0.5 + 0.5 * lax.erf(a * (0.5**0.5))
                slope = phi + a * (jnp.exp(a * a * -0.5) * 0.3989422804014327)
                g = (a * phi).astype(BF16)
                g_ref[0, :, cols] = g
                slope_ref[0, :, cols] = slope.astype(BF16)
            branch = nn(g_ref[0], down[...])

            @pl.when(c == 0)
            def _():
                h_scr[i] = branch

            @pl.when(jnp.logical_and(c > 0, c < parts - 1))
            def _():
                h_scr[i] += branch

            @pl.when(c == parts - 1)
            def _():
                finish_forward(
                    xv,
                    h_scr[i] + branch,
                    gain[kind : kind + 1, :],
                    shift[kind : kind + 1, :],
                    y_ref,
                    zn_ref,
                    rstd_ref,
                )

    def in_row(c, i, r, n):
        return (r[base + jnp.where(c == 0, i, OWN_CAP - 1)], 0, 0)

    def out_row(c, i, r, n):
        return (r[base + jnp.where(c == parts - 1, i, 0)], 0, 0)

    def place(i, n):
        at = jnp.maximum(jnp.minimum(i, n[part * 8 + kind] - 1), 0)
        return at if part == b * HALVES else at + n[b * HALVES * 8 + kind]

    def out_step(c, i, r, n):
        return (place(jnp.where(c == parts - 1, i, 0), n), 0, 0)

    def part_step(c, i, r, n):
        return (place(i, n), 0, c)

    seq = (1, length, width)
    in_specs = [
        pl.BlockSpec(seq, in_row),
        pl.BlockSpec((None, None, width, FF_PART), lambda c, i, r, n: (b, 0, 0, c)),
        pl.BlockSpec((None, None, FF_PART, width), lambda c, i, r, n: (b, 0, c, 0)),
        pl.BlockSpec((8, width), lambda c, i, r, n: (0, 0)),
        pl.BlockSpec((8, width), lambda c, i, r, n: (0, 0)),
    ]
    args = [rows, counts, x, ffn_up, ffn_down, gains, shifts]
    alias = {}
    for n, kept in enumerate(earlier or ()):
        in_specs.append(ANY_SPEC)
        alias[len(args)] = 1 + n
        args.append(kept)
    return pl.pallas_call(
        kernel,
        grid_spec=pltpu.PrefetchScalarGridSpec(
            num_scalar_prefetch=2,
            grid=(parts, OWN_CAP),
            in_specs=in_specs,
            out_specs=[
                pl.BlockSpec(seq, out_row),
                pl.BlockSpec((1, length, FF_PART), part_step),
                pl.BlockSpec((1, length, FF_PART), part_step),
                pl.BlockSpec(seq, out_step),
                pl.BlockSpec((1, length, LANES), out_step),
            ],
            scratch_shapes=[
                pltpu.VMEM((OWN_CAP, length, width), BF16),
                pltpu.VMEM((OWN_CAP, length, width), F32),
            ],
        ),
        out_shape=[
            jax.ShapeDtypeStruct((slots, length, width), BF16),
            jax.ShapeDtypeStruct((OWN_CAP + 1, length, hidden), BF16),
            jax.ShapeDtypeStruct((OWN_CAP + 1, length, hidden), BF16),
            jax.ShapeDtypeStruct((OWN_CAP + 1, length, width), BF16),
            jax.ShapeDtypeStruct((OWN_CAP + 1, length, LANES), F32),
        ],
        input_output_aliases=alias,
        compiler_params=params_of(2),
        cost_estimate=pl.CostEstimate(
            flops=4 * OWN_CAP * length * width * hidden,
            transcendentals=2 * OWN_CAP * length * hidden,
            bytes_accessed=40 * 2**20,
        ),
        name="feed_forward",
    )(*args)


def feed_backward(b, tables, x, dy, kept, weights, gains, dx_first, groups, wait_for):
    rows, counts = tables
    ffn_up, ffn_down = weights
    g, slope, zn, rstd = kept
    slots, length, width = x[0].shape
    hidden = ffn_up.shape[-1]
    parts = hidden // FF_PART
    kind = KINDS - 1
    bases = [(b * HALVES + half) * SLOTS + kind * OWN_CAP for half in range(HALVES)]
    tall = width // groups
    deep = hidden // groups
    shares = FF_PART // deep

    def present(n, half):
        return n[(b * HALVES + half) * 8 + kind]

    def kernel(
        rows_ref,
        counts_ref,
        x_ref0,
        x_ref1,
        dy_ref0,
        dy_ref1,
        g_ref,
        slope_ref,
        zn_ref,
        rstd_ref,
        up,
        down,
        gain,
        *rest,
    ):
        (
        small_ref,
        dx_ref0,
        dx_ref1,
        packed_ref,
        x_scr,
        dh_scr,
        dx_scr,
        da_scr,
        acc_up,
        acc_down,
        low_up,
        low_down,
        low_dx,
        tally,
        sems,
        dx_sem,
        ) = rest[-16:]
        c, i = pl.program_id(0), pl.program_id(1)
        n0 = present(counts_ref, 0)
        total_n = n0 + present(counts_ref, 1)
        in_first = i < n0

        @pl.when(jnp.logical_and(c == 0, i == 0))
        def _():
            small_ref[...] = jnp.zeros_like(small_ref)
            lane = lax.broadcasted_iota(jnp.int32, (COUNT_ROWS, width), 1)
            counted = jnp.zeros((COUNT_ROWS, width), F32)
            for k in range(KINDS):
                there = sum(counts_ref[(b * HALVES + half) * 8 + k] for half in range(HALVES))
                counted = jnp.where(lane == k, there.astype(F32), counted)
            tally[...] = counted.astype(BF16)

        @pl.when(i == 0)
        def _():
            acc_up[...] = jnp.zeros_like(acc_up)
            acc_down[...] = jnp.zeros_like(acc_down)

        @pl.when(i < total_n)
        def _():
            @pl.when(c == 0)
            def _():
                dz, gain_grad, shift_grad = norm_backward(
                    jnp.where(in_first, dy_ref0[0], dy_ref1[0]),
                    zn_ref,
                    rstd_ref,
                    gain[kind : kind + 1, :],
                )
                small_ref[0:1, :] += gain_grad
                small_ref[1:2, :] += shift_grad
                x_scr[i] = jnp.where(in_first, x_ref0[0], x_ref1[0])
                dh_scr[i] = dz.astype(BF16)
                dx_scr[i] = dz

            dh = dh_scr[i]
            for sub in range(FF_PART // FF_SUB):
                cols = slice(sub * FF_SUB, (sub + 1) * FF_SUB)
                dg = nt(dh, down[cols, :])
                da_scr[:, cols] = (dg * slope_ref[0, :, cols].astype(F32)).astype(BF16)
            acc_down[...] += tn(g_ref[0], dh)
            acc_up[...] += tn(x_scr[i], da_scr[...])
            total = dx_scr[i] + nt(da_scr[...], up[...])

            @pl.when(c < parts - 1)
            def _():
                dx_scr[i] = total

            @pl.when(c == parts - 1)
            def _():
                low_dx[...] = total.astype(BF16)
                for half, (inside, dx_ref) in enumerate(
                    ((in_first, dx_ref0), (jnp.logical_not(in_first), dx_ref1))
                ):

                    @pl.when(inside)
                    def _():
                        row = rows_ref[bases[half] + jnp.where(in_first, i, jnp.maximum(i - n0, 0))]
                        copy = pltpu.make_async_copy(low_dx, dx_ref.at[row], dx_sem)
                        copy.start()
                        copy.wait()

        def copies():
            pairs = [
                (low_up.at[pl.ds(z * tall, tall)], packed_ref.at[z, pl.ds(c * tall, tall)])
                for z in range(groups)
            ]
            pairs += [
                (
                    low_down.at[pl.ds(m * deep, deep)],
                    packed_ref.at[c * shares + m, pl.ds(parts * tall, deep)],
                )
                for m in range(shares)
            ]
            return [
                pltpu.make_async_copy(source, target, sems.at[n])
                for n, (source, target) in enumerate(pairs)
            ]

        def tallies():
            return [
                pltpu.make_async_copy(
                    tally,
                    packed_ref.at[z, pl.ds(parts * tall + deep, COUNT_ROWS)],
                    sems.at[groups + shares + z],
                )
                for z in range(groups)
            ]

        @pl.when(i == OWN_CAP - 1)
        def _():
            @pl.when(c > 0)
            def _():
                for copy in copies():
                    copy.wait()

            low_up[...] = acc_up[...].astype(BF16)
            low_down[...] = acc_down[...].astype(BF16)
            for copy in copies():
                copy.start()

            @pl.when(c == parts - 1)
            def _():
                for copy in tallies():
                    copy.start()
                for copy in copies() + tallies():
                    copy.wait()

    def first_row(c, i, r, n):
        return (r[bases[0] + jnp.where(c == 0, i, OWN_CAP - 1)], 0, 0)

    def second_row(c, i, r, n):
        at = jnp.where(c == 0, i, OWN_CAP - 1) - present(n, 0)
        return (r[bases[1] + jnp.maximum(at, 0)], 0, 0)

    def last(n):
        return present(n, 0) + present(n, 1) - 1

    def in_step(c, i, r, n):
        return (jnp.where(c == 0, jnp.minimum(i, last(n)), last(n)), 0, 0)

    def part_step(c, i, r, n):
        return (jnp.minimum(i, last(n)), 0, c)

    seq = (1, length, width)
    in_specs = [
        pl.BlockSpec(seq, first_row),
        pl.BlockSpec(seq, second_row),
        pl.BlockSpec(seq, first_row),
        pl.BlockSpec(seq, second_row),
        pl.BlockSpec((1, length, FF_PART), part_step),
        pl.BlockSpec((1, length, FF_PART), part_step),
        pl.BlockSpec(seq, in_step),
        pl.BlockSpec((1, length, LANES), in_step),
        pl.BlockSpec((None, None, width, FF_PART), lambda c, i, r, n: (b, 0, 0, c)),
        pl.BlockSpec((None, None, FF_PART, width), lambda c, i, r, n: (b, 0, c, 0)),
        pl.BlockSpec((8, width), lambda c, i, r, n: (0, 0)),
        ANY_SPEC,
    ] + [ANY_SPEC] * len(wait_for)
    args = [rows, counts, *x, *dy, g, slope, zn, rstd, ffn_up, ffn_down, gains, dx_first]
    alias = {len(args) - 1: 1}
    args += wait_for
    return pl.pallas_call(
        kernel,
        grid_spec=pltpu.PrefetchScalarGridSpec(
            num_scalar_prefetch=2,
            grid=(parts, OWN_CAP),
            in_specs=in_specs,
            out_specs=[
                pl.BlockSpec((8, width), lambda c, i, r, n: (0, 0)),
                ANY_SPEC,
                ANY_SPEC,
                ANY_SPEC,
            ],
            scratch_shapes=[
                pltpu.VMEM((OWN_CAP, length, width), BF16),
                pltpu.VMEM((OWN_CAP, length, width), BF16),
                pltpu.VMEM((OWN_CAP, length, width), F32),
                pltpu.VMEM((length, FF_PART), BF16),
                pltpu.VMEM((width, FF_PART), F32),
                pltpu.VMEM((FF_PART, width), F32),
                pltpu.VMEM((width, FF_PART), BF16),
                pltpu.VMEM((FF_PART, width), BF16),
                pltpu.VMEM((length, width), BF16),
                pltpu.VMEM((COUNT_ROWS, width), BF16),
                pltpu.SemaphoreType.DMA((2 * groups + shares,)),
                pltpu.SemaphoreType.DMA,
            ],
        ),
        out_shape=[
            jax.ShapeDtypeStruct((8, width), F32),
            jax.ShapeDtypeStruct((slots, length, width), BF16),
            jax.ShapeDtypeStruct((slots, length, width), BF16),
            jax.ShapeDtypeStruct((groups, parts * tall + deep + COUNT_ROWS, width), BF16),
        ],
        input_output_aliases=alias,
        compiler_params=params_of(2),
        cost_estimate=pl.CostEstimate(
            flops=7 * OWN_CAP * length * width * hidden,
            transcendentals=0,
            bytes_accessed=50 * 2**20,
        ),
        name="feed_backward",
    )(*args)


PAD = 8
ROW_TILE = 128
COL_TILE = 256


def fill_padded(padded, values):
    length = values.shape[0]
    edge = jnp.zeros((PAD, values.shape[1]), F32)
    padded[0:PAD, :] = edge
    padded[PAD + length : PAD + length + PAD, :] = edge
    padded[PAD : PAD + length, :] = values


def conv_forward(part, tables, x, weights, norms, y_in):
    rows, counts = tables
    b = part // HALVES
    taps, conv_point = weights
    gains, shifts = norms
    slots, length, width = x.shape
    base = part * SLOTS + OWN_CAP
    steps = (KINDS - 2) * OWN_CAP

    def kernel(rows_ref, counts_ref, x_ref, point, taps_ref, gain, shift, *rest):
        y_ref, u_ref, zn_ref, rstd_ref, xpad = rest[-5:]
        step = pl.program_id(0)
        which, j = step // OWN_CAP, step % OWN_CAP
        for kind in range(1, KINDS - 1):
            taps_n = 2 * kind + 1
            first = kind * kind - 1

            @pl.when(jnp.logical_and(which == kind - 1, j < counts_ref[part * 8 + kind]))
            def _():
                fill_padded(xpad, x_ref[0].astype(F32))
                for r in range(0, length, ROW_TILE):
                    for col in range(0, width, COL_TILE):
                        cols = slice(col, col + COL_TILE)
                        mixed = None
                        for t in range(taps_n):
                            start = PAD + r + t - kind
                            term = xpad[start : start + ROW_TILE, cols] * taps_ref[first + t : first + t + 1, cols]
                            mixed = term if mixed is None else mixed + term
                        u_ref[0, r : r + ROW_TILE, cols] = mixed.astype(BF16)
                branch = nn(u_ref[0], point[...])
                finish_forward(
                    x_ref[0],
                    branch,
                    gain[kind : kind + 1, :],
                    shift[kind : kind + 1, :],
                    y_ref,
                    zn_ref,
                    rstd_ref,
                )

    def at_row(i, r, c):
        return (r[base + i], 0, 0)

    def at_step(i, r, c):
        which = i // OWN_CAP
        last = c[part * 8 + 1 + which] - 1
        return (which * OWN_CAP + jnp.maximum(jnp.minimum(i % OWN_CAP, last), 0), 0, 0)

    def whole(i, r, c):
        return (0, 0)

    seq = (1, length, width)
    in_specs = [
        pl.BlockSpec(seq, at_row),
        pl.BlockSpec((None, None, None, width, width), lambda i, r, c: (b, 0, i // OWN_CAP, 0, 0)),
        pl.BlockSpec((16, width), whole),
        pl.BlockSpec((8, width), whole),
        pl.BlockSpec((8, width), whole),
    ]
    args = [rows, counts, x, conv_point, taps, gains, shifts]
    alias = {}
    if y_in is not None:
        in_specs.append(pl.BlockSpec(memory_space=pl.ANY))
        alias = {len(args): 0}
        args.append(y_in)
    return pl.pallas_call(
        kernel,
        grid_spec=pltpu.PrefetchScalarGridSpec(
            num_scalar_prefetch=2,
            grid=(steps,),
            in_specs=in_specs,
            out_specs=[
                pl.BlockSpec(seq, at_row),
                pl.BlockSpec(seq, at_step),
                pl.BlockSpec(seq, at_step),
                pl.BlockSpec((1, length, LANES), at_step),
            ],
            scratch_shapes=[pltpu.VMEM((length + 2 * PAD, width), F32)],
        ),
        out_shape=[
            jax.ShapeDtypeStruct((slots, length, width), BF16),
            jax.ShapeDtypeStruct((steps, length, width), BF16),
            jax.ShapeDtypeStruct((steps, length, width), BF16),
            jax.ShapeDtypeStruct((steps, length, LANES), F32),
        ],
        input_output_aliases=alias,
        compiler_params=params_of(1),
        cost_estimate=pl.CostEstimate(
            flops=2 * steps * length * width * width, transcendentals=0, bytes_accessed=36 * 2**20
        ),
        name="conv_forward",
    )(*args)


def conv_backward(part, tables, x, dy, kept, weights, gains, dx_in, sums, packed):
    rows, counts = tables
    b = part // HALVES
    taps, conv_point = weights
    u, zn, rstd = kept
    slots, length, width = x.shape
    base = part * SLOTS + OWN_CAP
    steps = (KINDS - 2) * OWN_CAP
    first_half = sums is None
    groups = packed[0]

    def kernel(rows_ref, counts_ref, x_ref, dy_ref, u_ref, zn_ref, rstd_ref, point, taps_ref, gain, *rest):
        if first_half:
            dx_ref, small_ref, acc, xpad, dupad, dz_scr = rest[-6:]
        else:
            sum_ref = rest[0]
            dx_ref, small_ref, packed_ref, xpad, dupad, dz_scr, acc = rest[-7:]
        step = pl.program_id(0)
        which, j = step // OWN_CAP, step % OWN_CAP

        @pl.when(step == 0)
        def _():
            small_ref[...] = jnp.zeros_like(small_ref)

        @pl.when(j == 0)
        def _():
            acc[...] = jnp.zeros_like(acc) if first_half else sum_ref[...]

        for kind in range(1, KINDS - 1):
            taps_n = 2 * kind + 1
            first = kind * kind - 1

            @pl.when(jnp.logical_and(which == kind - 1, j < counts_ref[part * 8 + kind]))
            def _():
                dz, gain_grad, shift_grad = norm_backward(
                    dy_ref[0], zn_ref, rstd_ref, gain[kind : kind + 1, :]
                )
                small_ref[14 + kind : 15 + kind, :] += gain_grad
                small_ref[17 + kind : 18 + kind, :] += shift_grad
                dz_scr[...] = dz
                dh = dz.astype(BF16)
                acc[...] += tn(u_ref[0], dh)
                fill_padded(xpad, x_ref[0].astype(F32))
                fill_padded(dupad, nt(dh, point[...]))
                for col in range(0, width, COL_TILE):
                    cols = slice(col, col + COL_TILE)
                    sums = [None] * taps_n
                    for r in range(0, length, ROW_TILE):
                        here = dupad[PAD + r : PAD + r + ROW_TILE, cols]
                        total = dz_scr[r : r + ROW_TILE, cols]
                        for t in range(taps_n):
                            back = PAD + r - t + kind
                            total = total + dupad[back : back + ROW_TILE, cols] * taps_ref[first + t : first + t + 1, cols]
                            ahead = PAD + r + t - kind
                            part = jnp.sum(
                                xpad[ahead : ahead + ROW_TILE, cols] * here, axis=0, keepdims=True
                            )
                            sums[t] = part if sums[t] is None else sums[t] + part
                        dx_ref[0, r : r + ROW_TILE, cols] = total.astype(BF16)
                    for t in range(taps_n):
                        small_ref[first + t : first + t + 1, cols] += sums[t]

        if not first_half:

            @pl.when(j == OWN_CAP - 1)
            def _():
                packed_ref[...] = acc[...].astype(BF16).reshape(packed_ref.shape)

    def at_row(i, r, c):
        return (r[base + i], 0, 0)

    def at_step(i, r, c):
        which = i // OWN_CAP
        last = c[part * 8 + 1 + which] - 1
        return (which * OWN_CAP + jnp.maximum(jnp.minimum(i % OWN_CAP, last), 0), 0, 0)

    def whole(i, r, c):
        return (0, 0)

    seq = (1, length, width)
    in_specs = [
        pl.BlockSpec(seq, at_row),
        pl.BlockSpec(seq, at_row),
        pl.BlockSpec(seq, at_step),
        pl.BlockSpec(seq, at_step),
        pl.BlockSpec((1, length, LANES), at_step),
        pl.BlockSpec((None, None, None, width, width), lambda i, r, c: (b, 0, i // OWN_CAP, 0, 0)),
        pl.BlockSpec((16, width), whole),
        pl.BlockSpec((8, width), whole),
    ]
    args = [rows, counts, x, dy, u, zn, rstd, conv_point, taps, gains]
    sum_spec = pl.BlockSpec((None, width, width), lambda i, r, c: (i // OWN_CAP, 0, 0))
    out_specs = [pl.BlockSpec(seq, at_row), pl.BlockSpec((24, width), whole)]
    out_shape = [
        jax.ShapeDtypeStruct((slots, length, width), BF16),
        jax.ShapeDtypeStruct((24, width), F32),
    ]
    scratch = [
        pltpu.VMEM((length + 2 * PAD, width), F32),
        pltpu.VMEM((length + 2 * PAD, width), F32),
        pltpu.VMEM((length, width), F32),
    ]
    alias = {}
    if first_half:
        out_specs.append(sum_spec)
        out_shape.append(jax.ShapeDtypeStruct((KINDS - 2, width, width), F32))
    else:
        in_specs.append(sum_spec)
        args.append(sums)
        out_specs.append(
            pl.BlockSpec((groups, width // groups, width), lambda i, r, c: (0, 4 + i // OWN_CAP, 0))
        )
        out_shape.append(jax.ShapeDtypeStruct(packed[1].shape, BF16))
        in_specs.append(ANY_SPEC)
        alias = {len(args): 2}
        args.append(packed[1])
        scratch.append(pltpu.VMEM((width, width), F32))
    in_specs.append(ANY_SPEC)
    alias = {**alias, len(args): 0}
    args.append(dx_in)
    return pl.pallas_call(
        kernel,
        grid_spec=pltpu.PrefetchScalarGridSpec(
            num_scalar_prefetch=2,
            grid=(steps,),
            in_specs=in_specs,
            out_specs=out_specs,
            scratch_shapes=scratch,
        ),
        out_shape=out_shape,
        input_output_aliases=alias,
        compiler_params=params_of(1),
        cost_estimate=pl.CostEstimate(
            flops=3 * steps * length * width * width, transcendentals=0, bytes_accessed=50 * 2**20
        ),
        name="conv_backward",
    )(*args)


def owner_forward(b, half, tables, x, weights, small_weights, earlier):
    part = b * HALVES + half
    attn_qkv, attn_out, ffn_up, ffn_down, conv_point = weights
    taps, gains, shifts = small_weights
    norms = (gains, shifts)
    y, *kept_f = feed_forward(part, tables, x, (ffn_up, ffn_down), norms, earlier)
    y, *kept_a = attention_forward(part, tables, x, (attn_qkv, attn_out), norms, y)
    y, *kept_c = conv_forward(part, tables, x, (taps, conv_point), norms, y)
    return y, kept_f, kept_a, kept_c


def both_forward(b, tables, x, weights, small_weights):
    y, kept_a, kept_c, kept_f = [], [], [], None
    for half in range(HALVES):
        yh, kept_f, ka, kc = owner_forward(
            b, half, tables, x[half], weights, small_weights, kept_f
        )
        y.append(yh)
        kept_a.append(ka)
        kept_c.append(kc)
    return y, (kept_f, kept_a, kept_c)


def join_small(small_f, small_a, small_c):
    return jnp.concatenate(
        [
            small_c[:15],
            small_a[0:1],
            small_c[15:18],
            small_f[0:1],
            small_a[1:2],
            small_c[18:21],
            small_f[1:2],
        ]
    )


def owner_backward(b, tables, x, dy, kept, weights, small_weights, groups, wait_for):
    attn_qkv, attn_out, ffn_up, ffn_down, conv_point = weights
    taps, gains, shifts = small_weights
    kept_f, kept_a, kept_c = kept
    width = x[0].shape[-1]
    rest_rows = 7 * width // groups + SMALL_ROWS
    attn, conv = (attn_qkv, attn_out), (taps, conv_point)
    first, second = b * HALVES, b * HALVES + 1
    d0, small_a0, *sum_a = attention_backward(
        first, tables, x[0], dy[0], kept_a[0], attn, gains, None, None, None
    )
    d0, small_c0, sum_c = conv_backward(
        first, tables, x[0], dy[0], kept_c[0], conv, gains, d0, None, (groups,)
    )
    small_f, d0, d1, feed_pack = feed_backward(
        b, tables, x, dy, kept_f, (ffn_up, ffn_down), gains, d0, groups, wait_for
    )
    d1, small_a1, rest_pack = attention_backward(
        second, tables, x[1], dy[1], kept_a[1], attn, gains, d1, sum_a, (groups, rest_rows)
    )
    d1, small_c1, rest_pack = conv_backward(
        second, tables, x[1], dy[1], kept_c[1], conv, gains, d1, sum_c, (groups, rest_pack)
    )
    dx = (d0, d1)
    small = join_small(small_f, small_a0 + small_a1, small_c0 + small_c1).astype(BF16)
    small = small.reshape(25, groups, width // groups)
    small = small.transpose(1, 0, 2)
    small = jnp.pad(small, ((0, 0), (0, SMALL_ROWS - 25), (0, width - width // groups)))
    rest_pack = lax.dynamic_update_slice(rest_pack, small, (0, rest_rows - SMALL_ROWS, 0))
    return dx, feed_pack, rest_pack


def finish_feed(b, feed, up_out, down_out, shapes):
    parts = shapes[0].shape[-1] // FF_PART
    tall, width = shapes[0].shape[2], FF_PART
    count_block = 2 * parts * tall // COUNT_ROWS

    def kernel(up_ref, down_ref, count_ref, *rest):
        up_to, down_to = rest[-2:]
        scale = 1.0 / count_ref[0:1, KINDS - 1 : KINDS].astype(F32)
        up_to[...] = up_ref[...].astype(F32) * scale
        down_to[...] = down_ref[...].astype(F32) * scale

    old = [] if up_out is None else [up_out, down_out]
    return pl.pallas_call(
        kernel,
        grid=(parts,),
        in_specs=[
            pl.BlockSpec((tall, width), lambda c: (c, 0)),
            pl.BlockSpec((tall, width), lambda c: (parts + c, 0)),
            pl.BlockSpec((COUNT_ROWS, width), lambda c: (count_block, 0)),
        ]
        + [ANY_SPEC] * len(old),
        out_specs=[
            pl.BlockSpec((None, None, tall, width), lambda c: (b, 0, 0, c)),
            pl.BlockSpec((None, None, tall, width), lambda c: (b, 0, c, 0)),
        ],
        out_shape=list(shapes),
        input_output_aliases={3 + n: n for n in range(len(old))},
        compiler_params=params_of(1),
        cost_estimate=pl.CostEstimate(flops=0, transcendentals=0, bytes_accessed=8 * 2**20),
        name="finish_feed",
    )(feed, feed, feed, *old)


def finish_rest(b, rest, feed, old, shapes):
    tall, width = shapes[1].shape[2:]
    count_block = (feed.shape[0] - COUNT_ROWS) // COUNT_ROWS
    small_block = 7 * tall // SMALL_ROWS

    def kernel(rest_ref, small_ref, count_ref, *refs):
        qkv_to, out_to, taps_to, point_to, gain_to, shift_to = refs[-6:]
        i = pl.program_id(0)
        scales = 1.0 / count_ref[0:1, 0:8].astype(F32)
        values = rest_ref[...].astype(F32)

        @pl.when(i < 3)
        def _():
            qkv_to[...] = values * scales[:, 0:1]

        @pl.when(i == 3)
        def _():
            out_to[...] = values * scales[:, 0:1]
            small = small_ref[...].astype(F32)
            row = lax.broadcasted_iota(jnp.int32, small.shape, 0)
            which = jnp.where(row < 3, 1, jnp.where(row < 8, 2, jnp.where(row < 15, 3, 0)))
            which = jnp.where(row >= 15, row - 15, which)
            which = jnp.where(row >= 20, row - 20, which)
            scale = jnp.zeros_like(small)
            for k in range(KINDS):
                scale = jnp.where(which == k, scales[:, k : k + 1], scale)
            small = small * scale
            taps_to[...] = small[:15, :tall]
            gain_to[...] = small[15:20, :tall]
            shift_to[...] = small[20:25, :tall]

        for k in range(1, KINDS - 1):

            @pl.when(i == 3 + k)
            def _():
                point_to[...] = values * scales[:, k : k + 1]

    old = list(old)
    return pl.pallas_call(
        kernel,
        grid=(7,),
        in_specs=[
            pl.BlockSpec((tall, width), lambda i: (i, 0)),
            pl.BlockSpec((SMALL_ROWS, width), lambda i: (small_block, 0)),
            pl.BlockSpec((COUNT_ROWS, width), lambda i: (count_block, 0)),
        ]
        + [ANY_SPEC] * len(old),
        out_specs=[
            pl.BlockSpec((None, None, tall, width), lambda i: (b, 0, 0, jnp.minimum(i, 2))),
            pl.BlockSpec((None, None, tall, width), lambda i: (b, 0, 0, 0)),
            pl.BlockSpec((None, None, 15, tall), lambda i: (b, 0, 0, 0)),
            pl.BlockSpec(
                (None, None, None, tall, width), lambda i: (b, 0, jnp.maximum(i - 4, 0), 0, 0)
            ),
            pl.BlockSpec((None, None, KINDS, tall), lambda i: (b, 0, 0, 0)),
            pl.BlockSpec((None, None, KINDS, tall), lambda i: (b, 0, 0, 0)),
        ],
        out_shape=list(shapes),
        input_output_aliases={3 + n: n for n in range(len(old))},
        compiler_params=params_of(1),
        cost_estimate=pl.CostEstimate(flops=0, transcendentals=0, bytes_accessed=8 * 2**20),
        name="finish_rest",
    )(rest, rest, feed, *old)


def small_params(b, conv_taps, norm_gain, norm_bias):
    taps = jnp.pad(conv_taps[b, 0].astype(F32), ((0, 1), (0, 0)))
    gains = jnp.pad(norm_gain[b, 0].astype(F32), ((0, 3), (0, 0)))
    shifts = jnp.pad(norm_bias[b, 0].astype(F32), ((0, 3), (0, 0)))
    return taps, gains, shifts


def exchange(rows):
    return lax.all_to_all(rows, "op", split_axis=0, concat_axis=0, tiled=True)


def group_sum(pack):
    return lax.psum_scatter(pack, "dp", scatter_dimension=0, tiled=False)


def per_device(
    inputs,
    candidate,
    attn_qkv,
    attn_out,
    ffn_up,
    ffn_down,
    conv_taps,
    conv_point,
    norm_gain,
    norm_bias,
    cotangent,
):
    owners = lax.axis_size("op")
    groups = lax.axis_size("dp")
    seqs = inputs.shape[0]
    width = inputs.shape[-1]
    hidden = ffn_up.shape[-1]
    weights = (attn_qkv, attn_out, ffn_up, ffn_down, conv_point)
    smalls = [small_params(b, conv_taps, norm_gain, norm_bias) for b in range(BLOCKS)]
    send, relay, tags = home_tables(candidate.reshape(-1), owners, seqs)
    arrived = exchange(tags.reshape(owners, BLOCKS * HALVES))
    tables = owner_tables(arrived.reshape(-1), owners)
    both = range(HALVES)

    def start(b, half):
        return (b * HALVES + half) * owners

    x0 = [
        exchange(move_rows(send, [start(0, h)], [inputs], owners, False, "send_inputs"))
        for h in both
    ]
    y0, kept0 = both_forward(0, tables, x0, weights, smalls[0])
    x1 = []
    for h in both:
        back = exchange(y0[h])
        x1.append(exchange(move_rows(relay, [start(0, h)], [back], owners, False, "relay_x")))
    y1, kept1 = both_forward(1, tables, x1, weights, smalls[1])
    dy1 = [
        exchange(
            move_rows(
                send, [start(1, h)], [cotangent], owners, False, "send_cotangent", (y1[h],)
            )
        )
        for h in both
    ]
    dx1, feed1, rest1 = owner_backward(1, tables, x1, dy1, kept1, weights, smalls[1], groups, ())
    feed1 = group_sum(feed1)
    rest1 = group_sum(rest1)
    dy0 = []
    for h in both:
        back = exchange(dx1[h])
        dy0.append(exchange(move_rows(relay, [start(1, h)], [back], owners, False, "relay_dx")))
    dx0, feed0, rest0 = owner_backward(
        0, tables, x0, dy0, kept0, weights, smalls[0], groups, (feed1,)
    )
    feed0 = group_sum(after(feed0, (rest1,)))
    rest0 = group_sum(rest0)
    starts = [start(1, h) for h in both]
    y_home = [exchange(after(y1[h], (dy0[1],))) for h in both]
    outputs = move_rows(send, starts, y_home, seqs, True, "outputs")
    starts = [start(0, h) for h in both]
    dx_home = [exchange(dx0[0]), exchange(after(dx0[1], (feed0,)))]
    input_grad = move_rows(send, starts, dx_home, seqs, True, "input_grad")

    tall, deep = width // groups, hidden // groups
    grad = lambda *dims: jax.ShapeDtypeStruct((BLOCKS, 1) + dims, F32)
    feed_shapes = (grad(tall, hidden), grad(deep, width))
    rest_shapes = (
        grad(tall, 3 * width),
        grad(tall, width),
        grad(15, tall),
        grad(KINDS - 2, tall, width),
        grad(KINDS, tall),
        grad(KINDS, tall),
    )
    feeds, rests = (None, None), ()
    for b, feed, rest in ((1, feed1, rest1), (0, feed0, rest0)):
        feeds = finish_feed(b, feed, *feeds, feed_shapes)
        rests = finish_rest(b, rest, feed, rests, rest_shapes)
    qkv, out, taps, point, gain, shift = rests
    grads = (qkv, out, *feeds, taps, point, gain, shift)
    return (outputs, input_grad) + grads


def solution(mesh):
    placed = (
        P(("dp", "op"), None, None),
        P(("dp", "op"), None),
        P(None, "op", None, None),
        P(None, "op", None, None),
        P(None, "op", None, None),
        P(None, "op", None, None),
        P(None, "op", None, None),
        P(None, "op", None, None, None),
        P(None, "op", None, None),
        P(None, "op", None, None),
        P(("dp", "op"), None, None),
    )
    return jax.shard_map(
        per_device,
        mesh=mesh,
        in_specs=placed,
        out_specs=(
            P(("dp", "op"), None, None),
            P(("dp", "op"), None, None),
            P(None, "op", "dp", None),
            P(None, "op", "dp", None),
            P(None, "op", "dp", None),
            P(None, "op", "dp", None),
            P(None, "op", None, "dp"),
            P(None, "op", None, "dp", None),
            P(None, "op", None, "dp"),
            P(None, "op", None, "dp"),
        ),
        check_vma=False,
    )
```

```python
import jax
import jax.numpy as jnp
from jax import lax
from jax.experimental import pallas as pl
from jax.experimental.pallas import tpu as pltpu
from jax.sharding import PartitionSpec as P

HEADS = 12
KINDS = 5
BLOCKS = 2
OWN_CAP = 3
HALVES = 2
SLOTS = KINDS * OWN_CAP
FF_PART = 768
FF_SUB = 256
LANES = 128
SMALL_ROWS = 32
COUNT_ROWS = 16
BF16 = jnp.bfloat16
F32 = jnp.float32
VMEM_BYTES = 60 * 2**20


def params_of(axes):
    return pltpu.CompilerParams(
        dimension_semantics=("arbitrary",) * axes, vmem_limit_bytes=VMEM_BYTES
    )


def nn(a, b):
    return lax.dot_general(a, b, (((1,), (0,)), ((), ())), preferred_element_type=F32)


def nt(a, b):
    return lax.dot_general(a, b, (((1,), (1,)), ((), ())), preferred_element_type=F32)


def tn(a, b):
    return lax.dot_general(a, b, (((0,), (0,)), ((), ())), preferred_element_type=F32)


def colour_home(owners, seqs, home, cand, color, partner, first, tally):
    base = home * seqs

    def clear_owner(o, _):
        first[o] = -1
        return 0

    lax.fori_loop(0, BLOCKS * owners, clear_owner, 0)
    for half in range(HALVES):
        tally[half] = 0

    def pair_up(j, _):
        color[base + j] = -1
        for b in range(BLOCKS):
            o = b * owners + lax.rem(cand[(base + j) * BLOCKS + b], owners)
            other = first[o]
            partner[b * seqs + j] = other
            first[o] = j

            @pl.when(other >= 0)
            def _():
                partner[b * seqs + other] = j

        return 0

    lax.fori_loop(0, seqs, pair_up, 0)

    def give(j, shade):
        color[base + j] = shade
        tally[shade] = tally[shade] + 1

    def paint(j, _):
        @pl.when(color[base + j] < 0)
        def _():
            shade = jnp.where(tally[0] > tally[1], 1, 0).astype(jnp.int32)
            give(j, shade)
            for side in range(2):

                def more(state):
                    return state[0] >= 0

                def walk(state):
                    now, use, tone = state
                    then = partner[use * seqs + now]
                    free = jnp.logical_and(then >= 0, color[base + jnp.maximum(then, 0)] < 0)

                    @pl.when(free)
                    def _():
                        give(then, 1 - tone)

                    return (jnp.where(free, then, -1), 1 - use, 1 - tone)

                lax.while_loop(more, walk, (j, jnp.int32(side), shade))

        return 0

    lax.fori_loop(0, seqs, paint, 0)


def home_kernel(owners, seqs, cand, send, relay, tags, color, partner, first, tally):
    for b in range(BLOCKS):

        def clear_owner(o, _):
            for half in range(HALVES):
                send[(b * HALVES + half) * owners + o] = -1
                relay[(b * HALVES + half) * owners + o] = -1
                tags[o * BLOCKS * HALVES + b * HALVES + half] = KINDS
            return 0

        lax.fori_loop(0, owners, clear_owner, 0)
    colour_home(owners, seqs, 0, cand, color, partner, first, tally)

    def place(j, _):
        half = color[j]
        spots = []
        for b in range(BLOCKS):
            c = cand[j * BLOCKS + b]
            o = lax.rem(c, owners)
            spots.append(o)
            send[(b * HALVES + half) * owners + o] = j
            tags[o * BLOCKS * HALVES + b * HALVES + half] = lax.div(c, owners)
        relay[half * owners + spots[1]] = spots[0]
        relay[(HALVES + half) * owners + spots[0]] = spots[1]
        return 0

    lax.fori_loop(0, seqs, place, 0)


ROUTES = 10
TRIES = 24


def route_kernel(
    owners, seqs, cand, me_ref, out, ok, color, partner, first, tally, leave, goal, hops, spill
):
    me = me_ref[0]
    square = owners * owners

    def colour(home, _):
        colour_home(owners, seqs, home, cand, color, partner, first, tally)
        return 0

    lax.fori_loop(0, owners, colour, 0)

    def ends(q, _):
        leave[q] = lax.rem(cand[q * BLOCKS], owners)
        goal[q] = lax.rem(cand[q * BLOCKS + 1], owners)
        return 0

    lax.fori_loop(0, owners * seqs, ends, 0)

    def attempt(state):
        turn, _ = state

        def clear(n, _):
            hops[n] = -1
            return 0

        lax.fori_loop(0, 3 * square, clear, 0)

        def direct(q, spilt):
            at = color[q] * 2 * square + leave[q] * owners + goal[q]
            free = hops[at] < 0

            @pl.when(free)
            def _():
                hops[at] = q

            @pl.when(jnp.logical_not(free))
            def _():
                spill[spilt] = q

            return jnp.where(free, spilt, spilt + 1)

        spilt = lax.fori_loop(0, owners * seqs, direct, jnp.int32(0))
        begin = lax.rem(turn * 5, jnp.maximum(spilt, 1))

        def two_hops(n, lost):
            q = spill[lax.rem(begin + n, jnp.maximum(spilt, 1))]
            o, p = leave[q], goal[q]
            early = color[q] * square
            shift = o * 3 + p * 5 + (n + 1) * turn

            def look(s, found):
                i = lax.rem(shift + s, owners)
                a = early + o * owners + i
                b = early + square + i * owners + p
                good = jnp.logical_and(hops[a] < 0, hops[b] < 0)
                return jnp.where(jnp.logical_and(good, found < 0), i, found)

            i = lax.fori_loop(0, owners, look, jnp.int32(-1))

            @pl.when(i >= 0)
            def _():
                hops[early + o * owners + i] = q
                hops[early + square + i * owners + p] = q

            return jnp.where(i >= 0, lost, lost + 1)

        lost = lax.fori_loop(0, spilt, two_hops, jnp.int32(0))
        return turn + 1, lost

    def again(state):
        return jnp.logical_and(state[0] < TRIES, state[1] > 0)

    _, lost = lax.while_loop(again, attempt, (jnp.int32(0), jnp.int32(1)))
    ok[0] = lost

    def clear_out(n, _):
        out[n] = -1
        return 0

    lax.fori_loop(0, ROUTES * owners, clear_out, 0)

    def note(d, _):
        def home(q):
            return lax.div(q, seqs)

        def put(table, at, value):
            out[table * owners + at] = value

        q = hops[me * owners + d]

        @pl.when(q >= 0)
        def _():
            put(0, d, home(q))
            put(9, home(q), d)

        q1 = hops[square + me * owners + d]

        @pl.when(q1 >= 0)
        def _():
            late = color[q1] == 1
            put(1, d, jnp.where(late, owners + home(q1), leave[q1]))

            @pl.when(late)
            def _():
                put(8, home(q1), owners + d)

        q2 = hops[2 * square + me * owners + d]

        @pl.when(q2 >= 0)
        def _():
            mine = leave[q2] == me
            put(2, d, jnp.where(mine, home(q2), owners + leave[q2]))

            @pl.when(mine)
            def _():
                put(8, home(q2), d)

        r = hops[d * owners + me]

        @pl.when(r >= 0)
        def _():
            there = goal[r] == me
            put(7, d, jnp.where(there, home(r), owners + goal[r]))

            @pl.when(there)
            def _():
                put(3, home(r), d)

        r1 = hops[square + d * owners + me]

        @pl.when(r1 >= 0)
        def _():
            late = color[r1] == 1
            put(6, d, jnp.where(late, owners + goal[r1], home(r1)))

            @pl.when(jnp.logical_not(late))
            def _():
                put(3, home(r1), owners + d)

        r2 = hops[2 * square + d * owners + me]

        @pl.when(r2 >= 0)
        def _():
            put(4, home(r2), d)
            put(5, d, home(r2))

        return 0

    lax.fori_loop(0, owners, note, 0)


SMEM_SPEC = pl.BlockSpec(memory_space=pltpu.SMEM)
ANY_SPEC = pl.BlockSpec(memory_space=pl.ANY)


def int_shape(n):
    return jax.ShapeDtypeStruct((n,), jnp.int32)


def home_tables(cand, owners, seqs):
    def kernel(*refs):
        home_kernel(owners, seqs, *refs)

    size = BLOCKS * HALVES * owners
    return pl.pallas_call(
        kernel,
        in_specs=[SMEM_SPEC],
        out_specs=[SMEM_SPEC] * 3,
        out_shape=[int_shape(size)] * 3,
        scratch_shapes=[
            pltpu.SMEM((seqs,), jnp.int32),
            pltpu.SMEM((BLOCKS * seqs,), jnp.int32),
            pltpu.SMEM((BLOCKS * owners,), jnp.int32),
            pltpu.SMEM((HALVES,), jnp.int32),
        ],
        name="home_tables",
    )(cand)


def owner_kernel(owners, tags, rows, counts):
    for b in range(BLOCKS):
        for half in range(HALVES):
            part = b * HALVES + half
            for k in range(8):
                counts[part * 8 + k] = 0

            def arrive(h, free):
                k = tags[h * BLOCKS * HALVES + part]
                there = k < KINDS

                @pl.when(there)
                def _():
                    n = jnp.minimum(counts[part * 8 + k], OWN_CAP - 1)
                    rows[part * SLOTS + k * OWN_CAP + n] = h
                    counts[part * 8 + k] = n + 1

                return jnp.where(there, free, h)

            free = lax.fori_loop(0, owners, arrive, jnp.int32(0))

            def spare(k, otherwise):
                return jnp.where(
                    counts[part * 8 + k] > 0, rows[part * SLOTS + k * OWN_CAP], otherwise
                )

            conv_spare = free
            for k in reversed(range(1, KINDS - 1)):
                conv_spare = spare(k, conv_spare)
            attn_spare = spare(0, conv_spare)
            feed_spare = spare(KINDS - 1, attn_spare)
            last = conv_spare
            for k, start in ((1, None), (2, None), (3, None), (0, attn_spare), (KINDS - 1, feed_spare)):
                last = last if start is None else start
                for i in range(OWN_CAP):
                    at = part * SLOTS + k * OWN_CAP + i
                    last = jnp.where(i < counts[part * 8 + k], rows[at], last)
                    rows[at] = last


def owner_tables(tags, owners):
    def kernel(*refs):
        owner_kernel(owners, *refs)

    return pl.pallas_call(
        kernel,
        in_specs=[SMEM_SPEC],
        out_specs=[SMEM_SPEC] * 2,
        out_shape=[int_shape(BLOCKS * HALVES * SLOTS), int_shape(BLOCKS * HALVES * 8)],
        name="owner_tables",
    )(tags)


def route_tables(cand, me, owners, seqs):
    def kernel(*refs):
        route_kernel(owners, seqs, *refs)

    smem = lambda n: pltpu.SMEM((n,), jnp.int32)
    return pl.pallas_call(
        kernel,
        in_specs=[SMEM_SPEC] * 2,
        out_specs=[SMEM_SPEC] * 2,
        out_shape=[int_shape(ROUTES * owners), int_shape(1)],
        scratch_shapes=[
            smem(owners * seqs),
            smem(BLOCKS * seqs),
            smem(BLOCKS * owners),
            smem(HALVES),
            smem(owners * seqs),
            smem(owners * seqs),
            smem(3 * owners * owners),
            smem(owners * seqs),
        ],
        name="route_tables",
    )(cand, me)


def bring_rows(table, start, sources, name):
    count, length, width = sources[0].shape

    def kernel(table_ref, *refs):
        ins = refs[: len(sources)]
        out_ref, buf, sem_in, sem_out = refs[-4:]

        def loads(n):
            e = table_ref[start + n]
            last = count * (len(sources) - 1)
            for which, source in enumerate(ins):
                low = count * which
                here = e >= low
                if low < last:
                    here = jnp.logical_and(here, e < low + count)
                row = jnp.clip(e - low, 0, count - 1)
                yield here, pltpu.make_async_copy(source.at[row], buf.at[n], sem_in.at[n])

        def store(n):
            return pltpu.make_async_copy(buf.at[n], out_ref.at[n], sem_out.at[n])

        for n in range(count):
            for here, copy in loads(n):

                @pl.when(here)
                def _():
                    copy.start()

        for n in range(count):

            @pl.when(table_ref[start + n] >= 0)
            def _():
                pltpu.make_async_copy(ins[0].at[0], buf.at[n], sem_in.at[n]).wait()
                store(n).start()

        for n in range(count):

            @pl.when(table_ref[start + n] >= 0)
            def _():
                store(n).wait()

    return pl.pallas_call(
        kernel,
        grid_spec=pltpu.PrefetchScalarGridSpec(
            num_scalar_prefetch=1,
            grid=(1,),
            in_specs=[ANY_SPEC] * len(sources),
            out_specs=ANY_SPEC,
            scratch_shapes=[
                pltpu.VMEM((count, length, width), BF16),
                pltpu.SemaphoreType.DMA((count,)),
                pltpu.SemaphoreType.DMA((count,)),
            ],
        ),
        out_shape=jax.ShapeDtypeStruct((count, length, width), BF16),
        compiler_params=params_of(1),
        cost_estimate=pl.CostEstimate(
            flops=0, transcendentals=0, bytes_accessed=4 * count * length * width
        ),
        name=name,
    )(table, *sources)


def move_rows(table, starts, sources, count, scatter, name, wait_for=()):
    length, width = sources[0].shape[1:]
    each = table.shape[0] // (BLOCKS * HALVES)
    total = each * len(sources)

    def kernel(table_ref, *refs):
        ins = refs[: len(sources)]
        out_ref, buf, sem_in, sem_out = refs[-4:]

        def load(part, s):
            idx = table_ref[starts[part] + s]
            at = s if scatter else idx
            to = part * each + s
            return pltpu.make_async_copy(ins[part].at[at], buf.at[to], sem_in.at[to])

        def store(part, s):
            idx = table_ref[starts[part] + s]
            at = part * each + s
            to = idx if scatter else at
            return pltpu.make_async_copy(buf.at[at], out_ref.at[to], sem_out.at[at])

        todo = [(part, s) for part in range(len(sources)) for s in range(each)]
        for part, s in todo:

            @pl.when(table_ref[starts[part] + s] >= 0)
            def _():
                load(part, s).start()

        for part, s in todo:

            @pl.when(table_ref[starts[part] + s] >= 0)
            def _():
                load(part, s).wait()
                store(part, s).start()

        for part, s in todo:

            @pl.when(table_ref[starts[part] + s] >= 0)
            def _():
                store(part, s).wait()

    return pl.pallas_call(
        kernel,
        grid_spec=pltpu.PrefetchScalarGridSpec(
            num_scalar_prefetch=1,
            grid=(1,),
            in_specs=[ANY_SPEC] * (len(sources) + len(wait_for)),
            out_specs=ANY_SPEC,
            scratch_shapes=[
                pltpu.VMEM((total, length, width), BF16),
                pltpu.SemaphoreType.DMA((total,)),
                pltpu.SemaphoreType.DMA((total,)),
            ],
        ),
        out_shape=jax.ShapeDtypeStruct((count, length, width), BF16),
        compiler_params=params_of(1),
        cost_estimate=pl.CostEstimate(
            flops=0, transcendentals=0, bytes_accessed=4 * total * length * width
        ),
        name=name,
    )(table, *sources, *wait_for)


def after(value, earlier):
    def kernel(*refs):
        return

    return pl.pallas_call(
        kernel,
        in_specs=[ANY_SPEC] * (1 + len(earlier)),
        out_specs=ANY_SPEC,
        out_shape=jax.ShapeDtypeStruct(value.shape, value.dtype),
        input_output_aliases={0: 0},
        name="after",
    )(value, *earlier)


def norm_forward(summed, gain_row, shift_row):
    center = summed - jnp.mean(summed, axis=-1, keepdims=True)
    spread = jnp.mean(center * center, axis=-1, keepdims=True)
    scale = lax.rsqrt(spread + 1e-05)
    normed = center * scale
    return normed, normed * gain_row + shift_row, scale


def finish_forward(x, branch, gain_row, shift_row, y_ref, zn_ref, rstd_ref):
    normed, result, scale = norm_forward(x.astype(F32) + branch, gain_row, shift_row)
    y_ref[0] = result.astype(BF16)
    zn_ref[0] = normed.astype(BF16)
    rstd_ref[0] = jnp.broadcast_to(scale, rstd_ref.shape[1:])


def norm_backward(dy, zn_ref, rstd_ref, gain_row):
    dy = dy.astype(F32)
    normed = zn_ref[0].astype(F32)
    scale = rstd_ref[0][:, :1]
    scaled = dy * gain_row
    first = jnp.mean(scaled, axis=-1, keepdims=True)
    second = jnp.mean(scaled * normed, axis=-1, keepdims=True)
    gain_grad = jnp.sum(dy * normed, axis=0, keepdims=True)
    shift_grad = jnp.sum(dy, axis=0, keepdims=True)
    return (scaled - first - normed * second) * scale, gain_grad, shift_grad


def head_masks(length):
    lane = lax.broadcasted_iota(jnp.int32, (length, LANES), 1)
    low = lane < LANES // 2
    return low


def attention_forward(part, tables, x, weights, norms, y_in):
    rows, counts = tables
    b = part // HALVES
    attn_qkv, attn_out = weights
    gains, shifts = norms
    slots, length, width = x.shape
    score_scale = (width // HEADS) ** (-0.5)
    base = part * SLOTS

    def kernel(rows_ref, counts_ref, x_ref, qkv_w, out_w, gain, shift, *rest):
        y_ref, qkv_ref, o_ref, zn_ref, rstd_ref = rest[-5:]
        i = pl.program_id(0)

        @pl.when(i < counts_ref[part * 8])
        def _():
            xv = x_ref[0]
            for third in range(3):
                cols = slice(third * width, (third + 1) * width)
                qkv_ref[0, :, cols] = nn(xv, qkv_w[:, cols]).astype(BF16)
            low = head_masks(length)
            zero = jnp.zeros((), BF16)
            for pair in range(width // LANES):
                at = pair * LANES
                q2 = qkv_ref[0, :, at : at + LANES] * jnp.asarray(score_scale, BF16)
                k2 = qkv_ref[0, :, width + at : width + at + LANES]
                v2 = qkv_ref[0, :, 2 * width + at : 2 * width + at + LANES]
                mixed = []
                for half in range(2):
                    qm = jnp.where(low if half == 0 else ~low, q2, zero)
                    s = nt(qm, k2)
                    e = jnp.exp(s - jnp.max(s, axis=-1, keepdims=True))
                    total = jnp.sum(e, axis=-1, keepdims=True)
                    mixed.append(nn(e.astype(BF16), v2) / total)
                o_ref[0, :, at : at + LANES] = jnp.where(low, mixed[0], mixed[1]).astype(BF16)
            branch = nn(o_ref[0], out_w[...])
            finish_forward(
                xv, branch, gain[0:1, :], shift[0:1, :], y_ref, zn_ref, rstd_ref
            )

    def at_row(i, r, c):
        return (r[base + i], 0, 0)

    def at_step(i, r, c):
        return (jnp.maximum(jnp.minimum(i, c[part * 8] - 1), 0), 0, 0)

    seq = (1, length, width)
    in_specs = [
        pl.BlockSpec(seq, at_row),
        pl.BlockSpec(
            (None, None, width, 3 * width), lambda i, r, c: (b, 0, 0, 0), pipeline_mode=pl.Buffered(1)
        ),
        pl.BlockSpec(
            (None, None, width, width), lambda i, r, c: (b, 0, 0, 0), pipeline_mode=pl.Buffered(1)
        ),
        pl.BlockSpec((8, width), lambda i, r, c: (0, 0)),
        pl.BlockSpec((8, width), lambda i, r, c: (0, 0)),
    ]
    args = [rows, counts, x, attn_qkv, attn_out, gains, shifts]
    alias = {}
    if y_in is not None:
        in_specs.append(pl.BlockSpec(memory_space=pl.ANY))
        alias = {len(args): 0}
        args.append(y_in)
    flops = OWN_CAP * length * width * (8 * width + 4 * length)
    return pl.pallas_call(
        kernel,
        grid_spec=pltpu.PrefetchScalarGridSpec(
            num_scalar_prefetch=2,
            grid=(OWN_CAP,),
            in_specs=in_specs,
            out_specs=[
                pl.BlockSpec(seq, at_row),
                pl.BlockSpec((1, length, 3 * width), at_step),
                pl.BlockSpec(seq, at_step),
                pl.BlockSpec(seq, at_step),
                pl.BlockSpec((1, length, LANES), at_step),
            ],
        ),
        out_shape=[
            jax.ShapeDtypeStruct((slots, length, width), BF16),
            jax.ShapeDtypeStruct((OWN_CAP, length, 3 * width), BF16),
            jax.ShapeDtypeStruct((OWN_CAP, length, width), BF16),
            jax.ShapeDtypeStruct((OWN_CAP, length, width), BF16),
            jax.ShapeDtypeStruct((OWN_CAP, length, LANES), F32),
        ],
        input_output_aliases=alias,
        compiler_params=params_of(1),
        cost_estimate=pl.CostEstimate(
            flops=2 * flops, transcendentals=OWN_CAP * HEADS * length * length, bytes_accessed=30 * 2**20
        ),
        name="attention_forward",
    )(*args)


def attention_backward(part, tables, x, dy, kept, weights, gains, dx_in, sums, packed):
    rows, counts = tables
    b = part // HALVES
    attn_qkv, attn_out = weights
    qkv, o, zn, rstd = kept
    slots, length, width = x.shape
    score_scale = (width // HEADS) ** (-0.5)
    base = part * SLOTS
    first = sums is None
    n_out = 4 if first else 3

    def kernel(rows_ref, counts_ref, x_ref, dy_ref, qkv_ref, o_ref, zn_ref, rstd_ref, qkv_w, out_w, gain, *rest):
        ins = rest[: len(rest) - n_out - 7]
        outs = rest[len(ins) : len(ins) + n_out]
        acc_qkv, acc_out, do_scr, dqkv_scr, dh_scr, dz_scr, sems = rest[-7:]
        dx_ref, small_ref = outs[0], outs[1]
        i = pl.program_id(0)
        here = i < counts_ref[part * 8]

        def copies():
            if first:
                pairs = ((acc_qkv, outs[2]), (acc_out, outs[3]))
            else:
                pairs = ((ins[0], acc_qkv), (ins[1], acc_out))
            return [
                pltpu.make_async_copy(source, target, sems.at[n])
                for n, (source, target) in enumerate(pairs)
            ]

        @pl.when(i == 0)
        def _():
            small_ref[...] = jnp.zeros_like(small_ref)
            if first:
                acc_qkv[...] = jnp.zeros_like(acc_qkv)
                acc_out[...] = jnp.zeros_like(acc_out)
            else:
                for copy in copies():
                    copy.start()

        @pl.when(here)
        def _():
            dz, gain_grad, shift_grad = norm_backward(dy_ref[0], zn_ref, rstd_ref, gain[0:1, :])
            small_ref[0:1, :] += gain_grad
            small_ref[1:2, :] += shift_grad
            dz_scr[...] = dz
            dh = dz.astype(BF16)
            dh_scr[...] = dh
            do_scr[...] = nt(dh, out_w[...]).astype(BF16)
            low = head_masks(length)
            zero = jnp.zeros((), BF16)
            for pair in range(width // LANES):
                at = pair * LANES
                q2 = qkv_ref[0, :, at : at + LANES] * jnp.asarray(score_scale, BF16)
                k2 = qkv_ref[0, :, width + at : width + at + LANES]
                v2 = qkv_ref[0, :, 2 * width + at : 2 * width + at + LANES]
                do2 = do_scr[:, at : at + LANES]
                dqs, dks, dvs = [], [], []
                for half in range(2):
                    mask = low if half == 0 else ~low
                    st = nt(jnp.where(mask, k2, zero), q2)
                    e = jnp.exp(st - jnp.max(st, axis=0, keepdims=True))
                    p = e * (1.0 / jnp.sum(e, axis=0, keepdims=True))
                    dvs.append(nn(p.astype(BF16), do2))
                    t = p * nt(jnp.where(mask, v2, zero), do2)
                    ds = (t - p * jnp.sum(t, axis=0, keepdims=True)).astype(BF16)
                    dks.append(nn(ds, q2))
                    dqs.append(tn(ds, k2))
                dqkv_scr[:, at : at + LANES] = (jnp.where(low, dqs[0], dqs[1]) * score_scale).astype(BF16)
                dqkv_scr[:, width + at : width + at + LANES] = jnp.where(low, dks[0], dks[1]).astype(BF16)
                dqkv_scr[:, 2 * width + at : 2 * width + at + LANES] = jnp.where(low, dvs[0], dvs[1]).astype(BF16)
            total = dz_scr[...]
            for third in range(3):
                cols = slice(third * width, (third + 1) * width)
                total = total + nt(dqkv_scr[:, cols], qkv_w[:, cols])
            dx_ref[0] = total.astype(BF16)

        if not first:

            @pl.when(i == 0)
            def _():
                for copy in copies():
                    copy.wait()

        @pl.when(here)
        def _():
            xv = x_ref[0]
            for third in range(3):
                cols = slice(third * width, (third + 1) * width)
                acc_qkv[:, cols] += tn(xv, dqkv_scr[:, cols])
            acc_out[...] += tn(o_ref[0], dh_scr[...])

        @pl.when(i == OWN_CAP - 1)
        def _():
            if first:
                for copy in copies():
                    copy.start()
                for copy in copies():
                    copy.wait()
            else:
                packed_ref = outs[2]
                groups, tall = packed_ref.shape[0], packed_ref.shape[1] // 4
                for third in range(3):
                    piece = acc_qkv[:, third * width : (third + 1) * width].astype(BF16)
                    packed_ref[:, third * tall : (third + 1) * tall, :] = piece.reshape(
                        groups, tall, width
                    )
                packed_ref[:, 3 * tall : 4 * tall, :] = (
                    acc_out[...].astype(BF16).reshape(groups, tall, width)
                )

    def at_row(i, r, c):
        return (r[base + i], 0, 0)

    def at_step(i, r, c):
        return (jnp.maximum(jnp.minimum(i, c[part * 8] - 1), 0), 0, 0)

    def whole(i, r, c):
        return (0, 0)

    seq = (1, length, width)
    in_specs = [
        pl.BlockSpec(seq, at_row),
        pl.BlockSpec(seq, at_row),
        pl.BlockSpec((1, length, 3 * width), at_step),
        pl.BlockSpec(seq, at_step),
        pl.BlockSpec(seq, at_step),
        pl.BlockSpec((1, length, LANES), at_step),
        pl.BlockSpec(
            (None, None, width, 3 * width), lambda i, r, c: (b, 0, 0, 0), pipeline_mode=pl.Buffered(1)
        ),
        pl.BlockSpec(
            (None, None, width, width), lambda i, r, c: (b, 0, 0, 0), pipeline_mode=pl.Buffered(1)
        ),
        pl.BlockSpec((8, width), whole),
    ]
    args = [rows, counts, x, dy, qkv, o, zn, rstd, attn_qkv, attn_out, gains]
    out_specs = [pl.BlockSpec(seq, at_row), pl.BlockSpec((8, width), whole)]
    out_shape = [
        jax.ShapeDtypeStruct((slots, length, width), BF16),
        jax.ShapeDtypeStruct((8, width), F32),
    ]
    if first:
        out_specs += [ANY_SPEC, ANY_SPEC]
        out_shape += [
            jax.ShapeDtypeStruct((width, 3 * width), F32),
            jax.ShapeDtypeStruct((width, width), F32),
        ]
    else:
        groups, total_rows = packed
        out_specs.append(
            pl.BlockSpec((groups, 4 * width // groups, width), lambda i, r, c: (0, 0, 0))
        )
        out_shape.append(jax.ShapeDtypeStruct((groups, total_rows, width), BF16))
        in_specs += [ANY_SPEC, ANY_SPEC]
        args += list(sums)
    alias = {}
    if dx_in is not None:
        in_specs.append(ANY_SPEC)
        alias = {len(args): 0}
        args.append(dx_in)
    flops = 2 * OWN_CAP * length * width * (8 * width + 4 * length)
    return pl.pallas_call(
        kernel,
        grid_spec=pltpu.PrefetchScalarGridSpec(
            num_scalar_prefetch=2,
            grid=(OWN_CAP,),
            in_specs=in_specs,
            out_specs=out_specs,
            scratch_shapes=[
                pltpu.VMEM((width, 3 * width), F32),
                pltpu.VMEM((width, width), F32),
                pltpu.VMEM((length, width), BF16),
                pltpu.VMEM((length, 3 * width), BF16),
                pltpu.VMEM((length, width), BF16),
                pltpu.VMEM((length, width), F32),
                pltpu.SemaphoreType.DMA((2,)),
            ],
        ),
        out_shape=out_shape,
        input_output_aliases=alias,
        compiler_params=params_of(1),
        cost_estimate=pl.CostEstimate(
            flops=flops, transcendentals=OWN_CAP * HEADS * length * length // 2, bytes_accessed=40 * 2**20
        ),
        name="attention_backward",
    )(*args)


def feed_forward(part, tables, x, weights, norms, earlier):
    rows, counts = tables
    b = part // HALVES
    ffn_up, ffn_down = weights
    gains, shifts = norms
    slots, length, width = x.shape
    hidden = ffn_up.shape[-1]
    parts = hidden // FF_PART
    kind = KINDS - 1
    base = part * SLOTS + kind * OWN_CAP

    def kernel(rows_ref, counts_ref, x_ref, up, down, gain, shift, *rest):
        y_ref, g_ref, slope_ref, zn_ref, rstd_ref, x_scr, h_scr = rest[-7:]
        c, i = pl.program_id(0), pl.program_id(1)

        @pl.when(i < counts_ref[part * 8 + kind])
        def _():
            @pl.when(c == 0)
            def _():
                x_scr[i] = x_ref[0]

            xv = x_scr[i]
            for sub in range(FF_PART // FF_SUB):
                cols = slice(sub * FF_SUB, (sub + 1) * FF_SUB)
                a = nn(xv, up[:, cols])
                phi = 0.5 + 0.5 * lax.erf(a * (0.5**0.5))
                slope = phi + a * (jnp.exp(a * a * -0.5) * 0.3989422804014327)
                g = (a * phi).astype(BF16)
                g_ref[0, :, cols] = g
                slope_ref[0, :, cols] = slope.astype(BF16)
            branch = nn(g_ref[0], down[...])

            @pl.when(c == 0)
            def _():
                h_scr[i] = branch

            @pl.when(jnp.logical_and(c > 0, c < parts - 1))
            def _():
                h_scr[i] += branch

            @pl.when(c == parts - 1)
            def _():
                finish_forward(
                    xv,
                    h_scr[i] + branch,
                    gain[kind : kind + 1, :],
                    shift[kind : kind + 1, :],
                    y_ref,
                    zn_ref,
                    rstd_ref,
                )

    def in_row(c, i, r, n):
        return (r[base + jnp.where(c == 0, i, OWN_CAP - 1)], 0, 0)

    def out_row(c, i, r, n):
        return (r[base + jnp.where(c == parts - 1, i, 0)], 0, 0)

    def place(i, n):
        at = jnp.maximum(jnp.minimum(i, n[part * 8 + kind] - 1), 0)
        return at if part == b * HALVES else at + n[b * HALVES * 8 + kind]

    def out_step(c, i, r, n):
        return (place(jnp.where(c == parts - 1, i, 0), n), 0, 0)

    def part_step(c, i, r, n):
        return (place(i, n), 0, c)

    seq = (1, length, width)
    in_specs = [
        pl.BlockSpec(seq, in_row),
        pl.BlockSpec((None, None, width, FF_PART), lambda c, i, r, n: (b, 0, 0, c)),
        pl.BlockSpec((None, None, FF_PART, width), lambda c, i, r, n: (b, 0, c, 0)),
        pl.BlockSpec((8, width), lambda c, i, r, n: (0, 0)),
        pl.BlockSpec((8, width), lambda c, i, r, n: (0, 0)),
    ]
    args = [rows, counts, x, ffn_up, ffn_down, gains, shifts]
    alias = {}
    for n, kept in enumerate(earlier or ()):
        in_specs.append(ANY_SPEC)
        alias[len(args)] = 1 + n
        args.append(kept)
    return pl.pallas_call(
        kernel,
        grid_spec=pltpu.PrefetchScalarGridSpec(
            num_scalar_prefetch=2,
            grid=(parts, OWN_CAP),
            in_specs=in_specs,
            out_specs=[
                pl.BlockSpec(seq, out_row),
                pl.BlockSpec((1, length, FF_PART), part_step),
                pl.BlockSpec((1, length, FF_PART), part_step),
                pl.BlockSpec(seq, out_step),
                pl.BlockSpec((1, length, LANES), out_step),
            ],
            scratch_shapes=[
                pltpu.VMEM((OWN_CAP, length, width), BF16),
                pltpu.VMEM((OWN_CAP, length, width), F32),
            ],
        ),
        out_shape=[
            jax.ShapeDtypeStruct((slots, length, width), BF16),
            jax.ShapeDtypeStruct((OWN_CAP + 1, length, hidden), BF16),
            jax.ShapeDtypeStruct((OWN_CAP + 1, length, hidden), BF16),
            jax.ShapeDtypeStruct((OWN_CAP + 1, length, width), BF16),
            jax.ShapeDtypeStruct((OWN_CAP + 1, length, LANES), F32),
        ],
        input_output_aliases=alias,
        compiler_params=params_of(2),
        cost_estimate=pl.CostEstimate(
            flops=4 * OWN_CAP * length * width * hidden,
            transcendentals=2 * OWN_CAP * length * hidden,
            bytes_accessed=40 * 2**20,
        ),
        name="feed_forward",
    )(*args)


def feed_backward(b, tables, x, dy, kept, weights, gains, dx_lead, lead, groups, wait_for):
    rows, counts = tables
    ffn_up, ffn_down = weights
    g, slope, zn, rstd = kept
    slots, length, width = x[0].shape
    hidden = ffn_up.shape[-1]
    parts = hidden // FF_PART
    kind = KINDS - 1
    bases = [(b * HALVES + half) * SLOTS + kind * OWN_CAP for half in range(HALVES)]
    tall = width // groups
    deep = hidden // groups
    shares = FF_PART // deep

    def present(n, half):
        return n[(b * HALVES + half) * 8 + kind]

    def kernel(
        rows_ref,
        counts_ref,
        x_ref0,
        x_ref1,
        dy_ref0,
        dy_ref1,
        g_ref,
        slope_ref,
        zn_ref,
        rstd_ref,
        up,
        down,
        gain,
        *rest,
    ):
        (
        small_ref,
        dx_ref0,
        dx_ref1,
        packed_ref,
        x_scr,
        dh_scr,
        dx_scr,
        da_scr,
        acc_up,
        acc_down,
        low_up,
        low_down,
        low_dx,
        tally,
        sems,
        dx_sem,
        ) = rest[-16:]
        c, i = pl.program_id(0), pl.program_id(1)
        n0 = present(counts_ref, 0)
        total_n = n0 + present(counts_ref, 1)
        in_first = i < n0

        @pl.when(jnp.logical_and(c == 0, i == 0))
        def _():
            small_ref[...] = jnp.zeros_like(small_ref)
            lane = lax.broadcasted_iota(jnp.int32, (COUNT_ROWS, width), 1)
            counted = jnp.zeros((COUNT_ROWS, width), F32)
            for k in range(KINDS):
                there = sum(counts_ref[(b * HALVES + half) * 8 + k] for half in range(HALVES))
                counted = jnp.where(lane == k, there.astype(F32), counted)
            tally[...] = counted.astype(BF16)

        @pl.when(i == 0)
        def _():
            acc_up[...] = jnp.zeros_like(acc_up)
            acc_down[...] = jnp.zeros_like(acc_down)

        @pl.when(i < total_n)
        def _():
            @pl.when(c == 0)
            def _():
                dz, gain_grad, shift_grad = norm_backward(
                    jnp.where(in_first, dy_ref0[0], dy_ref1[0]),
                    zn_ref,
                    rstd_ref,
                    gain[kind : kind + 1, :],
                )
                small_ref[0:1, :] += gain_grad
                small_ref[1:2, :] += shift_grad
                x_scr[i] = jnp.where(in_first, x_ref0[0], x_ref1[0])
                dh_scr[i] = dz.astype(BF16)
                dx_scr[i] = dz

            dh = dh_scr[i]
            for sub in range(FF_PART // FF_SUB):
                cols = slice(sub * FF_SUB, (sub + 1) * FF_SUB)
                dg = nt(dh, down[cols, :])
                da_scr[:, cols] = (dg * slope_ref[0, :, cols].astype(F32)).astype(BF16)
            acc_down[...] += tn(g_ref[0], dh)
            acc_up[...] += tn(x_scr[i], da_scr[...])
            total = dx_scr[i] + nt(da_scr[...], up[...])

            @pl.when(c < parts - 1)
            def _():
                dx_scr[i] = total

            @pl.when(c == parts - 1)
            def _():
                low_dx[...] = total.astype(BF16)
                for half, (inside, dx_ref) in enumerate(
                    ((in_first, dx_ref0), (jnp.logical_not(in_first), dx_ref1))
                ):

                    @pl.when(inside)
                    def _():
                        row = rows_ref[bases[half] + jnp.where(in_first, i, jnp.maximum(i - n0, 0))]
                        copy = pltpu.make_async_copy(low_dx, dx_ref.at[row], dx_sem)
                        copy.start()
                        copy.wait()

        def copies():
            pairs = [
                (low_up.at[pl.ds(z * tall, tall)], packed_ref.at[z, pl.ds(c * tall, tall)])
                for z in range(groups)
            ]
            pairs += [
                (
                    low_down.at[pl.ds(m * deep, deep)],
                    packed_ref.at[c * shares + m, pl.ds(parts * tall, deep)],
                )
                for m in range(shares)
            ]
            return [
                pltpu.make_async_copy(source, target, sems.at[n])
                for n, (source, target) in enumerate(pairs)
            ]

        def tallies():
            return [
                pltpu.make_async_copy(
                    tally,
                    packed_ref.at[z, pl.ds(parts * tall + deep, COUNT_ROWS)],
                    sems.at[groups + shares + z],
                )
                for z in range(groups)
            ]

        @pl.when(i == OWN_CAP - 1)
        def _():
            @pl.when(c > 0)
            def _():
                for copy in copies():
                    copy.wait()

            low_up[...] = acc_up[...].astype(BF16)
            low_down[...] = acc_down[...].astype(BF16)
            for copy in copies():
                copy.start()

            @pl.when(c == parts - 1)
            def _():
                for copy in tallies():
                    copy.start()
                for copy in copies() + tallies():
                    copy.wait()

    def first_row(c, i, r, n):
        return (r[bases[0] + jnp.where(c == 0, i, OWN_CAP - 1)], 0, 0)

    def second_row(c, i, r, n):
        at = jnp.where(c == 0, i, OWN_CAP - 1) - present(n, 0)
        return (r[bases[1] + jnp.maximum(at, 0)], 0, 0)

    def last(n):
        return present(n, 0) + present(n, 1) - 1

    def in_step(c, i, r, n):
        return (jnp.where(c == 0, jnp.minimum(i, last(n)), last(n)), 0, 0)

    def part_step(c, i, r, n):
        return (jnp.minimum(i, last(n)), 0, c)

    seq = (1, length, width)
    in_specs = [
        pl.BlockSpec(seq, first_row),
        pl.BlockSpec(seq, second_row),
        pl.BlockSpec(seq, first_row),
        pl.BlockSpec(seq, second_row),
        pl.BlockSpec((1, length, FF_PART), part_step),
        pl.BlockSpec((1, length, FF_PART), part_step),
        pl.BlockSpec(seq, in_step),
        pl.BlockSpec((1, length, LANES), in_step),
        pl.BlockSpec((None, None, width, FF_PART), lambda c, i, r, n: (b, 0, 0, c)),
        pl.BlockSpec((None, None, FF_PART, width), lambda c, i, r, n: (b, 0, c, 0)),
        pl.BlockSpec((8, width), lambda c, i, r, n: (0, 0)),
        ANY_SPEC,
    ] + [ANY_SPEC] * len(wait_for)
    args = [rows, counts, *x, *dy, g, slope, zn, rstd, ffn_up, ffn_down, gains, dx_lead]
    alias = {len(args) - 1: 1 + lead}
    args += wait_for
    return pl.pallas_call(
        kernel,
        grid_spec=pltpu.PrefetchScalarGridSpec(
            num_scalar_prefetch=2,
            grid=(parts, OWN_CAP),
            in_specs=in_specs,
            out_specs=[
                pl.BlockSpec((8, width), lambda c, i, r, n: (0, 0)),
                ANY_SPEC,
                ANY_SPEC,
                ANY_SPEC,
            ],
            scratch_shapes=[
                pltpu.VMEM((OWN_CAP, length, width), BF16),
                pltpu.VMEM((OWN_CAP, length, width), BF16),
                pltpu.VMEM((OWN_CAP, length, width), F32),
                pltpu.VMEM((length, FF_PART), BF16),
                pltpu.VMEM((width, FF_PART), F32),
                pltpu.VMEM((FF_PART, width), F32),
                pltpu.VMEM((width, FF_PART), BF16),
                pltpu.VMEM((FF_PART, width), BF16),
                pltpu.VMEM((length, width), BF16),
                pltpu.VMEM((COUNT_ROWS, width), BF16),
                pltpu.SemaphoreType.DMA((2 * groups + shares,)),
                pltpu.SemaphoreType.DMA,
            ],
        ),
        out_shape=[
            jax.ShapeDtypeStruct((8, width), F32),
            jax.ShapeDtypeStruct((slots, length, width), BF16),
            jax.ShapeDtypeStruct((slots, length, width), BF16),
            jax.ShapeDtypeStruct((groups, parts * tall + deep + COUNT_ROWS, width), BF16),
        ],
        input_output_aliases=alias,
        compiler_params=params_of(2),
        cost_estimate=pl.CostEstimate(
            flops=7 * OWN_CAP * length * width * hidden,
            transcendentals=0,
            bytes_accessed=50 * 2**20,
        ),
        name="feed_backward",
    )(*args)


PAD = 8
ROW_TILE = 128
COL_TILE = 256


def fill_padded(padded, values):
    length = values.shape[0]
    edge = jnp.zeros((PAD, values.shape[1]), F32)
    padded[0:PAD, :] = edge
    padded[PAD + length : PAD + length + PAD, :] = edge
    padded[PAD : PAD + length, :] = values


def conv_forward(part, tables, x, weights, norms, y_in):
    rows, counts = tables
    b = part // HALVES
    taps, conv_point = weights
    gains, shifts = norms
    slots, length, width = x.shape
    base = part * SLOTS + OWN_CAP
    steps = (KINDS - 2) * OWN_CAP

    def kernel(rows_ref, counts_ref, x_ref, point, taps_ref, gain, shift, *rest):
        y_ref, u_ref, zn_ref, rstd_ref, xpad = rest[-5:]
        step = pl.program_id(0)
        which, j = step // OWN_CAP, step % OWN_CAP
        for kind in range(1, KINDS - 1):
            taps_n = 2 * kind + 1
            first = kind * kind - 1

            @pl.when(jnp.logical_and(which == kind - 1, j < counts_ref[part * 8 + kind]))
            def _():
                fill_padded(xpad, x_ref[0].astype(F32))
                for r in range(0, length, ROW_TILE):
                    for col in range(0, width, COL_TILE):
                        cols = slice(col, col + COL_TILE)
                        mixed = None
                        for t in range(taps_n):
                            start = PAD + r + t - kind
                            term = xpad[start : start + ROW_TILE, cols] * taps_ref[first + t : first + t + 1, cols]
                            mixed = term if mixed is None else mixed + term
                        u_ref[0, r : r + ROW_TILE, cols] = mixed.astype(BF16)
                branch = nn(u_ref[0], point[...])
                finish_forward(
                    x_ref[0],
                    branch,
                    gain[kind : kind + 1, :],
                    shift[kind : kind + 1, :],
                    y_ref,
                    zn_ref,
                    rstd_ref,
                )

    def at_row(i, r, c):
        return (r[base + i], 0, 0)

    def at_step(i, r, c):
        which = i // OWN_CAP
        last = c[part * 8 + 1 + which] - 1
        return (which * OWN_CAP + jnp.maximum(jnp.minimum(i % OWN_CAP, last), 0), 0, 0)

    def whole(i, r, c):
        return (0, 0)

    seq = (1, length, width)
    in_specs = [
        pl.BlockSpec(seq, at_row),
        pl.BlockSpec((None, None, None, width, width), lambda i, r, c: (b, 0, i // OWN_CAP, 0, 0)),
        pl.BlockSpec((16, width), whole),
        pl.BlockSpec((8, width), whole),
        pl.BlockSpec((8, width), whole),
    ]
    args = [rows, counts, x, conv_point, taps, gains, shifts]
    alias = {}
    if y_in is not None:
        in_specs.append(pl.BlockSpec(memory_space=pl.ANY))
        alias = {len(args): 0}
        args.append(y_in)
    return pl.pallas_call(
        kernel,
        grid_spec=pltpu.PrefetchScalarGridSpec(
            num_scalar_prefetch=2,
            grid=(steps,),
            in_specs=in_specs,
            out_specs=[
                pl.BlockSpec(seq, at_row),
                pl.BlockSpec(seq, at_step),
                pl.BlockSpec(seq, at_step),
                pl.BlockSpec((1, length, LANES), at_step),
            ],
            scratch_shapes=[pltpu.VMEM((length + 2 * PAD, width), F32)],
        ),
        out_shape=[
            jax.ShapeDtypeStruct((slots, length, width), BF16),
            jax.ShapeDtypeStruct((steps, length, width), BF16),
            jax.ShapeDtypeStruct((steps, length, width), BF16),
            jax.ShapeDtypeStruct((steps, length, LANES), F32),
        ],
        input_output_aliases=alias,
        compiler_params=params_of(1),
        cost_estimate=pl.CostEstimate(
            flops=2 * steps * length * width * width, transcendentals=0, bytes_accessed=36 * 2**20
        ),
        name="conv_forward",
    )(*args)


def conv_backward(part, tables, x, dy, kept, weights, gains, dx_in, sums, packed):
    rows, counts = tables
    b = part // HALVES
    taps, conv_point = weights
    u, zn, rstd = kept
    slots, length, width = x.shape
    base = part * SLOTS + OWN_CAP
    steps = (KINDS - 2) * OWN_CAP
    first_half = sums is None
    groups = packed[0]

    def kernel(rows_ref, counts_ref, x_ref, dy_ref, u_ref, zn_ref, rstd_ref, point, taps_ref, gain, *rest):
        if first_half:
            dx_ref, small_ref, acc, xpad, dupad, dz_scr = rest[-6:]
        else:
            sum_ref = rest[0]
            dx_ref, small_ref, packed_ref, xpad, dupad, dz_scr, acc = rest[-7:]
        step = pl.program_id(0)
        which, j = step // OWN_CAP, step % OWN_CAP

        @pl.when(step == 0)
        def _():
            small_ref[...] = jnp.zeros_like(small_ref)

        @pl.when(j == 0)
        def _():
            acc[...] = jnp.zeros_like(acc) if first_half else sum_ref[...]

        for kind in range(1, KINDS - 1):
            taps_n = 2 * kind + 1
            first = kind * kind - 1

            @pl.when(jnp.logical_and(which == kind - 1, j < counts_ref[part * 8 + kind]))
            def _():
                dz, gain_grad, shift_grad = norm_backward(
                    dy_ref[0], zn_ref, rstd_ref, gain[kind : kind + 1, :]
                )
                small_ref[14 + kind : 15 + kind, :] += gain_grad
                small_ref[17 + kind : 18 + kind, :] += shift_grad
                dz_scr[...] = dz
                dh = dz.astype(BF16)
                acc[...] += tn(u_ref[0], dh)
                fill_padded(xpad, x_ref[0].astype(F32))
                fill_padded(dupad, nt(dh, point[...]))
                for col in range(0, width, COL_TILE):
                    cols = slice(col, col + COL_TILE)
                    sums = [None] * taps_n
                    for r in range(0, length, ROW_TILE):
                        here = dupad[PAD + r : PAD + r + ROW_TILE, cols]
                        total = dz_scr[r : r + ROW_TILE, cols]
                        for t in range(taps_n):
                            back = PAD + r - t + kind
                            total = total + dupad[back : back + ROW_TILE, cols] * taps_ref[first + t : first + t + 1, cols]
                            ahead = PAD + r + t - kind
                            part = jnp.sum(
                                xpad[ahead : ahead + ROW_TILE, cols] * here, axis=0, keepdims=True
                            )
                            sums[t] = part if sums[t] is None else sums[t] + part
                        dx_ref[0, r : r + ROW_TILE, cols] = total.astype(BF16)
                    for t in range(taps_n):
                        small_ref[first + t : first + t + 1, cols] += sums[t]

        if not first_half:

            @pl.when(j == OWN_CAP - 1)
            def _():
                packed_ref[...] = acc[...].astype(BF16).reshape(packed_ref.shape)

    def at_row(i, r, c):
        return (r[base + i], 0, 0)

    def at_step(i, r, c):
        which = i // OWN_CAP
        last = c[part * 8 + 1 + which] - 1
        return (which * OWN_CAP + jnp.maximum(jnp.minimum(i % OWN_CAP, last), 0), 0, 0)

    def whole(i, r, c):
        return (0, 0)

    seq = (1, length, width)
    in_specs = [
        pl.BlockSpec(seq, at_row),
        pl.BlockSpec(seq, at_row),
        pl.BlockSpec(seq, at_step),
        pl.BlockSpec(seq, at_step),
        pl.BlockSpec((1, length, LANES), at_step),
        pl.BlockSpec((None, None, None, width, width), lambda i, r, c: (b, 0, i // OWN_CAP, 0, 0)),
        pl.BlockSpec((16, width), whole),
        pl.BlockSpec((8, width), whole),
    ]
    args = [rows, counts, x, dy, u, zn, rstd, conv_point, taps, gains]
    sum_spec = pl.BlockSpec((None, width, width), lambda i, r, c: (i // OWN_CAP, 0, 0))
    out_specs = [pl.BlockSpec(seq, at_row), pl.BlockSpec((24, width), whole)]
    out_shape = [
        jax.ShapeDtypeStruct((slots, length, width), BF16),
        jax.ShapeDtypeStruct((24, width), F32),
    ]
    scratch = [
        pltpu.VMEM((length + 2 * PAD, width), F32),
        pltpu.VMEM((length + 2 * PAD, width), F32),
        pltpu.VMEM((length, width), F32),
    ]
    alias = {}
    if first_half:
        out_specs.append(sum_spec)
        out_shape.append(jax.ShapeDtypeStruct((KINDS - 2, width, width), F32))
    else:
        in_specs.append(sum_spec)
        args.append(sums)
        out_specs.append(
            pl.BlockSpec((groups, width // groups, width), lambda i, r, c: (0, 4 + i // OWN_CAP, 0))
        )
        out_shape.append(jax.ShapeDtypeStruct(packed[1].shape, BF16))
        in_specs.append(ANY_SPEC)
        alias = {len(args): 2}
        args.append(packed[1])
        scratch.append(pltpu.VMEM((width, width), F32))
    in_specs.append(ANY_SPEC)
    alias = {**alias, len(args): 0}
    args.append(dx_in)
    return pl.pallas_call(
        kernel,
        grid_spec=pltpu.PrefetchScalarGridSpec(
            num_scalar_prefetch=2,
            grid=(steps,),
            in_specs=in_specs,
            out_specs=out_specs,
            scratch_shapes=scratch,
        ),
        out_shape=out_shape,
        input_output_aliases=alias,
        compiler_params=params_of(1),
        cost_estimate=pl.CostEstimate(
            flops=3 * steps * length * width * width, transcendentals=0, bytes_accessed=50 * 2**20
        ),
        name="conv_backward",
    )(*args)


def owner_forward(b, half, tables, x, weights, small_weights, earlier):
    part = b * HALVES + half
    attn_qkv, attn_out, ffn_up, ffn_down, conv_point = weights
    taps, gains, shifts = small_weights
    norms = (gains, shifts)
    y, *kept_f = feed_forward(part, tables, x, (ffn_up, ffn_down), norms, earlier)
    y, *kept_a = attention_forward(part, tables, x, (attn_qkv, attn_out), norms, y)
    y, *kept_c = conv_forward(part, tables, x, (taps, conv_point), norms, y)
    return y, kept_f, kept_a, kept_c


def both_forward(b, tables, x, weights, small_weights):
    y, kept_a, kept_c, kept_f = [], [], [], None
    for half in range(HALVES):
        yh, kept_f, ka, kc = owner_forward(
            b, half, tables, x[half], weights, small_weights, kept_f
        )
        y.append(yh)
        kept_a.append(ka)
        kept_c.append(kc)
    return y, (kept_f, kept_a, kept_c)


def join_small(small_f, small_a, small_c):
    return jnp.concatenate(
        [
            small_c[:15],
            small_a[0:1],
            small_c[15:18],
            small_f[0:1],
            small_a[1:2],
            small_c[18:21],
            small_f[1:2],
        ]
    )


def owner_backward(b, tables, x, dy, kept, weights, small_weights, groups, wait_for):
    attn_qkv, attn_out, ffn_up, ffn_down, conv_point = weights
    taps, gains, shifts = small_weights
    kept_f, kept_a, kept_c = kept
    width = x[0].shape[-1]
    rest_rows = 7 * width // groups + SMALL_ROWS
    attn, conv = (attn_qkv, attn_out), (taps, conv_point)
    lead, other = 1, 0
    first, second = b * HALVES + lead, b * HALVES + other
    d_lead, small_a0, *sum_a = attention_backward(
        first, tables, x[lead], dy[lead], kept_a[lead], attn, gains, None, None, None
    )
    d_lead, small_c0, sum_c = conv_backward(
        first, tables, x[lead], dy[lead], kept_c[lead], conv, gains, d_lead, None, (groups,)
    )
    small_f, *dx, feed_pack = feed_backward(
        b, tables, x, dy, kept_f, (ffn_up, ffn_down), gains, d_lead, lead, groups, wait_for
    )
    dx[other], small_a1, rest_pack = attention_backward(
        second,
        tables,
        x[other],
        dy[other],
        kept_a[other],
        attn,
        gains,
        dx[other],
        sum_a,
        (groups, rest_rows),
    )
    dx[other], small_c1, rest_pack = conv_backward(
        second,
        tables,
        x[other],
        dy[other],
        kept_c[other],
        conv,
        gains,
        dx[other],
        sum_c,
        (groups, rest_pack),
    )
    small = join_small(small_f, small_a0 + small_a1, small_c0 + small_c1).astype(BF16)
    small = small.reshape(25, groups, width // groups)
    small = small.transpose(1, 0, 2)
    small = jnp.pad(small, ((0, 0), (0, SMALL_ROWS - 25), (0, width - width // groups)))
    rest_pack = lax.dynamic_update_slice(rest_pack, small, (0, rest_rows - SMALL_ROWS, 0))
    return dx, feed_pack, rest_pack


def finish_feed(b, feed, up_out, down_out, shapes):
    parts = shapes[0].shape[-1] // FF_PART
    tall, width = shapes[0].shape[2], FF_PART
    count_block = 2 * parts * tall // COUNT_ROWS

    def kernel(up_ref, down_ref, count_ref, *rest):
        up_to, down_to = rest[-2:]
        scale = 1.0 / count_ref[0:1, KINDS - 1 : KINDS].astype(F32)
        up_to[...] = up_ref[...].astype(F32) * scale
        down_to[...] = down_ref[...].astype(F32) * scale

    old = [] if up_out is None else [up_out, down_out]
    return pl.pallas_call(
        kernel,
        grid=(parts,),
        in_specs=[
            pl.BlockSpec((tall, width), lambda c: (c, 0)),
            pl.BlockSpec((tall, width), lambda c: (parts + c, 0)),
            pl.BlockSpec((COUNT_ROWS, width), lambda c: (count_block, 0)),
        ]
        + [ANY_SPEC] * len(old),
        out_specs=[
            pl.BlockSpec((None, None, tall, width), lambda c: (b, 0, 0, c)),
            pl.BlockSpec((None, None, tall, width), lambda c: (b, 0, c, 0)),
        ],
        out_shape=list(shapes),
        input_output_aliases={3 + n: n for n in range(len(old))},
        compiler_params=params_of(1),
        cost_estimate=pl.CostEstimate(flops=0, transcendentals=0, bytes_accessed=8 * 2**20),
        name="finish_feed",
    )(feed, feed, feed, *old)


def finish_rest(b, rest, feed, old, shapes, wait_for):
    tall, width = shapes[1].shape[2:]
    count_block = (feed.shape[0] - COUNT_ROWS) // COUNT_ROWS
    small_block = 7 * tall // SMALL_ROWS

    def kernel(rest_ref, small_ref, count_ref, *refs):
        qkv_to, out_to, taps_to, point_to, gain_to, shift_to = refs[-6:]
        i = pl.program_id(0)
        scales = 1.0 / count_ref[0:1, 0:8].astype(F32)
        values = rest_ref[...].astype(F32)

        @pl.when(i < 3)
        def _():
            qkv_to[...] = values * scales[:, 0:1]

        @pl.when(i == 3)
        def _():
            out_to[...] = values * scales[:, 0:1]
            small = small_ref[...].astype(F32)
            row = lax.broadcasted_iota(jnp.int32, small.shape, 0)
            which = jnp.where(row < 3, 1, jnp.where(row < 8, 2, jnp.where(row < 15, 3, 0)))
            which = jnp.where(row >= 15, row - 15, which)
            which = jnp.where(row >= 20, row - 20, which)
            scale = jnp.zeros_like(small)
            for k in range(KINDS):
                scale = jnp.where(which == k, scales[:, k : k + 1], scale)
            small = small * scale
            taps_to[...] = small[:15, :tall]
            gain_to[...] = small[15:20, :tall]
            shift_to[...] = small[20:25, :tall]

        for k in range(1, KINDS - 1):

            @pl.when(i == 3 + k)
            def _():
                point_to[...] = values * scales[:, k : k + 1]

    old = list(old)
    return pl.pallas_call(
        kernel,
        grid=(7,),
        in_specs=[
            pl.BlockSpec((tall, width), lambda i: (i, 0)),
            pl.BlockSpec((SMALL_ROWS, width), lambda i: (small_block, 0)),
            pl.BlockSpec((COUNT_ROWS, width), lambda i: (count_block, 0)),
        ]
        + [ANY_SPEC] * (len(old) + len(wait_for)),
        out_specs=[
            pl.BlockSpec((None, None, tall, width), lambda i: (b, 0, 0, jnp.minimum(i, 2))),
            pl.BlockSpec((None, None, tall, width), lambda i: (b, 0, 0, 0)),
            pl.BlockSpec((None, None, 15, tall), lambda i: (b, 0, 0, 0)),
            pl.BlockSpec(
                (None, None, None, tall, width), lambda i: (b, 0, jnp.maximum(i - 4, 0), 0, 0)
            ),
            pl.BlockSpec((None, None, KINDS, tall), lambda i: (b, 0, 0, 0)),
            pl.BlockSpec((None, None, KINDS, tall), lambda i: (b, 0, 0, 0)),
        ],
        out_shape=list(shapes),
        input_output_aliases={3 + n: n for n in range(len(old))},
        compiler_params=params_of(1),
        cost_estimate=pl.CostEstimate(flops=0, transcendentals=0, bytes_accessed=8 * 2**20),
        name="finish_rest",
    )(rest, rest, feed, *old, *wait_for)


def small_params(b, conv_taps, norm_gain, norm_bias):
    taps = jnp.pad(conv_taps[b, 0].astype(F32), ((0, 1), (0, 0)))
    gains = jnp.pad(norm_gain[b, 0].astype(F32), ((0, 3), (0, 0)))
    shifts = jnp.pad(norm_bias[b, 0].astype(F32), ((0, 3), (0, 0)))
    return taps, gains, shifts


def exchange(rows):
    return lax.all_to_all(rows, "op", split_axis=0, concat_axis=0, tiled=True)


def group_sum(pack):
    return lax.psum_scatter(pack, "dp", scatter_dimension=0, tiled=False)


def per_device(
    inputs,
    candidate,
    attn_qkv,
    attn_out,
    ffn_up,
    ffn_down,
    conv_taps,
    conv_point,
    norm_gain,
    norm_bias,
    cotangent,
):
    owners = lax.axis_size("op")
    groups = lax.axis_size("dp")
    seqs = inputs.shape[0]
    width = inputs.shape[-1]
    hidden = ffn_up.shape[-1]
    weights = (attn_qkv, attn_out, ffn_up, ffn_down, conv_point)
    smalls = [small_params(b, conv_taps, norm_gain, norm_bias) for b in range(BLOCKS)]
    send, relay, tags = home_tables(candidate.reshape(-1), owners, seqs)
    arrived = exchange(tags.reshape(owners, BLOCKS * HALVES))
    tables = owner_tables(arrived.reshape(-1), owners)
    both = range(HALVES)

    def start(b, half):
        return (b * HALVES + half) * owners

    me = lax.axis_index("op").astype(jnp.int32)[None]
    routed = owners < seqs
    if routed:
        everyone = lax.all_gather(candidate, "op", axis=0, tiled=True)
        route, lost = route_tables(everyone.reshape(-1), me, owners, seqs)
        lost = lax.psum(lost[0], "dp")

    x0 = [
        exchange(
            move_rows(send, [start(0, h)], [inputs], owners, False, "send_inputs", (route,) * h if routed else ())
        )
        for h in both
    ]
    first = owner_forward(0, 0, tables, x0[0], weights, smalls[0], None)

    def on_the_way(table, sources, name):
        return bring_rows(route, table * owners, sources, name)

    def straight_there(y):
        hop0 = exchange(on_the_way(0, [y[0]], "hop_x"))
        hop1 = exchange(on_the_way(1, [hop0, y[1]], "hop_x"))
        hop2 = exchange(on_the_way(2, [y[1], hop1], "hop_x"))
        return [on_the_way(3, [hop0, hop1], "land_x"), on_the_way(4, [hop2], "land_x")]

    def straight_back(dx):
        hop0 = exchange(on_the_way(5, [dx[1]], "hop_dx"))
        hop1 = exchange(on_the_way(6, [dx[0], hop0], "hop_dx"))
        hop2 = exchange(on_the_way(7, [dx[0], hop1], "hop_dx"))
        return [on_the_way(9, [hop2], "land_dx"), on_the_way(8, [hop0, hop1], "land_dx")]

    def home_there(y):
        return [
            exchange(move_rows(relay, [start(0, h)], [exchange(y[h])], owners, False, "relay_x"))
            for h in both
        ]

    def home_back(dx):
        return [
            exchange(move_rows(relay, [start(1, h)], [exchange(dx[h])], owners, False, "relay_dx"))
            for h in both
        ]

    def after_first(there, back, x0, first):
        y00, kept_f, ka0, kc0 = first
        y01, kept_f, ka1, kc1 = owner_forward(
            0, 1, tables, x0[1], weights, smalls[0], kept_f
        )
        kept0 = (kept_f, [ka0, ka1], [kc0, kc1])
        x1 = there([y00, y01])
        y1, kept1 = both_forward(1, tables, x1, weights, smalls[1])
        dy1 = [
            exchange(
                move_rows(
                    send,
                    [start(1, h)],
                    [cotangent],
                    owners,
                    False,
                    "send_cotangent",
                    (y1[1 - h],),
                )
            )
            for h in both
        ]
        dx1, feed1, rest1 = owner_backward(
            1, tables, x1, dy1, kept1, weights, smalls[1], groups, ()
        )
        feed1 = group_sum(feed1)
        rest1 = group_sum(rest1)
        dy0 = back(dx1)
        dx0, feed0, rest0 = owner_backward(
            0, tables, x0, dy0, kept0, weights, smalls[0], groups, (feed1,)
        )
        feed0 = group_sum(feed0)
        rest0 = group_sum(rest0)
        y_home = [exchange(after(y1[h], (dy0[0],))) for h in both]
        outputs = move_rows(send, [start(1, h) for h in both], y_home, seqs, True, "outputs")
        dx_home = [
            exchange(after(dx0[0], (feed0,))),
            exchange(after(dx0[1], (rest1,))),
        ]
        input_grad = move_rows(
            send, [start(0, h) for h in both], dx_home, seqs, True, "input_grad"
        )
        tall, deep = width // groups, hidden // groups
        grad = lambda *dims: jax.ShapeDtypeStruct((BLOCKS, 1) + dims, F32)
        feed_shapes = (grad(tall, hidden), grad(deep, width))
        rest_shapes = (
            grad(tall, 3 * width),
            grad(tall, width),
            grad(15, tall),
            grad(KINDS - 2, tall, width),
            grad(KINDS, tall),
            grad(KINDS, tall),
        )
        feeds = finish_feed(1, feed1, None, None, feed_shapes)
        rests = finish_rest(1, rest1, feed1, (), rest_shapes, ())
        feeds = finish_feed(0, feed0, *feeds, feed_shapes)
        rests = finish_rest(0, rest0, feed0, rests, rest_shapes, (outputs, input_grad, feeds[0]))
        qkv, out, taps, point, gain, shift = rests
        return (outputs, input_grad, qkv, out, *feeds, taps, point, gain, shift)

    if not routed:
        return after_first(home_there, home_back, x0, first)
    return lax.cond(
        lost == 0,
        lambda x0, first: after_first(straight_there, straight_back, x0, first),
        lambda x0, first: after_first(home_there, home_back, x0, first),
        x0,
        first,
    )


def solution(mesh):
    placed = (
        P(("dp", "op"), None, None),
        P(("dp", "op"), None),
        P(None, "op", None, None),
        P(None, "op", None, None),
        P(None, "op", None, None),
        P(None, "op", None, None),
        P(None, "op", None, None),
        P(None, "op", None, None, None),
        P(None, "op", None, None),
        P(None, "op", None, None),
        P(("dp", "op"), None, None),
    )
    return jax.shard_map(
        per_device,
        mesh=mesh,
        in_specs=placed,
        out_specs=(
            P(("dp", "op"), None, None),
            P(("dp", "op"), None, None),
            P(None, "op", "dp", None),
            P(None, "op", "dp", None),
            P(None, "op", "dp", None),
            P(None, "op", "dp", None),
            P(None, "op", None, "dp"),
            P(None, "op", None, "dp", None),
            P(None, "op", None, "dp"),
            P(None, "op", None, "dp"),
        ),
        check_vma=False,
    )
```

```python
import jax
import jax.numpy as jnp
from jax import lax
from jax.experimental import pallas as pl
from jax.experimental.pallas import tpu as pltpu
from jax.sharding import PartitionSpec as P

HEADS = 12
KINDS = 5
BLOCKS = 2
OWN_CAP = 3
HALVES = 2
SLOTS = KINDS * OWN_CAP
FF_PART = 768
FF_SUB = 256
LANES = 128
SMALL_ROWS = 32
COUNT_ROWS = 16
BF16 = jnp.bfloat16
F32 = jnp.float32
VMEM_BYTES = 60 * 2**20


def params_of(axes):
    return pltpu.CompilerParams(
        dimension_semantics=("arbitrary",) * axes, vmem_limit_bytes=VMEM_BYTES
    )


def nn(a, b):
    return lax.dot_general(a, b, (((1,), (0,)), ((), ())), preferred_element_type=F32)


def nt(a, b):
    return lax.dot_general(a, b, (((1,), (1,)), ((), ())), preferred_element_type=F32)


def tn(a, b):
    return lax.dot_general(a, b, (((0,), (0,)), ((), ())), preferred_element_type=F32)


def colour_home(owners, seqs, home, cand, color, partner, first, tally):
    base = home * seqs

    def clear_owner(o, _):
        first[o] = -1
        return 0

    lax.fori_loop(0, BLOCKS * owners, clear_owner, 0)
    for half in range(HALVES):
        tally[half] = 0

    def pair_up(j, _):
        color[base + j] = -1
        for b in range(BLOCKS):
            o = b * owners + lax.rem(cand[(base + j) * BLOCKS + b], owners)
            other = first[o]
            partner[b * seqs + j] = other
            first[o] = j

            @pl.when(other >= 0)
            def _():
                partner[b * seqs + other] = j

        return 0

    lax.fori_loop(0, seqs, pair_up, 0)

    def give(j, shade):
        color[base + j] = shade
        tally[shade] = tally[shade] + 1

    def paint(j, _):
        @pl.when(color[base + j] < 0)
        def _():
            shade = jnp.where(tally[0] > tally[1], 1, 0).astype(jnp.int32)
            give(j, shade)
            for side in range(2):

                def more(state):
                    return state[0] >= 0

                def walk(state):
                    now, use, tone = state
                    then = partner[use * seqs + now]
                    free = jnp.logical_and(then >= 0, color[base + jnp.maximum(then, 0)] < 0)

                    @pl.when(free)
                    def _():
                        give(then, 1 - tone)

                    return (jnp.where(free, then, -1), 1 - use, 1 - tone)

                lax.while_loop(more, walk, (j, jnp.int32(side), shade))

        return 0

    lax.fori_loop(0, seqs, paint, 0)


def home_kernel(owners, seqs, cand, send, relay, tags, color, partner, first, tally):
    for b in range(BLOCKS):

        def clear_owner(o, _):
            for half in range(HALVES):
                send[(b * HALVES + half) * owners + o] = -1
                relay[(b * HALVES + half) * owners + o] = -1
                tags[o * BLOCKS * HALVES + b * HALVES + half] = KINDS
            return 0

        lax.fori_loop(0, owners, clear_owner, 0)
    colour_home(owners, seqs, 0, cand, color, partner, first, tally)

    def place(j, _):
        half = color[j]
        spots = []
        for b in range(BLOCKS):
            c = cand[j * BLOCKS + b]
            o = lax.rem(c, owners)
            spots.append(o)
            send[(b * HALVES + half) * owners + o] = j
            tags[o * BLOCKS * HALVES + b * HALVES + half] = lax.div(c, owners)
        relay[half * owners + spots[1]] = spots[0]
        relay[(HALVES + half) * owners + spots[0]] = spots[1]
        return 0

    lax.fori_loop(0, seqs, place, 0)


ROUTES = 10
TRIES = 24


def route_kernel(
    owners, seqs, cand, me_ref, out, ok, color, partner, first, tally, leave, goal, hops, spill
):
    me = me_ref[0]
    square = owners * owners

    def colour(home, _):
        colour_home(owners, seqs, home, cand, color, partner, first, tally)
        return 0

    lax.fori_loop(0, owners, colour, 0)

    def ends(q, _):
        leave[q] = lax.rem(cand[q * BLOCKS], owners)
        goal[q] = lax.rem(cand[q * BLOCKS + 1], owners)
        return 0

    lax.fori_loop(0, owners * seqs, ends, 0)

    def attempt(state):
        turn, _ = state

        def clear(n, _):
            hops[n] = -1
            return 0

        lax.fori_loop(0, 3 * square, clear, 0)

        def direct(q, spilt):
            at = color[q] * 2 * square + leave[q] * owners + goal[q]
            free = hops[at] < 0

            @pl.when(free)
            def _():
                hops[at] = q

            @pl.when(jnp.logical_not(free))
            def _():
                spill[spilt] = q

            return jnp.where(free, spilt, spilt + 1)

        spilt = lax.fori_loop(0, owners * seqs, direct, jnp.int32(0))
        begin = lax.rem(turn * 5, jnp.maximum(spilt, 1))

        def two_hops(n, lost):
            q = spill[lax.rem(begin + n, jnp.maximum(spilt, 1))]
            o, p = leave[q], goal[q]
            early = color[q] * square
            shift = o * 3 + p * 5 + (n + 1) * turn

            def look(s, found):
                i = lax.rem(shift + s, owners)
                a = early + o * owners + i
                b = early + square + i * owners + p
                good = jnp.logical_and(hops[a] < 0, hops[b] < 0)
                return jnp.where(jnp.logical_and(good, found < 0), i, found)

            i = lax.fori_loop(0, owners, look, jnp.int32(-1))

            @pl.when(i >= 0)
            def _():
                hops[early + o * owners + i] = q
                hops[early + square + i * owners + p] = q

            return jnp.where(i >= 0, lost, lost + 1)

        lost = lax.fori_loop(0, spilt, two_hops, jnp.int32(0))
        return turn + 1, lost

    def again(state):
        return jnp.logical_and(state[0] < TRIES, state[1] > 0)

    _, lost = lax.while_loop(again, attempt, (jnp.int32(0), jnp.int32(1)))
    ok[0] = lost

    def clear_out(n, _):
        out[n] = -1
        return 0

    lax.fori_loop(0, ROUTES * owners, clear_out, 0)

    def note(d, _):
        def home(q):
            return lax.div(q, seqs)

        def put(table, at, value):
            out[table * owners + at] = value

        q = hops[me * owners + d]

        @pl.when(q >= 0)
        def _():
            put(0, d, home(q))
            put(9, home(q), d)

        q1 = hops[square + me * owners + d]

        @pl.when(q1 >= 0)
        def _():
            late = color[q1] == 1
            put(1, d, jnp.where(late, owners + home(q1), leave[q1]))

            @pl.when(late)
            def _():
                put(8, home(q1), owners + d)

        q2 = hops[2 * square + me * owners + d]

        @pl.when(q2 >= 0)
        def _():
            mine = leave[q2] == me
            put(2, d, jnp.where(mine, home(q2), owners + leave[q2]))

            @pl.when(mine)
            def _():
                put(8, home(q2), d)

        r = hops[d * owners + me]

        @pl.when(r >= 0)
        def _():
            there = goal[r] == me
            put(7, d, jnp.where(there, home(r), owners + goal[r]))

            @pl.when(there)
            def _():
                put(3, home(r), d)

        r1 = hops[square + d * owners + me]

        @pl.when(r1 >= 0)
        def _():
            late = color[r1] == 1
            put(6, d, jnp.where(late, owners + goal[r1], home(r1)))

            @pl.when(jnp.logical_not(late))
            def _():
                put(3, home(r1), owners + d)

        r2 = hops[2 * square + d * owners + me]

        @pl.when(r2 >= 0)
        def _():
            put(4, home(r2), d)
            put(5, d, home(r2))

        return 0

    lax.fori_loop(0, owners, note, 0)


SMEM_SPEC = pl.BlockSpec(memory_space=pltpu.SMEM)
ANY_SPEC = pl.BlockSpec(memory_space=pl.ANY)


def int_shape(n):
    return jax.ShapeDtypeStruct((n,), jnp.int32)


def home_tables(cand, owners, seqs):
    def kernel(*refs):
        home_kernel(owners, seqs, *refs)

    size = BLOCKS * HALVES * owners
    return pl.pallas_call(
        kernel,
        in_specs=[SMEM_SPEC],
        out_specs=[SMEM_SPEC] * 3,
        out_shape=[int_shape(size)] * 3,
        scratch_shapes=[
            pltpu.SMEM((seqs,), jnp.int32),
            pltpu.SMEM((BLOCKS * seqs,), jnp.int32),
            pltpu.SMEM((BLOCKS * owners,), jnp.int32),
            pltpu.SMEM((HALVES,), jnp.int32),
        ],
        name="home_tables",
    )(cand)


def owner_kernel(owners, tags, rows, counts):
    for b in range(BLOCKS):
        for half in range(HALVES):
            part = b * HALVES + half
            for k in range(8):
                counts[part * 8 + k] = 0

            def arrive(h, free):
                k = tags[h * BLOCKS * HALVES + part]
                there = k < KINDS

                @pl.when(there)
                def _():
                    n = jnp.minimum(counts[part * 8 + k], OWN_CAP - 1)
                    rows[part * SLOTS + k * OWN_CAP + n] = h
                    counts[part * 8 + k] = n + 1

                return jnp.where(there, free, h)

            free = lax.fori_loop(0, owners, arrive, jnp.int32(0))

            def spare(k, otherwise):
                return jnp.where(
                    counts[part * 8 + k] > 0, rows[part * SLOTS + k * OWN_CAP], otherwise
                )

            conv_spare = free
            for k in reversed(range(1, KINDS - 1)):
                conv_spare = spare(k, conv_spare)
            attn_spare = spare(0, conv_spare)
            feed_spare = spare(KINDS - 1, attn_spare)
            last = conv_spare
            for k, start in ((1, None), (2, None), (3, None), (0, attn_spare), (KINDS - 1, feed_spare)):
                last = last if start is None else start
                for i in range(OWN_CAP):
                    at = part * SLOTS + k * OWN_CAP + i
                    last = jnp.where(i < counts[part * 8 + k], rows[at], last)
                    rows[at] = last


def owner_tables(tags, owners):
    def kernel(*refs):
        owner_kernel(owners, *refs)

    return pl.pallas_call(
        kernel,
        in_specs=[SMEM_SPEC],
        out_specs=[SMEM_SPEC] * 2,
        out_shape=[int_shape(BLOCKS * HALVES * SLOTS), int_shape(BLOCKS * HALVES * 8)],
        name="owner_tables",
    )(tags)


def route_tables(cand, me, owners, seqs):
    def kernel(*refs):
        route_kernel(owners, seqs, *refs)

    smem = lambda n: pltpu.SMEM((n,), jnp.int32)
    return pl.pallas_call(
        kernel,
        in_specs=[SMEM_SPEC] * 2,
        out_specs=[SMEM_SPEC] * 2,
        out_shape=[int_shape(ROUTES * owners), int_shape(1)],
        scratch_shapes=[
            smem(owners * seqs),
            smem(BLOCKS * seqs),
            smem(BLOCKS * owners),
            smem(HALVES),
            smem(owners * seqs),
            smem(owners * seqs),
            smem(3 * owners * owners),
            smem(owners * seqs),
        ],
        name="route_tables",
    )(cand, me)


def bring_rows(table, start, sources, name):
    count, length, width = sources[0].shape

    def kernel(table_ref, *refs):
        ins = refs[: len(sources)]
        out_ref, buf, sem_in, sem_out = refs[-4:]

        def loads(n):
            e = table_ref[start + n]
            last = count * (len(sources) - 1)
            for which, source in enumerate(ins):
                low = count * which
                here = e >= low
                if low < last:
                    here = jnp.logical_and(here, e < low + count)
                row = jnp.clip(e - low, 0, count - 1)
                yield here, pltpu.make_async_copy(source.at[row], buf.at[n], sem_in.at[n])

        def store(n):
            return pltpu.make_async_copy(buf.at[n], out_ref.at[n], sem_out.at[n])

        for n in range(count):
            for here, copy in loads(n):

                @pl.when(here)
                def _():
                    copy.start()

        for n in range(count):

            @pl.when(table_ref[start + n] >= 0)
            def _():
                pltpu.make_async_copy(ins[0].at[0], buf.at[n], sem_in.at[n]).wait()
                store(n).start()

        for n in range(count):

            @pl.when(table_ref[start + n] >= 0)
            def _():
                store(n).wait()

    return pl.pallas_call(
        kernel,
        grid_spec=pltpu.PrefetchScalarGridSpec(
            num_scalar_prefetch=1,
            grid=(1,),
            in_specs=[ANY_SPEC] * len(sources),
            out_specs=ANY_SPEC,
            scratch_shapes=[
                pltpu.VMEM((count, length, width), BF16),
                pltpu.SemaphoreType.DMA((count,)),
                pltpu.SemaphoreType.DMA((count,)),
            ],
        ),
        out_shape=jax.ShapeDtypeStruct((count, length, width), BF16),
        compiler_params=params_of(1),
        cost_estimate=pl.CostEstimate(
            flops=0, transcendentals=0, bytes_accessed=4 * count * length * width
        ),
        name=name,
    )(table, *sources)


def move_rows(table, starts, sources, count, scatter, name, wait_for=()):
    length, width = sources[0].shape[1:]
    each = table.shape[0] // (BLOCKS * HALVES)
    total = each * len(sources)

    def kernel(table_ref, *refs):
        ins = refs[: len(sources)]
        out_ref, buf, sem_in, sem_out = refs[-4:]

        def load(part, s):
            idx = table_ref[starts[part] + s]
            at = s if scatter else idx
            to = part * each + s
            return pltpu.make_async_copy(ins[part].at[at], buf.at[to], sem_in.at[to])

        def store(part, s):
            idx = table_ref[starts[part] + s]
            at = part * each + s
            to = idx if scatter else at
            return pltpu.make_async_copy(buf.at[at], out_ref.at[to], sem_out.at[at])

        todo = [(part, s) for part in range(len(sources)) for s in range(each)]
        for part, s in todo:

            @pl.when(table_ref[starts[part] + s] >= 0)
            def _():
                load(part, s).start()

        for part, s in todo:

            @pl.when(table_ref[starts[part] + s] >= 0)
            def _():
                load(part, s).wait()
                store(part, s).start()

        for part, s in todo:

            @pl.when(table_ref[starts[part] + s] >= 0)
            def _():
                store(part, s).wait()

    return pl.pallas_call(
        kernel,
        grid_spec=pltpu.PrefetchScalarGridSpec(
            num_scalar_prefetch=1,
            grid=(1,),
            in_specs=[ANY_SPEC] * (len(sources) + len(wait_for)),
            out_specs=ANY_SPEC,
            scratch_shapes=[
                pltpu.VMEM((total, length, width), BF16),
                pltpu.SemaphoreType.DMA((total,)),
                pltpu.SemaphoreType.DMA((total,)),
            ],
        ),
        out_shape=jax.ShapeDtypeStruct((count, length, width), BF16),
        compiler_params=params_of(1),
        cost_estimate=pl.CostEstimate(
            flops=0, transcendentals=0, bytes_accessed=4 * total * length * width
        ),
        name=name,
    )(table, *sources, *wait_for)


def after(value, earlier):
    def kernel(*refs):
        return

    return pl.pallas_call(
        kernel,
        in_specs=[ANY_SPEC] * (1 + len(earlier)),
        out_specs=ANY_SPEC,
        out_shape=jax.ShapeDtypeStruct(value.shape, value.dtype),
        input_output_aliases={0: 0},
        name="after",
    )(value, *earlier)


def norm_forward(summed, gain_row, shift_row):
    center = summed - jnp.mean(summed, axis=-1, keepdims=True)
    spread = jnp.mean(center * center, axis=-1, keepdims=True)
    scale = lax.rsqrt(spread + 1e-05)
    normed = center * scale
    return normed, normed * gain_row + shift_row, scale


def finish_forward(x, branch, gain_row, shift_row, y_ref, zn_ref, rstd_ref):
    normed, result, scale = norm_forward(x.astype(F32) + branch, gain_row, shift_row)
    y_ref[0] = result.astype(BF16)
    zn_ref[0] = normed.astype(BF16)
    rstd_ref[0] = jnp.broadcast_to(scale, rstd_ref.shape[1:])


def norm_backward(dy, zn_ref, rstd_ref, gain_row):
    dy = dy.astype(F32)
    normed = zn_ref[0].astype(F32)
    scale = rstd_ref[0][:, :1]
    scaled = dy * gain_row
    first = jnp.mean(scaled, axis=-1, keepdims=True)
    second = jnp.mean(scaled * normed, axis=-1, keepdims=True)
    gain_grad = jnp.sum(dy * normed, axis=0, keepdims=True)
    shift_grad = jnp.sum(dy, axis=0, keepdims=True)
    return (scaled - first - normed * second) * scale, gain_grad, shift_grad


def head_masks(length):
    lane = lax.broadcasted_iota(jnp.int32, (length, LANES), 1)
    low = lane < LANES // 2
    return low


def attention_forward(part, tables, x, weights, norms, y_in):
    rows, counts = tables
    b = part // HALVES
    attn_qkv, attn_out = weights
    gains, shifts = norms
    slots, length, width = x.shape
    score_scale = (width // HEADS) ** (-0.5)
    base = part * SLOTS

    def kernel(rows_ref, counts_ref, x_ref, qkv_w, out_w, gain, shift, *rest):
        y_ref, qkv_ref, o_ref, zn_ref, rstd_ref = rest[-5:]
        i = pl.program_id(0)

        @pl.when(i < counts_ref[part * 8])
        def _():
            xv = x_ref[0]
            for third in range(3):
                cols = slice(third * width, (third + 1) * width)
                qkv_ref[0, :, cols] = nn(xv, qkv_w[:, cols]).astype(BF16)
            low = head_masks(length)
            zero = jnp.zeros((), BF16)
            for pair in range(width // LANES):
                at = pair * LANES
                q2 = qkv_ref[0, :, at : at + LANES] * jnp.asarray(score_scale, BF16)
                k2 = qkv_ref[0, :, width + at : width + at + LANES]
                v2 = qkv_ref[0, :, 2 * width + at : 2 * width + at + LANES]
                mixed = []
                for half in range(2):
                    qm = jnp.where(low if half == 0 else ~low, q2, zero)
                    s = nt(qm, k2)
                    e = jnp.exp(s - jnp.max(s, axis=-1, keepdims=True))
                    total = jnp.sum(e, axis=-1, keepdims=True)
                    mixed.append(nn(e.astype(BF16), v2) / total)
                o_ref[0, :, at : at + LANES] = jnp.where(low, mixed[0], mixed[1]).astype(BF16)
            branch = nn(o_ref[0], out_w[...])
            finish_forward(
                xv, branch, gain[0:1, :], shift[0:1, :], y_ref, zn_ref, rstd_ref
            )

    def at_row(i, r, c):
        return (r[base + i], 0, 0)

    def at_step(i, r, c):
        return (jnp.maximum(jnp.minimum(i, c[part * 8] - 1), 0), 0, 0)

    seq = (1, length, width)
    in_specs = [
        pl.BlockSpec(seq, at_row),
        pl.BlockSpec(
            (None, None, width, 3 * width), lambda i, r, c: (b, 0, 0, 0), pipeline_mode=pl.Buffered(1)
        ),
        pl.BlockSpec(
            (None, None, width, width), lambda i, r, c: (b, 0, 0, 0), pipeline_mode=pl.Buffered(1)
        ),
        pl.BlockSpec((8, width), lambda i, r, c: (0, 0)),
        pl.BlockSpec((8, width), lambda i, r, c: (0, 0)),
    ]
    args = [rows, counts, x, attn_qkv, attn_out, gains, shifts]
    alias = {}
    if y_in is not None:
        in_specs.append(pl.BlockSpec(memory_space=pl.ANY))
        alias = {len(args): 0}
        args.append(y_in)
    flops = OWN_CAP * length * width * (8 * width + 4 * length)
    return pl.pallas_call(
        kernel,
        grid_spec=pltpu.PrefetchScalarGridSpec(
            num_scalar_prefetch=2,
            grid=(OWN_CAP,),
            in_specs=in_specs,
            out_specs=[
                pl.BlockSpec(seq, at_row),
                pl.BlockSpec((1, length, 3 * width), at_step),
                pl.BlockSpec(seq, at_step),
                pl.BlockSpec(seq, at_step),
                pl.BlockSpec((1, length, LANES), at_step),
            ],
        ),
        out_shape=[
            jax.ShapeDtypeStruct((slots, length, width), BF16),
            jax.ShapeDtypeStruct((OWN_CAP, length, 3 * width), BF16),
            jax.ShapeDtypeStruct((OWN_CAP, length, width), BF16),
            jax.ShapeDtypeStruct((OWN_CAP, length, width), BF16),
            jax.ShapeDtypeStruct((OWN_CAP, length, LANES), F32),
        ],
        input_output_aliases=alias,
        compiler_params=params_of(1),
        cost_estimate=pl.CostEstimate(
            flops=2 * flops, transcendentals=OWN_CAP * HEADS * length * length, bytes_accessed=30 * 2**20
        ),
        name="attention_forward",
    )(*args)


def attention_backward(part, tables, x, dy, kept, weights, gains, dx_in, sums, packed):
    rows, counts = tables
    b = part // HALVES
    attn_qkv, attn_out = weights
    qkv, o, zn, rstd = kept
    slots, length, width = x.shape
    score_scale = (width // HEADS) ** (-0.5)
    base = part * SLOTS
    first = sums is None
    n_out = 4 if first else 3

    def kernel(rows_ref, counts_ref, x_ref, dy_ref, qkv_ref, o_ref, zn_ref, rstd_ref, qkv_w, out_w, gain, *rest):
        ins = rest[: len(rest) - n_out - 7]
        outs = rest[len(ins) : len(ins) + n_out]
        acc_qkv, acc_out, do_scr, dqkv_scr, dh_scr, dz_scr, sems = rest[-7:]
        dx_ref, small_ref = outs[0], outs[1]
        i = pl.program_id(0)
        here = i < counts_ref[part * 8]

        def copies():
            if first:
                pairs = ((acc_qkv, outs[2]), (acc_out, outs[3]))
            else:
                pairs = ((ins[0], acc_qkv), (ins[1], acc_out))
            return [
                pltpu.make_async_copy(source, target, sems.at[n])
                for n, (source, target) in enumerate(pairs)
            ]

        @pl.when(i == 0)
        def _():
            small_ref[...] = jnp.zeros_like(small_ref)
            if first:
                acc_qkv[...] = jnp.zeros_like(acc_qkv)
                acc_out[...] = jnp.zeros_like(acc_out)
            else:
                for copy in copies():
                    copy.start()

        @pl.when(here)
        def _():
            dz, gain_grad, shift_grad = norm_backward(dy_ref[0], zn_ref, rstd_ref, gain[0:1, :])
            small_ref[0:1, :] += gain_grad
            small_ref[1:2, :] += shift_grad
            dz_scr[...] = dz
            dh = dz.astype(BF16)
            dh_scr[...] = dh
            do_scr[...] = nt(dh, out_w[...]).astype(BF16)
            low = head_masks(length)
            zero = jnp.zeros((), BF16)
            for pair in range(width // LANES):
                at = pair * LANES
                q2 = qkv_ref[0, :, at : at + LANES] * jnp.asarray(score_scale, BF16)
                k2 = qkv_ref[0, :, width + at : width + at + LANES]
                v2 = qkv_ref[0, :, 2 * width + at : 2 * width + at + LANES]
                do2 = do_scr[:, at : at + LANES]
                dqs, dks, dvs = [], [], []
                for half in range(2):
                    mask = low if half == 0 else ~low
                    st = nt(jnp.where(mask, k2, zero), q2)
                    e = jnp.exp(st - jnp.max(st, axis=0, keepdims=True))
                    p = e * (1.0 / jnp.sum(e, axis=0, keepdims=True))
                    dvs.append(nn(p.astype(BF16), do2))
                    t = p * nt(jnp.where(mask, v2, zero), do2)
                    ds = (t - p * jnp.sum(t, axis=0, keepdims=True)).astype(BF16)
                    dks.append(nn(ds, q2))
                    dqs.append(tn(ds, k2))
                dqkv_scr[:, at : at + LANES] = (jnp.where(low, dqs[0], dqs[1]) * score_scale).astype(BF16)
                dqkv_scr[:, width + at : width + at + LANES] = jnp.where(low, dks[0], dks[1]).astype(BF16)
                dqkv_scr[:, 2 * width + at : 2 * width + at + LANES] = jnp.where(low, dvs[0], dvs[1]).astype(BF16)
            total = dz_scr[...]
            for third in range(3):
                cols = slice(third * width, (third + 1) * width)
                total = total + nt(dqkv_scr[:, cols], qkv_w[:, cols])
            dx_ref[0] = total.astype(BF16)

        if not first:

            @pl.when(i == 0)
            def _():
                for copy in copies():
                    copy.wait()

        @pl.when(here)
        def _():
            xv = x_ref[0]
            for third in range(3):
                cols = slice(third * width, (third + 1) * width)
                acc_qkv[:, cols] += tn(xv, dqkv_scr[:, cols])
            acc_out[...] += tn(o_ref[0], dh_scr[...])

        @pl.when(i == OWN_CAP - 1)
        def _():
            if first:
                for copy in copies():
                    copy.start()
                for copy in copies():
                    copy.wait()
            else:
                packed_ref = outs[2]
                groups, tall = packed_ref.shape[0], packed_ref.shape[1] // 4
                for third in range(3):
                    piece = acc_qkv[:, third * width : (third + 1) * width].astype(BF16)
                    packed_ref[:, third * tall : (third + 1) * tall, :] = piece.reshape(
                        groups, tall, width
                    )
                packed_ref[:, 3 * tall : 4 * tall, :] = (
                    acc_out[...].astype(BF16).reshape(groups, tall, width)
                )

    def at_row(i, r, c):
        return (r[base + i], 0, 0)

    def at_step(i, r, c):
        return (jnp.maximum(jnp.minimum(i, c[part * 8] - 1), 0), 0, 0)

    def whole(i, r, c):
        return (0, 0)

    seq = (1, length, width)
    in_specs = [
        pl.BlockSpec(seq, at_row),
        pl.BlockSpec(seq, at_row),
        pl.BlockSpec((1, length, 3 * width), at_step),
        pl.BlockSpec(seq, at_step),
        pl.BlockSpec(seq, at_step),
        pl.BlockSpec((1, length, LANES), at_step),
        pl.BlockSpec(
            (None, None, width, 3 * width), lambda i, r, c: (b, 0, 0, 0), pipeline_mode=pl.Buffered(1)
        ),
        pl.BlockSpec(
            (None, None, width, width), lambda i, r, c: (b, 0, 0, 0), pipeline_mode=pl.Buffered(1)
        ),
        pl.BlockSpec((8, width), whole),
    ]
    args = [rows, counts, x, dy, qkv, o, zn, rstd, attn_qkv, attn_out, gains]
    out_specs = [pl.BlockSpec(seq, at_row), pl.BlockSpec((8, width), whole)]
    out_shape = [
        jax.ShapeDtypeStruct((slots, length, width), BF16),
        jax.ShapeDtypeStruct((8, width), F32),
    ]
    if first:
        out_specs += [ANY_SPEC, ANY_SPEC]
        out_shape += [
            jax.ShapeDtypeStruct((width, 3 * width), F32),
            jax.ShapeDtypeStruct((width, width), F32),
        ]
    else:
        groups, total_rows = packed
        out_specs.append(
            pl.BlockSpec((groups, 4 * width // groups, width), lambda i, r, c: (0, 0, 0))
        )
        out_shape.append(jax.ShapeDtypeStruct((groups, total_rows, width), BF16))
        in_specs += [ANY_SPEC, ANY_SPEC]
        args += list(sums)
    alias = {}
    if dx_in is not None:
        in_specs.append(ANY_SPEC)
        alias = {len(args): 0}
        args.append(dx_in)
    flops = 2 * OWN_CAP * length * width * (8 * width + 4 * length)
    return pl.pallas_call(
        kernel,
        grid_spec=pltpu.PrefetchScalarGridSpec(
            num_scalar_prefetch=2,
            grid=(OWN_CAP,),
            in_specs=in_specs,
            out_specs=out_specs,
            scratch_shapes=[
                pltpu.VMEM((width, 3 * width), F32),
                pltpu.VMEM((width, width), F32),
                pltpu.VMEM((length, width), BF16),
                pltpu.VMEM((length, 3 * width), BF16),
                pltpu.VMEM((length, width), BF16),
                pltpu.VMEM((length, width), F32),
                pltpu.SemaphoreType.DMA((2,)),
            ],
        ),
        out_shape=out_shape,
        input_output_aliases=alias,
        compiler_params=params_of(1),
        cost_estimate=pl.CostEstimate(
            flops=flops, transcendentals=OWN_CAP * HEADS * length * length // 2, bytes_accessed=40 * 2**20
        ),
        name="attention_backward",
    )(*args)


def feed_forward(part, tables, x, weights, norms, earlier):
    rows, counts = tables
    b = part // HALVES
    ffn_up, ffn_down = weights
    gains, shifts = norms
    slots, length, width = x.shape
    hidden = ffn_up.shape[-1]
    parts = hidden // FF_PART
    kind = KINDS - 1
    base = part * SLOTS + kind * OWN_CAP

    def kernel(rows_ref, counts_ref, x_ref, up, down, gain, shift, *rest):
        y_ref, g_ref, slope_ref, zn_ref, rstd_ref, x_scr, h_scr = rest[-7:]
        c, i = pl.program_id(0), pl.program_id(1)

        @pl.when(i < counts_ref[part * 8 + kind])
        def _():
            @pl.when(c == 0)
            def _():
                x_scr[i] = x_ref[0]

            xv = x_scr[i]
            for sub in range(FF_PART // FF_SUB):
                cols = slice(sub * FF_SUB, (sub + 1) * FF_SUB)
                a = nn(xv, up[:, cols])
                phi = 0.5 + 0.5 * lax.erf(a * (0.5**0.5))
                slope = phi + a * (jnp.exp(a * a * -0.5) * 0.3989422804014327)
                g = (a * phi).astype(BF16)
                g_ref[0, :, cols] = g
                slope_ref[0, :, cols] = slope.astype(BF16)
            branch = nn(g_ref[0], down[...])

            @pl.when(c == 0)
            def _():
                h_scr[i] = branch

            @pl.when(jnp.logical_and(c > 0, c < parts - 1))
            def _():
                h_scr[i] += branch

            @pl.when(c == parts - 1)
            def _():
                finish_forward(
                    xv,
                    h_scr[i] + branch,
                    gain[kind : kind + 1, :],
                    shift[kind : kind + 1, :],
                    y_ref,
                    zn_ref,
                    rstd_ref,
                )

    def in_row(c, i, r, n):
        return (r[base + jnp.where(c == 0, i, OWN_CAP - 1)], 0, 0)

    def out_row(c, i, r, n):
        return (r[base + jnp.where(c == parts - 1, i, 0)], 0, 0)

    def place(i, n):
        at = jnp.maximum(jnp.minimum(i, n[part * 8 + kind] - 1), 0)
        return at if part == b * HALVES else at + n[b * HALVES * 8 + kind]

    def out_step(c, i, r, n):
        return (place(jnp.where(c == parts - 1, i, 0), n), 0, 0)

    def part_step(c, i, r, n):
        return (place(i, n), 0, c)

    seq = (1, length, width)
    in_specs = [
        pl.BlockSpec(seq, in_row),
        pl.BlockSpec((None, None, width, FF_PART), lambda c, i, r, n: (b, 0, 0, c)),
        pl.BlockSpec((None, None, FF_PART, width), lambda c, i, r, n: (b, 0, c, 0)),
        pl.BlockSpec((8, width), lambda c, i, r, n: (0, 0)),
        pl.BlockSpec((8, width), lambda c, i, r, n: (0, 0)),
    ]
    args = [rows, counts, x, ffn_up, ffn_down, gains, shifts]
    alias = {}
    for n, kept in enumerate(earlier or ()):
        in_specs.append(ANY_SPEC)
        alias[len(args)] = 1 + n
        args.append(kept)
    return pl.pallas_call(
        kernel,
        grid_spec=pltpu.PrefetchScalarGridSpec(
            num_scalar_prefetch=2,
            grid=(parts, OWN_CAP),
            in_specs=in_specs,
            out_specs=[
                pl.BlockSpec(seq, out_row),
                pl.BlockSpec((1, length, FF_PART), part_step),
                pl.BlockSpec((1, length, FF_PART), part_step),
                pl.BlockSpec(seq, out_step),
                pl.BlockSpec((1, length, LANES), out_step),
            ],
            scratch_shapes=[
                pltpu.VMEM((OWN_CAP, length, width), BF16),
                pltpu.VMEM((OWN_CAP, length, width), F32),
            ],
        ),
        out_shape=[
            jax.ShapeDtypeStruct((slots, length, width), BF16),
            jax.ShapeDtypeStruct((OWN_CAP + 1, length, hidden), BF16),
            jax.ShapeDtypeStruct((OWN_CAP + 1, length, hidden), BF16),
            jax.ShapeDtypeStruct((OWN_CAP + 1, length, width), BF16),
            jax.ShapeDtypeStruct((OWN_CAP + 1, length, LANES), F32),
        ],
        input_output_aliases=alias,
        compiler_params=params_of(2),
        cost_estimate=pl.CostEstimate(
            flops=4 * OWN_CAP * length * width * hidden,
            transcendentals=2 * OWN_CAP * length * hidden,
            bytes_accessed=40 * 2**20,
        ),
        name="feed_forward",
    )(*args)


def feed_backward(b, tables, x, dy, kept, weights, gains, dx_lead, lead, groups, wait_for):
    rows, counts = tables
    ffn_up, ffn_down = weights
    g, slope, zn, rstd = kept
    slots, length, width = x[0].shape
    hidden = ffn_up.shape[-1]
    parts = hidden // FF_PART
    kind = KINDS - 1
    bases = [(b * HALVES + half) * SLOTS + kind * OWN_CAP for half in range(HALVES)]
    tall = width // groups
    deep = hidden // groups
    shares = FF_PART // deep

    def present(n, half):
        return n[(b * HALVES + half) * 8 + kind]

    def kernel(
        rows_ref,
        counts_ref,
        x_ref0,
        x_ref1,
        dy_ref0,
        dy_ref1,
        g_ref,
        slope_ref,
        zn_ref,
        rstd_ref,
        up,
        down,
        gain,
        *rest,
    ):
        (
        small_ref,
        dx_ref0,
        dx_ref1,
        packed_ref,
        x_scr,
        dh_scr,
        dx_scr,
        da_scr,
        acc_up,
        acc_down,
        low_up,
        low_down,
        low_dx,
        tally,
        sems,
        dx_sem,
        ) = rest[-16:]
        c, i = pl.program_id(0), pl.program_id(1)
        n0 = present(counts_ref, 0)
        total_n = n0 + present(counts_ref, 1)
        in_first = i < n0

        @pl.when(jnp.logical_and(c == 0, i == 0))
        def _():
            small_ref[...] = jnp.zeros_like(small_ref)
            lane = lax.broadcasted_iota(jnp.int32, (COUNT_ROWS, width), 1)
            counted = jnp.zeros((COUNT_ROWS, width), F32)
            for k in range(KINDS):
                there = sum(counts_ref[(b * HALVES + half) * 8 + k] for half in range(HALVES))
                counted = jnp.where(lane == k, there.astype(F32), counted)
            tally[...] = counted.astype(BF16)

        @pl.when(i == 0)
        def _():
            acc_up[...] = jnp.zeros_like(acc_up)
            acc_down[...] = jnp.zeros_like(acc_down)

        @pl.when(i < total_n)
        def _():
            @pl.when(c == 0)
            def _():
                dz, gain_grad, shift_grad = norm_backward(
                    jnp.where(in_first, dy_ref0[0], dy_ref1[0]),
                    zn_ref,
                    rstd_ref,
                    gain[kind : kind + 1, :],
                )
                small_ref[0:1, :] += gain_grad
                small_ref[1:2, :] += shift_grad
                x_scr[i] = jnp.where(in_first, x_ref0[0], x_ref1[0])
                dh_scr[i] = dz.astype(BF16)
                dx_scr[i] = dz

            dh = dh_scr[i]
            for sub in range(FF_PART // FF_SUB):
                cols = slice(sub * FF_SUB, (sub + 1) * FF_SUB)
                dg = nt(dh, down[cols, :])
                da_scr[:, cols] = (dg * slope_ref[0, :, cols].astype(F32)).astype(BF16)
            acc_down[...] += tn(g_ref[0], dh)
            acc_up[...] += tn(x_scr[i], da_scr[...])
            total = dx_scr[i] + nt(da_scr[...], up[...])

            @pl.when(c < parts - 1)
            def _():
                dx_scr[i] = total

            @pl.when(c == parts - 1)
            def _():
                low_dx[...] = total.astype(BF16)
                for half, (inside, dx_ref) in enumerate(
                    ((in_first, dx_ref0), (jnp.logical_not(in_first), dx_ref1))
                ):

                    @pl.when(inside)
                    def _():
                        row = rows_ref[bases[half] + jnp.where(in_first, i, jnp.maximum(i - n0, 0))]
                        copy = pltpu.make_async_copy(low_dx, dx_ref.at[row], dx_sem)
                        copy.start()
                        copy.wait()

        def copies():
            pairs = [
                (low_up.at[pl.ds(z * tall, tall)], packed_ref.at[z, pl.ds(c * tall, tall)])
                for z in range(groups)
            ]
            pairs += [
                (
                    low_down.at[pl.ds(m * deep, deep)],
                    packed_ref.at[c * shares + m, pl.ds(parts * tall, deep)],
                )
                for m in range(shares)
            ]
            return [
                pltpu.make_async_copy(source, target, sems.at[n])
                for n, (source, target) in enumerate(pairs)
            ]

        def tallies():
            return [
                pltpu.make_async_copy(
                    tally,
                    packed_ref.at[z, pl.ds(parts * tall + deep, COUNT_ROWS)],
                    sems.at[groups + shares + z],
                )
                for z in range(groups)
            ]

        @pl.when(i == OWN_CAP - 1)
        def _():
            @pl.when(c > 0)
            def _():
                for copy in copies():
                    copy.wait()

            low_up[...] = acc_up[...].astype(BF16)
            low_down[...] = acc_down[...].astype(BF16)
            for copy in copies():
                copy.start()

            @pl.when(c == parts - 1)
            def _():
                for copy in tallies():
                    copy.start()
                for copy in copies() + tallies():
                    copy.wait()

    def first_row(c, i, r, n):
        return (r[bases[0] + jnp.where(c == 0, i, OWN_CAP - 1)], 0, 0)

    def second_row(c, i, r, n):
        at = jnp.where(c == 0, i, OWN_CAP - 1) - present(n, 0)
        return (r[bases[1] + jnp.maximum(at, 0)], 0, 0)

    def last(n):
        return present(n, 0) + present(n, 1) - 1

    def in_step(c, i, r, n):
        return (jnp.where(c == 0, jnp.minimum(i, last(n)), last(n)), 0, 0)

    def part_step(c, i, r, n):
        return (jnp.minimum(i, last(n)), 0, c)

    seq = (1, length, width)
    in_specs = [
        pl.BlockSpec(seq, first_row),
        pl.BlockSpec(seq, second_row),
        pl.BlockSpec(seq, first_row),
        pl.BlockSpec(seq, second_row),
        pl.BlockSpec((1, length, FF_PART), part_step),
        pl.BlockSpec((1, length, FF_PART), part_step),
        pl.BlockSpec(seq, in_step),
        pl.BlockSpec((1, length, LANES), in_step),
        pl.BlockSpec((None, None, width, FF_PART), lambda c, i, r, n: (b, 0, 0, c)),
        pl.BlockSpec((None, None, FF_PART, width), lambda c, i, r, n: (b, 0, c, 0)),
        pl.BlockSpec((8, width), lambda c, i, r, n: (0, 0)),
        ANY_SPEC,
    ] + [ANY_SPEC] * len(wait_for)
    args = [rows, counts, *x, *dy, g, slope, zn, rstd, ffn_up, ffn_down, gains, dx_lead]
    alias = {len(args) - 1: 1 + lead}
    args += wait_for
    return pl.pallas_call(
        kernel,
        grid_spec=pltpu.PrefetchScalarGridSpec(
            num_scalar_prefetch=2,
            grid=(parts, OWN_CAP),
            in_specs=in_specs,
            out_specs=[
                pl.BlockSpec((8, width), lambda c, i, r, n: (0, 0)),
                ANY_SPEC,
                ANY_SPEC,
                ANY_SPEC,
            ],
            scratch_shapes=[
                pltpu.VMEM((OWN_CAP, length, width), BF16),
                pltpu.VMEM((OWN_CAP, length, width), BF16),
                pltpu.VMEM((OWN_CAP, length, width), F32),
                pltpu.VMEM((length, FF_PART), BF16),
                pltpu.VMEM((width, FF_PART), F32),
                pltpu.VMEM((FF_PART, width), F32),
                pltpu.VMEM((width, FF_PART), BF16),
                pltpu.VMEM((FF_PART, width), BF16),
                pltpu.VMEM((length, width), BF16),
                pltpu.VMEM((COUNT_ROWS, width), BF16),
                pltpu.SemaphoreType.DMA((2 * groups + shares,)),
                pltpu.SemaphoreType.DMA,
            ],
        ),
        out_shape=[
            jax.ShapeDtypeStruct((8, width), F32),
            jax.ShapeDtypeStruct((slots, length, width), BF16),
            jax.ShapeDtypeStruct((slots, length, width), BF16),
            jax.ShapeDtypeStruct((groups, parts * tall + deep + COUNT_ROWS, width), BF16),
        ],
        input_output_aliases=alias,
        compiler_params=params_of(2),
        cost_estimate=pl.CostEstimate(
            flops=7 * OWN_CAP * length * width * hidden,
            transcendentals=0,
            bytes_accessed=50 * 2**20,
        ),
        name="feed_backward",
    )(*args)


PAD = 8
ROW_TILE = 128
COL_TILE = 256


def fill_padded(padded, values):
    length = values.shape[0]
    edge = jnp.zeros((PAD, values.shape[1]), F32)
    padded[0:PAD, :] = edge
    padded[PAD + length : PAD + length + PAD, :] = edge
    padded[PAD : PAD + length, :] = values


def conv_forward(part, tables, x, weights, norms, y_in):
    rows, counts = tables
    b = part // HALVES
    taps, conv_point = weights
    gains, shifts = norms
    slots, length, width = x.shape
    base = part * SLOTS + OWN_CAP
    steps = (KINDS - 2) * OWN_CAP

    def kernel(rows_ref, counts_ref, x_ref, point, taps_ref, gain, shift, *rest):
        y_ref, u_ref, zn_ref, rstd_ref, xpad = rest[-5:]
        step = pl.program_id(0)
        which, j = step // OWN_CAP, step % OWN_CAP
        for kind in range(1, KINDS - 1):
            taps_n = 2 * kind + 1
            first = kind * kind - 1

            @pl.when(jnp.logical_and(which == kind - 1, j < counts_ref[part * 8 + kind]))
            def _():
                fill_padded(xpad, x_ref[0].astype(F32))
                for r in range(0, length, ROW_TILE):
                    for col in range(0, width, COL_TILE):
                        cols = slice(col, col + COL_TILE)
                        mixed = None
                        for t in range(taps_n):
                            start = PAD + r + t - kind
                            term = xpad[start : start + ROW_TILE, cols] * taps_ref[first + t : first + t + 1, cols]
                            mixed = term if mixed is None else mixed + term
                        u_ref[0, r : r + ROW_TILE, cols] = mixed.astype(BF16)
                branch = nn(u_ref[0], point[...])
                finish_forward(
                    x_ref[0],
                    branch,
                    gain[kind : kind + 1, :],
                    shift[kind : kind + 1, :],
                    y_ref,
                    zn_ref,
                    rstd_ref,
                )

    def at_row(i, r, c):
        return (r[base + i], 0, 0)

    def at_step(i, r, c):
        which = i // OWN_CAP
        last = c[part * 8 + 1 + which] - 1
        return (which * OWN_CAP + jnp.maximum(jnp.minimum(i % OWN_CAP, last), 0), 0, 0)

    def whole(i, r, c):
        return (0, 0)

    seq = (1, length, width)
    in_specs = [
        pl.BlockSpec(seq, at_row),
        pl.BlockSpec((None, None, None, width, width), lambda i, r, c: (b, 0, i // OWN_CAP, 0, 0)),
        pl.BlockSpec((16, width), whole),
        pl.BlockSpec((8, width), whole),
        pl.BlockSpec((8, width), whole),
    ]
    args = [rows, counts, x, conv_point, taps, gains, shifts]
    alias = {}
    if y_in is not None:
        in_specs.append(pl.BlockSpec(memory_space=pl.ANY))
        alias = {len(args): 0}
        args.append(y_in)
    return pl.pallas_call(
        kernel,
        grid_spec=pltpu.PrefetchScalarGridSpec(
            num_scalar_prefetch=2,
            grid=(steps,),
            in_specs=in_specs,
            out_specs=[
                pl.BlockSpec(seq, at_row),
                pl.BlockSpec(seq, at_step),
                pl.BlockSpec(seq, at_step),
                pl.BlockSpec((1, length, LANES), at_step),
            ],
            scratch_shapes=[pltpu.VMEM((length + 2 * PAD, width), F32)],
        ),
        out_shape=[
            jax.ShapeDtypeStruct((slots, length, width), BF16),
            jax.ShapeDtypeStruct((steps, length, width), BF16),
            jax.ShapeDtypeStruct((steps, length, width), BF16),
            jax.ShapeDtypeStruct((steps, length, LANES), F32),
        ],
        input_output_aliases=alias,
        compiler_params=params_of(1),
        cost_estimate=pl.CostEstimate(
            flops=2 * steps * length * width * width, transcendentals=0, bytes_accessed=36 * 2**20
        ),
        name="conv_forward",
    )(*args)


def conv_backward(part, tables, x, dy, kept, weights, gains, dx_in, sums, packed):
    rows, counts = tables
    b = part // HALVES
    taps, conv_point = weights
    u, zn, rstd = kept
    slots, length, width = x.shape
    base = part * SLOTS + OWN_CAP
    steps = (KINDS - 2) * OWN_CAP
    first_half = sums is None
    groups = packed[0]

    def kernel(rows_ref, counts_ref, x_ref, dy_ref, u_ref, zn_ref, rstd_ref, point, taps_ref, gain, *rest):
        if first_half:
            dx_ref, small_ref, acc, xpad, dupad, dz_scr = rest[-6:]
        else:
            sum_ref = rest[0]
            dx_ref, small_ref, packed_ref, xpad, dupad, dz_scr, acc = rest[-7:]
        step = pl.program_id(0)
        which, j = step // OWN_CAP, step % OWN_CAP

        @pl.when(step == 0)
        def _():
            small_ref[...] = jnp.zeros_like(small_ref)

        @pl.when(j == 0)
        def _():
            acc[...] = jnp.zeros_like(acc) if first_half else sum_ref[...]

        for kind in range(1, KINDS - 1):
            taps_n = 2 * kind + 1
            first = kind * kind - 1

            @pl.when(jnp.logical_and(which == kind - 1, j < counts_ref[part * 8 + kind]))
            def _():
                dz, gain_grad, shift_grad = norm_backward(
                    dy_ref[0], zn_ref, rstd_ref, gain[kind : kind + 1, :]
                )
                small_ref[14 + kind : 15 + kind, :] += gain_grad
                small_ref[17 + kind : 18 + kind, :] += shift_grad
                dz_scr[...] = dz
                dh = dz.astype(BF16)
                acc[...] += tn(u_ref[0], dh)
                fill_padded(xpad, x_ref[0].astype(F32))
                fill_padded(dupad, nt(dh, point[...]))
                for col in range(0, width, COL_TILE):
                    cols = slice(col, col + COL_TILE)
                    sums = [None] * taps_n
                    for r in range(0, length, ROW_TILE):
                        here = dupad[PAD + r : PAD + r + ROW_TILE, cols]
                        total = dz_scr[r : r + ROW_TILE, cols]
                        for t in range(taps_n):
                            back = PAD + r - t + kind
                            total = total + dupad[back : back + ROW_TILE, cols] * taps_ref[first + t : first + t + 1, cols]
                            ahead = PAD + r + t - kind
                            part = jnp.sum(
                                xpad[ahead : ahead + ROW_TILE, cols] * here, axis=0, keepdims=True
                            )
                            sums[t] = part if sums[t] is None else sums[t] + part
                        dx_ref[0, r : r + ROW_TILE, cols] = total.astype(BF16)
                    for t in range(taps_n):
                        small_ref[first + t : first + t + 1, cols] += sums[t]

        if not first_half:

            @pl.when(j == OWN_CAP - 1)
            def _():
                packed_ref[...] = acc[...].astype(BF16).reshape(packed_ref.shape)

    def at_row(i, r, c):
        return (r[base + i], 0, 0)

    def at_step(i, r, c):
        which = i // OWN_CAP
        last = c[part * 8 + 1 + which] - 1
        return (which * OWN_CAP + jnp.maximum(jnp.minimum(i % OWN_CAP, last), 0), 0, 0)

    def whole(i, r, c):
        return (0, 0)

    seq = (1, length, width)
    in_specs = [
        pl.BlockSpec(seq, at_row),
        pl.BlockSpec(seq, at_row),
        pl.BlockSpec(seq, at_step),
        pl.BlockSpec(seq, at_step),
        pl.BlockSpec((1, length, LANES), at_step),
        pl.BlockSpec((None, None, None, width, width), lambda i, r, c: (b, 0, i // OWN_CAP, 0, 0)),
        pl.BlockSpec((16, width), whole),
        pl.BlockSpec((8, width), whole),
    ]
    args = [rows, counts, x, dy, u, zn, rstd, conv_point, taps, gains]
    sum_spec = pl.BlockSpec((None, width, width), lambda i, r, c: (i // OWN_CAP, 0, 0))
    out_specs = [pl.BlockSpec(seq, at_row), pl.BlockSpec((24, width), whole)]
    out_shape = [
        jax.ShapeDtypeStruct((slots, length, width), BF16),
        jax.ShapeDtypeStruct((24, width), F32),
    ]
    scratch = [
        pltpu.VMEM((length + 2 * PAD, width), F32),
        pltpu.VMEM((length + 2 * PAD, width), F32),
        pltpu.VMEM((length, width), F32),
    ]
    alias = {}
    if first_half:
        out_specs.append(sum_spec)
        out_shape.append(jax.ShapeDtypeStruct((KINDS - 2, width, width), F32))
    else:
        in_specs.append(sum_spec)
        args.append(sums)
        out_specs.append(
            pl.BlockSpec((groups, width // groups, width), lambda i, r, c: (0, 4 + i // OWN_CAP, 0))
        )
        out_shape.append(jax.ShapeDtypeStruct(packed[1].shape, BF16))
        in_specs.append(ANY_SPEC)
        alias = {len(args): 2}
        args.append(packed[1])
        scratch.append(pltpu.VMEM((width, width), F32))
    in_specs.append(ANY_SPEC)
    alias = {**alias, len(args): 0}
    args.append(dx_in)
    return pl.pallas_call(
        kernel,
        grid_spec=pltpu.PrefetchScalarGridSpec(
            num_scalar_prefetch=2,
            grid=(steps,),
            in_specs=in_specs,
            out_specs=out_specs,
            scratch_shapes=scratch,
        ),
        out_shape=out_shape,
        input_output_aliases=alias,
        compiler_params=params_of(1),
        cost_estimate=pl.CostEstimate(
            flops=3 * steps * length * width * width, transcendentals=0, bytes_accessed=50 * 2**20
        ),
        name="conv_backward",
    )(*args)


def owner_forward(b, half, tables, x, weights, small_weights, earlier):
    part = b * HALVES + half
    attn_qkv, attn_out, ffn_up, ffn_down, conv_point = weights
    taps, gains, shifts = small_weights
    norms = (gains, shifts)
    y, *kept_f = feed_forward(part, tables, x, (ffn_up, ffn_down), norms, earlier)
    y, *kept_a = attention_forward(part, tables, x, (attn_qkv, attn_out), norms, y)
    y, *kept_c = conv_forward(part, tables, x, (taps, conv_point), norms, y)
    return y, kept_f, kept_a, kept_c


def both_forward(b, tables, x, weights, small_weights):
    y, kept_a, kept_c, kept_f = [], [], [], None
    for half in range(HALVES):
        yh, kept_f, ka, kc = owner_forward(
            b, half, tables, x[half], weights, small_weights, kept_f
        )
        y.append(yh)
        kept_a.append(ka)
        kept_c.append(kc)
    return y, (kept_f, kept_a, kept_c)


def join_small(small_f, small_a, small_c):
    return jnp.concatenate(
        [
            small_c[:15],
            small_a[0:1],
            small_c[15:18],
            small_f[0:1],
            small_a[1:2],
            small_c[18:21],
            small_f[1:2],
        ]
    )


def owner_backward(b, tables, x, dy, kept, weights, small_weights, groups, wait_for):
    attn_qkv, attn_out, ffn_up, ffn_down, conv_point = weights
    taps, gains, shifts = small_weights
    kept_f, kept_a, kept_c = kept
    width = x[0].shape[-1]
    rest_rows = 7 * width // groups + SMALL_ROWS
    attn, conv = (attn_qkv, attn_out), (taps, conv_point)
    lead, other = 1, 0
    first, second = b * HALVES + lead, b * HALVES + other
    d_lead, small_a0, *sum_a = attention_backward(
        first, tables, x[lead], dy[lead], kept_a[lead], attn, gains, None, None, None
    )
    d_lead, small_c0, sum_c = conv_backward(
        first, tables, x[lead], dy[lead], kept_c[lead], conv, gains, d_lead, None, (groups,)
    )
    small_f, *dx, feed_pack = feed_backward(
        b, tables, x, dy, kept_f, (ffn_up, ffn_down), gains, d_lead, lead, groups, wait_for
    )
    dx[other], small_a1, rest_pack = attention_backward(
        second,
        tables,
        x[other],
        dy[other],
        kept_a[other],
        attn,
        gains,
        dx[other],
        sum_a,
        (groups, rest_rows),
    )
    dx[other], small_c1, rest_pack = conv_backward(
        second,
        tables,
        x[other],
        dy[other],
        kept_c[other],
        conv,
        gains,
        dx[other],
        sum_c,
        (groups, rest_pack),
    )
    small = join_small(small_f, small_a0 + small_a1, small_c0 + small_c1).astype(BF16)
    small = small.reshape(25, groups, width // groups)
    small = small.transpose(1, 0, 2)
    small = jnp.pad(small, ((0, 0), (0, SMALL_ROWS - 25), (0, width - width // groups)))
    rest_pack = lax.dynamic_update_slice(rest_pack, small, (0, rest_rows - SMALL_ROWS, 0))
    return dx, feed_pack, rest_pack


def finish_feed(b, feed, up_out, down_out, shapes):
    parts = shapes[0].shape[-1] // FF_PART
    tall, width = shapes[0].shape[2], FF_PART
    count_block = 2 * parts * tall // COUNT_ROWS

    def kernel(up_ref, down_ref, count_ref, *rest):
        up_to, down_to = rest[-2:]
        scale = 1.0 / count_ref[0:1, KINDS - 1 : KINDS].astype(F32)
        up_to[...] = up_ref[...].astype(F32) * scale
        down_to[...] = down_ref[...].astype(F32) * scale

    old = [] if up_out is None else [up_out, down_out]
    return pl.pallas_call(
        kernel,
        grid=(parts,),
        in_specs=[
            pl.BlockSpec((tall, width), lambda c: (c, 0)),
            pl.BlockSpec((tall, width), lambda c: (parts + c, 0)),
            pl.BlockSpec((COUNT_ROWS, width), lambda c: (count_block, 0)),
        ]
        + [ANY_SPEC] * len(old),
        out_specs=[
            pl.BlockSpec((None, None, tall, width), lambda c: (b, 0, 0, c)),
            pl.BlockSpec((None, None, tall, width), lambda c: (b, 0, c, 0)),
        ],
        out_shape=list(shapes),
        input_output_aliases={3 + n: n for n in range(len(old))},
        compiler_params=params_of(1),
        cost_estimate=pl.CostEstimate(flops=0, transcendentals=0, bytes_accessed=8 * 2**20),
        name="finish_feed",
    )(feed, feed, feed, *old)


def finish_rest(b, rest, feed, old, shapes, wait_for):
    tall, width = shapes[1].shape[2:]
    count_block = (feed.shape[0] - COUNT_ROWS) // COUNT_ROWS
    small_block = 7 * tall // SMALL_ROWS

    def kernel(rest_ref, small_ref, count_ref, *refs):
        qkv_to, out_to, taps_to, point_to, gain_to, shift_to = refs[-6:]
        i = pl.program_id(0)
        scales = 1.0 / count_ref[0:1, 0:8].astype(F32)
        values = rest_ref[...].astype(F32)

        @pl.when(i < 3)
        def _():
            qkv_to[...] = values * scales[:, 0:1]

        @pl.when(i == 3)
        def _():
            out_to[...] = values * scales[:, 0:1]
            small = small_ref[...].astype(F32)
            row = lax.broadcasted_iota(jnp.int32, small.shape, 0)
            which = jnp.where(row < 3, 1, jnp.where(row < 8, 2, jnp.where(row < 15, 3, 0)))
            which = jnp.where(row >= 15, row - 15, which)
            which = jnp.where(row >= 20, row - 20, which)
            scale = jnp.zeros_like(small)
            for k in range(KINDS):
                scale = jnp.where(which == k, scales[:, k : k + 1], scale)
            small = small * scale
            taps_to[...] = small[:15, :tall]
            gain_to[...] = small[15:20, :tall]
            shift_to[...] = small[20:25, :tall]

        for k in range(1, KINDS - 1):

            @pl.when(i == 3 + k)
            def _():
                point_to[...] = values * scales[:, k : k + 1]

    old = list(old)
    return pl.pallas_call(
        kernel,
        grid=(7,),
        in_specs=[
            pl.BlockSpec((tall, width), lambda i: (i, 0)),
            pl.BlockSpec((SMALL_ROWS, width), lambda i: (small_block, 0)),
            pl.BlockSpec((COUNT_ROWS, width), lambda i: (count_block, 0)),
        ]
        + [ANY_SPEC] * (len(old) + len(wait_for)),
        out_specs=[
            pl.BlockSpec((None, None, tall, width), lambda i: (b, 0, 0, jnp.minimum(i, 2))),
            pl.BlockSpec((None, None, tall, width), lambda i: (b, 0, 0, 0)),
            pl.BlockSpec((None, None, 15, tall), lambda i: (b, 0, 0, 0)),
            pl.BlockSpec(
                (None, None, None, tall, width), lambda i: (b, 0, jnp.maximum(i - 4, 0), 0, 0)
            ),
            pl.BlockSpec((None, None, KINDS, tall), lambda i: (b, 0, 0, 0)),
            pl.BlockSpec((None, None, KINDS, tall), lambda i: (b, 0, 0, 0)),
        ],
        out_shape=list(shapes),
        input_output_aliases={3 + n: n for n in range(len(old))},
        compiler_params=params_of(1),
        cost_estimate=pl.CostEstimate(flops=0, transcendentals=0, bytes_accessed=8 * 2**20),
        name="finish_rest",
    )(rest, rest, feed, *old, *wait_for)


def small_params(b, conv_taps, norm_gain, norm_bias):
    taps = jnp.pad(conv_taps[b, 0].astype(F32), ((0, 1), (0, 0)))
    gains = jnp.pad(norm_gain[b, 0].astype(F32), ((0, 3), (0, 0)))
    shifts = jnp.pad(norm_bias[b, 0].astype(F32), ((0, 3), (0, 0)))
    return taps, gains, shifts


def exchange(rows):
    return lax.all_to_all(rows, "op", split_axis=0, concat_axis=0, tiled=True)


def group_sum(pack):
    return lax.psum_scatter(pack, "dp", scatter_dimension=0, tiled=False)


def per_device(
    inputs,
    candidate,
    attn_qkv,
    attn_out,
    ffn_up,
    ffn_down,
    conv_taps,
    conv_point,
    norm_gain,
    norm_bias,
    cotangent,
):
    owners = lax.axis_size("op")
    groups = lax.axis_size("dp")
    seqs = inputs.shape[0]
    width = inputs.shape[-1]
    hidden = ffn_up.shape[-1]
    weights = (attn_qkv, attn_out, ffn_up, ffn_down, conv_point)
    smalls = [small_params(b, conv_taps, norm_gain, norm_bias) for b in range(BLOCKS)]
    send, relay, tags = home_tables(candidate.reshape(-1), owners, seqs)
    marks = BLOCKS * HALVES
    told = jnp.concatenate(
        [tags.reshape(owners, marks), jnp.broadcast_to(candidate.reshape(1, -1), (owners, BLOCKS * seqs))],
        axis=1,
    )
    told = exchange(told)
    everyone = told[:, marks:].reshape(-1)
    tables = owner_tables(told[:, :marks].reshape(-1), owners)
    both = range(HALVES)

    def start(b, half):
        return (b * HALVES + half) * owners

    me = lax.axis_index("op").astype(jnp.int32)[None]
    routed = owners < seqs
    if routed:
        route, lost = route_tables(everyone, me, owners, seqs)
        lost = lax.psum(lost, "dp")

    x0 = [
        exchange(
            move_rows(send, [start(0, h)], [inputs], owners, False, "send_inputs", (lost,) * h if routed else ())
        )
        for h in both
    ]
    first = owner_forward(0, 0, tables, x0[0], weights, smalls[0], None)
    leaving = bring_rows(route, 0, [first[0]], "hop_x") if routed else None

    def on_the_way(table, sources, name):
        return bring_rows(route, table * owners, sources, name)

    def straight_there(y):
        hop0 = exchange(leaving)
        hop1 = exchange(on_the_way(1, [hop0, y[1]], "hop_x"))
        hop2 = exchange(on_the_way(2, [y[1], hop1], "hop_x"))
        return [on_the_way(3, [hop0, hop1], "land_x"), on_the_way(4, [hop2], "land_x")]

    def straight_back(dx):
        hop0 = exchange(on_the_way(5, [dx[1]], "hop_dx"))
        hop1 = exchange(on_the_way(6, [dx[0], hop0], "hop_dx"))
        hop2 = exchange(on_the_way(7, [dx[0], hop1], "hop_dx"))
        return [on_the_way(9, [hop2], "land_dx"), on_the_way(8, [hop0, hop1], "land_dx")]

    def home_there(y):
        return [
            exchange(move_rows(relay, [start(0, h)], [exchange(y[h])], owners, False, "relay_x"))
            for h in both
        ]

    def home_back(dx):
        return [
            exchange(move_rows(relay, [start(1, h)], [exchange(dx[h])], owners, False, "relay_dx"))
            for h in both
        ]

    def after_first(there, back, x0, first):
        y00, kept_f, ka0, kc0 = first
        y01, kept_f, ka1, kc1 = owner_forward(
            0, 1, tables, x0[1], weights, smalls[0], kept_f
        )
        kept0 = (kept_f, [ka0, ka1], [kc0, kc1])
        x1 = there([y00, y01])
        y1, kept1 = both_forward(1, tables, x1, weights, smalls[1])
        dy1 = [
            exchange(
                move_rows(
                    send,
                    [start(1, h)],
                    [cotangent],
                    owners,
                    False,
                    "send_cotangent",
                    (y1[1 - h],),
                )
            )
            for h in both
        ]
        dx1, feed1, rest1 = owner_backward(
            1, tables, x1, dy1, kept1, weights, smalls[1], groups, ()
        )
        feed1 = group_sum(feed1)
        rest1 = group_sum(rest1)
        dy0 = back(dx1)
        dx0, feed0, rest0 = owner_backward(
            0, tables, x0, dy0, kept0, weights, smalls[0], groups, (feed1,)
        )
        feed0 = group_sum(feed0)
        rest0 = group_sum(rest0)
        y_home = [exchange(after(y1[h], (dy0[0],))) for h in both]
        outputs = move_rows(send, [start(1, h) for h in both], y_home, seqs, True, "outputs")
        dx_home = [
            exchange(after(dx0[0], (feed0,))),
            exchange(after(dx0[1], (rest1,))),
        ]
        input_grad = move_rows(
            send, [start(0, h) for h in both], dx_home, seqs, True, "input_grad"
        )
        tall, deep = width // groups, hidden // groups
        grad = lambda *dims: jax.ShapeDtypeStruct((BLOCKS, 1) + dims, F32)
        feed_shapes = (grad(tall, hidden), grad(deep, width))
        rest_shapes = (
            grad(tall, 3 * width),
            grad(tall, width),
            grad(15, tall),
            grad(KINDS - 2, tall, width),
            grad(KINDS, tall),
            grad(KINDS, tall),
        )
        feeds = finish_feed(1, feed1, None, None, feed_shapes)
        rests = finish_rest(1, rest1, feed1, (), rest_shapes, ())
        feeds = finish_feed(0, feed0, *feeds, feed_shapes)
        rests = finish_rest(0, rest0, feed0, rests, rest_shapes, (outputs, input_grad, feeds[0]))
        qkv, out, taps, point, gain, shift = rests
        return (outputs, input_grad, qkv, out, *feeds, taps, point, gain, shift)

    if not routed:
        return after_first(home_there, home_back, x0, first)
    return lax.cond(
        lost[0] == 0,
        lambda x0, first: after_first(straight_there, straight_back, x0, first),
        lambda x0, first: after_first(home_there, home_back, x0, first),
        x0,
        first,
    )


def solution(mesh):
    placed = (
        P(("dp", "op"), None, None),
        P(("dp", "op"), None),
        P(None, "op", None, None),
        P(None, "op", None, None),
        P(None, "op", None, None),
        P(None, "op", None, None),
        P(None, "op", None, None),
        P(None, "op", None, None, None),
        P(None, "op", None, None),
        P(None, "op", None, None),
        P(("dp", "op"), None, None),
    )
    return jax.shard_map(
        per_device,
        mesh=mesh,
        in_specs=placed,
        out_specs=(
            P(("dp", "op"), None, None),
            P(("dp", "op"), None, None),
            P(None, "op", "dp", None),
            P(None, "op", "dp", None),
            P(None, "op", "dp", None),
            P(None, "op", "dp", None),
            P(None, "op", None, "dp"),
            P(None, "op", None, "dp", None),
            P(None, "op", None, "dp"),
            P(None, "op", None, "dp"),
        ),
        check_vma=False,
    )
```

```python
import jax
import jax.numpy as jnp
from jax import lax
from jax.experimental import pallas as pl
from jax.experimental.pallas import tpu as pltpu
from jax.sharding import PartitionSpec as P

HEADS = 12
KINDS = 5
BLOCKS = 2
OWN_CAP = 3
HALVES = 2
SLOTS = KINDS * OWN_CAP
FF_PART = 768
FF_SUB = 256
LANES = 128
SMALL_ROWS = 32
BF16 = jnp.bfloat16
F32 = jnp.float32
VMEM_BYTES = 60 * 2**20


def params_of(axes):
    return pltpu.CompilerParams(
        dimension_semantics=("arbitrary",) * axes, vmem_limit_bytes=VMEM_BYTES
    )


def nn(a, b):
    return lax.dot_general(a, b, (((1,), (0,)), ((), ())), preferred_element_type=F32)


def nt(a, b):
    return lax.dot_general(a, b, (((1,), (1,)), ((), ())), preferred_element_type=F32)


def tn(a, b):
    return lax.dot_general(a, b, (((0,), (0,)), ((), ())), preferred_element_type=F32)


def colour_home(owners, seqs, home, cand, color, partner, first, tally):
    base = home * seqs

    def clear_owner(o, _):
        first[o] = -1
        return 0

    lax.fori_loop(0, BLOCKS * owners, clear_owner, 0)
    for half in range(HALVES):
        tally[half] = 0

    def pair_up(j, _):
        color[base + j] = -1
        for b in range(BLOCKS):
            o = b * owners + lax.rem(cand[(base + j) * BLOCKS + b], owners)
            other = first[o]
            partner[b * seqs + j] = other
            first[o] = j

            @pl.when(other >= 0)
            def _():
                partner[b * seqs + other] = j

        return 0

    lax.fori_loop(0, seqs, pair_up, 0)

    def give(j, shade):
        color[base + j] = shade
        tally[shade] = tally[shade] + 1

    def paint(j, _):
        @pl.when(color[base + j] < 0)
        def _():
            shade = jnp.where(tally[0] > tally[1], 1, 0).astype(jnp.int32)
            give(j, shade)
            for side in range(2):

                def more(state):
                    return state[0] >= 0

                def walk(state):
                    now, use, tone = state
                    then = partner[use * seqs + now]
                    free = jnp.logical_and(then >= 0, color[base + jnp.maximum(then, 0)] < 0)

                    @pl.when(free)
                    def _():
                        give(then, 1 - tone)

                    return (jnp.where(free, then, -1), 1 - use, 1 - tone)

                lax.while_loop(more, walk, (j, jnp.int32(side), shade))

        return 0

    lax.fori_loop(0, seqs, paint, 0)


def home_kernel(owners, seqs, cand, send, relay, tags, color, partner, first, tally):
    for b in range(BLOCKS):

        def clear_owner(o, _):
            for half in range(HALVES):
                send[(b * HALVES + half) * owners + o] = -1
                relay[(b * HALVES + half) * owners + o] = -1
                tags[o * BLOCKS * HALVES + b * HALVES + half] = KINDS
            return 0

        lax.fori_loop(0, owners, clear_owner, 0)
    colour_home(owners, seqs, 0, cand, color, partner, first, tally)

    def place(j, _):
        half = color[j]
        spots = []
        for b in range(BLOCKS):
            c = cand[j * BLOCKS + b]
            o = lax.rem(c, owners)
            spots.append(o)
            send[(b * HALVES + half) * owners + o] = j
            tags[o * BLOCKS * HALVES + b * HALVES + half] = lax.div(c, owners)
        relay[half * owners + spots[1]] = spots[0]
        relay[(HALVES + half) * owners + spots[0]] = spots[1]
        return 0

    lax.fori_loop(0, seqs, place, 0)


ROUTES = 10
TRIES = 24


def route_kernel(
    owners, seqs, cand, me_ref, out, ok, color, partner, first, tally, leave, goal, hops, spill
):
    me = me_ref[0]
    square = owners * owners

    def colour(home, _):
        colour_home(owners, seqs, home, cand, color, partner, first, tally)
        return 0

    lax.fori_loop(0, owners, colour, 0)

    def ends(q, _):
        leave[q] = lax.rem(cand[q * BLOCKS], owners)
        goal[q] = lax.rem(cand[q * BLOCKS + 1], owners)
        return 0

    lax.fori_loop(0, owners * seqs, ends, 0)

    def attempt(state):
        turn, _ = state

        def clear(n, _):
            hops[n] = -1
            return 0

        lax.fori_loop(0, 3 * square, clear, 0)

        def direct(q, spilt):
            at = color[q] * 2 * square + leave[q] * owners + goal[q]
            free = hops[at] < 0

            @pl.when(free)
            def _():
                hops[at] = q

            @pl.when(jnp.logical_not(free))
            def _():
                spill[spilt] = q

            return jnp.where(free, spilt, spilt + 1)

        spilt = lax.fori_loop(0, owners * seqs, direct, jnp.int32(0))
        begin = lax.rem(turn * 5, jnp.maximum(spilt, 1))

        def two_hops(n, lost):
            q = spill[lax.rem(begin + n, jnp.maximum(spilt, 1))]
            o, p = leave[q], goal[q]
            early = color[q] * square
            shift = o * 3 + p * 5 + (n + 1) * turn

            def look(s, found):
                i = lax.rem(shift + s, owners)
                a = early + o * owners + i
                b = early + square + i * owners + p
                good = jnp.logical_and(hops[a] < 0, hops[b] < 0)
                return jnp.where(jnp.logical_and(good, found < 0), i, found)

            i = lax.fori_loop(0, owners, look, jnp.int32(-1))

            @pl.when(i >= 0)
            def _():
                hops[early + o * owners + i] = q
                hops[early + square + i * owners + p] = q

            return jnp.where(i >= 0, lost, lost + 1)

        lost = lax.fori_loop(0, spilt, two_hops, jnp.int32(0))
        return turn + 1, lost

    def again(state):
        return jnp.logical_and(state[0] < TRIES, state[1] > 0)

    _, lost = lax.while_loop(again, attempt, (jnp.int32(0), jnp.int32(1)))
    ok[0] = lost

    def clear_out(n, _):
        out[n] = -1
        return 0

    lax.fori_loop(0, ROUTES * owners, clear_out, 0)

    def note(d, _):
        def home(q):
            return lax.div(q, seqs)

        def put(table, at, value):
            out[table * owners + at] = value

        q = hops[me * owners + d]

        @pl.when(q >= 0)
        def _():
            put(0, d, home(q))
            put(9, home(q), d)

        q1 = hops[square + me * owners + d]

        @pl.when(q1 >= 0)
        def _():
            late = color[q1] == 1
            put(1, d, jnp.where(late, owners + home(q1), leave[q1]))

            @pl.when(late)
            def _():
                put(8, home(q1), owners + d)

        q2 = hops[2 * square + me * owners + d]

        @pl.when(q2 >= 0)
        def _():
            mine = leave[q2] == me
            put(2, d, jnp.where(mine, home(q2), owners + leave[q2]))

            @pl.when(mine)
            def _():
                put(8, home(q2), d)

        r = hops[d * owners + me]

        @pl.when(r >= 0)
        def _():
            there = goal[r] == me
            put(7, d, jnp.where(there, home(r), owners + goal[r]))

            @pl.when(there)
            def _():
                put(3, home(r), d)

        r1 = hops[square + d * owners + me]

        @pl.when(r1 >= 0)
        def _():
            late = color[r1] == 1
            put(6, d, jnp.where(late, owners + goal[r1], home(r1)))

            @pl.when(jnp.logical_not(late))
            def _():
                put(3, home(r1), owners + d)

        r2 = hops[2 * square + d * owners + me]

        @pl.when(r2 >= 0)
        def _():
            put(4, home(r2), d)
            put(5, d, home(r2))

        return 0

    lax.fori_loop(0, owners, note, 0)


SMEM_SPEC = pl.BlockSpec(memory_space=pltpu.SMEM)
ANY_SPEC = pl.BlockSpec(memory_space=pl.ANY)


def int_shape(n):
    return jax.ShapeDtypeStruct((n,), jnp.int32)


def home_tables(cand, owners, seqs):
    def kernel(*refs):
        home_kernel(owners, seqs, *refs)

    size = BLOCKS * HALVES * owners
    return pl.pallas_call(
        kernel,
        in_specs=[SMEM_SPEC],
        out_specs=[SMEM_SPEC] * 3,
        out_shape=[int_shape(size)] * 3,
        scratch_shapes=[
            pltpu.SMEM((seqs,), jnp.int32),
            pltpu.SMEM((BLOCKS * seqs,), jnp.int32),
            pltpu.SMEM((BLOCKS * owners,), jnp.int32),
            pltpu.SMEM((HALVES,), jnp.int32),
        ],
        name="home_tables",
    )(cand)


def owner_kernel(owners, tags, rows, counts):
    for b in range(BLOCKS):
        for half in range(HALVES):
            part = b * HALVES + half
            for k in range(8):
                counts[part * 8 + k] = 0

            def arrive(h, free):
                k = tags[h * BLOCKS * HALVES + part]
                there = k < KINDS

                @pl.when(there)
                def _():
                    n = jnp.minimum(counts[part * 8 + k], OWN_CAP - 1)
                    rows[part * SLOTS + k * OWN_CAP + n] = h
                    counts[part * 8 + k] = n + 1

                return jnp.where(there, free, h)

            free = lax.fori_loop(0, owners, arrive, jnp.int32(0))

            def spare(k, otherwise):
                return jnp.where(
                    counts[part * 8 + k] > 0, rows[part * SLOTS + k * OWN_CAP], otherwise
                )

            conv_spare = free
            for k in reversed(range(1, KINDS - 1)):
                conv_spare = spare(k, conv_spare)
            attn_spare = spare(0, conv_spare)
            feed_spare = spare(KINDS - 1, attn_spare)
            last = conv_spare
            for k, start in ((1, None), (2, None), (3, None), (0, attn_spare), (KINDS - 1, feed_spare)):
                last = last if start is None else start
                for i in range(OWN_CAP):
                    at = part * SLOTS + k * OWN_CAP + i
                    last = jnp.where(i < counts[part * 8 + k], rows[at], last)
                    rows[at] = last


def owner_tables(tags, owners):
    def kernel(*refs):
        owner_kernel(owners, *refs)

    return pl.pallas_call(
        kernel,
        in_specs=[SMEM_SPEC],
        out_specs=[SMEM_SPEC] * 2,
        out_shape=[int_shape(BLOCKS * HALVES * SLOTS), int_shape(BLOCKS * HALVES * 8)],
        name="owner_tables",
    )(tags)


def route_tables(cand, me, owners, seqs):
    def kernel(*refs):
        route_kernel(owners, seqs, *refs)

    smem = lambda n: pltpu.SMEM((n,), jnp.int32)
    return pl.pallas_call(
        kernel,
        in_specs=[SMEM_SPEC] * 2,
        out_specs=[SMEM_SPEC] * 2,
        out_shape=[int_shape(ROUTES * owners), int_shape(1)],
        scratch_shapes=[
            smem(owners * seqs),
            smem(BLOCKS * seqs),
            smem(BLOCKS * owners),
            smem(HALVES),
            smem(owners * seqs),
            smem(owners * seqs),
            smem(3 * owners * owners),
            smem(owners * seqs),
        ],
        name="route_tables",
    )(cand, me)


def bring_rows(table, start, sources, name):
    count, length, width = sources[0].shape

    def kernel(table_ref, *refs):
        ins = refs[: len(sources)]
        out_ref, buf, sem_in, sem_out = refs[-4:]

        def loads(n):
            e = table_ref[start + n]
            last = count * (len(sources) - 1)
            for which, source in enumerate(ins):
                low = count * which
                here = e >= low
                if low < last:
                    here = jnp.logical_and(here, e < low + count)
                row = jnp.clip(e - low, 0, count - 1)
                yield here, pltpu.make_async_copy(source.at[row], buf.at[n], sem_in.at[n])

        def store(n):
            return pltpu.make_async_copy(buf.at[n], out_ref.at[n], sem_out.at[n])

        for n in range(count):
            for here, copy in loads(n):

                @pl.when(here)
                def _():
                    copy.start()

        for n in range(count):

            @pl.when(table_ref[start + n] >= 0)
            def _():
                pltpu.make_async_copy(ins[0].at[0], buf.at[n], sem_in.at[n]).wait()
                store(n).start()

        for n in range(count):

            @pl.when(table_ref[start + n] >= 0)
            def _():
                store(n).wait()

    return pl.pallas_call(
        kernel,
        grid_spec=pltpu.PrefetchScalarGridSpec(
            num_scalar_prefetch=1,
            grid=(1,),
            in_specs=[ANY_SPEC] * len(sources),
            out_specs=ANY_SPEC,
            scratch_shapes=[
                pltpu.VMEM((count, length, width), BF16),
                pltpu.SemaphoreType.DMA((count,)),
                pltpu.SemaphoreType.DMA((count,)),
            ],
        ),
        out_shape=jax.ShapeDtypeStruct((count, length, width), BF16),
        compiler_params=params_of(1),
        cost_estimate=pl.CostEstimate(
            flops=0, transcendentals=0, bytes_accessed=4 * count * length * width
        ),
        name=name,
    )(table, *sources)


def move_rows(table, starts, sources, count, scatter, name, wait_for=()):
    length, width = sources[0].shape[1:]
    each = table.shape[0] // (BLOCKS * HALVES)
    total = each * len(sources)

    def kernel(table_ref, *refs):
        ins = refs[: len(sources)]
        out_ref, buf, sem_in, sem_out = refs[-4:]

        def load(part, s):
            idx = table_ref[starts[part] + s]
            at = s if scatter else idx
            to = part * each + s
            return pltpu.make_async_copy(ins[part].at[at], buf.at[to], sem_in.at[to])

        def store(part, s):
            idx = table_ref[starts[part] + s]
            at = part * each + s
            to = idx if scatter else at
            return pltpu.make_async_copy(buf.at[at], out_ref.at[to], sem_out.at[at])

        todo = [(part, s) for part in range(len(sources)) for s in range(each)]
        for part, s in todo:

            @pl.when(table_ref[starts[part] + s] >= 0)
            def _():
                load(part, s).start()

        for part, s in todo:

            @pl.when(table_ref[starts[part] + s] >= 0)
            def _():
                load(part, s).wait()
                store(part, s).start()

        for part, s in todo:

            @pl.when(table_ref[starts[part] + s] >= 0)
            def _():
                store(part, s).wait()

    return pl.pallas_call(
        kernel,
        grid_spec=pltpu.PrefetchScalarGridSpec(
            num_scalar_prefetch=1,
            grid=(1,),
            in_specs=[ANY_SPEC] * (len(sources) + len(wait_for)),
            out_specs=ANY_SPEC,
            scratch_shapes=[
                pltpu.VMEM((total, length, width), BF16),
                pltpu.SemaphoreType.DMA((total,)),
                pltpu.SemaphoreType.DMA((total,)),
            ],
        ),
        out_shape=jax.ShapeDtypeStruct((count, length, width), BF16),
        compiler_params=params_of(1),
        cost_estimate=pl.CostEstimate(
            flops=0, transcendentals=0, bytes_accessed=4 * total * length * width
        ),
        name=name,
    )(table, *sources, *wait_for)


def after(value, earlier):
    def kernel(*refs):
        return

    return pl.pallas_call(
        kernel,
        in_specs=[ANY_SPEC] * (1 + len(earlier)),
        out_specs=ANY_SPEC,
        out_shape=jax.ShapeDtypeStruct(value.shape, value.dtype),
        input_output_aliases={0: 0},
        name="after",
    )(value, *earlier)


def norm_forward(summed, gain_row, shift_row):
    center = summed - jnp.mean(summed, axis=-1, keepdims=True)
    spread = jnp.mean(center * center, axis=-1, keepdims=True)
    scale = lax.rsqrt(spread + 1e-05)
    normed = center * scale
    return normed, normed * gain_row + shift_row, scale


def finish_forward(x, branch, gain_row, shift_row, y_ref, zn_ref, rstd_ref):
    normed, result, scale = norm_forward(x.astype(F32) + branch, gain_row, shift_row)
    y_ref[0] = result.astype(BF16)
    zn_ref[0] = normed.astype(BF16)
    rstd_ref[0] = jnp.broadcast_to(scale, rstd_ref.shape[1:])


def norm_backward(dy, zn_ref, rstd_ref, gain_row):
    dy = dy.astype(F32)
    normed = zn_ref[0].astype(F32)
    scale = rstd_ref[0][:, :1]
    scaled = dy * gain_row
    first = jnp.mean(scaled, axis=-1, keepdims=True)
    second = jnp.mean(scaled * normed, axis=-1, keepdims=True)
    gain_grad = jnp.sum(dy * normed, axis=0, keepdims=True)
    shift_grad = jnp.sum(dy, axis=0, keepdims=True)
    return (scaled - first - normed * second) * scale, gain_grad, shift_grad


def head_masks(length):
    lane = lax.broadcasted_iota(jnp.int32, (length, LANES), 1)
    low = lane < LANES // 2
    return low


def attention_forward(part, tables, x, weights, norms, y_in):
    rows, counts = tables
    b = part // HALVES
    attn_qkv, attn_out = weights
    gains, shifts = norms
    slots, length, width = x.shape
    score_scale = (width // HEADS) ** (-0.5)
    base = part * SLOTS

    def kernel(rows_ref, counts_ref, x_ref, qkv_w, out_w, gain, shift, *rest):
        y_ref, qkv_ref, o_ref, zn_ref, rstd_ref = rest[-5:]
        i = pl.program_id(0)

        @pl.when(i < counts_ref[part * 8])
        def _():
            xv = x_ref[0]
            for third in range(3):
                cols = slice(third * width, (third + 1) * width)
                qkv_ref[0, :, cols] = nn(xv, qkv_w[:, cols]).astype(BF16)
            low = head_masks(length)
            zero = jnp.zeros((), BF16)
            for pair in range(width // LANES):
                at = pair * LANES
                q2 = qkv_ref[0, :, at : at + LANES] * jnp.asarray(score_scale, BF16)
                k2 = qkv_ref[0, :, width + at : width + at + LANES]
                v2 = qkv_ref[0, :, 2 * width + at : 2 * width + at + LANES]
                mixed = []
                for half in range(2):
                    qm = jnp.where(low if half == 0 else ~low, q2, zero)
                    s = nt(qm, k2)
                    e = jnp.exp(s - jnp.max(s, axis=-1, keepdims=True))
                    total = jnp.sum(e, axis=-1, keepdims=True)
                    mixed.append(nn(e.astype(BF16), v2) / total)
                o_ref[0, :, at : at + LANES] = jnp.where(low, mixed[0], mixed[1]).astype(BF16)
            branch = nn(o_ref[0], out_w[...])
            finish_forward(
                xv, branch, gain[0:1, :], shift[0:1, :], y_ref, zn_ref, rstd_ref
            )

    def at_row(i, r, c):
        return (r[base + i], 0, 0)

    def at_step(i, r, c):
        return (jnp.maximum(jnp.minimum(i, c[part * 8] - 1), 0), 0, 0)

    seq = (1, length, width)
    in_specs = [
        pl.BlockSpec(seq, at_row),
        pl.BlockSpec(
            (None, None, width, 3 * width), lambda i, r, c: (b, 0, 0, 0), pipeline_mode=pl.Buffered(1)
        ),
        pl.BlockSpec(
            (None, None, width, width), lambda i, r, c: (b, 0, 0, 0), pipeline_mode=pl.Buffered(1)
        ),
        pl.BlockSpec((8, width), lambda i, r, c: (0, 0)),
        pl.BlockSpec((8, width), lambda i, r, c: (0, 0)),
    ]
    args = [rows, counts, x, attn_qkv, attn_out, gains, shifts]
    alias = {}
    if y_in is not None:
        in_specs.append(pl.BlockSpec(memory_space=pl.ANY))
        alias = {len(args): 0}
        args.append(y_in)
    flops = OWN_CAP * length * width * (8 * width + 4 * length)
    return pl.pallas_call(
        kernel,
        grid_spec=pltpu.PrefetchScalarGridSpec(
            num_scalar_prefetch=2,
            grid=(OWN_CAP,),
            in_specs=in_specs,
            out_specs=[
                pl.BlockSpec(seq, at_row),
                pl.BlockSpec((1, length, 3 * width), at_step),
                pl.BlockSpec(seq, at_step),
                pl.BlockSpec(seq, at_step),
                pl.BlockSpec((1, length, LANES), at_step),
            ],
        ),
        out_shape=[
            jax.ShapeDtypeStruct((slots, length, width), BF16),
            jax.ShapeDtypeStruct((OWN_CAP, length, 3 * width), BF16),
            jax.ShapeDtypeStruct((OWN_CAP, length, width), BF16),
            jax.ShapeDtypeStruct((OWN_CAP, length, width), BF16),
            jax.ShapeDtypeStruct((OWN_CAP, length, LANES), F32),
        ],
        input_output_aliases=alias,
        compiler_params=params_of(1),
        cost_estimate=pl.CostEstimate(
            flops=2 * flops, transcendentals=OWN_CAP * HEADS * length * length, bytes_accessed=30 * 2**20
        ),
        name="attention_forward",
    )(*args)


def attention_backward(part, tables, x, dy, kept, weights, gains, dx_in, sums, packed):
    rows, counts = tables
    b = part // HALVES
    attn_qkv, attn_out = weights
    qkv, o, zn, rstd = kept
    slots, length, width = x.shape
    score_scale = (width // HEADS) ** (-0.5)
    base = part * SLOTS
    first = sums is None
    n_out = 4 if first else 3

    def kernel(rows_ref, counts_ref, x_ref, dy_ref, qkv_ref, o_ref, zn_ref, rstd_ref, qkv_w, out_w, gain, *rest):
        ins = rest[: len(rest) - n_out - 7]
        outs = rest[len(ins) : len(ins) + n_out]
        acc_qkv, acc_out, do_scr, dqkv_scr, dh_scr, dz_scr, sems = rest[-7:]
        dx_ref, small_ref = outs[0], outs[1]
        i = pl.program_id(0)
        here = i < counts_ref[part * 8]

        def copies():
            if first:
                pairs = ((acc_qkv, outs[2]), (acc_out, outs[3]))
            else:
                pairs = ((ins[0], acc_qkv), (ins[1], acc_out))
            return [
                pltpu.make_async_copy(source, target, sems.at[n])
                for n, (source, target) in enumerate(pairs)
            ]

        @pl.when(i == 0)
        def _():
            small_ref[...] = jnp.zeros_like(small_ref)
            if first:
                acc_qkv[...] = jnp.zeros_like(acc_qkv)
                acc_out[...] = jnp.zeros_like(acc_out)
            else:
                for copy in copies():
                    copy.start()

        @pl.when(here)
        def _():
            dz, gain_grad, shift_grad = norm_backward(dy_ref[0], zn_ref, rstd_ref, gain[0:1, :])
            small_ref[0:1, :] += gain_grad
            small_ref[1:2, :] += shift_grad
            dz_scr[...] = dz
            dh = dz.astype(BF16)
            dh_scr[...] = dh
            do_scr[...] = nt(dh, out_w[...]).astype(BF16)
            low = head_masks(length)
            zero = jnp.zeros((), BF16)
            for pair in range(width // LANES):
                at = pair * LANES
                q2 = qkv_ref[0, :, at : at + LANES] * jnp.asarray(score_scale, BF16)
                k2 = qkv_ref[0, :, width + at : width + at + LANES]
                v2 = qkv_ref[0, :, 2 * width + at : 2 * width + at + LANES]
                do2 = do_scr[:, at : at + LANES]
                dqs, dks, dvs = [], [], []
                for half in range(2):
                    mask = low if half == 0 else ~low
                    st = nt(jnp.where(mask, k2, zero), q2)
                    e = jnp.exp(st - jnp.max(st, axis=0, keepdims=True))
                    p = e * (1.0 / jnp.sum(e, axis=0, keepdims=True))
                    dvs.append(nn(p.astype(BF16), do2))
                    t = p * nt(jnp.where(mask, v2, zero), do2)
                    ds = (t - p * jnp.sum(t, axis=0, keepdims=True)).astype(BF16)
                    dks.append(nn(ds, q2))
                    dqs.append(tn(ds, k2))
                dqkv_scr[:, at : at + LANES] = (jnp.where(low, dqs[0], dqs[1]) * score_scale).astype(BF16)
                dqkv_scr[:, width + at : width + at + LANES] = jnp.where(low, dks[0], dks[1]).astype(BF16)
                dqkv_scr[:, 2 * width + at : 2 * width + at + LANES] = jnp.where(low, dvs[0], dvs[1]).astype(BF16)
            total = dz_scr[...]
            for third in range(3):
                cols = slice(third * width, (third + 1) * width)
                total = total + nt(dqkv_scr[:, cols], qkv_w[:, cols])
            dx_ref[0] = total.astype(BF16)

        if not first:

            @pl.when(i == 0)
            def _():
                for copy in copies():
                    copy.wait()

        @pl.when(here)
        def _():
            xv = x_ref[0]
            for third in range(3):
                cols = slice(third * width, (third + 1) * width)
                acc_qkv[:, cols] += tn(xv, dqkv_scr[:, cols])
            acc_out[...] += tn(o_ref[0], dh_scr[...])

        @pl.when(i == OWN_CAP - 1)
        def _():
            if first:
                for copy in copies():
                    copy.start()
                for copy in copies():
                    copy.wait()
            else:
                packed_ref = outs[2]
                groups, tall = packed_ref.shape[0], packed_ref.shape[1] // 4
                for third in range(3):
                    piece = acc_qkv[:, third * width : (third + 1) * width].astype(BF16)
                    packed_ref[:, third * tall : (third + 1) * tall, :] = piece.reshape(
                        groups, tall, width
                    )
                packed_ref[:, 3 * tall : 4 * tall, :] = (
                    acc_out[...].astype(BF16).reshape(groups, tall, width)
                )

    def at_row(i, r, c):
        return (r[base + i], 0, 0)

    def at_step(i, r, c):
        return (jnp.maximum(jnp.minimum(i, c[part * 8] - 1), 0), 0, 0)

    def whole(i, r, c):
        return (0, 0)

    seq = (1, length, width)
    in_specs = [
        pl.BlockSpec(seq, at_row),
        pl.BlockSpec(seq, at_row),
        pl.BlockSpec((1, length, 3 * width), at_step),
        pl.BlockSpec(seq, at_step),
        pl.BlockSpec(seq, at_step),
        pl.BlockSpec((1, length, LANES), at_step),
        pl.BlockSpec(
            (None, None, width, 3 * width), lambda i, r, c: (b, 0, 0, 0), pipeline_mode=pl.Buffered(1)
        ),
        pl.BlockSpec(
            (None, None, width, width), lambda i, r, c: (b, 0, 0, 0), pipeline_mode=pl.Buffered(1)
        ),
        pl.BlockSpec((8, width), whole),
    ]
    args = [rows, counts, x, dy, qkv, o, zn, rstd, attn_qkv, attn_out, gains]
    out_specs = [pl.BlockSpec(seq, at_row), pl.BlockSpec((8, width), whole)]
    out_shape = [
        jax.ShapeDtypeStruct((slots, length, width), BF16),
        jax.ShapeDtypeStruct((8, width), F32),
    ]
    if first:
        out_specs += [ANY_SPEC, ANY_SPEC]
        out_shape += [
            jax.ShapeDtypeStruct((width, 3 * width), F32),
            jax.ShapeDtypeStruct((width, width), F32),
        ]
    else:
        groups, total_rows = packed
        out_specs.append(
            pl.BlockSpec((groups, 4 * width // groups, width), lambda i, r, c: (0, 0, 0))
        )
        out_shape.append(jax.ShapeDtypeStruct((groups, total_rows, width), BF16))
        in_specs += [ANY_SPEC, ANY_SPEC]
        args += list(sums)
    alias = {}
    if dx_in is not None:
        in_specs.append(ANY_SPEC)
        alias = {len(args): 0}
        args.append(dx_in)
    flops = 2 * OWN_CAP * length * width * (8 * width + 4 * length)
    return pl.pallas_call(
        kernel,
        grid_spec=pltpu.PrefetchScalarGridSpec(
            num_scalar_prefetch=2,
            grid=(OWN_CAP,),
            in_specs=in_specs,
            out_specs=out_specs,
            scratch_shapes=[
                pltpu.VMEM((width, 3 * width), F32),
                pltpu.VMEM((width, width), F32),
                pltpu.VMEM((length, width), BF16),
                pltpu.VMEM((length, 3 * width), BF16),
                pltpu.VMEM((length, width), BF16),
                pltpu.VMEM((length, width), F32),
                pltpu.SemaphoreType.DMA((2,)),
            ],
        ),
        out_shape=out_shape,
        input_output_aliases=alias,
        compiler_params=params_of(1),
        cost_estimate=pl.CostEstimate(
            flops=flops, transcendentals=OWN_CAP * HEADS * length * length // 2, bytes_accessed=40 * 2**20
        ),
        name="attention_backward",
    )(*args)


def feed_forward(part, tables, x, weights, norms, earlier):
    rows, counts = tables
    b = part // HALVES
    ffn_up, ffn_down = weights
    gains, shifts = norms
    slots, length, width = x.shape
    hidden = ffn_up.shape[-1]
    parts = hidden // FF_PART
    kind = KINDS - 1
    base = part * SLOTS + kind * OWN_CAP

    def kernel(rows_ref, counts_ref, x_ref, up, down, gain, shift, *rest):
        y_ref, g_ref, slope_ref, zn_ref, rstd_ref, x_scr, h_scr = rest[-7:]
        c, i = pl.program_id(0), pl.program_id(1)

        @pl.when(i < counts_ref[part * 8 + kind])
        def _():
            @pl.when(c == 0)
            def _():
                x_scr[i] = x_ref[0]

            xv = x_scr[i]
            for sub in range(FF_PART // FF_SUB):
                cols = slice(sub * FF_SUB, (sub + 1) * FF_SUB)
                a = nn(xv, up[:, cols])
                phi = 0.5 + 0.5 * lax.erf(a * (0.5**0.5))
                slope = phi + a * (jnp.exp(a * a * -0.5) * 0.3989422804014327)
                g = (a * phi).astype(BF16)
                g_ref[0, :, cols] = g
                slope_ref[0, :, cols] = slope.astype(BF16)
            branch = nn(g_ref[0], down[...])

            @pl.when(c == 0)
            def _():
                h_scr[i] = branch

            @pl.when(jnp.logical_and(c > 0, c < parts - 1))
            def _():
                h_scr[i] += branch

            @pl.when(c == parts - 1)
            def _():
                finish_forward(
                    xv,
                    h_scr[i] + branch,
                    gain[kind : kind + 1, :],
                    shift[kind : kind + 1, :],
                    y_ref,
                    zn_ref,
                    rstd_ref,
                )

    def in_row(c, i, r, n):
        return (r[base + jnp.where(c == 0, i, OWN_CAP - 1)], 0, 0)

    def out_row(c, i, r, n):
        return (r[base + jnp.where(c == parts - 1, i, 0)], 0, 0)

    def place(i, n):
        at = jnp.maximum(jnp.minimum(i, n[part * 8 + kind] - 1), 0)
        return at if part == b * HALVES else at + n[b * HALVES * 8 + kind]

    def out_step(c, i, r, n):
        return (place(jnp.where(c == parts - 1, i, 0), n), 0, 0)

    def part_step(c, i, r, n):
        return (place(i, n), 0, c)

    seq = (1, length, width)
    in_specs = [
        pl.BlockSpec(seq, in_row),
        pl.BlockSpec((None, None, width, FF_PART), lambda c, i, r, n: (b, 0, 0, c)),
        pl.BlockSpec((None, None, FF_PART, width), lambda c, i, r, n: (b, 0, c, 0)),
        pl.BlockSpec((8, width), lambda c, i, r, n: (0, 0)),
        pl.BlockSpec((8, width), lambda c, i, r, n: (0, 0)),
    ]
    args = [rows, counts, x, ffn_up, ffn_down, gains, shifts]
    alias = {}
    for n, kept in enumerate(earlier or ()):
        in_specs.append(ANY_SPEC)
        alias[len(args)] = 1 + n
        args.append(kept)
    return pl.pallas_call(
        kernel,
        grid_spec=pltpu.PrefetchScalarGridSpec(
            num_scalar_prefetch=2,
            grid=(parts, OWN_CAP),
            in_specs=in_specs,
            out_specs=[
                pl.BlockSpec(seq, out_row),
                pl.BlockSpec((1, length, FF_PART), part_step),
                pl.BlockSpec((1, length, FF_PART), part_step),
                pl.BlockSpec(seq, out_step),
                pl.BlockSpec((1, length, LANES), out_step),
            ],
            scratch_shapes=[
                pltpu.VMEM((OWN_CAP, length, width), BF16),
                pltpu.VMEM((OWN_CAP, length, width), F32),
            ],
        ),
        out_shape=[
            jax.ShapeDtypeStruct((slots, length, width), BF16),
            jax.ShapeDtypeStruct((OWN_CAP + 1, length, hidden), BF16),
            jax.ShapeDtypeStruct((OWN_CAP + 1, length, hidden), BF16),
            jax.ShapeDtypeStruct((OWN_CAP + 1, length, width), BF16),
            jax.ShapeDtypeStruct((OWN_CAP + 1, length, LANES), F32),
        ],
        input_output_aliases=alias,
        compiler_params=params_of(2),
        cost_estimate=pl.CostEstimate(
            flops=4 * OWN_CAP * length * width * hidden,
            transcendentals=2 * OWN_CAP * length * hidden,
            bytes_accessed=40 * 2**20,
        ),
        name="feed_forward",
    )(*args)


def feed_backward(b, tables, x, dy, kept, weights, gains, dx_lead, lead, groups, wait_for):
    rows, counts = tables
    ffn_up, ffn_down = weights
    g, slope, zn, rstd = kept
    slots, length, width = x[0].shape
    hidden = ffn_up.shape[-1]
    parts = hidden // FF_PART
    kind = KINDS - 1
    bases = [(b * HALVES + half) * SLOTS + kind * OWN_CAP for half in range(HALVES)]
    tall = width // groups
    deep = hidden // groups
    shares = FF_PART // deep

    def present(n, half):
        return n[(b * HALVES + half) * 8 + kind]

    def kernel(
        rows_ref,
        counts_ref,
        x_ref0,
        x_ref1,
        dy_ref0,
        dy_ref1,
        g_ref,
        slope_ref,
        zn_ref,
        rstd_ref,
        up,
        down,
        gain,
        *rest,
    ):
        (
        small_ref,
        dx_ref0,
        dx_ref1,
        packed_ref,
        x_scr,
        dh_scr,
        dx_scr,
        da_scr,
        acc_up,
        acc_down,
        low_up,
        low_down,
        low_dx,
        sems,
        dx_sem,
        ) = rest[-15:]
        c, i = pl.program_id(0), pl.program_id(1)
        n0 = present(counts_ref, 0)
        total_n = n0 + present(counts_ref, 1)
        in_first = i < n0

        @pl.when(jnp.logical_and(c == 0, i == 0))
        def _():
            small_ref[...] = jnp.zeros_like(small_ref)

        @pl.when(i == 0)
        def _():
            acc_up[...] = jnp.zeros_like(acc_up)
            acc_down[...] = jnp.zeros_like(acc_down)

        @pl.when(i < total_n)
        def _():
            @pl.when(c == 0)
            def _():
                dz, gain_grad, shift_grad = norm_backward(
                    jnp.where(in_first, dy_ref0[0], dy_ref1[0]),
                    zn_ref,
                    rstd_ref,
                    gain[kind : kind + 1, :],
                )
                small_ref[0:1, :] += gain_grad
                small_ref[1:2, :] += shift_grad
                x_scr[i] = jnp.where(in_first, x_ref0[0], x_ref1[0])
                dh_scr[i] = dz.astype(BF16)
                dx_scr[i] = dz

            dh = dh_scr[i]
            for sub in range(FF_PART // FF_SUB):
                cols = slice(sub * FF_SUB, (sub + 1) * FF_SUB)
                dg = nt(dh, down[cols, :])
                da_scr[:, cols] = (dg * slope_ref[0, :, cols].astype(F32)).astype(BF16)
            acc_down[...] += tn(g_ref[0], dh)
            acc_up[...] += tn(x_scr[i], da_scr[...])
            total = dx_scr[i] + nt(da_scr[...], up[...])

            @pl.when(c < parts - 1)
            def _():
                dx_scr[i] = total

            @pl.when(c == parts - 1)
            def _():
                low_dx[...] = total.astype(BF16)
                for half, (inside, dx_ref) in enumerate(
                    ((in_first, dx_ref0), (jnp.logical_not(in_first), dx_ref1))
                ):

                    @pl.when(inside)
                    def _():
                        row = rows_ref[bases[half] + jnp.where(in_first, i, jnp.maximum(i - n0, 0))]
                        copy = pltpu.make_async_copy(low_dx, dx_ref.at[row], dx_sem)
                        copy.start()
                        copy.wait()

        def copies():
            pairs = [
                (low_up.at[pl.ds(z * tall, tall)], packed_ref.at[z, pl.ds(c * tall, tall)])
                for z in range(groups)
            ]
            pairs += [
                (
                    low_down.at[pl.ds(m * deep, deep)],
                    packed_ref.at[c * shares + m, pl.ds(parts * tall, deep)],
                )
                for m in range(shares)
            ]
            return [
                pltpu.make_async_copy(source, target, sems.at[n])
                for n, (source, target) in enumerate(pairs)
            ]

        @pl.when(i == OWN_CAP - 1)
        def _():
            @pl.when(c > 0)
            def _():
                for copy in copies():
                    copy.wait()

            low_up[...] = acc_up[...].astype(BF16)
            low_down[...] = acc_down[...].astype(BF16)
            for copy in copies():
                copy.start()

            @pl.when(c == parts - 1)
            def _():
                for copy in copies():
                    copy.wait()

    def first_row(c, i, r, n):
        return (r[bases[0] + jnp.where(c == 0, i, OWN_CAP - 1)], 0, 0)

    def second_row(c, i, r, n):
        at = jnp.where(c == 0, i, OWN_CAP - 1) - present(n, 0)
        return (r[bases[1] + jnp.maximum(at, 0)], 0, 0)

    def last(n):
        return present(n, 0) + present(n, 1) - 1

    def in_step(c, i, r, n):
        return (jnp.where(c == 0, jnp.minimum(i, last(n)), last(n)), 0, 0)

    def part_step(c, i, r, n):
        return (jnp.minimum(i, last(n)), 0, c)

    seq = (1, length, width)
    in_specs = [
        pl.BlockSpec(seq, first_row),
        pl.BlockSpec(seq, second_row),
        pl.BlockSpec(seq, first_row),
        pl.BlockSpec(seq, second_row),
        pl.BlockSpec((1, length, FF_PART), part_step),
        pl.BlockSpec((1, length, FF_PART), part_step),
        pl.BlockSpec(seq, in_step),
        pl.BlockSpec((1, length, LANES), in_step),
        pl.BlockSpec((None, None, width, FF_PART), lambda c, i, r, n: (b, 0, 0, c)),
        pl.BlockSpec((None, None, FF_PART, width), lambda c, i, r, n: (b, 0, c, 0)),
        pl.BlockSpec((8, width), lambda c, i, r, n: (0, 0)),
        ANY_SPEC,
    ] + [ANY_SPEC] * len(wait_for)
    args = [rows, counts, *x, *dy, g, slope, zn, rstd, ffn_up, ffn_down, gains, dx_lead]
    alias = {len(args) - 1: 1 + lead}
    args += wait_for
    return pl.pallas_call(
        kernel,
        grid_spec=pltpu.PrefetchScalarGridSpec(
            num_scalar_prefetch=2,
            grid=(parts, OWN_CAP),
            in_specs=in_specs,
            out_specs=[
                pl.BlockSpec((8, width), lambda c, i, r, n: (0, 0)),
                ANY_SPEC,
                ANY_SPEC,
                ANY_SPEC,
            ],
            scratch_shapes=[
                pltpu.VMEM((OWN_CAP, length, width), BF16),
                pltpu.VMEM((OWN_CAP, length, width), BF16),
                pltpu.VMEM((OWN_CAP, length, width), F32),
                pltpu.VMEM((length, FF_PART), BF16),
                pltpu.VMEM((width, FF_PART), F32),
                pltpu.VMEM((FF_PART, width), F32),
                pltpu.VMEM((width, FF_PART), BF16),
                pltpu.VMEM((FF_PART, width), BF16),
                pltpu.VMEM((length, width), BF16),
                pltpu.SemaphoreType.DMA((groups + shares,)),
                pltpu.SemaphoreType.DMA,
            ],
        ),
        out_shape=[
            jax.ShapeDtypeStruct((8, width), F32),
            jax.ShapeDtypeStruct((slots, length, width), BF16),
            jax.ShapeDtypeStruct((slots, length, width), BF16),
            jax.ShapeDtypeStruct((groups, parts * tall + deep, width), BF16),
        ],
        input_output_aliases=alias,
        compiler_params=params_of(2),
        cost_estimate=pl.CostEstimate(
            flops=7 * OWN_CAP * length * width * hidden,
            transcendentals=0,
            bytes_accessed=50 * 2**20,
        ),
        name="feed_backward",
    )(*args)


PAD = 8
ROW_TILE = 128
COL_TILE = 256


def fill_padded(padded, values):
    length = values.shape[0]
    edge = jnp.zeros((PAD, values.shape[1]), F32)
    padded[0:PAD, :] = edge
    padded[PAD + length : PAD + length + PAD, :] = edge
    padded[PAD : PAD + length, :] = values


def conv_forward(part, tables, x, weights, norms, y_in):
    rows, counts = tables
    b = part // HALVES
    taps, conv_point = weights
    gains, shifts = norms
    slots, length, width = x.shape
    base = part * SLOTS + OWN_CAP
    steps = (KINDS - 2) * OWN_CAP

    def kernel(rows_ref, counts_ref, x_ref, point, taps_ref, gain, shift, *rest):
        y_ref, u_ref, zn_ref, rstd_ref, xpad = rest[-5:]
        step = pl.program_id(0)
        which, j = step // OWN_CAP, step % OWN_CAP
        for kind in range(1, KINDS - 1):
            taps_n = 2 * kind + 1
            first = kind * kind - 1

            @pl.when(jnp.logical_and(which == kind - 1, j < counts_ref[part * 8 + kind]))
            def _():
                fill_padded(xpad, x_ref[0].astype(F32))
                for r in range(0, length, ROW_TILE):
                    for col in range(0, width, COL_TILE):
                        cols = slice(col, col + COL_TILE)
                        mixed = None
                        for t in range(taps_n):
                            start = PAD + r + t - kind
                            term = xpad[start : start + ROW_TILE, cols] * taps_ref[first + t : first + t + 1, cols]
                            mixed = term if mixed is None else mixed + term
                        u_ref[0, r : r + ROW_TILE, cols] = mixed.astype(BF16)
                branch = nn(u_ref[0], point[...])
                finish_forward(
                    x_ref[0],
                    branch,
                    gain[kind : kind + 1, :],
                    shift[kind : kind + 1, :],
                    y_ref,
                    zn_ref,
                    rstd_ref,
                )

    def at_row(i, r, c):
        return (r[base + i], 0, 0)

    def at_step(i, r, c):
        which = i // OWN_CAP
        last = c[part * 8 + 1 + which] - 1
        return (which * OWN_CAP + jnp.maximum(jnp.minimum(i % OWN_CAP, last), 0), 0, 0)

    def whole(i, r, c):
        return (0, 0)

    seq = (1, length, width)
    in_specs = [
        pl.BlockSpec(seq, at_row),
        pl.BlockSpec((None, None, None, width, width), lambda i, r, c: (b, 0, i // OWN_CAP, 0, 0)),
        pl.BlockSpec((16, width), whole),
        pl.BlockSpec((8, width), whole),
        pl.BlockSpec((8, width), whole),
    ]
    args = [rows, counts, x, conv_point, taps, gains, shifts]
    alias = {}
    if y_in is not None:
        in_specs.append(pl.BlockSpec(memory_space=pl.ANY))
        alias = {len(args): 0}
        args.append(y_in)
    return pl.pallas_call(
        kernel,
        grid_spec=pltpu.PrefetchScalarGridSpec(
            num_scalar_prefetch=2,
            grid=(steps,),
            in_specs=in_specs,
            out_specs=[
                pl.BlockSpec(seq, at_row),
                pl.BlockSpec(seq, at_step),
                pl.BlockSpec(seq, at_step),
                pl.BlockSpec((1, length, LANES), at_step),
            ],
            scratch_shapes=[pltpu.VMEM((length + 2 * PAD, width), F32)],
        ),
        out_shape=[
            jax.ShapeDtypeStruct((slots, length, width), BF16),
            jax.ShapeDtypeStruct((steps, length, width), BF16),
            jax.ShapeDtypeStruct((steps, length, width), BF16),
            jax.ShapeDtypeStruct((steps, length, LANES), F32),
        ],
        input_output_aliases=alias,
        compiler_params=params_of(1),
        cost_estimate=pl.CostEstimate(
            flops=2 * steps * length * width * width, transcendentals=0, bytes_accessed=36 * 2**20
        ),
        name="conv_forward",
    )(*args)


def conv_backward(part, tables, x, dy, kept, weights, gains, dx_in, sums, packed):
    rows, counts = tables
    b = part // HALVES
    taps, conv_point = weights
    u, zn, rstd = kept
    slots, length, width = x.shape
    base = part * SLOTS + OWN_CAP
    steps = (KINDS - 2) * OWN_CAP
    first_half = sums is None
    groups = packed[0]

    def kernel(rows_ref, counts_ref, x_ref, dy_ref, u_ref, zn_ref, rstd_ref, point, taps_ref, gain, *rest):
        if first_half:
            dx_ref, small_ref, acc, xpad, dupad, dz_scr = rest[-6:]
        else:
            sum_ref = rest[0]
            dx_ref, small_ref, packed_ref, xpad, dupad, dz_scr, acc = rest[-7:]
        step = pl.program_id(0)
        which, j = step // OWN_CAP, step % OWN_CAP

        @pl.when(step == 0)
        def _():
            small_ref[...] = jnp.zeros_like(small_ref)

        @pl.when(j == 0)
        def _():
            acc[...] = jnp.zeros_like(acc) if first_half else sum_ref[...]

        for kind in range(1, KINDS - 1):
            taps_n = 2 * kind + 1
            first = kind * kind - 1

            @pl.when(jnp.logical_and(which == kind - 1, j < counts_ref[part * 8 + kind]))
            def _():
                dz, gain_grad, shift_grad = norm_backward(
                    dy_ref[0], zn_ref, rstd_ref, gain[kind : kind + 1, :]
                )
                small_ref[14 + kind : 15 + kind, :] += gain_grad
                small_ref[17 + kind : 18 + kind, :] += shift_grad
                dz_scr[...] = dz
                dh = dz.astype(BF16)
                acc[...] += tn(u_ref[0], dh)
                fill_padded(xpad, x_ref[0].astype(F32))
                fill_padded(dupad, nt(dh, point[...]))
                for col in range(0, width, COL_TILE):
                    cols = slice(col, col + COL_TILE)
                    sums = [None] * taps_n
                    for r in range(0, length, ROW_TILE):
                        here = dupad[PAD + r : PAD + r + ROW_TILE, cols]
                        total = dz_scr[r : r + ROW_TILE, cols]
                        for t in range(taps_n):
                            back = PAD + r - t + kind
                            total = total + dupad[back : back + ROW_TILE, cols] * taps_ref[first + t : first + t + 1, cols]
                            ahead = PAD + r + t - kind
                            part = jnp.sum(
                                xpad[ahead : ahead + ROW_TILE, cols] * here, axis=0, keepdims=True
                            )
                            sums[t] = part if sums[t] is None else sums[t] + part
                        dx_ref[0, r : r + ROW_TILE, cols] = total.astype(BF16)
                    for t in range(taps_n):
                        small_ref[first + t : first + t + 1, cols] += sums[t]

        if not first_half:

            @pl.when(j == OWN_CAP - 1)
            def _():
                packed_ref[...] = acc[...].astype(BF16).reshape(packed_ref.shape)

    def at_row(i, r, c):
        return (r[base + i], 0, 0)

    def at_step(i, r, c):
        which = i // OWN_CAP
        last = c[part * 8 + 1 + which] - 1
        return (which * OWN_CAP + jnp.maximum(jnp.minimum(i % OWN_CAP, last), 0), 0, 0)

    def whole(i, r, c):
        return (0, 0)

    seq = (1, length, width)
    in_specs = [
        pl.BlockSpec(seq, at_row),
        pl.BlockSpec(seq, at_row),
        pl.BlockSpec(seq, at_step),
        pl.BlockSpec(seq, at_step),
        pl.BlockSpec((1, length, LANES), at_step),
        pl.BlockSpec((None, None, None, width, width), lambda i, r, c: (b, 0, i // OWN_CAP, 0, 0)),
        pl.BlockSpec((16, width), whole),
        pl.BlockSpec((8, width), whole),
    ]
    args = [rows, counts, x, dy, u, zn, rstd, conv_point, taps, gains]
    sum_spec = pl.BlockSpec((None, width, width), lambda i, r, c: (i // OWN_CAP, 0, 0))
    out_specs = [pl.BlockSpec(seq, at_row), pl.BlockSpec((24, width), whole)]
    out_shape = [
        jax.ShapeDtypeStruct((slots, length, width), BF16),
        jax.ShapeDtypeStruct((24, width), F32),
    ]
    scratch = [
        pltpu.VMEM((length + 2 * PAD, width), F32),
        pltpu.VMEM((length + 2 * PAD, width), F32),
        pltpu.VMEM((length, width), F32),
    ]
    alias = {}
    if first_half:
        out_specs.append(sum_spec)
        out_shape.append(jax.ShapeDtypeStruct((KINDS - 2, width, width), F32))
    else:
        in_specs.append(sum_spec)
        args.append(sums)
        out_specs.append(
            pl.BlockSpec((groups, width // groups, width), lambda i, r, c: (0, 4 + i // OWN_CAP, 0))
        )
        out_shape.append(jax.ShapeDtypeStruct(packed[1].shape, BF16))
        in_specs.append(ANY_SPEC)
        alias = {len(args): 2}
        args.append(packed[1])
        scratch.append(pltpu.VMEM((width, width), F32))
    in_specs.append(ANY_SPEC)
    alias = {**alias, len(args): 0}
    args.append(dx_in)
    return pl.pallas_call(
        kernel,
        grid_spec=pltpu.PrefetchScalarGridSpec(
            num_scalar_prefetch=2,
            grid=(steps,),
            in_specs=in_specs,
            out_specs=out_specs,
            scratch_shapes=scratch,
        ),
        out_shape=out_shape,
        input_output_aliases=alias,
        compiler_params=params_of(1),
        cost_estimate=pl.CostEstimate(
            flops=3 * steps * length * width * width, transcendentals=0, bytes_accessed=50 * 2**20
        ),
        name="conv_backward",
    )(*args)


def owner_forward(b, half, tables, x, weights, small_weights, earlier):
    part = b * HALVES + half
    attn_qkv, attn_out, ffn_up, ffn_down, conv_point = weights
    taps, gains, shifts = small_weights
    norms = (gains, shifts)
    y, *kept_f = feed_forward(part, tables, x, (ffn_up, ffn_down), norms, earlier)
    y, *kept_a = attention_forward(part, tables, x, (attn_qkv, attn_out), norms, y)
    y, *kept_c = conv_forward(part, tables, x, (taps, conv_point), norms, y)
    return y, kept_f, kept_a, kept_c


def both_forward(b, tables, x, weights, small_weights):
    y, kept_a, kept_c, kept_f = [], [], [], None
    for half in range(HALVES):
        yh, kept_f, ka, kc = owner_forward(
            b, half, tables, x[half], weights, small_weights, kept_f
        )
        y.append(yh)
        kept_a.append(ka)
        kept_c.append(kc)
    return y, (kept_f, kept_a, kept_c)


def join_small(small_f, small_a, small_c):
    return jnp.concatenate(
        [
            small_c[:15],
            small_a[0:1],
            small_c[15:18],
            small_f[0:1],
            small_a[1:2],
            small_c[18:21],
            small_f[1:2],
        ]
    )


def owner_backward(b, tables, x, dy, kept, weights, small_weights, groups, wait_for):
    attn_qkv, attn_out, ffn_up, ffn_down, conv_point = weights
    taps, gains, shifts = small_weights
    kept_f, kept_a, kept_c = kept
    width = x[0].shape[-1]
    rest_rows = 7 * width // groups + SMALL_ROWS
    attn, conv = (attn_qkv, attn_out), (taps, conv_point)
    lead, other = 1, 0
    first, second = b * HALVES + lead, b * HALVES + other
    d_lead, small_a0, *sum_a = attention_backward(
        first, tables, x[lead], dy[lead], kept_a[lead], attn, gains, None, None, None
    )
    d_lead, small_c0, sum_c = conv_backward(
        first, tables, x[lead], dy[lead], kept_c[lead], conv, gains, d_lead, None, (groups,)
    )
    small_f, *dx, feed_pack = feed_backward(
        b, tables, x, dy, kept_f, (ffn_up, ffn_down), gains, d_lead, lead, groups, wait_for
    )
    dx[other], small_a1, rest_pack = attention_backward(
        second,
        tables,
        x[other],
        dy[other],
        kept_a[other],
        attn,
        gains,
        dx[other],
        sum_a,
        (groups, rest_rows),
    )
    dx[other], small_c1, rest_pack = conv_backward(
        second,
        tables,
        x[other],
        dy[other],
        kept_c[other],
        conv,
        gains,
        dx[other],
        sum_c,
        (groups, rest_pack),
    )
    small = join_small(small_f, small_a0 + small_a1, small_c0 + small_c1).astype(BF16)
    small = small.reshape(25, groups, width // groups)
    small = small.transpose(1, 0, 2)
    small = jnp.pad(small, ((0, 0), (0, SMALL_ROWS - 25), (0, width - width // groups)))
    rest_pack = lax.dynamic_update_slice(rest_pack, small, (0, rest_rows - SMALL_ROWS, 0))
    return dx, feed_pack, rest_pack


def finish_feed(b, feed, totals, up_out, down_out, shapes):
    parts = shapes[0].shape[-1] // FF_PART
    tall, width = shapes[0].shape[2], FF_PART

    def kernel(up_ref, down_ref, count_ref, *rest):
        up_to, down_to = rest[-2:]
        scale = 1.0 / count_ref[b : b + 1, KINDS - 1 : KINDS]
        up_to[...] = up_ref[...].astype(F32) * scale
        down_to[...] = down_ref[...].astype(F32) * scale

    old = [] if up_out is None else [up_out, down_out]
    return pl.pallas_call(
        kernel,
        grid=(parts,),
        in_specs=[
            pl.BlockSpec((tall, width), lambda c: (c, 0)),
            pl.BlockSpec((tall, width), lambda c: (parts + c, 0)),
            pl.BlockSpec((BLOCKS, 8), lambda c: (0, 0)),
        ]
        + [ANY_SPEC] * len(old),
        out_specs=[
            pl.BlockSpec((None, None, tall, width), lambda c: (b, 0, 0, c)),
            pl.BlockSpec((None, None, tall, width), lambda c: (b, 0, c, 0)),
        ],
        out_shape=list(shapes),
        input_output_aliases={3 + n: n for n in range(len(old))},
        compiler_params=params_of(1),
        cost_estimate=pl.CostEstimate(flops=0, transcendentals=0, bytes_accessed=8 * 2**20),
        name="finish_feed",
    )(feed, feed, totals, *old)


def finish_rest(b, rest, totals, old, shapes, wait_for):
    tall, width = shapes[1].shape[2:]
    small_block = 7 * tall // SMALL_ROWS

    def kernel(rest_ref, small_ref, count_ref, *refs):
        qkv_to, out_to, taps_to, point_to, gain_to, shift_to = refs[-6:]
        i = pl.program_id(0)
        scales = 1.0 / jnp.maximum(count_ref[b : b + 1, :], 1.0)
        values = rest_ref[...].astype(F32)

        @pl.when(i < 3)
        def _():
            qkv_to[...] = values * scales[:, 0:1]

        @pl.when(i == 3)
        def _():
            out_to[...] = values * scales[:, 0:1]
            small = small_ref[...].astype(F32)
            row = lax.broadcasted_iota(jnp.int32, small.shape, 0)
            which = jnp.where(row < 3, 1, jnp.where(row < 8, 2, jnp.where(row < 15, 3, 0)))
            which = jnp.where(row >= 15, row - 15, which)
            which = jnp.where(row >= 20, row - 20, which)
            scale = jnp.zeros_like(small)
            for k in range(KINDS):
                scale = jnp.where(which == k, scales[:, k : k + 1], scale)
            small = small * scale
            for r in range(15):
                taps_to[r] = small[r : r + 1, :tall]
            for r in range(KINDS):
                gain_to[r] = small[15 + r : 16 + r, :tall]
                shift_to[r] = small[20 + r : 21 + r, :tall]

        for k in range(1, KINDS - 1):

            @pl.when(i == 3 + k)
            def _():
                point_to[...] = values * scales[:, k : k + 1]

    old = list(old)
    return pl.pallas_call(
        kernel,
        grid=(7,),
        in_specs=[
            pl.BlockSpec((tall, width), lambda i: (i, 0)),
            pl.BlockSpec((SMALL_ROWS, width), lambda i: (small_block, 0)),
            pl.BlockSpec((BLOCKS, 8), lambda i: (0, 0)),
        ]
        + [ANY_SPEC] * (len(old) + len(wait_for)),
        out_specs=[
            pl.BlockSpec((None, None, tall, width), lambda i: (b, 0, 0, jnp.minimum(i, 2))),
            pl.BlockSpec((None, None, tall, width), lambda i: (b, 0, 0, 0)),
            pl.BlockSpec((None, 15, 1, tall), lambda i: (b, 0, 0, 0)),
            pl.BlockSpec(
                (None, None, None, tall, width), lambda i: (b, 0, jnp.maximum(i - 4, 0), 0, 0)
            ),
            pl.BlockSpec((None, KINDS, 1, tall), lambda i: (b, 0, 0, 0)),
            pl.BlockSpec((None, KINDS, 1, tall), lambda i: (b, 0, 0, 0)),
        ],
        out_shape=list(shapes),
        input_output_aliases={3 + n: n for n in range(len(old))},
        compiler_params=params_of(1),
        cost_estimate=pl.CostEstimate(flops=0, transcendentals=0, bytes_accessed=8 * 2**20),
        name="finish_rest",
    )(rest, rest, totals, *old, *wait_for)


def small_params(b, conv_taps, norm_gain, norm_bias):
    taps = jnp.pad(conv_taps[b, 0].astype(F32), ((0, 1), (0, 0)))
    gains = jnp.pad(norm_gain[b, 0].astype(F32), ((0, 3), (0, 0)))
    shifts = jnp.pad(norm_bias[b, 0].astype(F32), ((0, 3), (0, 0)))
    return taps, gains, shifts


def exchange(rows):
    return lax.all_to_all(rows, "op", split_axis=0, concat_axis=0, tiled=True)


def group_sum(pack):
    return lax.psum_scatter(pack, "dp", scatter_dimension=0, tiled=False)


def per_device(
    inputs,
    candidate,
    attn_qkv,
    attn_out,
    ffn_up,
    ffn_down,
    conv_taps,
    conv_point,
    norm_gain,
    norm_bias,
    cotangent,
):
    owners = lax.axis_size("op")
    groups = lax.axis_size("dp")
    seqs = inputs.shape[0]
    width = inputs.shape[-1]
    hidden = ffn_up.shape[-1]
    weights = (attn_qkv, attn_out, ffn_up, ffn_down, conv_point)
    smalls = [small_params(b, conv_taps, norm_gain, norm_bias) for b in range(BLOCKS)]
    send, relay, tags = home_tables(candidate.reshape(-1), owners, seqs)
    marks = BLOCKS * HALVES
    told = jnp.concatenate(
        [tags.reshape(owners, marks), jnp.broadcast_to(candidate.reshape(1, -1), (owners, BLOCKS * seqs))],
        axis=1,
    )
    told = exchange(told)
    everyone = told[:, marks:].reshape(-1)
    tables = owner_tables(told[:, :marks].reshape(-1), owners)
    both = range(HALVES)

    def start(b, half):
        return (b * HALVES + half) * owners

    me = lax.axis_index("op").astype(jnp.int32)[None]
    routed = owners < seqs
    if routed:
        route, lost = route_tables(everyone, me, owners, seqs)
    else:
        lost = jnp.zeros((1,), jnp.int32)
    lost = lax.psum(jnp.concatenate([lost, tables[1]]), "dp")
    totals = lost[1:].reshape(BLOCKS, HALVES, 8).sum(axis=1).astype(F32)

    x0 = [
        exchange(
            move_rows(send, [start(0, h)], [inputs], owners, False, "send_inputs", (lost,) * h if routed else ())
        )
        for h in both
    ]
    first = owner_forward(0, 0, tables, x0[0], weights, smalls[0], None)
    leaving = bring_rows(route, 0, [first[0]], "hop_x") if routed else None

    def on_the_way(table, sources, name):
        return bring_rows(route, table * owners, sources, name)

    def straight_there(y):
        hop0 = exchange(leaving)
        hop1 = exchange(on_the_way(1, [hop0, y[1]], "hop_x"))
        hop2 = exchange(on_the_way(2, [y[1], hop1], "hop_x"))
        return [on_the_way(3, [hop0, hop1], "land_x"), on_the_way(4, [hop2], "land_x")]

    def straight_back(dx):
        hop0 = exchange(on_the_way(5, [dx[1]], "hop_dx"))
        hop1 = exchange(on_the_way(6, [dx[0], hop0], "hop_dx"))
        hop2 = exchange(on_the_way(7, [dx[0], hop1], "hop_dx"))
        return [on_the_way(9, [hop2], "land_dx"), on_the_way(8, [hop0, hop1], "land_dx")]

    def home_there(y):
        return [
            exchange(move_rows(relay, [start(0, h)], [exchange(y[h])], owners, False, "relay_x"))
            for h in both
        ]

    def home_back(dx):
        return [
            exchange(move_rows(relay, [start(1, h)], [exchange(dx[h])], owners, False, "relay_dx"))
            for h in both
        ]

    def after_first(there, back, x0, first):
        y00, kept_f, ka0, kc0 = first
        y01, kept_f, ka1, kc1 = owner_forward(
            0, 1, tables, x0[1], weights, smalls[0], kept_f
        )
        kept0 = (kept_f, [ka0, ka1], [kc0, kc1])
        x1 = there([y00, y01])
        y1, kept1 = both_forward(1, tables, x1, weights, smalls[1])
        dy1 = [
            exchange(
                move_rows(
                    send,
                    [start(1, h)],
                    [cotangent],
                    owners,
                    False,
                    "send_cotangent",
                    (y1[1 - h],),
                )
            )
            for h in both
        ]
        dx1, feed1, rest1 = owner_backward(
            1, tables, x1, dy1, kept1, weights, smalls[1], groups, ()
        )
        feed1 = group_sum(feed1)
        rest1 = group_sum(rest1)
        dy0 = back(dx1)
        dx0, feed0, rest0 = owner_backward(
            0, tables, x0, dy0, kept0, weights, smalls[0], groups, (feed1,)
        )
        feed0 = group_sum(feed0)
        rest0 = group_sum(rest0)
        y_home = [exchange(after(y1[h], (dy0[0],))) for h in both]
        outputs = move_rows(send, [start(1, h) for h in both], y_home, seqs, True, "outputs")
        dx_home = [
            exchange(after(dx0[0], (feed0,))),
            exchange(after(dx0[1], (rest1,))),
        ]
        input_grad = move_rows(
            send, [start(0, h) for h in both], dx_home, seqs, True, "input_grad"
        )
        tall, deep = width // groups, hidden // groups
        grad = lambda *dims: jax.ShapeDtypeStruct((BLOCKS, 1) + dims, F32)
        feed_shapes = (grad(tall, hidden), grad(deep, width))
        rest_shapes = (
            grad(tall, 3 * width),
            grad(tall, width),
            jax.ShapeDtypeStruct((BLOCKS, 15, 1, tall), F32),
            grad(KINDS - 2, tall, width),
            jax.ShapeDtypeStruct((BLOCKS, KINDS, 1, tall), F32),
            jax.ShapeDtypeStruct((BLOCKS, KINDS, 1, tall), F32),
        )
        feeds = finish_feed(1, feed1, totals, None, None, feed_shapes)
        rests = finish_rest(1, rest1, totals, (), rest_shapes, ())
        feeds = finish_feed(0, feed0, totals, *feeds, feed_shapes)
        rests = finish_rest(0, rest0, totals, rests, rest_shapes, (outputs, input_grad, feeds[0]))
        qkv, out, taps, point, gain, shift = rests
        taps, gain, shift = (rows.transpose(0, 2, 1, 3) for rows in (taps, gain, shift))
        return (outputs, input_grad, qkv, out, *feeds, taps, point, gain, shift)

    if not routed:
        return after_first(home_there, home_back, x0, first)
    return lax.cond(
        lost[0] == 0,
        lambda x0, first: after_first(straight_there, straight_back, x0, first),
        lambda x0, first: after_first(home_there, home_back, x0, first),
        x0,
        first,
    )


def solution(mesh):
    placed = (
        P(("dp", "op"), None, None),
        P(("dp", "op"), None),
        P(None, "op", None, None),
        P(None, "op", None, None),
        P(None, "op", None, None),
        P(None, "op", None, None),
        P(None, "op", None, None),
        P(None, "op", None, None, None),
        P(None, "op", None, None),
        P(None, "op", None, None),
        P(("dp", "op"), None, None),
    )
    return jax.shard_map(
        per_device,
        mesh=mesh,
        in_specs=placed,
        out_specs=(
            P(("dp", "op"), None, None),
            P(("dp", "op"), None, None),
            P(None, "op", "dp", None),
            P(None, "op", "dp", None),
            P(None, "op", "dp", None),
            P(None, "op", "dp", None),
            P(None, "op", None, "dp"),
            P(None, "op", None, "dp", None),
            P(None, "op", None, "dp"),
            P(None, "op", None, "dp"),
        ),
        check_vma=False,
    )
```

```python
import jax
import jax.numpy as jnp
from jax import lax
from jax.experimental import pallas as pl
from jax.experimental.pallas import tpu as pltpu
from jax.sharding import PartitionSpec as P

HEADS = 12
KINDS = 5
BLOCKS = 2
OWN_CAP = 3
HALVES = 2
SLOTS = KINDS * OWN_CAP
FF_PART = 768
FF_SUB = 256
LANES = 128
SMALL_ROWS = 32
BF16 = jnp.bfloat16
F32 = jnp.float32
VMEM_BYTES = 60 * 2**20


def params_of(axes):
    return pltpu.CompilerParams(
        dimension_semantics=("arbitrary",) * axes, vmem_limit_bytes=VMEM_BYTES
    )


def nn(a, b):
    return lax.dot_general(a, b, (((1,), (0,)), ((), ())), preferred_element_type=F32)


def nt(a, b):
    return lax.dot_general(a, b, (((1,), (1,)), ((), ())), preferred_element_type=F32)


def tn(a, b):
    return lax.dot_general(a, b, (((0,), (0,)), ((), ())), preferred_element_type=F32)


def colour_home(owners, seqs, home, cand, color, partner, first, tally):
    base = home * seqs

    def clear_owner(o, _):
        first[o] = -1
        return 0

    lax.fori_loop(0, BLOCKS * owners, clear_owner, 0)
    for half in range(HALVES):
        tally[half] = 0

    def pair_up(j, _):
        color[base + j] = -1
        for b in range(BLOCKS):
            o = b * owners + lax.rem(cand[(base + j) * BLOCKS + b], owners)
            other = first[o]
            partner[b * seqs + j] = other
            first[o] = j

            @pl.when(other >= 0)
            def _():
                partner[b * seqs + other] = j

        return 0

    lax.fori_loop(0, seqs, pair_up, 0)

    def give(j, shade):
        color[base + j] = shade
        tally[shade] = tally[shade] + 1

    def paint(j, _):
        @pl.when(color[base + j] < 0)
        def _():
            shade = jnp.where(tally[0] > tally[1], 1, 0).astype(jnp.int32)
            give(j, shade)
            for side in range(2):

                def more(state):
                    return state[0] >= 0

                def walk(state):
                    now, use, tone = state
                    then = partner[use * seqs + now]
                    free = jnp.logical_and(then >= 0, color[base + jnp.maximum(then, 0)] < 0)

                    @pl.when(free)
                    def _():
                        give(then, 1 - tone)

                    return (jnp.where(free, then, -1), 1 - use, 1 - tone)

                lax.while_loop(more, walk, (j, jnp.int32(side), shade))

        return 0

    lax.fori_loop(0, seqs, paint, 0)


def home_kernel(owners, seqs, cand, send, relay, tags, color, partner, first, tally):
    for b in range(BLOCKS):

        def clear_owner(o, _):
            for half in range(HALVES):
                send[(b * HALVES + half) * owners + o] = -1
                relay[(b * HALVES + half) * owners + o] = -1
                tags[o * BLOCKS * HALVES + b * HALVES + half] = KINDS
            return 0

        lax.fori_loop(0, owners, clear_owner, 0)
    colour_home(owners, seqs, 0, cand, color, partner, first, tally)

    def place(j, _):
        half = color[j]
        spots = []
        for b in range(BLOCKS):
            c = cand[j * BLOCKS + b]
            o = lax.rem(c, owners)
            spots.append(o)
            send[(b * HALVES + half) * owners + o] = j
            tags[o * BLOCKS * HALVES + b * HALVES + half] = lax.div(c, owners)
        relay[half * owners + spots[1]] = spots[0]
        relay[(HALVES + half) * owners + spots[0]] = spots[1]
        return 0

    lax.fori_loop(0, seqs, place, 0)


ROUTES = 10
TRIES = 24


def route_kernel(
    owners, seqs, cand, me_ref, out, ok, color, partner, first, tally, leave, goal, hops, spill
):
    me = me_ref[0]
    square = owners * owners

    def colour(home, _):
        colour_home(owners, seqs, home, cand, color, partner, first, tally)
        return 0

    lax.fori_loop(0, owners, colour, 0)

    def ends(q, _):
        leave[q] = lax.rem(cand[q * BLOCKS], owners)
        goal[q] = lax.rem(cand[q * BLOCKS + 1], owners)
        return 0

    lax.fori_loop(0, owners * seqs, ends, 0)

    def attempt(state):
        turn, _ = state

        def clear(n, _):
            hops[n] = -1
            return 0

        lax.fori_loop(0, 3 * square, clear, 0)

        def direct(q, spilt):
            at = color[q] * 2 * square + leave[q] * owners + goal[q]
            free = hops[at] < 0

            @pl.when(free)
            def _():
                hops[at] = q

            @pl.when(jnp.logical_not(free))
            def _():
                spill[spilt] = q

            return jnp.where(free, spilt, spilt + 1)

        spilt = lax.fori_loop(0, owners * seqs, direct, jnp.int32(0))
        begin = lax.rem(turn * 5, jnp.maximum(spilt, 1))

        def two_hops(n, lost):
            q = spill[lax.rem(begin + n, jnp.maximum(spilt, 1))]
            o, p = leave[q], goal[q]
            early = color[q] * square
            shift = o * 3 + p * 5 + (n + 1) * turn

            def look(s, found):
                i = lax.rem(shift + s, owners)
                a = early + o * owners + i
                b = early + square + i * owners + p
                good = jnp.logical_and(hops[a] < 0, hops[b] < 0)
                return jnp.where(jnp.logical_and(good, found < 0), i, found)

            i = lax.fori_loop(0, owners, look, jnp.int32(-1))

            @pl.when(i >= 0)
            def _():
                hops[early + o * owners + i] = q
                hops[early + square + i * owners + p] = q

            return jnp.where(i >= 0, lost, lost + 1)

        lost = lax.fori_loop(0, spilt, two_hops, jnp.int32(0))
        return turn + 1, lost

    def again(state):
        return jnp.logical_and(state[0] < TRIES, state[1] > 0)

    _, lost = lax.while_loop(again, attempt, (jnp.int32(0), jnp.int32(1)))
    ok[0] = lost

    def clear_out(n, _):
        out[n] = -1
        return 0

    lax.fori_loop(0, ROUTES * owners, clear_out, 0)

    def note(d, _):
        def home(q):
            return lax.div(q, seqs)

        def put(table, at, value):
            out[table * owners + at] = value

        q = hops[me * owners + d]

        @pl.when(q >= 0)
        def _():
            put(0, d, home(q))
            put(9, home(q), d)

        q1 = hops[square + me * owners + d]

        @pl.when(q1 >= 0)
        def _():
            late = color[q1] == 1
            put(1, d, jnp.where(late, owners + home(q1), leave[q1]))

            @pl.when(late)
            def _():
                put(8, home(q1), owners + d)

        q2 = hops[2 * square + me * owners + d]

        @pl.when(q2 >= 0)
        def _():
            mine = leave[q2] == me
            put(2, d, jnp.where(mine, home(q2), owners + leave[q2]))

            @pl.when(mine)
            def _():
                put(8, home(q2), d)

        r = hops[d * owners + me]

        @pl.when(r >= 0)
        def _():
            there = goal[r] == me
            put(7, d, jnp.where(there, home(r), owners + goal[r]))

            @pl.when(there)
            def _():
                put(3, home(r), d)

        r1 = hops[square + d * owners + me]

        @pl.when(r1 >= 0)
        def _():
            late = color[r1] == 1
            put(6, d, jnp.where(late, owners + goal[r1], home(r1)))

            @pl.when(jnp.logical_not(late))
            def _():
                put(3, home(r1), owners + d)

        r2 = hops[2 * square + d * owners + me]

        @pl.when(r2 >= 0)
        def _():
            put(4, home(r2), d)
            put(5, d, home(r2))

        return 0

    lax.fori_loop(0, owners, note, 0)


SMEM_SPEC = pl.BlockSpec(memory_space=pltpu.SMEM)
ANY_SPEC = pl.BlockSpec(memory_space=pl.ANY)


def int_shape(n):
    return jax.ShapeDtypeStruct((n,), jnp.int32)


def home_tables(cand, owners, seqs):
    def kernel(*refs):
        home_kernel(owners, seqs, *refs)

    size = BLOCKS * HALVES * owners
    return pl.pallas_call(
        kernel,
        in_specs=[SMEM_SPEC],
        out_specs=[SMEM_SPEC] * 3,
        out_shape=[int_shape(size)] * 3,
        scratch_shapes=[
            pltpu.SMEM((seqs,), jnp.int32),
            pltpu.SMEM((BLOCKS * seqs,), jnp.int32),
            pltpu.SMEM((BLOCKS * owners,), jnp.int32),
            pltpu.SMEM((HALVES,), jnp.int32),
        ],
        name="home_tables",
    )(cand)


def owner_kernel(owners, tags, rows, counts):
    for b in range(BLOCKS):
        for half in range(HALVES):
            part = b * HALVES + half
            for k in range(8):
                counts[part * 8 + k] = 0

            def arrive(h, free):
                k = tags[h * BLOCKS * HALVES + part]
                there = k < KINDS

                @pl.when(there)
                def _():
                    n = jnp.minimum(counts[part * 8 + k], OWN_CAP - 1)
                    rows[part * SLOTS + k * OWN_CAP + n] = h
                    counts[part * 8 + k] = n + 1

                return jnp.where(there, free, h)

            free = lax.fori_loop(0, owners, arrive, jnp.int32(0))

            def spare(k, otherwise):
                return jnp.where(
                    counts[part * 8 + k] > 0, rows[part * SLOTS + k * OWN_CAP], otherwise
                )

            conv_spare = free
            for k in reversed(range(1, KINDS - 1)):
                conv_spare = spare(k, conv_spare)
            attn_spare = spare(0, conv_spare)
            feed_spare = spare(KINDS - 1, attn_spare)
            last = conv_spare
            for k, start in ((1, None), (2, None), (3, None), (0, attn_spare), (KINDS - 1, feed_spare)):
                last = last if start is None else start
                for i in range(OWN_CAP):
                    at = part * SLOTS + k * OWN_CAP + i
                    last = jnp.where(i < counts[part * 8 + k], rows[at], last)
                    rows[at] = last


def owner_tables(tags, owners):
    def kernel(*refs):
        owner_kernel(owners, *refs)

    return pl.pallas_call(
        kernel,
        in_specs=[SMEM_SPEC],
        out_specs=[SMEM_SPEC] * 2,
        out_shape=[int_shape(BLOCKS * HALVES * SLOTS), int_shape(BLOCKS * HALVES * 8)],
        name="owner_tables",
    )(tags)


def route_tables(cand, me, owners, seqs):
    def kernel(*refs):
        route_kernel(owners, seqs, *refs)

    smem = lambda n: pltpu.SMEM((n,), jnp.int32)
    return pl.pallas_call(
        kernel,
        in_specs=[SMEM_SPEC] * 2,
        out_specs=[SMEM_SPEC] * 2,
        out_shape=[int_shape(ROUTES * owners), int_shape(1)],
        scratch_shapes=[
            smem(owners * seqs),
            smem(BLOCKS * seqs),
            smem(BLOCKS * owners),
            smem(HALVES),
            smem(owners * seqs),
            smem(owners * seqs),
            smem(3 * owners * owners),
            smem(owners * seqs),
        ],
        name="route_tables",
    )(cand, me)


def bring_rows(table, start, sources, name):
    count, length, width = sources[0].shape

    def kernel(table_ref, *refs):
        ins = refs[: len(sources)]
        out_ref, buf, sem_in, sem_out = refs[-4:]

        def loads(n):
            e = table_ref[start + n]
            last = count * (len(sources) - 1)
            for which, source in enumerate(ins):
                low = count * which
                here = e >= low
                if low < last:
                    here = jnp.logical_and(here, e < low + count)
                row = jnp.clip(e - low, 0, count - 1)
                yield here, pltpu.make_async_copy(source.at[row], buf.at[n], sem_in.at[n])

        def store(n):
            return pltpu.make_async_copy(buf.at[n], out_ref.at[n], sem_out.at[n])

        for n in range(count):
            for here, copy in loads(n):

                @pl.when(here)
                def _():
                    copy.start()

        for n in range(count):

            @pl.when(table_ref[start + n] >= 0)
            def _():
                pltpu.make_async_copy(ins[0].at[0], buf.at[n], sem_in.at[n]).wait()
                store(n).start()

        for n in range(count):

            @pl.when(table_ref[start + n] >= 0)
            def _():
                store(n).wait()

    return pl.pallas_call(
        kernel,
        grid_spec=pltpu.PrefetchScalarGridSpec(
            num_scalar_prefetch=1,
            grid=(1,),
            in_specs=[ANY_SPEC] * len(sources),
            out_specs=ANY_SPEC,
            scratch_shapes=[
                pltpu.VMEM((count, length, width), BF16),
                pltpu.SemaphoreType.DMA((count,)),
                pltpu.SemaphoreType.DMA((count,)),
            ],
        ),
        out_shape=jax.ShapeDtypeStruct((count, length, width), BF16),
        compiler_params=params_of(1),
        cost_estimate=pl.CostEstimate(
            flops=0, transcendentals=0, bytes_accessed=4 * count * length * width
        ),
        name=name,
    )(table, *sources)


def move_rows(table, starts, sources, count, scatter, name, wait_for=()):
    length, width = sources[0].shape[1:]
    each = table.shape[0] // (BLOCKS * HALVES)
    total = each * len(sources)

    def kernel(table_ref, *refs):
        ins = refs[: len(sources)]
        out_ref, buf, sem_in, sem_out = refs[-4:]

        def load(part, s):
            idx = table_ref[starts[part] + s]
            at = s if scatter else idx
            to = part * each + s
            return pltpu.make_async_copy(ins[part].at[at], buf.at[to], sem_in.at[to])

        def store(part, s):
            idx = table_ref[starts[part] + s]
            at = part * each + s
            to = idx if scatter else at
            return pltpu.make_async_copy(buf.at[at], out_ref.at[to], sem_out.at[at])

        todo = [(part, s) for part in range(len(sources)) for s in range(each)]
        for part, s in todo:

            @pl.when(table_ref[starts[part] + s] >= 0)
            def _():
                load(part, s).start()

        for part, s in todo:

            @pl.when(table_ref[starts[part] + s] >= 0)
            def _():
                load(part, s).wait()
                store(part, s).start()

        for part, s in todo:

            @pl.when(table_ref[starts[part] + s] >= 0)
            def _():
                store(part, s).wait()

    return pl.pallas_call(
        kernel,
        grid_spec=pltpu.PrefetchScalarGridSpec(
            num_scalar_prefetch=1,
            grid=(1,),
            in_specs=[ANY_SPEC] * (len(sources) + len(wait_for)),
            out_specs=ANY_SPEC,
            scratch_shapes=[
                pltpu.VMEM((total, length, width), BF16),
                pltpu.SemaphoreType.DMA((total,)),
                pltpu.SemaphoreType.DMA((total,)),
            ],
        ),
        out_shape=jax.ShapeDtypeStruct((count, length, width), BF16),
        compiler_params=params_of(1),
        cost_estimate=pl.CostEstimate(
            flops=0, transcendentals=0, bytes_accessed=4 * total * length * width
        ),
        name=name,
    )(table, *sources, *wait_for)


def after(value, earlier):
    def kernel(*refs):
        return

    return pl.pallas_call(
        kernel,
        in_specs=[ANY_SPEC] * (1 + len(earlier)),
        out_specs=ANY_SPEC,
        out_shape=jax.ShapeDtypeStruct(value.shape, value.dtype),
        input_output_aliases={0: 0},
        name="after",
    )(value, *earlier)


def norm_forward(summed, gain_row, shift_row):
    center = summed - jnp.mean(summed, axis=-1, keepdims=True)
    spread = jnp.mean(center * center, axis=-1, keepdims=True)
    scale = lax.rsqrt(spread + 1e-05)
    normed = center * scale
    return normed, normed * gain_row + shift_row, scale


def finish_forward(x, branch, gain_row, shift_row, y_ref, zn_ref, rstd_ref):
    normed, result, scale = norm_forward(x.astype(F32) + branch, gain_row, shift_row)
    y_ref[0] = result.astype(BF16)
    zn_ref[0] = normed.astype(BF16)
    rstd_ref[0] = jnp.broadcast_to(scale, rstd_ref.shape[1:])


def norm_backward(dy, zn_ref, rstd_ref, gain_row):
    dy = dy.astype(F32)
    normed = zn_ref[0].astype(F32)
    scale = rstd_ref[0][:, :1]
    scaled = dy * gain_row
    first = jnp.mean(scaled, axis=-1, keepdims=True)
    second = jnp.mean(scaled * normed, axis=-1, keepdims=True)
    gain_grad = jnp.sum(dy * normed, axis=0, keepdims=True)
    shift_grad = jnp.sum(dy, axis=0, keepdims=True)
    return (scaled - first - normed * second) * scale, gain_grad, shift_grad


def head_masks(length):
    lane = lax.broadcasted_iota(jnp.int32, (length, LANES), 1)
    low = lane < LANES // 2
    return low


def attention_forward(part, tables, x, weights, norms, y_in):
    rows, counts = tables
    b = part // HALVES
    attn_qkv, attn_out = weights
    gains, shifts = norms
    slots, length, width = x.shape
    score_scale = (width // HEADS) ** (-0.5)
    base = part * SLOTS

    def kernel(rows_ref, counts_ref, x_ref, qkv_w, out_w, gain, shift, *rest):
        y_ref, qkv_ref, o_ref, zn_ref, rstd_ref = rest[-5:]
        i = pl.program_id(0)

        @pl.when(i < counts_ref[part * 8])
        def _():
            xv = x_ref[0]
            for third in range(3):
                cols = slice(third * width, (third + 1) * width)
                qkv_ref[0, :, cols] = nn(xv, qkv_w[:, cols]).astype(BF16)
            low = head_masks(length)
            zero = jnp.zeros((), BF16)
            for pair in range(width // LANES):
                at = pair * LANES
                q2 = qkv_ref[0, :, at : at + LANES] * jnp.asarray(score_scale, BF16)
                k2 = qkv_ref[0, :, width + at : width + at + LANES]
                v2 = qkv_ref[0, :, 2 * width + at : 2 * width + at + LANES]
                mixed = []
                for half in range(2):
                    qm = jnp.where(low if half == 0 else ~low, q2, zero)
                    s = nt(qm, k2)
                    e = jnp.exp(s - jnp.max(s, axis=-1, keepdims=True))
                    total = jnp.sum(e, axis=-1, keepdims=True)
                    mixed.append(nn(e.astype(BF16), v2) / total)
                o_ref[0, :, at : at + LANES] = jnp.where(low, mixed[0], mixed[1]).astype(BF16)
            branch = nn(o_ref[0], out_w[...])
            finish_forward(
                xv, branch, gain[0:1, :], shift[0:1, :], y_ref, zn_ref, rstd_ref
            )

    def at_row(i, r, c):
        return (r[base + i], 0, 0)

    def at_step(i, r, c):
        return (jnp.maximum(jnp.minimum(i, c[part * 8] - 1), 0), 0, 0)

    seq = (1, length, width)
    in_specs = [
        pl.BlockSpec(seq, at_row),
        pl.BlockSpec(
            (None, None, width, 3 * width), lambda i, r, c: (b, 0, 0, 0), pipeline_mode=pl.Buffered(1)
        ),
        pl.BlockSpec(
            (None, None, width, width), lambda i, r, c: (b, 0, 0, 0), pipeline_mode=pl.Buffered(1)
        ),
        pl.BlockSpec((8, width), lambda i, r, c: (0, 0)),
        pl.BlockSpec((8, width), lambda i, r, c: (0, 0)),
    ]
    args = [rows, counts, x, attn_qkv, attn_out, gains, shifts]
    alias = {}
    if y_in is not None:
        in_specs.append(pl.BlockSpec(memory_space=pl.ANY))
        alias = {len(args): 0}
        args.append(y_in)
    flops = OWN_CAP * length * width * (8 * width + 4 * length)
    return pl.pallas_call(
        kernel,
        grid_spec=pltpu.PrefetchScalarGridSpec(
            num_scalar_prefetch=2,
            grid=(OWN_CAP,),
            in_specs=in_specs,
            out_specs=[
                pl.BlockSpec(seq, at_row),
                pl.BlockSpec((1, length, 3 * width), at_step),
                pl.BlockSpec(seq, at_step),
                pl.BlockSpec(seq, at_step),
                pl.BlockSpec((1, length, LANES), at_step),
            ],
        ),
        out_shape=[
            jax.ShapeDtypeStruct((slots, length, width), BF16),
            jax.ShapeDtypeStruct((OWN_CAP, length, 3 * width), BF16),
            jax.ShapeDtypeStruct((OWN_CAP, length, width), BF16),
            jax.ShapeDtypeStruct((OWN_CAP, length, width), BF16),
            jax.ShapeDtypeStruct((OWN_CAP, length, LANES), F32),
        ],
        input_output_aliases=alias,
        compiler_params=params_of(1),
        cost_estimate=pl.CostEstimate(
            flops=2 * flops, transcendentals=OWN_CAP * HEADS * length * length, bytes_accessed=30 * 2**20
        ),
        name="attention_forward",
    )(*args)


def attention_backward(part, tables, x, dy, kept, weights, gains, dx_in, sums, packed):
    rows, counts = tables
    b = part // HALVES
    attn_qkv, attn_out = weights
    qkv, o, zn, rstd = kept
    slots, length, width = x.shape
    score_scale = (width // HEADS) ** (-0.5)
    base = part * SLOTS
    first = sums is None
    n_out = 4 if first else 3

    def kernel(rows_ref, counts_ref, x_ref, dy_ref, qkv_ref, o_ref, zn_ref, rstd_ref, qkv_w, out_w, gain, *rest):
        ins = rest[: len(rest) - n_out - 7]
        outs = rest[len(ins) : len(ins) + n_out]
        acc_qkv, acc_out, do_scr, dqkv_scr, dh_scr, dz_scr, sems = rest[-7:]
        dx_ref, small_ref = outs[0], outs[1]
        i = pl.program_id(0)
        here = i < counts_ref[part * 8]

        def copies():
            if first:
                pairs = ((acc_qkv, outs[2]), (acc_out, outs[3]))
            else:
                pairs = ((ins[0], acc_qkv), (ins[1], acc_out))
            return [
                pltpu.make_async_copy(source, target, sems.at[n])
                for n, (source, target) in enumerate(pairs)
            ]

        @pl.when(i == 0)
        def _():
            small_ref[...] = jnp.zeros_like(small_ref)
            if first:
                acc_qkv[...] = jnp.zeros_like(acc_qkv)
                acc_out[...] = jnp.zeros_like(acc_out)
            else:
                for copy in copies():
                    copy.start()

        @pl.when(here)
        def _():
            dz, gain_grad, shift_grad = norm_backward(dy_ref[0], zn_ref, rstd_ref, gain[0:1, :])
            small_ref[0:1, :] += gain_grad
            small_ref[1:2, :] += shift_grad
            dz_scr[...] = dz
            dh = dz.astype(BF16)
            dh_scr[...] = dh
            do_scr[...] = nt(dh, out_w[...]).astype(BF16)
            low = head_masks(length)
            zero = jnp.zeros((), BF16)
            for pair in range(width // LANES):
                at = pair * LANES
                q2 = qkv_ref[0, :, at : at + LANES] * jnp.asarray(score_scale, BF16)
                k2 = qkv_ref[0, :, width + at : width + at + LANES]
                v2 = qkv_ref[0, :, 2 * width + at : 2 * width + at + LANES]
                do2 = do_scr[:, at : at + LANES]
                dqs, dks, dvs = [], [], []
                for half in range(2):
                    mask = low if half == 0 else ~low
                    st = nt(jnp.where(mask, k2, zero), q2)
                    e = jnp.exp(st - jnp.max(st, axis=0, keepdims=True))
                    p = e * (1.0 / jnp.sum(e, axis=0, keepdims=True))
                    dvs.append(nn(p.astype(BF16), do2))
                    t = p * nt(jnp.where(mask, v2, zero), do2)
                    ds = (t - p * jnp.sum(t, axis=0, keepdims=True)).astype(BF16)
                    dks.append(nn(ds, q2))
                    dqs.append(tn(ds, k2))
                dqkv_scr[:, at : at + LANES] = (jnp.where(low, dqs[0], dqs[1]) * score_scale).astype(BF16)
                dqkv_scr[:, width + at : width + at + LANES] = jnp.where(low, dks[0], dks[1]).astype(BF16)
                dqkv_scr[:, 2 * width + at : 2 * width + at + LANES] = jnp.where(low, dvs[0], dvs[1]).astype(BF16)
            total = dz_scr[...]
            for third in range(3):
                cols = slice(third * width, (third + 1) * width)
                total = total + nt(dqkv_scr[:, cols], qkv_w[:, cols])
            dx_ref[0] = total.astype(BF16)

        if not first:

            @pl.when(i == 0)
            def _():
                for copy in copies():
                    copy.wait()

        @pl.when(here)
        def _():
            xv = x_ref[0]
            for third in range(3):
                cols = slice(third * width, (third + 1) * width)
                acc_qkv[:, cols] += tn(xv, dqkv_scr[:, cols])
            acc_out[...] += tn(o_ref[0], dh_scr[...])

        @pl.when(i == OWN_CAP - 1)
        def _():
            if first:
                for copy in copies():
                    copy.start()
                for copy in copies():
                    copy.wait()
            else:
                packed_ref = outs[2]
                groups, tall = packed_ref.shape[0], packed_ref.shape[1] // 4
                for third in range(3):
                    piece = acc_qkv[:, third * width : (third + 1) * width].astype(BF16)
                    packed_ref[:, third * tall : (third + 1) * tall, :] = piece.reshape(
                        groups, tall, width
                    )
                packed_ref[:, 3 * tall : 4 * tall, :] = (
                    acc_out[...].astype(BF16).reshape(groups, tall, width)
                )

    def at_row(i, r, c):
        return (r[base + i], 0, 0)

    def at_step(i, r, c):
        return (jnp.maximum(jnp.minimum(i, c[part * 8] - 1), 0), 0, 0)

    def whole(i, r, c):
        return (0, 0)

    seq = (1, length, width)
    in_specs = [
        pl.BlockSpec(seq, at_row),
        pl.BlockSpec(seq, at_row),
        pl.BlockSpec((1, length, 3 * width), at_step),
        pl.BlockSpec(seq, at_step),
        pl.BlockSpec(seq, at_step),
        pl.BlockSpec((1, length, LANES), at_step),
        pl.BlockSpec(
            (None, None, width, 3 * width), lambda i, r, c: (b, 0, 0, 0), pipeline_mode=pl.Buffered(1)
        ),
        pl.BlockSpec(
            (None, None, width, width), lambda i, r, c: (b, 0, 0, 0), pipeline_mode=pl.Buffered(1)
        ),
        pl.BlockSpec((8, width), whole),
    ]
    args = [rows, counts, x, dy, qkv, o, zn, rstd, attn_qkv, attn_out, gains]
    out_specs = [pl.BlockSpec(seq, at_row), pl.BlockSpec((8, width), whole)]
    out_shape = [
        jax.ShapeDtypeStruct((slots, length, width), BF16),
        jax.ShapeDtypeStruct((8, width), F32),
    ]
    if first:
        out_specs += [ANY_SPEC, ANY_SPEC]
        out_shape += [
            jax.ShapeDtypeStruct((width, 3 * width), F32),
            jax.ShapeDtypeStruct((width, width), F32),
        ]
    else:
        groups, total_rows = packed
        out_specs.append(
            pl.BlockSpec((groups, 4 * width // groups, width), lambda i, r, c: (0, 0, 0))
        )
        out_shape.append(jax.ShapeDtypeStruct((groups, total_rows, width), BF16))
        in_specs += [ANY_SPEC, ANY_SPEC]
        args += list(sums)
    alias = {}
    if dx_in is not None:
        in_specs.append(ANY_SPEC)
        alias = {len(args): 0}
        args.append(dx_in)
    flops = 2 * OWN_CAP * length * width * (8 * width + 4 * length)
    return pl.pallas_call(
        kernel,
        grid_spec=pltpu.PrefetchScalarGridSpec(
            num_scalar_prefetch=2,
            grid=(OWN_CAP,),
            in_specs=in_specs,
            out_specs=out_specs,
            scratch_shapes=[
                pltpu.VMEM((width, 3 * width), F32),
                pltpu.VMEM((width, width), F32),
                pltpu.VMEM((length, width), BF16),
                pltpu.VMEM((length, 3 * width), BF16),
                pltpu.VMEM((length, width), BF16),
                pltpu.VMEM((length, width), F32),
                pltpu.SemaphoreType.DMA((2,)),
            ],
        ),
        out_shape=out_shape,
        input_output_aliases=alias,
        compiler_params=params_of(1),
        cost_estimate=pl.CostEstimate(
            flops=flops, transcendentals=OWN_CAP * HEADS * length * length // 2, bytes_accessed=40 * 2**20
        ),
        name="attention_backward",
    )(*args)


def feed_forward(part, tables, x, weights, norms, earlier):
    rows, counts = tables
    b = part // HALVES
    ffn_up, ffn_down = weights
    gains, shifts = norms
    slots, length, width = x.shape
    hidden = ffn_up.shape[-1]
    parts = hidden // FF_PART
    kind = KINDS - 1
    base = part * SLOTS + kind * OWN_CAP

    def kernel(rows_ref, counts_ref, x_ref, up, down, gain, shift, *rest):
        y_ref, g_ref, slope_ref, zn_ref, rstd_ref, x_scr, h_scr = rest[-7:]
        c, i = pl.program_id(0), pl.program_id(1)

        @pl.when(i < counts_ref[part * 8 + kind])
        def _():
            @pl.when(c == 0)
            def _():
                x_scr[i] = x_ref[0]

            xv = x_scr[i]
            for sub in range(FF_PART // FF_SUB):
                cols = slice(sub * FF_SUB, (sub + 1) * FF_SUB)
                a = nn(xv, up[:, cols])
                phi = 0.5 + 0.5 * lax.erf(a * (0.5**0.5))
                slope = phi + a * (jnp.exp(a * a * -0.5) * 0.3989422804014327)
                g = (a * phi).astype(BF16)
                g_ref[0, :, cols] = g
                slope_ref[0, :, cols] = slope.astype(BF16)
            branch = nn(g_ref[0], down[...])

            @pl.when(c == 0)
            def _():
                h_scr[i] = branch

            @pl.when(jnp.logical_and(c > 0, c < parts - 1))
            def _():
                h_scr[i] += branch

            @pl.when(c == parts - 1)
            def _():
                finish_forward(
                    xv,
                    h_scr[i] + branch,
                    gain[kind : kind + 1, :],
                    shift[kind : kind + 1, :],
                    y_ref,
                    zn_ref,
                    rstd_ref,
                )

    def in_row(c, i, r, n):
        return (r[base + jnp.where(c == 0, i, OWN_CAP - 1)], 0, 0)

    def out_row(c, i, r, n):
        return (r[base + jnp.where(c == parts - 1, i, 0)], 0, 0)

    def place(i, n):
        at = jnp.maximum(jnp.minimum(i, n[part * 8 + kind] - 1), 0)
        return at if part == b * HALVES else at + n[b * HALVES * 8 + kind]

    def out_step(c, i, r, n):
        return (place(jnp.where(c == parts - 1, i, 0), n), 0, 0)

    def part_step(c, i, r, n):
        return (place(i, n), 0, c)

    seq = (1, length, width)
    in_specs = [
        pl.BlockSpec(seq, in_row),
        pl.BlockSpec((None, None, width, FF_PART), lambda c, i, r, n: (b, 0, 0, c)),
        pl.BlockSpec((None, None, FF_PART, width), lambda c, i, r, n: (b, 0, c, 0)),
        pl.BlockSpec((8, width), lambda c, i, r, n: (0, 0)),
        pl.BlockSpec((8, width), lambda c, i, r, n: (0, 0)),
    ]
    args = [rows, counts, x, ffn_up, ffn_down, gains, shifts]
    alias = {}
    for n, kept in enumerate(earlier or ()):
        in_specs.append(ANY_SPEC)
        alias[len(args)] = 1 + n
        args.append(kept)
    return pl.pallas_call(
        kernel,
        grid_spec=pltpu.PrefetchScalarGridSpec(
            num_scalar_prefetch=2,
            grid=(parts, OWN_CAP),
            in_specs=in_specs,
            out_specs=[
                pl.BlockSpec(seq, out_row),
                pl.BlockSpec((1, length, FF_PART), part_step),
                pl.BlockSpec((1, length, FF_PART), part_step),
                pl.BlockSpec(seq, out_step),
                pl.BlockSpec((1, length, LANES), out_step),
            ],
            scratch_shapes=[
                pltpu.VMEM((OWN_CAP, length, width), BF16),
                pltpu.VMEM((OWN_CAP, length, width), F32),
            ],
        ),
        out_shape=[
            jax.ShapeDtypeStruct((slots, length, width), BF16),
            jax.ShapeDtypeStruct((OWN_CAP + 1, length, hidden), BF16),
            jax.ShapeDtypeStruct((OWN_CAP + 1, length, hidden), BF16),
            jax.ShapeDtypeStruct((OWN_CAP + 1, length, width), BF16),
            jax.ShapeDtypeStruct((OWN_CAP + 1, length, LANES), F32),
        ],
        input_output_aliases=alias,
        compiler_params=params_of(2),
        cost_estimate=pl.CostEstimate(
            flops=4 * OWN_CAP * length * width * hidden,
            transcendentals=2 * OWN_CAP * length * hidden,
            bytes_accessed=40 * 2**20,
        ),
        name="feed_forward",
    )(*args)


def feed_backward(b, tables, x, dy, kept, weights, gains, dx_lead, lead, groups, wait_for):
    rows, counts = tables
    ffn_up, ffn_down = weights
    g, slope, zn, rstd = kept
    slots, length, width = x[0].shape
    hidden = ffn_up.shape[-1]
    parts = hidden // FF_PART
    kind = KINDS - 1
    bases = [(b * HALVES + half) * SLOTS + kind * OWN_CAP for half in range(HALVES)]
    tall = width // groups
    deep = hidden // groups
    shares = FF_PART // deep

    def present(n, half):
        return n[(b * HALVES + half) * 8 + kind]

    def kernel(
        rows_ref,
        counts_ref,
        x_ref0,
        x_ref1,
        dy_ref0,
        dy_ref1,
        g_ref,
        slope_ref,
        zn_ref,
        rstd_ref,
        up,
        down,
        gain,
        *rest,
    ):
        (
        small_ref,
        dx_ref0,
        dx_ref1,
        packed_ref,
        x_scr,
        dh_scr,
        dx_scr,
        da_scr,
        acc_up,
        acc_down,
        low_up,
        low_down,
        low_dx,
        sems,
        dx_sem,
        ) = rest[-15:]
        c, i = pl.program_id(0), pl.program_id(1)
        n0 = present(counts_ref, 0)
        total_n = n0 + present(counts_ref, 1)
        in_first = i < n0

        @pl.when(jnp.logical_and(c == 0, i == 0))
        def _():
            small_ref[...] = jnp.zeros_like(small_ref)

        @pl.when(i == 0)
        def _():
            acc_up[...] = jnp.zeros_like(acc_up)
            acc_down[...] = jnp.zeros_like(acc_down)

        @pl.when(i < total_n)
        def _():
            @pl.when(c == 0)
            def _():
                dz, gain_grad, shift_grad = norm_backward(
                    jnp.where(in_first, dy_ref0[0], dy_ref1[0]),
                    zn_ref,
                    rstd_ref,
                    gain[kind : kind + 1, :],
                )
                small_ref[0:1, :] += gain_grad
                small_ref[1:2, :] += shift_grad
                x_scr[i] = jnp.where(in_first, x_ref0[0], x_ref1[0])
                dh_scr[i] = dz.astype(BF16)
                dx_scr[i] = dz

            dh = dh_scr[i]
            for sub in range(FF_PART // FF_SUB):
                cols = slice(sub * FF_SUB, (sub + 1) * FF_SUB)
                dg = nt(dh, down[cols, :])
                da_scr[:, cols] = (dg * slope_ref[0, :, cols].astype(F32)).astype(BF16)
            acc_down[...] += tn(g_ref[0], dh)
            acc_up[...] += tn(x_scr[i], da_scr[...])
            total = dx_scr[i] + nt(da_scr[...], up[...])

            @pl.when(c < parts - 1)
            def _():
                dx_scr[i] = total

            @pl.when(c == parts - 1)
            def _():
                low_dx[...] = total.astype(BF16)
                for half, (inside, dx_ref) in enumerate(
                    ((in_first, dx_ref0), (jnp.logical_not(in_first), dx_ref1))
                ):

                    @pl.when(inside)
                    def _():
                        row = rows_ref[bases[half] + jnp.where(in_first, i, jnp.maximum(i - n0, 0))]
                        copy = pltpu.make_async_copy(low_dx, dx_ref.at[row], dx_sem)
                        copy.start()
                        copy.wait()

        def copies():
            pairs = [
                (low_up.at[pl.ds(z * tall, tall)], packed_ref.at[z, pl.ds(c * tall, tall)])
                for z in range(groups)
            ]
            pairs += [
                (
                    low_down.at[pl.ds(m * deep, deep)],
                    packed_ref.at[c * shares + m, pl.ds(parts * tall, deep)],
                )
                for m in range(shares)
            ]
            return [
                pltpu.make_async_copy(source, target, sems.at[n])
                for n, (source, target) in enumerate(pairs)
            ]

        @pl.when(i == OWN_CAP - 1)
        def _():
            @pl.when(c > 0)
            def _():
                for copy in copies():
                    copy.wait()

            low_up[...] = acc_up[...].astype(BF16)
            low_down[...] = acc_down[...].astype(BF16)
            for copy in copies():
                copy.start()

            @pl.when(c == parts - 1)
            def _():
                for copy in copies():
                    copy.wait()

    def first_row(c, i, r, n):
        return (r[bases[0] + jnp.where(c == 0, i, OWN_CAP - 1)], 0, 0)

    def second_row(c, i, r, n):
        at = jnp.where(c == 0, i, OWN_CAP - 1) - present(n, 0)
        return (r[bases[1] + jnp.maximum(at, 0)], 0, 0)

    def last(n):
        return present(n, 0) + present(n, 1) - 1

    def in_step(c, i, r, n):
        return (jnp.where(c == 0, jnp.minimum(i, last(n)), last(n)), 0, 0)

    def part_step(c, i, r, n):
        return (jnp.minimum(i, last(n)), 0, c)

    seq = (1, length, width)
    in_specs = [
        pl.BlockSpec(seq, first_row),
        pl.BlockSpec(seq, second_row),
        pl.BlockSpec(seq, first_row),
        pl.BlockSpec(seq, second_row),
        pl.BlockSpec((1, length, FF_PART), part_step),
        pl.BlockSpec((1, length, FF_PART), part_step),
        pl.BlockSpec(seq, in_step),
        pl.BlockSpec((1, length, LANES), in_step),
        pl.BlockSpec((None, None, width, FF_PART), lambda c, i, r, n: (b, 0, 0, c)),
        pl.BlockSpec((None, None, FF_PART, width), lambda c, i, r, n: (b, 0, c, 0)),
        pl.BlockSpec((8, width), lambda c, i, r, n: (0, 0)),
        ANY_SPEC,
    ] + [ANY_SPEC] * len(wait_for)
    args = [rows, counts, *x, *dy, g, slope, zn, rstd, ffn_up, ffn_down, gains, dx_lead]
    alias = {len(args) - 1: 1 + lead}
    args += wait_for
    return pl.pallas_call(
        kernel,
        grid_spec=pltpu.PrefetchScalarGridSpec(
            num_scalar_prefetch=2,
            grid=(parts, OWN_CAP),
            in_specs=in_specs,
            out_specs=[
                pl.BlockSpec((8, width), lambda c, i, r, n: (0, 0)),
                ANY_SPEC,
                ANY_SPEC,
                ANY_SPEC,
            ],
            scratch_shapes=[
                pltpu.VMEM((OWN_CAP, length, width), BF16),
                pltpu.VMEM((OWN_CAP, length, width), BF16),
                pltpu.VMEM((OWN_CAP, length, width), F32),
                pltpu.VMEM((length, FF_PART), BF16),
                pltpu.VMEM((width, FF_PART), F32),
                pltpu.VMEM((FF_PART, width), F32),
                pltpu.VMEM((width, FF_PART), BF16),
                pltpu.VMEM((FF_PART, width), BF16),
                pltpu.VMEM((length, width), BF16),
                pltpu.SemaphoreType.DMA((groups + shares,)),
                pltpu.SemaphoreType.DMA,
            ],
        ),
        out_shape=[
            jax.ShapeDtypeStruct((8, width), F32),
            jax.ShapeDtypeStruct((slots, length, width), BF16),
            jax.ShapeDtypeStruct((slots, length, width), BF16),
            jax.ShapeDtypeStruct((groups, parts * tall + deep, width), BF16),
        ],
        input_output_aliases=alias,
        compiler_params=params_of(2),
        cost_estimate=pl.CostEstimate(
            flops=7 * OWN_CAP * length * width * hidden,
            transcendentals=0,
            bytes_accessed=50 * 2**20,
        ),
        name="feed_backward",
    )(*args)


PAD = 8
ROW_TILE = 128
COL_TILE = 256


def fill_padded(padded, values):
    length = values.shape[0]
    edge = jnp.zeros((PAD, values.shape[1]), F32)
    padded[0:PAD, :] = edge
    padded[PAD + length : PAD + length + PAD, :] = edge
    padded[PAD : PAD + length, :] = values


def conv_forward(part, tables, x, weights, norms, y_in):
    rows, counts = tables
    b = part // HALVES
    taps, conv_point = weights
    gains, shifts = norms
    slots, length, width = x.shape
    base = part * SLOTS + OWN_CAP
    steps = (KINDS - 2) * OWN_CAP

    def kernel(rows_ref, counts_ref, x_ref, point, taps_ref, gain, shift, *rest):
        y_ref, u_ref, zn_ref, rstd_ref, xpad = rest[-5:]
        step = pl.program_id(0)
        which, j = step // OWN_CAP, step % OWN_CAP
        for kind in range(1, KINDS - 1):
            taps_n = 2 * kind + 1
            first = kind * kind - 1

            @pl.when(jnp.logical_and(which == kind - 1, j < counts_ref[part * 8 + kind]))
            def _():
                fill_padded(xpad, x_ref[0].astype(F32))
                for r in range(0, length, ROW_TILE):
                    for col in range(0, width, COL_TILE):
                        cols = slice(col, col + COL_TILE)
                        mixed = None
                        for t in range(taps_n):
                            start = PAD + r + t - kind
                            term = xpad[start : start + ROW_TILE, cols] * taps_ref[first + t : first + t + 1, cols]
                            mixed = term if mixed is None else mixed + term
                        u_ref[0, r : r + ROW_TILE, cols] = mixed.astype(BF16)
                branch = nn(u_ref[0], point[...])
                finish_forward(
                    x_ref[0],
                    branch,
                    gain[kind : kind + 1, :],
                    shift[kind : kind + 1, :],
                    y_ref,
                    zn_ref,
                    rstd_ref,
                )

    def at_row(i, r, c):
        return (r[base + i], 0, 0)

    def at_step(i, r, c):
        which = i // OWN_CAP
        last = c[part * 8 + 1 + which] - 1
        return (which * OWN_CAP + jnp.maximum(jnp.minimum(i % OWN_CAP, last), 0), 0, 0)

    def whole(i, r, c):
        return (0, 0)

    seq = (1, length, width)
    in_specs = [
        pl.BlockSpec(seq, at_row),
        pl.BlockSpec((None, None, None, width, width), lambda i, r, c: (b, 0, i // OWN_CAP, 0, 0)),
        pl.BlockSpec((16, width), whole),
        pl.BlockSpec((8, width), whole),
        pl.BlockSpec((8, width), whole),
    ]
    args = [rows, counts, x, conv_point, taps, gains, shifts]
    alias = {}
    if y_in is not None:
        in_specs.append(pl.BlockSpec(memory_space=pl.ANY))
        alias = {len(args): 0}
        args.append(y_in)
    return pl.pallas_call(
        kernel,
        grid_spec=pltpu.PrefetchScalarGridSpec(
            num_scalar_prefetch=2,
            grid=(steps,),
            in_specs=in_specs,
            out_specs=[
                pl.BlockSpec(seq, at_row),
                pl.BlockSpec(seq, at_step),
                pl.BlockSpec(seq, at_step),
                pl.BlockSpec((1, length, LANES), at_step),
            ],
            scratch_shapes=[pltpu.VMEM((length + 2 * PAD, width), F32)],
        ),
        out_shape=[
            jax.ShapeDtypeStruct((slots, length, width), BF16),
            jax.ShapeDtypeStruct((steps, length, width), BF16),
            jax.ShapeDtypeStruct((steps, length, width), BF16),
            jax.ShapeDtypeStruct((steps, length, LANES), F32),
        ],
        input_output_aliases=alias,
        compiler_params=params_of(1),
        cost_estimate=pl.CostEstimate(
            flops=2 * steps * length * width * width, transcendentals=0, bytes_accessed=36 * 2**20
        ),
        name="conv_forward",
    )(*args)


def conv_backward(part, tables, x, dy, kept, weights, gains, dx_in, sums, packed):
    rows, counts = tables
    b = part // HALVES
    taps, conv_point = weights
    u, zn, rstd = kept
    slots, length, width = x.shape
    base = part * SLOTS + OWN_CAP
    steps = (KINDS - 2) * OWN_CAP
    first_half = sums is None
    groups = packed[0]

    def kernel(rows_ref, counts_ref, x_ref, dy_ref, u_ref, zn_ref, rstd_ref, point, taps_ref, gain, *rest):
        if first_half:
            dx_ref, small_ref, acc, xpad, dupad, dz_scr = rest[-6:]
        else:
            sum_ref = rest[0]
            dx_ref, small_ref, packed_ref, xpad, dupad, dz_scr, acc = rest[-7:]
        step = pl.program_id(0)
        which, j = step // OWN_CAP, step % OWN_CAP

        @pl.when(step == 0)
        def _():
            small_ref[...] = jnp.zeros_like(small_ref)

        @pl.when(j == 0)
        def _():
            acc[...] = jnp.zeros_like(acc) if first_half else sum_ref[...]

        for kind in range(1, KINDS - 1):
            taps_n = 2 * kind + 1
            first = kind * kind - 1

            @pl.when(jnp.logical_and(which == kind - 1, j < counts_ref[part * 8 + kind]))
            def _():
                dz, gain_grad, shift_grad = norm_backward(
                    dy_ref[0], zn_ref, rstd_ref, gain[kind : kind + 1, :]
                )
                small_ref[14 + kind : 15 + kind, :] += gain_grad
                small_ref[17 + kind : 18 + kind, :] += shift_grad
                dz_scr[...] = dz
                dh = dz.astype(BF16)
                acc[...] += tn(u_ref[0], dh)
                fill_padded(xpad, x_ref[0].astype(F32))
                fill_padded(dupad, nt(dh, point[...]))
                for col in range(0, width, COL_TILE):
                    cols = slice(col, col + COL_TILE)
                    sums = [None] * taps_n
                    for r in range(0, length, ROW_TILE):
                        here = dupad[PAD + r : PAD + r + ROW_TILE, cols]
                        total = dz_scr[r : r + ROW_TILE, cols]
                        for t in range(taps_n):
                            back = PAD + r - t + kind
                            total = total + dupad[back : back + ROW_TILE, cols] * taps_ref[first + t : first + t + 1, cols]
                            ahead = PAD + r + t - kind
                            part = jnp.sum(
                                xpad[ahead : ahead + ROW_TILE, cols] * here, axis=0, keepdims=True
                            )
                            sums[t] = part if sums[t] is None else sums[t] + part
                        dx_ref[0, r : r + ROW_TILE, cols] = total.astype(BF16)
                    for t in range(taps_n):
                        small_ref[first + t : first + t + 1, cols] += sums[t]

        if not first_half:

            @pl.when(j == OWN_CAP - 1)
            def _():
                packed_ref[...] = acc[...].astype(BF16).reshape(packed_ref.shape)

    def at_row(i, r, c):
        return (r[base + i], 0, 0)

    def at_step(i, r, c):
        which = i // OWN_CAP
        last = c[part * 8 + 1 + which] - 1
        return (which * OWN_CAP + jnp.maximum(jnp.minimum(i % OWN_CAP, last), 0), 0, 0)

    def whole(i, r, c):
        return (0, 0)

    seq = (1, length, width)
    in_specs = [
        pl.BlockSpec(seq, at_row),
        pl.BlockSpec(seq, at_row),
        pl.BlockSpec(seq, at_step),
        pl.BlockSpec(seq, at_step),
        pl.BlockSpec((1, length, LANES), at_step),
        pl.BlockSpec((None, None, None, width, width), lambda i, r, c: (b, 0, i // OWN_CAP, 0, 0)),
        pl.BlockSpec((16, width), whole),
        pl.BlockSpec((8, width), whole),
    ]
    args = [rows, counts, x, dy, u, zn, rstd, conv_point, taps, gains]
    sum_spec = pl.BlockSpec((None, width, width), lambda i, r, c: (i // OWN_CAP, 0, 0))
    out_specs = [pl.BlockSpec(seq, at_row), pl.BlockSpec((24, width), whole)]
    out_shape = [
        jax.ShapeDtypeStruct((slots, length, width), BF16),
        jax.ShapeDtypeStruct((24, width), F32),
    ]
    scratch = [
        pltpu.VMEM((length + 2 * PAD, width), F32),
        pltpu.VMEM((length + 2 * PAD, width), F32),
        pltpu.VMEM((length, width), F32),
    ]
    alias = {}
    if first_half:
        out_specs.append(sum_spec)
        out_shape.append(jax.ShapeDtypeStruct((KINDS - 2, width, width), F32))
    else:
        in_specs.append(sum_spec)
        args.append(sums)
        out_specs.append(
            pl.BlockSpec((groups, width // groups, width), lambda i, r, c: (0, 4 + i // OWN_CAP, 0))
        )
        out_shape.append(jax.ShapeDtypeStruct(packed[1].shape, BF16))
        in_specs.append(ANY_SPEC)
        alias = {len(args): 2}
        args.append(packed[1])
        scratch.append(pltpu.VMEM((width, width), F32))
    in_specs.append(ANY_SPEC)
    alias = {**alias, len(args): 0}
    args.append(dx_in)
    return pl.pallas_call(
        kernel,
        grid_spec=pltpu.PrefetchScalarGridSpec(
            num_scalar_prefetch=2,
            grid=(steps,),
            in_specs=in_specs,
            out_specs=out_specs,
            scratch_shapes=scratch,
        ),
        out_shape=out_shape,
        input_output_aliases=alias,
        compiler_params=params_of(1),
        cost_estimate=pl.CostEstimate(
            flops=3 * steps * length * width * width, transcendentals=0, bytes_accessed=50 * 2**20
        ),
        name="conv_backward",
    )(*args)


def owner_forward(b, half, tables, x, weights, small_weights, earlier):
    part = b * HALVES + half
    attn_qkv, attn_out, ffn_up, ffn_down, conv_point = weights
    taps, gains, shifts = small_weights
    norms = (gains, shifts)
    y, *kept_f = feed_forward(part, tables, x, (ffn_up, ffn_down), norms, earlier)
    y, *kept_a = attention_forward(part, tables, x, (attn_qkv, attn_out), norms, y)
    y, *kept_c = conv_forward(part, tables, x, (taps, conv_point), norms, y)
    return y, kept_f, kept_a, kept_c


def both_forward(b, tables, x, weights, small_weights):
    y, kept_a, kept_c, kept_f = [], [], [], None
    for half in range(HALVES):
        yh, kept_f, ka, kc = owner_forward(
            b, half, tables, x[half], weights, small_weights, kept_f
        )
        y.append(yh)
        kept_a.append(ka)
        kept_c.append(kc)
    return y, (kept_f, kept_a, kept_c)


def join_small(small_f, small_a, small_c):
    return jnp.concatenate(
        [
            small_c[:15],
            small_a[0:1],
            small_c[15:18],
            small_f[0:1],
            small_a[1:2],
            small_c[18:21],
            small_f[1:2],
        ]
    )


def owner_backward(b, tables, x, dy, kept, weights, small_weights, groups, wait_for):
    attn_qkv, attn_out, ffn_up, ffn_down, conv_point = weights
    taps, gains, shifts = small_weights
    kept_f, kept_a, kept_c = kept
    width = x[0].shape[-1]
    rest_rows = 7 * width // groups + SMALL_ROWS
    attn, conv = (attn_qkv, attn_out), (taps, conv_point)
    lead, other = 1, 0
    first, second = b * HALVES + lead, b * HALVES + other
    d_lead, small_a0, *sum_a = attention_backward(
        first, tables, x[lead], dy[lead], kept_a[lead], attn, gains, None, None, None
    )
    d_lead, small_c0, sum_c = conv_backward(
        first, tables, x[lead], dy[lead], kept_c[lead], conv, gains, d_lead, None, (groups,)
    )
    small_f, *dx, feed_pack = feed_backward(
        b, tables, x, dy, kept_f, (ffn_up, ffn_down), gains, d_lead, lead, groups, wait_for
    )
    dx[other], small_a1, rest_pack = attention_backward(
        second,
        tables,
        x[other],
        dy[other],
        kept_a[other],
        attn,
        gains,
        dx[other],
        sum_a,
        (groups, rest_rows),
    )
    dx[other], small_c1, rest_pack = conv_backward(
        second,
        tables,
        x[other],
        dy[other],
        kept_c[other],
        conv,
        gains,
        dx[other],
        sum_c,
        (groups, rest_pack),
    )
    small = join_small(small_f, small_a0 + small_a1, small_c0 + small_c1).astype(BF16)
    small = small.reshape(25, groups, width // groups)
    small = small.transpose(1, 0, 2)
    small = jnp.pad(small, ((0, 0), (0, SMALL_ROWS - 25), (0, width - width // groups)))
    rest_pack = lax.dynamic_update_slice(rest_pack, small, (0, rest_rows - SMALL_ROWS, 0))
    return dx, feed_pack, rest_pack


def finish_feed(b, feed, totals, up_out, down_out, shapes):
    parts = shapes[0].shape[-1] // FF_PART
    tall, width = shapes[0].shape[2], FF_PART

    def kernel(up_ref, down_ref, count_ref, *rest):
        up_to, down_to = rest[-2:]
        scale = 1.0 / count_ref[b : b + 1, KINDS - 1 : KINDS]
        up_to[...] = up_ref[...].astype(F32) * scale
        down_to[...] = down_ref[...].astype(F32) * scale

    old = [] if up_out is None else [up_out, down_out]
    return pl.pallas_call(
        kernel,
        grid=(parts,),
        in_specs=[
            pl.BlockSpec((tall, width), lambda c: (c, 0)),
            pl.BlockSpec((tall, width), lambda c: (parts + c, 0)),
            pl.BlockSpec((BLOCKS, 8), lambda c: (0, 0)),
        ]
        + [ANY_SPEC] * len(old),
        out_specs=[
            pl.BlockSpec((None, None, tall, width), lambda c: (b, 0, 0, c)),
            pl.BlockSpec((None, None, tall, width), lambda c: (b, 0, c, 0)),
        ],
        out_shape=list(shapes),
        input_output_aliases={3 + n: n for n in range(len(old))},
        compiler_params=params_of(1),
        cost_estimate=pl.CostEstimate(flops=0, transcendentals=0, bytes_accessed=8 * 2**20),
        name="finish_feed",
    )(feed, feed, totals, *old)


def finish_rest(b, rest, totals, old, shapes, wait_for):
    tall, width = shapes[1].shape[2:]
    small_block = 7 * tall // SMALL_ROWS

    def kernel(rest_ref, small_ref, count_ref, *refs):
        qkv_to, out_to, taps_to, point_to, gain_to, shift_to = refs[-6:]
        i = pl.program_id(0)
        scales = 1.0 / jnp.maximum(count_ref[b : b + 1, :], 1.0)
        values = rest_ref[...].astype(F32)

        @pl.when(i < 3)
        def _():
            qkv_to[...] = values * scales[:, 0:1]

        @pl.when(i == 3)
        def _():
            out_to[...] = values * scales[:, 0:1]
            small = small_ref[...].astype(F32)
            row = lax.broadcasted_iota(jnp.int32, small.shape, 0)
            which = jnp.where(row < 3, 1, jnp.where(row < 8, 2, jnp.where(row < 15, 3, 0)))
            which = jnp.where(row >= 15, row - 15, which)
            which = jnp.where(row >= 20, row - 20, which)
            scale = jnp.zeros_like(small)
            for k in range(KINDS):
                scale = jnp.where(which == k, scales[:, k : k + 1], scale)
            small = small * scale
            for r in range(15):
                taps_to[r] = small[r : r + 1, :tall]
            for r in range(KINDS):
                gain_to[r] = small[15 + r : 16 + r, :tall]
                shift_to[r] = small[20 + r : 21 + r, :tall]

        for k in range(1, KINDS - 1):

            @pl.when(i == 3 + k)
            def _():
                point_to[...] = values * scales[:, k : k + 1]

    old = list(old)
    return pl.pallas_call(
        kernel,
        grid=(7,),
        in_specs=[
            pl.BlockSpec((tall, width), lambda i: (i, 0)),
            pl.BlockSpec((SMALL_ROWS, width), lambda i: (small_block, 0)),
            pl.BlockSpec((BLOCKS, 8), lambda i: (0, 0)),
        ]
        + [ANY_SPEC] * (len(old) + len(wait_for)),
        out_specs=[
            pl.BlockSpec((None, None, tall, width), lambda i: (b, 0, 0, jnp.minimum(i, 2))),
            pl.BlockSpec((None, None, tall, width), lambda i: (b, 0, 0, 0)),
            pl.BlockSpec((None, 15, 1, tall), lambda i: (b, 0, 0, 0)),
            pl.BlockSpec(
                (None, None, None, tall, width), lambda i: (b, 0, jnp.maximum(i - 4, 0), 0, 0)
            ),
            pl.BlockSpec((None, KINDS, 1, tall), lambda i: (b, 0, 0, 0)),
            pl.BlockSpec((None, KINDS, 1, tall), lambda i: (b, 0, 0, 0)),
        ],
        out_shape=list(shapes),
        input_output_aliases={3 + n: n for n in range(len(old))},
        compiler_params=params_of(1),
        cost_estimate=pl.CostEstimate(flops=0, transcendentals=0, bytes_accessed=8 * 2**20),
        name="finish_rest",
    )(rest, rest, totals, *old, *wait_for)


def small_params(b, conv_taps, norm_gain, norm_bias):
    taps = jnp.pad(conv_taps[b, 0].astype(F32), ((0, 1), (0, 0)))
    gains = jnp.pad(norm_gain[b, 0].astype(F32), ((0, 3), (0, 0)))
    shifts = jnp.pad(norm_bias[b, 0].astype(F32), ((0, 3), (0, 0)))
    return taps, gains, shifts


def exchange(rows):
    return lax.all_to_all(rows, "op", split_axis=0, concat_axis=0, tiled=True)


def group_sum(pack):
    return lax.psum_scatter(pack, "dp", scatter_dimension=0, tiled=False)


def per_device(
    inputs,
    candidate,
    attn_qkv,
    attn_out,
    ffn_up,
    ffn_down,
    conv_taps,
    conv_point,
    norm_gain,
    norm_bias,
    cotangent,
):
    owners = lax.axis_size("op")
    groups = lax.axis_size("dp")
    seqs = inputs.shape[0]
    width = inputs.shape[-1]
    hidden = ffn_up.shape[-1]
    weights = (attn_qkv, attn_out, ffn_up, ffn_down, conv_point)
    smalls = [small_params(b, conv_taps, norm_gain, norm_bias) for b in range(BLOCKS)]
    send, relay, tags = home_tables(candidate.reshape(-1), owners, seqs)
    marks = BLOCKS * HALVES
    told = jnp.concatenate(
        [tags.reshape(owners, marks), jnp.broadcast_to(candidate.reshape(1, -1), (owners, BLOCKS * seqs))],
        axis=1,
    )
    told = exchange(told)
    everyone = told[:, marks:].reshape(-1)
    tables = owner_tables(told[:, :marks].reshape(-1), owners)
    both = range(HALVES)

    def start(b, half):
        return (b * HALVES + half) * owners

    me = lax.axis_index("op").astype(jnp.int32)[None]
    routed = owners < seqs
    if routed:
        route, lost = route_tables(everyone, me, owners, seqs)
    else:
        lost = jnp.zeros((1,), jnp.int32)
    lost = lax.psum(jnp.concatenate([lost, tables[1]]), "dp")
    totals = lost[1:].reshape(BLOCKS, HALVES, 8).sum(axis=1).astype(F32)

    x0 = [
        exchange(
            move_rows(send, [start(0, h)], [inputs], owners, False, "send_inputs", (lost,) * h if routed else ())
        )
        for h in both
    ]
    first = owner_forward(0, 0, tables, x0[0], weights, smalls[0], None)
    leaving = bring_rows(route, 0, [first[0]], "hop_x") if routed else None

    def on_the_way(table, sources, name):
        return bring_rows(route, table * owners, sources, name)

    def straight_there(y):
        hop0 = exchange(leaving)
        hop1 = exchange(on_the_way(1, [hop0, y[1]], "hop_x"))
        hop2 = exchange(on_the_way(2, [y[1], hop1], "hop_x"))
        return [on_the_way(3, [hop0, hop1], "land_x"), on_the_way(4, [hop2], "land_x")]

    def straight_back(dx):
        hop0 = exchange(on_the_way(5, [dx[1]], "hop_dx"))
        hop1 = exchange(on_the_way(6, [dx[0], hop0], "hop_dx"))
        hop2 = exchange(on_the_way(7, [dx[0], hop1], "hop_dx"))
        return [on_the_way(9, [hop2], "land_dx"), on_the_way(8, [hop0, hop1], "land_dx")]

    def home_there(y):
        return [
            exchange(move_rows(relay, [start(0, h)], [exchange(y[h])], owners, False, "relay_x"))
            for h in both
        ]

    def home_back(dx):
        return [
            exchange(move_rows(relay, [start(1, h)], [exchange(dx[h])], owners, False, "relay_dx"))
            for h in both
        ]

    def after_first(there, back, x0, first):
        y00, kept_f, ka0, kc0 = first
        y01, kept_f, ka1, kc1 = owner_forward(
            0, 1, tables, x0[1], weights, smalls[0], kept_f
        )
        kept0 = (kept_f, [ka0, ka1], [kc0, kc1])
        x1 = there([y00, y01])
        y1, kept1 = both_forward(1, tables, x1, weights, smalls[1])
        dy1 = [
            exchange(
                move_rows(
                    send,
                    [start(1, h)],
                    [cotangent],
                    owners,
                    False,
                    "send_cotangent",
                    (y1[1 - h],),
                )
            )
            for h in both
        ]
        dx1, feed1, rest1 = owner_backward(
            1, tables, x1, dy1, kept1, weights, smalls[1], groups, ()
        )
        feed1 = group_sum(feed1)
        rest1 = group_sum(rest1)
        dy0 = back(dx1)
        dx0, feed0, rest0 = owner_backward(
            0, tables, x0, dy0, kept0, weights, smalls[0], groups, (feed1,)
        )
        feed0 = group_sum(feed0)
        rest0 = group_sum(rest0)
        y_home = [exchange(after(y1[h], (dy0[0],))) for h in both]
        outputs = move_rows(send, [start(1, h) for h in both], y_home, seqs, True, "outputs")
        dx_home = [
            exchange(after(dx0[0], (feed0,))),
            exchange(after(dx0[1], (rest1,))),
        ]
        input_grad = move_rows(
            send, [start(0, h) for h in both], dx_home, seqs, True, "input_grad"
        )
        tall, deep = width // groups, hidden // groups
        grad = lambda *dims: jax.ShapeDtypeStruct((BLOCKS, 1) + dims, F32)
        feed_shapes = (grad(tall, hidden), grad(deep, width))
        rest_shapes = (
            grad(tall, 3 * width),
            grad(tall, width),
            jax.ShapeDtypeStruct((BLOCKS, 15, 1, tall), F32),
            grad(KINDS - 2, tall, width),
            jax.ShapeDtypeStruct((BLOCKS, KINDS, 1, tall), F32),
            jax.ShapeDtypeStruct((BLOCKS, KINDS, 1, tall), F32),
        )
        feeds = finish_feed(1, feed1, totals, None, None, feed_shapes)
        rests = finish_rest(1, rest1, totals, (), rest_shapes, ())
        feeds = finish_feed(0, feed0, totals, *feeds, feed_shapes)
        rests = finish_rest(0, rest0, totals, rests, rest_shapes, (outputs, input_grad, feeds[0]))
        qkv, out, taps, point, gain, shift = rests
        return (outputs, input_grad, qkv, out, *feeds, taps, point, gain, shift)

    def in_place(results):
        turned = [rows.transpose(0, 2, 1, 3) if n in (6, 8, 9) else rows for n, rows in enumerate(results)]
        return tuple(turned)

    if not routed:
        return in_place(after_first(home_there, home_back, x0, first))
    results = lax.cond(
        lost[0] == 0,
        lambda x0, first: after_first(straight_there, straight_back, x0, first),
        lambda x0, first: after_first(home_there, home_back, x0, first),
        x0,
        first,
    )
    return in_place(results)


def solution(mesh):
    placed = (
        P(("dp", "op"), None, None),
        P(("dp", "op"), None),
        P(None, "op", None, None),
        P(None, "op", None, None),
        P(None, "op", None, None),
        P(None, "op", None, None),
        P(None, "op", None, None),
        P(None, "op", None, None, None),
        P(None, "op", None, None),
        P(None, "op", None, None),
        P(("dp", "op"), None, None),
    )
    return jax.shard_map(
        per_device,
        mesh=mesh,
        in_specs=placed,
        out_specs=(
            P(("dp", "op"), None, None),
            P(("dp", "op"), None, None),
            P(None, "op", "dp", None),
            P(None, "op", "dp", None),
            P(None, "op", "dp", None),
            P(None, "op", "dp", None),
            P(None, "op", None, "dp"),
            P(None, "op", None, "dp", None),
            P(None, "op", None, "dp"),
            P(None, "op", None, "dp"),
        ),
        check_vma=False,
    )
```

```python
import jax
import jax.numpy as jnp
from jax import lax
from jax.experimental import pallas as pl
from jax.experimental.pallas import tpu as pltpu
from jax.sharding import PartitionSpec as P

HEADS = 12
KINDS = 5
BLOCKS = 2
OWN_CAP = 3
HALVES = 2
SLOTS = KINDS * OWN_CAP
FF_PART = 768
FF_SUB = 256
LANES = 128
SMALL_ROWS = 32
BF16 = jnp.bfloat16
F32 = jnp.float32
VMEM_BYTES = 60 * 2**20


def params_of(axes):
    return pltpu.CompilerParams(
        dimension_semantics=("arbitrary",) * axes, vmem_limit_bytes=VMEM_BYTES
    )


def nn(a, b):
    return lax.dot_general(a, b, (((1,), (0,)), ((), ())), preferred_element_type=F32)


def nt(a, b):
    return lax.dot_general(a, b, (((1,), (1,)), ((), ())), preferred_element_type=F32)


def tn(a, b):
    return lax.dot_general(a, b, (((0,), (0,)), ((), ())), preferred_element_type=F32)


def colour_home(owners, seqs, home, cand, color, partner, first, tally):
    base = home * seqs

    def clear_owner(o, _):
        first[o] = -1
        return 0

    lax.fori_loop(0, BLOCKS * owners, clear_owner, 0)
    for half in range(HALVES):
        tally[half] = 0

    def pair_up(j, _):
        color[base + j] = -1
        for b in range(BLOCKS):
            o = b * owners + lax.rem(cand[(base + j) * BLOCKS + b], owners)
            other = first[o]
            partner[b * seqs + j] = other
            first[o] = j

            @pl.when(other >= 0)
            def _():
                partner[b * seqs + other] = j

        return 0

    lax.fori_loop(0, seqs, pair_up, 0)

    def give(j, shade):
        color[base + j] = shade
        tally[shade] = tally[shade] + 1

    def paint(j, _):
        @pl.when(color[base + j] < 0)
        def _():
            shade = jnp.where(tally[0] > tally[1], 1, 0).astype(jnp.int32)
            give(j, shade)
            for side in range(2):

                def more(state):
                    return state[0] >= 0

                def walk(state):
                    now, use, tone = state
                    then = partner[use * seqs + now]
                    free = jnp.logical_and(then >= 0, color[base + jnp.maximum(then, 0)] < 0)

                    @pl.when(free)
                    def _():
                        give(then, 1 - tone)

                    return (jnp.where(free, then, -1), 1 - use, 1 - tone)

                lax.while_loop(more, walk, (j, jnp.int32(side), shade))

        return 0

    lax.fori_loop(0, seqs, paint, 0)


def home_kernel(owners, seqs, cand, send, relay, tags, color, partner, first, tally):
    told = BLOCKS * (HALVES + seqs)

    def tell(n, _):
        value = cand[n]
        for o in range(owners):
            tags[o * told + BLOCKS * HALVES + n] = value
        return 0

    lax.fori_loop(0, BLOCKS * seqs, tell, 0)
    for b in range(BLOCKS):

        def clear_owner(o, _):
            for half in range(HALVES):
                send[(b * HALVES + half) * owners + o] = -1
                relay[(b * HALVES + half) * owners + o] = -1
                tags[o * told + b * HALVES + half] = KINDS
            return 0

        lax.fori_loop(0, owners, clear_owner, 0)
    colour_home(owners, seqs, 0, cand, color, partner, first, tally)

    def place(j, _):
        half = color[j]
        spots = []
        for b in range(BLOCKS):
            c = cand[j * BLOCKS + b]
            o = lax.rem(c, owners)
            spots.append(o)
            send[(b * HALVES + half) * owners + o] = j
            tags[o * told + b * HALVES + half] = lax.div(c, owners)
        relay[half * owners + spots[1]] = spots[0]
        relay[(HALVES + half) * owners + spots[0]] = spots[1]
        return 0

    lax.fori_loop(0, seqs, place, 0)


ROUTES = 10
TRIES = 24


def route_kernel(
    owners, seqs, cand, me_ref, out, ok, color, partner, first, tally, leave, goal, hops, spill
):
    me = me_ref[0]
    square = owners * owners

    def colour(home, _):
        colour_home(owners, seqs, home, cand, color, partner, first, tally)
        return 0

    lax.fori_loop(0, owners, colour, 0)

    def ends(q, _):
        leave[q] = lax.rem(cand[q * BLOCKS], owners)
        goal[q] = lax.rem(cand[q * BLOCKS + 1], owners)
        return 0

    lax.fori_loop(0, owners * seqs, ends, 0)

    def attempt(state):
        turn, _ = state

        def clear(n, _):
            hops[n] = -1
            return 0

        lax.fori_loop(0, 3 * square, clear, 0)

        def direct(q, spilt):
            at = color[q] * 2 * square + leave[q] * owners + goal[q]
            free = hops[at] < 0

            @pl.when(free)
            def _():
                hops[at] = q

            @pl.when(jnp.logical_not(free))
            def _():
                spill[spilt] = q

            return jnp.where(free, spilt, spilt + 1)

        spilt = lax.fori_loop(0, owners * seqs, direct, jnp.int32(0))
        begin = lax.rem(turn * 5, jnp.maximum(spilt, 1))

        def two_hops(n, lost):
            q = spill[lax.rem(begin + n, jnp.maximum(spilt, 1))]
            o, p = leave[q], goal[q]
            early = color[q] * square
            shift = o * 3 + p * 5 + (n + 1) * turn

            def look(s, found):
                i = lax.rem(shift + s, owners)
                a = early + o * owners + i
                b = early + square + i * owners + p
                good = jnp.logical_and(hops[a] < 0, hops[b] < 0)
                return jnp.where(jnp.logical_and(good, found < 0), i, found)

            i = lax.fori_loop(0, owners, look, jnp.int32(-1))

            @pl.when(i >= 0)
            def _():
                hops[early + o * owners + i] = q
                hops[early + square + i * owners + p] = q

            return jnp.where(i >= 0, lost, lost + 1)

        lost = lax.fori_loop(0, spilt, two_hops, jnp.int32(0))
        return turn + 1, lost

    def again(state):
        return jnp.logical_and(state[0] < TRIES, state[1] > 0)

    _, lost = lax.while_loop(again, attempt, (jnp.int32(0), jnp.int32(1)))
    ok[0] = lost

    def clear_out(n, _):
        out[n] = -1
        return 0

    lax.fori_loop(0, ROUTES * owners, clear_out, 0)

    def note(d, _):
        def home(q):
            return lax.div(q, seqs)

        def put(table, at, value):
            out[table * owners + at] = value

        q = hops[me * owners + d]

        @pl.when(q >= 0)
        def _():
            put(0, d, home(q))
            put(9, home(q), d)

        q1 = hops[square + me * owners + d]

        @pl.when(q1 >= 0)
        def _():
            late = color[q1] == 1
            put(1, d, jnp.where(late, owners + home(q1), leave[q1]))

            @pl.when(late)
            def _():
                put(8, home(q1), owners + d)

        q2 = hops[2 * square + me * owners + d]

        @pl.when(q2 >= 0)
        def _():
            mine = leave[q2] == me
            put(2, d, jnp.where(mine, home(q2), owners + leave[q2]))

            @pl.when(mine)
            def _():
                put(8, home(q2), d)

        r = hops[d * owners + me]

        @pl.when(r >= 0)
        def _():
            there = goal[r] == me
            put(7, d, jnp.where(there, home(r), owners + goal[r]))

            @pl.when(there)
            def _():
                put(3, home(r), d)

        r1 = hops[square + d * owners + me]

        @pl.when(r1 >= 0)
        def _():
            late = color[r1] == 1
            put(6, d, jnp.where(late, owners + goal[r1], home(r1)))

            @pl.when(jnp.logical_not(late))
            def _():
                put(3, home(r1), owners + d)

        r2 = hops[2 * square + d * owners + me]

        @pl.when(r2 >= 0)
        def _():
            put(4, home(r2), d)
            put(5, d, home(r2))

        return 0

    lax.fori_loop(0, owners, note, 0)


SMEM_SPEC = pl.BlockSpec(memory_space=pltpu.SMEM)
ANY_SPEC = pl.BlockSpec(memory_space=pl.ANY)


def int_shape(n):
    return jax.ShapeDtypeStruct((n,), jnp.int32)


def home_tables(cand, owners, seqs):
    def kernel(*refs):
        home_kernel(owners, seqs, *refs)

    size = BLOCKS * HALVES * owners
    return pl.pallas_call(
        kernel,
        in_specs=[SMEM_SPEC],
        out_specs=[SMEM_SPEC] * 3,
        out_shape=[
            int_shape(size),
            int_shape(size),
            int_shape(owners * BLOCKS * (HALVES + seqs)),
        ],
        scratch_shapes=[
            pltpu.SMEM((seqs,), jnp.int32),
            pltpu.SMEM((BLOCKS * seqs,), jnp.int32),
            pltpu.SMEM((BLOCKS * owners,), jnp.int32),
            pltpu.SMEM((HALVES,), jnp.int32),
        ],
        name="home_tables",
    )(cand)


def owner_kernel(owners, tags, rows, counts):
    for b in range(BLOCKS):
        for half in range(HALVES):
            part = b * HALVES + half
            for k in range(8):
                counts[part * 8 + k] = 0

            def arrive(h, free):
                k = tags[h * BLOCKS * HALVES + part]
                there = k < KINDS

                @pl.when(there)
                def _():
                    n = jnp.minimum(counts[part * 8 + k], OWN_CAP - 1)
                    rows[part * SLOTS + k * OWN_CAP + n] = h
                    counts[part * 8 + k] = n + 1

                return jnp.where(there, free, h)

            free = lax.fori_loop(0, owners, arrive, jnp.int32(0))

            def spare(k, otherwise):
                return jnp.where(
                    counts[part * 8 + k] > 0, rows[part * SLOTS + k * OWN_CAP], otherwise
                )

            conv_spare = free
            for k in reversed(range(1, KINDS - 1)):
                conv_spare = spare(k, conv_spare)
            attn_spare = spare(0, conv_spare)
            feed_spare = spare(KINDS - 1, attn_spare)
            last = conv_spare
            for k, start in ((1, None), (2, None), (3, None), (0, attn_spare), (KINDS - 1, feed_spare)):
                last = last if start is None else start
                for i in range(OWN_CAP):
                    at = part * SLOTS + k * OWN_CAP + i
                    last = jnp.where(i < counts[part * 8 + k], rows[at], last)
                    rows[at] = last


def owner_tables(tags, owners):
    def kernel(*refs):
        owner_kernel(owners, *refs)

    return pl.pallas_call(
        kernel,
        in_specs=[SMEM_SPEC],
        out_specs=[SMEM_SPEC] * 2,
        out_shape=[int_shape(BLOCKS * HALVES * SLOTS), int_shape(BLOCKS * HALVES * 8)],
        name="owner_tables",
    )(tags)


def route_tables(cand, me, owners, seqs):
    def kernel(*refs):
        route_kernel(owners, seqs, *refs)

    smem = lambda n: pltpu.SMEM((n,), jnp.int32)
    return pl.pallas_call(
        kernel,
        in_specs=[SMEM_SPEC] * 2,
        out_specs=[SMEM_SPEC] * 2,
        out_shape=[int_shape(ROUTES * owners), int_shape(1)],
        scratch_shapes=[
            smem(owners * seqs),
            smem(BLOCKS * seqs),
            smem(BLOCKS * owners),
            smem(HALVES),
            smem(owners * seqs),
            smem(owners * seqs),
            smem(3 * owners * owners),
            smem(owners * seqs),
        ],
        name="route_tables",
    )(cand, me)


def bring_rows(table, start, sources, name):
    count, length, width = sources[0].shape

    def kernel(table_ref, *refs):
        ins = refs[: len(sources)]
        out_ref, buf, sem_in, sem_out = refs[-4:]

        def loads(n):
            e = table_ref[start + n]
            last = count * (len(sources) - 1)
            for which, source in enumerate(ins):
                low = count * which
                here = e >= low
                if low < last:
                    here = jnp.logical_and(here, e < low + count)
                row = jnp.clip(e - low, 0, count - 1)
                yield here, pltpu.make_async_copy(source.at[row], buf.at[n], sem_in.at[n])

        def store(n):
            return pltpu.make_async_copy(buf.at[n], out_ref.at[n], sem_out.at[n])

        for n in range(count):
            for here, copy in loads(n):

                @pl.when(here)
                def _():
                    copy.start()

        for n in range(count):

            @pl.when(table_ref[start + n] >= 0)
            def _():
                pltpu.make_async_copy(ins[0].at[0], buf.at[n], sem_in.at[n]).wait()
                store(n).start()

        for n in range(count):

            @pl.when(table_ref[start + n] >= 0)
            def _():
                store(n).wait()

    return pl.pallas_call(
        kernel,
        grid_spec=pltpu.PrefetchScalarGridSpec(
            num_scalar_prefetch=1,
            grid=(1,),
            in_specs=[ANY_SPEC] * len(sources),
            out_specs=ANY_SPEC,
            scratch_shapes=[
                pltpu.VMEM((count, length, width), BF16),
                pltpu.SemaphoreType.DMA((count,)),
                pltpu.SemaphoreType.DMA((count,)),
            ],
        ),
        out_shape=jax.ShapeDtypeStruct((count, length, width), BF16),
        compiler_params=params_of(1),
        cost_estimate=pl.CostEstimate(
            flops=0, transcendentals=0, bytes_accessed=4 * count * length * width
        ),
        name=name,
    )(table, *sources)


def move_rows(table, starts, sources, count, scatter, name, wait_for=()):
    length, width = sources[0].shape[1:]
    each = table.shape[0] // (BLOCKS * HALVES)
    total = each * len(sources)

    def kernel(table_ref, *refs):
        ins = refs[: len(sources)]
        out_ref, buf, sem_in, sem_out = refs[-4:]

        def load(part, s):
            idx = table_ref[starts[part] + s]
            at = s if scatter else idx
            to = part * each + s
            return pltpu.make_async_copy(ins[part].at[at], buf.at[to], sem_in.at[to])

        def store(part, s):
            idx = table_ref[starts[part] + s]
            at = part * each + s
            to = idx if scatter else at
            return pltpu.make_async_copy(buf.at[at], out_ref.at[to], sem_out.at[at])

        todo = [(part, s) for part in range(len(sources)) for s in range(each)]
        for part, s in todo:

            @pl.when(table_ref[starts[part] + s] >= 0)
            def _():
                load(part, s).start()

        for part, s in todo:

            @pl.when(table_ref[starts[part] + s] >= 0)
            def _():
                load(part, s).wait()
                store(part, s).start()

        for part, s in todo:

            @pl.when(table_ref[starts[part] + s] >= 0)
            def _():
                store(part, s).wait()

    return pl.pallas_call(
        kernel,
        grid_spec=pltpu.PrefetchScalarGridSpec(
            num_scalar_prefetch=1,
            grid=(1,),
            in_specs=[ANY_SPEC] * (len(sources) + len(wait_for)),
            out_specs=ANY_SPEC,
            scratch_shapes=[
                pltpu.VMEM((total, length, width), BF16),
                pltpu.SemaphoreType.DMA((total,)),
                pltpu.SemaphoreType.DMA((total,)),
            ],
        ),
        out_shape=jax.ShapeDtypeStruct((count, length, width), BF16),
        compiler_params=params_of(1),
        cost_estimate=pl.CostEstimate(
            flops=0, transcendentals=0, bytes_accessed=4 * total * length * width
        ),
        name=name,
    )(table, *sources, *wait_for)


def after(value, earlier):
    def kernel(*refs):
        return

    return pl.pallas_call(
        kernel,
        in_specs=[ANY_SPEC] * (1 + len(earlier)),
        out_specs=ANY_SPEC,
        out_shape=jax.ShapeDtypeStruct(value.shape, value.dtype),
        input_output_aliases={0: 0},
        name="after",
    )(value, *earlier)


def norm_forward(summed, gain_row, shift_row):
    center = summed - jnp.mean(summed, axis=-1, keepdims=True)
    spread = jnp.mean(center * center, axis=-1, keepdims=True)
    scale = lax.rsqrt(spread + 1e-05)
    normed = center * scale
    return normed, normed * gain_row + shift_row, scale


def finish_forward(x, branch, gain_row, shift_row, y_ref, zn_ref, rstd_ref):
    normed, result, scale = norm_forward(x.astype(F32) + branch, gain_row, shift_row)
    y_ref[0] = result.astype(BF16)
    zn_ref[0] = normed.astype(BF16)
    rstd_ref[0] = jnp.broadcast_to(scale, rstd_ref.shape[1:])


def norm_backward(dy, zn_ref, rstd_ref, gain_row):
    dy = dy.astype(F32)
    normed = zn_ref[0].astype(F32)
    scale = rstd_ref[0][:, :1]
    scaled = dy * gain_row
    first = jnp.mean(scaled, axis=-1, keepdims=True)
    second = jnp.mean(scaled * normed, axis=-1, keepdims=True)
    gain_grad = jnp.sum(dy * normed, axis=0, keepdims=True)
    shift_grad = jnp.sum(dy, axis=0, keepdims=True)
    return (scaled - first - normed * second) * scale, gain_grad, shift_grad


def head_masks(length):
    lane = lax.broadcasted_iota(jnp.int32, (length, LANES), 1)
    low = lane < LANES // 2
    return low


def attention_forward(part, tables, x, weights, norms, y_in):
    rows, counts = tables
    b = part // HALVES
    attn_qkv, attn_out = weights
    gains, shifts = norms
    slots, length, width = x.shape
    score_scale = (width // HEADS) ** (-0.5)
    base = part * SLOTS

    def kernel(rows_ref, counts_ref, x_ref, qkv_w, out_w, gain, shift, *rest):
        y_ref, qkv_ref, o_ref, zn_ref, rstd_ref = rest[-5:]
        i = pl.program_id(0)

        @pl.when(i < counts_ref[part * 8])
        def _():
            xv = x_ref[0]
            for third in range(3):
                cols = slice(third * width, (third + 1) * width)
                qkv_ref[0, :, cols] = nn(xv, qkv_w[:, cols]).astype(BF16)
            low = head_masks(length)
            zero = jnp.zeros((), BF16)
            for pair in range(width // LANES):
                at = pair * LANES
                q2 = qkv_ref[0, :, at : at + LANES] * jnp.asarray(score_scale, BF16)
                k2 = qkv_ref[0, :, width + at : width + at + LANES]
                v2 = qkv_ref[0, :, 2 * width + at : 2 * width + at + LANES]
                mixed = []
                for half in range(2):
                    qm = jnp.where(low if half == 0 else ~low, q2, zero)
                    s = nt(qm, k2)
                    e = jnp.exp(s - jnp.max(s, axis=-1, keepdims=True))
                    total = jnp.sum(e, axis=-1, keepdims=True)
                    mixed.append(nn(e.astype(BF16), v2) / total)
                o_ref[0, :, at : at + LANES] = jnp.where(low, mixed[0], mixed[1]).astype(BF16)
            branch = nn(o_ref[0], out_w[...])
            finish_forward(
                xv, branch, gain[0:1, :], shift[0:1, :], y_ref, zn_ref, rstd_ref
            )

    def at_row(i, r, c):
        return (r[base + i], 0, 0)

    def at_step(i, r, c):
        return (jnp.maximum(jnp.minimum(i, c[part * 8] - 1), 0), 0, 0)

    seq = (1, length, width)
    in_specs = [
        pl.BlockSpec(seq, at_row),
        pl.BlockSpec(
            (None, None, width, 3 * width), lambda i, r, c: (b, 0, 0, 0), pipeline_mode=pl.Buffered(1)
        ),
        pl.BlockSpec(
            (None, None, width, width), lambda i, r, c: (b, 0, 0, 0), pipeline_mode=pl.Buffered(1)
        ),
        pl.BlockSpec((8, width), lambda i, r, c: (0, 0)),
        pl.BlockSpec((8, width), lambda i, r, c: (0, 0)),
    ]
    args = [rows, counts, x, attn_qkv, attn_out, gains, shifts]
    alias = {}
    if y_in is not None:
        in_specs.append(pl.BlockSpec(memory_space=pl.ANY))
        alias = {len(args): 0}
        args.append(y_in)
    flops = OWN_CAP * length * width * (8 * width + 4 * length)
    return pl.pallas_call(
        kernel,
        grid_spec=pltpu.PrefetchScalarGridSpec(
            num_scalar_prefetch=2,
            grid=(OWN_CAP,),
            in_specs=in_specs,
            out_specs=[
                pl.BlockSpec(seq, at_row),
                pl.BlockSpec((1, length, 3 * width), at_step),
                pl.BlockSpec(seq, at_step),
                pl.BlockSpec(seq, at_step),
                pl.BlockSpec((1, length, LANES), at_step),
            ],
        ),
        out_shape=[
            jax.ShapeDtypeStruct((slots, length, width), BF16),
            jax.ShapeDtypeStruct((OWN_CAP, length, 3 * width), BF16),
            jax.ShapeDtypeStruct((OWN_CAP, length, width), BF16),
            jax.ShapeDtypeStruct((OWN_CAP, length, width), BF16),
            jax.ShapeDtypeStruct((OWN_CAP, length, LANES), F32),
        ],
        input_output_aliases=alias,
        compiler_params=params_of(1),
        cost_estimate=pl.CostEstimate(
            flops=2 * flops, transcendentals=OWN_CAP * HEADS * length * length, bytes_accessed=30 * 2**20
        ),
        name="attention_forward",
    )(*args)


def attention_backward(part, tables, x, dy, kept, weights, gains, dx_in, sums, packed):
    rows, counts = tables
    b = part // HALVES
    attn_qkv, attn_out = weights
    qkv, o, zn, rstd = kept
    slots, length, width = x.shape
    score_scale = (width // HEADS) ** (-0.5)
    base = part * SLOTS
    first = sums is None
    n_out = 4 if first else 3

    def kernel(rows_ref, counts_ref, x_ref, dy_ref, qkv_ref, o_ref, zn_ref, rstd_ref, qkv_w, out_w, gain, *rest):
        ins = rest[: len(rest) - n_out - 7]
        outs = rest[len(ins) : len(ins) + n_out]
        acc_qkv, acc_out, do_scr, dqkv_scr, dh_scr, dz_scr, sems = rest[-7:]
        dx_ref, small_ref = outs[0], outs[1]
        i = pl.program_id(0)
        here = i < counts_ref[part * 8]

        def copies():
            if first:
                pairs = ((acc_qkv, outs[2]), (acc_out, outs[3]))
            else:
                pairs = ((ins[0], acc_qkv), (ins[1], acc_out))
            return [
                pltpu.make_async_copy(source, target, sems.at[n])
                for n, (source, target) in enumerate(pairs)
            ]

        @pl.when(i == 0)
        def _():
            small_ref[...] = jnp.zeros_like(small_ref)
            if first:
                acc_qkv[...] = jnp.zeros_like(acc_qkv)
                acc_out[...] = jnp.zeros_like(acc_out)
            else:
                for copy in copies():
                    copy.start()

        @pl.when(here)
        def _():
            dz, gain_grad, shift_grad = norm_backward(dy_ref[0], zn_ref, rstd_ref, gain[0:1, :])
            small_ref[0:1, :] += gain_grad
            small_ref[1:2, :] += shift_grad
            dz_scr[...] = dz
            dh = dz.astype(BF16)
            dh_scr[...] = dh
            do_scr[...] = nt(dh, out_w[...]).astype(BF16)
            low = head_masks(length)
            zero = jnp.zeros((), BF16)
            for pair in range(width // LANES):
                at = pair * LANES
                q2 = qkv_ref[0, :, at : at + LANES] * jnp.asarray(score_scale, BF16)
                k2 = qkv_ref[0, :, width + at : width + at + LANES]
                v2 = qkv_ref[0, :, 2 * width + at : 2 * width + at + LANES]
                do2 = do_scr[:, at : at + LANES]
                dqs, dks, dvs = [], [], []
                for half in range(2):
                    mask = low if half == 0 else ~low
                    st = nt(jnp.where(mask, k2, zero), q2)
                    e = jnp.exp(st - jnp.max(st, axis=0, keepdims=True))
                    p = e * (1.0 / jnp.sum(e, axis=0, keepdims=True))
                    dvs.append(nn(p.astype(BF16), do2))
                    t = p * nt(jnp.where(mask, v2, zero), do2)
                    ds = (t - p * jnp.sum(t, axis=0, keepdims=True)).astype(BF16)
                    dks.append(nn(ds, q2))
                    dqs.append(tn(ds, k2))
                dqkv_scr[:, at : at + LANES] = (jnp.where(low, dqs[0], dqs[1]) * score_scale).astype(BF16)
                dqkv_scr[:, width + at : width + at + LANES] = jnp.where(low, dks[0], dks[1]).astype(BF16)
                dqkv_scr[:, 2 * width + at : 2 * width + at + LANES] = jnp.where(low, dvs[0], dvs[1]).astype(BF16)
            total = dz_scr[...]
            for third in range(3):
                cols = slice(third * width, (third + 1) * width)
                total = total + nt(dqkv_scr[:, cols], qkv_w[:, cols])
            dx_ref[0] = total.astype(BF16)

        if not first:

            @pl.when(i == 0)
            def _():
                for copy in copies():
                    copy.wait()

        @pl.when(here)
        def _():
            xv = x_ref[0]
            for third in range(3):
                cols = slice(third * width, (third + 1) * width)
                acc_qkv[:, cols] += tn(xv, dqkv_scr[:, cols])
            acc_out[...] += tn(o_ref[0], dh_scr[...])

        @pl.when(i == OWN_CAP - 1)
        def _():
            if first:
                for copy in copies():
                    copy.start()
                for copy in copies():
                    copy.wait()
            else:
                packed_ref = outs[2]
                groups, tall = packed_ref.shape[0], packed_ref.shape[1] // 4
                for third in range(3):
                    piece = acc_qkv[:, third * width : (third + 1) * width].astype(BF16)
                    packed_ref[:, third * tall : (third + 1) * tall, :] = piece.reshape(
                        groups, tall, width
                    )
                packed_ref[:, 3 * tall : 4 * tall, :] = (
                    acc_out[...].astype(BF16).reshape(groups, tall, width)
                )

    def at_row(i, r, c):
        return (r[base + i], 0, 0)

    def at_step(i, r, c):
        return (jnp.maximum(jnp.minimum(i, c[part * 8] - 1), 0), 0, 0)

    def whole(i, r, c):
        return (0, 0)

    seq = (1, length, width)
    in_specs = [
        pl.BlockSpec(seq, at_row),
        pl.BlockSpec(seq, at_row),
        pl.BlockSpec((1, length, 3 * width), at_step),
        pl.BlockSpec(seq, at_step),
        pl.BlockSpec(seq, at_step),
        pl.BlockSpec((1, length, LANES), at_step),
        pl.BlockSpec(
            (None, None, width, 3 * width), lambda i, r, c: (b, 0, 0, 0), pipeline_mode=pl.Buffered(1)
        ),
        pl.BlockSpec(
            (None, None, width, width), lambda i, r, c: (b, 0, 0, 0), pipeline_mode=pl.Buffered(1)
        ),
        pl.BlockSpec((8, width), whole),
    ]
    args = [rows, counts, x, dy, qkv, o, zn, rstd, attn_qkv, attn_out, gains]
    out_specs = [pl.BlockSpec(seq, at_row), pl.BlockSpec((8, width), whole)]
    out_shape = [
        jax.ShapeDtypeStruct((slots, length, width), BF16),
        jax.ShapeDtypeStruct((8, width), F32),
    ]
    if first:
        out_specs += [ANY_SPEC, ANY_SPEC]
        out_shape += [
            jax.ShapeDtypeStruct((width, 3 * width), F32),
            jax.ShapeDtypeStruct((width, width), F32),
        ]
    else:
        groups, total_rows = packed
        out_specs.append(
            pl.BlockSpec((groups, 4 * width // groups, width), lambda i, r, c: (0, 0, 0))
        )
        out_shape.append(jax.ShapeDtypeStruct((groups, total_rows, width), BF16))
        in_specs += [ANY_SPEC, ANY_SPEC]
        args += list(sums)
    alias = {}
    if dx_in is not None:
        in_specs.append(ANY_SPEC)
        alias = {len(args): 0}
        args.append(dx_in)
    flops = 2 * OWN_CAP * length * width * (8 * width + 4 * length)
    return pl.pallas_call(
        kernel,
        grid_spec=pltpu.PrefetchScalarGridSpec(
            num_scalar_prefetch=2,
            grid=(OWN_CAP,),
            in_specs=in_specs,
            out_specs=out_specs,
            scratch_shapes=[
                pltpu.VMEM((width, 3 * width), F32),
                pltpu.VMEM((width, width), F32),
                pltpu.VMEM((length, width), BF16),
                pltpu.VMEM((length, 3 * width), BF16),
                pltpu.VMEM((length, width), BF16),
                pltpu.VMEM((length, width), F32),
                pltpu.SemaphoreType.DMA((2,)),
            ],
        ),
        out_shape=out_shape,
        input_output_aliases=alias,
        compiler_params=params_of(1),
        cost_estimate=pl.CostEstimate(
            flops=flops, transcendentals=OWN_CAP * HEADS * length * length // 2, bytes_accessed=40 * 2**20
        ),
        name="attention_backward",
    )(*args)


def feed_forward(part, tables, x, weights, norms, earlier):
    rows, counts = tables
    b = part // HALVES
    ffn_up, ffn_down = weights
    gains, shifts = norms
    slots, length, width = x.shape
    hidden = ffn_up.shape[-1]
    parts = hidden // FF_PART
    kind = KINDS - 1
    base = part * SLOTS + kind * OWN_CAP

    def kernel(rows_ref, counts_ref, x_ref, up, down, gain, shift, *rest):
        y_ref, g_ref, slope_ref, zn_ref, rstd_ref, x_scr, h_scr = rest[-7:]
        c, i = pl.program_id(0), pl.program_id(1)

        @pl.when(i < counts_ref[part * 8 + kind])
        def _():
            @pl.when(c == 0)
            def _():
                x_scr[i] = x_ref[0]

            xv = x_scr[i]
            for sub in range(FF_PART // FF_SUB):
                cols = slice(sub * FF_SUB, (sub + 1) * FF_SUB)
                a = nn(xv, up[:, cols])
                phi = 0.5 + 0.5 * lax.erf(a * (0.5**0.5))
                slope = phi + a * (jnp.exp(a * a * -0.5) * 0.3989422804014327)
                g = (a * phi).astype(BF16)
                g_ref[0, :, cols] = g
                slope_ref[0, :, cols] = slope.astype(BF16)
            branch = nn(g_ref[0], down[...])

            @pl.when(c == 0)
            def _():
                h_scr[i] = branch

            @pl.when(jnp.logical_and(c > 0, c < parts - 1))
            def _():
                h_scr[i] += branch

            @pl.when(c == parts - 1)
            def _():
                finish_forward(
                    xv,
                    h_scr[i] + branch,
                    gain[kind : kind + 1, :],
                    shift[kind : kind + 1, :],
                    y_ref,
                    zn_ref,
                    rstd_ref,
                )

    def in_row(c, i, r, n):
        return (r[base + jnp.where(c == 0, i, OWN_CAP - 1)], 0, 0)

    def out_row(c, i, r, n):
        return (r[base + jnp.where(c == parts - 1, i, 0)], 0, 0)

    def place(i, n):
        at = jnp.maximum(jnp.minimum(i, n[part * 8 + kind] - 1), 0)
        return at if part == b * HALVES else at + n[b * HALVES * 8 + kind]

    def out_step(c, i, r, n):
        return (place(jnp.where(c == parts - 1, i, 0), n), 0, 0)

    def part_step(c, i, r, n):
        return (place(i, n), 0, c)

    seq = (1, length, width)
    in_specs = [
        pl.BlockSpec(seq, in_row),
        pl.BlockSpec((None, None, width, FF_PART), lambda c, i, r, n: (b, 0, 0, c)),
        pl.BlockSpec((None, None, FF_PART, width), lambda c, i, r, n: (b, 0, c, 0)),
        pl.BlockSpec((8, width), lambda c, i, r, n: (0, 0)),
        pl.BlockSpec((8, width), lambda c, i, r, n: (0, 0)),
    ]
    args = [rows, counts, x, ffn_up, ffn_down, gains, shifts]
    alias = {}
    for n, kept in enumerate(earlier or ()):
        in_specs.append(ANY_SPEC)
        alias[len(args)] = 1 + n
        args.append(kept)
    return pl.pallas_call(
        kernel,
        grid_spec=pltpu.PrefetchScalarGridSpec(
            num_scalar_prefetch=2,
            grid=(parts, OWN_CAP),
            in_specs=in_specs,
            out_specs=[
                pl.BlockSpec(seq, out_row),
                pl.BlockSpec((1, length, FF_PART), part_step),
                pl.BlockSpec((1, length, FF_PART), part_step),
                pl.BlockSpec(seq, out_step),
                pl.BlockSpec((1, length, LANES), out_step),
            ],
            scratch_shapes=[
                pltpu.VMEM((OWN_CAP, length, width), BF16),
                pltpu.VMEM((OWN_CAP, length, width), F32),
            ],
        ),
        out_shape=[
            jax.ShapeDtypeStruct((slots, length, width), BF16),
            jax.ShapeDtypeStruct((OWN_CAP + 1, length, hidden), BF16),
            jax.ShapeDtypeStruct((OWN_CAP + 1, length, hidden), BF16),
            jax.ShapeDtypeStruct((OWN_CAP + 1, length, width), BF16),
            jax.ShapeDtypeStruct((OWN_CAP + 1, length, LANES), F32),
        ],
        input_output_aliases=alias,
        compiler_params=params_of(2),
        cost_estimate=pl.CostEstimate(
            flops=4 * OWN_CAP * length * width * hidden,
            transcendentals=2 * OWN_CAP * length * hidden,
            bytes_accessed=40 * 2**20,
        ),
        name="feed_forward",
    )(*args)


def feed_backward(b, tables, x, dy, kept, weights, gains, dx_lead, lead, groups, wait_for):
    rows, counts = tables
    ffn_up, ffn_down = weights
    g, slope, zn, rstd = kept
    slots, length, width = x[0].shape
    hidden = ffn_up.shape[-1]
    parts = hidden // FF_PART
    kind = KINDS - 1
    bases = [(b * HALVES + half) * SLOTS + kind * OWN_CAP for half in range(HALVES)]
    tall = width // groups
    deep = hidden // groups
    shares = FF_PART // deep

    def present(n, half):
        return n[(b * HALVES + half) * 8 + kind]

    def kernel(
        rows_ref,
        counts_ref,
        x_ref0,
        x_ref1,
        dy_ref0,
        dy_ref1,
        g_ref,
        slope_ref,
        zn_ref,
        rstd_ref,
        up,
        down,
        gain,
        *rest,
    ):
        (
        small_ref,
        dx_ref0,
        dx_ref1,
        packed_ref,
        x_scr,
        dh_scr,
        dx_scr,
        da_scr,
        acc_up,
        acc_down,
        low_up,
        low_down,
        low_dx,
        sems,
        dx_sem,
        ) = rest[-15:]
        c, i = pl.program_id(0), pl.program_id(1)
        n0 = present(counts_ref, 0)
        total_n = n0 + present(counts_ref, 1)
        in_first = i < n0

        @pl.when(jnp.logical_and(c == 0, i == 0))
        def _():
            small_ref[...] = jnp.zeros_like(small_ref)

        @pl.when(i == 0)
        def _():
            acc_up[...] = jnp.zeros_like(acc_up)
            acc_down[...] = jnp.zeros_like(acc_down)

        @pl.when(i < total_n)
        def _():
            @pl.when(c == 0)
            def _():
                dz, gain_grad, shift_grad = norm_backward(
                    jnp.where(in_first, dy_ref0[0], dy_ref1[0]),
                    zn_ref,
                    rstd_ref,
                    gain[kind : kind + 1, :],
                )
                small_ref[0:1, :] += gain_grad
                small_ref[1:2, :] += shift_grad
                x_scr[i] = jnp.where(in_first, x_ref0[0], x_ref1[0])
                dh_scr[i] = dz.astype(BF16)
                dx_scr[i] = dz

            dh = dh_scr[i]
            for sub in range(FF_PART // FF_SUB):
                cols = slice(sub * FF_SUB, (sub + 1) * FF_SUB)
                dg = nt(dh, down[cols, :])
                da_scr[:, cols] = (dg * slope_ref[0, :, cols].astype(F32)).astype(BF16)
            acc_down[...] += tn(g_ref[0], dh)
            acc_up[...] += tn(x_scr[i], da_scr[...])
            total = dx_scr[i] + nt(da_scr[...], up[...])

            @pl.when(c < parts - 1)
            def _():
                dx_scr[i] = total

            @pl.when(c == parts - 1)
            def _():
                low_dx[...] = total.astype(BF16)
                for half, (inside, dx_ref) in enumerate(
                    ((in_first, dx_ref0), (jnp.logical_not(in_first), dx_ref1))
                ):

                    @pl.when(inside)
                    def _():
                        row = rows_ref[bases[half] + jnp.where(in_first, i, jnp.maximum(i - n0, 0))]
                        copy = pltpu.make_async_copy(low_dx, dx_ref.at[row], dx_sem)
                        copy.start()
                        copy.wait()

        def copies():
            pairs = [
                (low_up.at[pl.ds(z * tall, tall)], packed_ref.at[z, pl.ds(c * tall, tall)])
                for z in range(groups)
            ]
            pairs += [
                (
                    low_down.at[pl.ds(m * deep, deep)],
                    packed_ref.at[c * shares + m, pl.ds(parts * tall, deep)],
                )
                for m in range(shares)
            ]
            return [
                pltpu.make_async_copy(source, target, sems.at[n])
                for n, (source, target) in enumerate(pairs)
            ]

        @pl.when(i == OWN_CAP - 1)
        def _():
            @pl.when(c > 0)
            def _():
                for copy in copies():
                    copy.wait()

            low_up[...] = acc_up[...].astype(BF16)
            low_down[...] = acc_down[...].astype(BF16)
            for copy in copies():
                copy.start()

            @pl.when(c == parts - 1)
            def _():
                for copy in copies():
                    copy.wait()

    def first_row(c, i, r, n):
        return (r[bases[0] + jnp.where(c == 0, i, OWN_CAP - 1)], 0, 0)

    def second_row(c, i, r, n):
        at = jnp.where(c == 0, i, OWN_CAP - 1) - present(n, 0)
        return (r[bases[1] + jnp.maximum(at, 0)], 0, 0)

    def last(n):
        return present(n, 0) + present(n, 1) - 1

    def in_step(c, i, r, n):
        return (jnp.where(c == 0, jnp.minimum(i, last(n)), last(n)), 0, 0)

    def part_step(c, i, r, n):
        return (jnp.minimum(i, last(n)), 0, c)

    seq = (1, length, width)
    in_specs = [
        pl.BlockSpec(seq, first_row),
        pl.BlockSpec(seq, second_row),
        pl.BlockSpec(seq, first_row),
        pl.BlockSpec(seq, second_row),
        pl.BlockSpec((1, length, FF_PART), part_step),
        pl.BlockSpec((1, length, FF_PART), part_step),
        pl.BlockSpec(seq, in_step),
        pl.BlockSpec((1, length, LANES), in_step),
        pl.BlockSpec((None, None, width, FF_PART), lambda c, i, r, n: (b, 0, 0, c)),
        pl.BlockSpec((None, None, FF_PART, width), lambda c, i, r, n: (b, 0, c, 0)),
        pl.BlockSpec((8, width), lambda c, i, r, n: (0, 0)),
        ANY_SPEC,
    ] + [ANY_SPEC] * len(wait_for)
    args = [rows, counts, *x, *dy, g, slope, zn, rstd, ffn_up, ffn_down, gains, dx_lead]
    alias = {len(args) - 1: 1 + lead}
    args += wait_for
    return pl.pallas_call(
        kernel,
        grid_spec=pltpu.PrefetchScalarGridSpec(
            num_scalar_prefetch=2,
            grid=(parts, OWN_CAP),
            in_specs=in_specs,
            out_specs=[
                pl.BlockSpec((8, width), lambda c, i, r, n: (0, 0)),
                ANY_SPEC,
                ANY_SPEC,
                ANY_SPEC,
            ],
            scratch_shapes=[
                pltpu.VMEM((OWN_CAP, length, width), BF16),
                pltpu.VMEM((OWN_CAP, length, width), BF16),
                pltpu.VMEM((OWN_CAP, length, width), F32),
                pltpu.VMEM((length, FF_PART), BF16),
                pltpu.VMEM((width, FF_PART), F32),
                pltpu.VMEM((FF_PART, width), F32),
                pltpu.VMEM((width, FF_PART), BF16),
                pltpu.VMEM((FF_PART, width), BF16),
                pltpu.VMEM((length, width), BF16),
                pltpu.SemaphoreType.DMA((groups + shares,)),
                pltpu.SemaphoreType.DMA,
            ],
        ),
        out_shape=[
            jax.ShapeDtypeStruct((8, width), F32),
            jax.ShapeDtypeStruct((slots, length, width), BF16),
            jax.ShapeDtypeStruct((slots, length, width), BF16),
            jax.ShapeDtypeStruct((groups, parts * tall + deep, width), BF16),
        ],
        input_output_aliases=alias,
        compiler_params=params_of(2),
        cost_estimate=pl.CostEstimate(
            flops=7 * OWN_CAP * length * width * hidden,
            transcendentals=0,
            bytes_accessed=50 * 2**20,
        ),
        name="feed_backward",
    )(*args)


PAD = 8
ROW_TILE = 128
COL_TILE = 256


def fill_padded(padded, values):
    length = values.shape[0]
    edge = jnp.zeros((PAD, values.shape[1]), F32)
    padded[0:PAD, :] = edge
    padded[PAD + length : PAD + length + PAD, :] = edge
    padded[PAD : PAD + length, :] = values


def conv_forward(part, tables, x, weights, norms, y_in):
    rows, counts = tables
    b = part // HALVES
    taps, conv_point = weights
    gains, shifts = norms
    slots, length, width = x.shape
    base = part * SLOTS + OWN_CAP
    steps = (KINDS - 2) * OWN_CAP

    def kernel(rows_ref, counts_ref, x_ref, point, taps_ref, gain, shift, *rest):
        y_ref, u_ref, zn_ref, rstd_ref, xpad = rest[-5:]
        step = pl.program_id(0)
        which, j = step // OWN_CAP, step % OWN_CAP
        for kind in range(1, KINDS - 1):
            taps_n = 2 * kind + 1
            first = kind * kind - 1

            @pl.when(jnp.logical_and(which == kind - 1, j < counts_ref[part * 8 + kind]))
            def _():
                fill_padded(xpad, x_ref[0].astype(F32))
                for r in range(0, length, ROW_TILE):
                    for col in range(0, width, COL_TILE):
                        cols = slice(col, col + COL_TILE)
                        mixed = None
                        for t in range(taps_n):
                            start = PAD + r + t - kind
                            term = xpad[start : start + ROW_TILE, cols] * taps_ref[first + t : first + t + 1, cols]
                            mixed = term if mixed is None else mixed + term
                        u_ref[0, r : r + ROW_TILE, cols] = mixed.astype(BF16)
                branch = nn(u_ref[0], point[...])
                finish_forward(
                    x_ref[0],
                    branch,
                    gain[kind : kind + 1, :],
                    shift[kind : kind + 1, :],
                    y_ref,
                    zn_ref,
                    rstd_ref,
                )

    def at_row(i, r, c):
        return (r[base + i], 0, 0)

    def at_step(i, r, c):
        which = i // OWN_CAP
        last = c[part * 8 + 1 + which] - 1
        return (which * OWN_CAP + jnp.maximum(jnp.minimum(i % OWN_CAP, last), 0), 0, 0)

    def whole(i, r, c):
        return (0, 0)

    seq = (1, length, width)
    in_specs = [
        pl.BlockSpec(seq, at_row),
        pl.BlockSpec((None, None, None, width, width), lambda i, r, c: (b, 0, i // OWN_CAP, 0, 0)),
        pl.BlockSpec((16, width), whole),
        pl.BlockSpec((8, width), whole),
        pl.BlockSpec((8, width), whole),
    ]
    args = [rows, counts, x, conv_point, taps, gains, shifts]
    alias = {}
    if y_in is not None:
        in_specs.append(pl.BlockSpec(memory_space=pl.ANY))
        alias = {len(args): 0}
        args.append(y_in)
    return pl.pallas_call(
        kernel,
        grid_spec=pltpu.PrefetchScalarGridSpec(
            num_scalar_prefetch=2,
            grid=(steps,),
            in_specs=in_specs,
            out_specs=[
                pl.BlockSpec(seq, at_row),
                pl.BlockSpec(seq, at_step),
                pl.BlockSpec(seq, at_step),
                pl.BlockSpec((1, length, LANES), at_step),
            ],
            scratch_shapes=[pltpu.VMEM((length + 2 * PAD, width), F32)],
        ),
        out_shape=[
            jax.ShapeDtypeStruct((slots, length, width), BF16),
            jax.ShapeDtypeStruct((steps, length, width), BF16),
            jax.ShapeDtypeStruct((steps, length, width), BF16),
            jax.ShapeDtypeStruct((steps, length, LANES), F32),
        ],
        input_output_aliases=alias,
        compiler_params=params_of(1),
        cost_estimate=pl.CostEstimate(
            flops=2 * steps * length * width * width, transcendentals=0, bytes_accessed=36 * 2**20
        ),
        name="conv_forward",
    )(*args)


def conv_backward(part, tables, x, dy, kept, weights, gains, dx_in, sums, packed):
    rows, counts = tables
    b = part // HALVES
    taps, conv_point = weights
    u, zn, rstd = kept
    slots, length, width = x.shape
    base = part * SLOTS + OWN_CAP
    steps = (KINDS - 2) * OWN_CAP
    first_half = sums is None
    groups = packed[0]

    def kernel(rows_ref, counts_ref, x_ref, dy_ref, u_ref, zn_ref, rstd_ref, point, taps_ref, gain, *rest):
        if first_half:
            dx_ref, small_ref, acc, xpad, dupad, dz_scr = rest[-6:]
        else:
            sum_ref = rest[0]
            dx_ref, small_ref, packed_ref, xpad, dupad, dz_scr, acc = rest[-7:]
        step = pl.program_id(0)
        which, j = step // OWN_CAP, step % OWN_CAP

        @pl.when(step == 0)
        def _():
            small_ref[...] = jnp.zeros_like(small_ref)

        @pl.when(j == 0)
        def _():
            acc[...] = jnp.zeros_like(acc) if first_half else sum_ref[...]

        for kind in range(1, KINDS - 1):
            taps_n = 2 * kind + 1
            first = kind * kind - 1

            @pl.when(jnp.logical_and(which == kind - 1, j < counts_ref[part * 8 + kind]))
            def _():
                dz, gain_grad, shift_grad = norm_backward(
                    dy_ref[0], zn_ref, rstd_ref, gain[kind : kind + 1, :]
                )
                small_ref[14 + kind : 15 + kind, :] += gain_grad
                small_ref[17 + kind : 18 + kind, :] += shift_grad
                dz_scr[...] = dz
                dh = dz.astype(BF16)
                acc[...] += tn(u_ref[0], dh)
                fill_padded(xpad, x_ref[0].astype(F32))
                fill_padded(dupad, nt(dh, point[...]))
                for col in range(0, width, COL_TILE):
                    cols = slice(col, col + COL_TILE)
                    sums = [None] * taps_n
                    for r in range(0, length, ROW_TILE):
                        here = dupad[PAD + r : PAD + r + ROW_TILE, cols]
                        total = dz_scr[r : r + ROW_TILE, cols]
                        for t in range(taps_n):
                            back = PAD + r - t + kind
                            total = total + dupad[back : back + ROW_TILE, cols] * taps_ref[first + t : first + t + 1, cols]
                            ahead = PAD + r + t - kind
                            part = jnp.sum(
                                xpad[ahead : ahead + ROW_TILE, cols] * here, axis=0, keepdims=True
                            )
                            sums[t] = part if sums[t] is None else sums[t] + part
                        dx_ref[0, r : r + ROW_TILE, cols] = total.astype(BF16)
                    for t in range(taps_n):
                        small_ref[first + t : first + t + 1, cols] += sums[t]

        if not first_half:

            @pl.when(j == OWN_CAP - 1)
            def _():
                packed_ref[...] = acc[...].astype(BF16).reshape(packed_ref.shape)

    def at_row(i, r, c):
        return (r[base + i], 0, 0)

    def at_step(i, r, c):
        which = i // OWN_CAP
        last = c[part * 8 + 1 + which] - 1
        return (which * OWN_CAP + jnp.maximum(jnp.minimum(i % OWN_CAP, last), 0), 0, 0)

    def whole(i, r, c):
        return (0, 0)

    seq = (1, length, width)
    in_specs = [
        pl.BlockSpec(seq, at_row),
        pl.BlockSpec(seq, at_row),
        pl.BlockSpec(seq, at_step),
        pl.BlockSpec(seq, at_step),
        pl.BlockSpec((1, length, LANES), at_step),
        pl.BlockSpec((None, None, None, width, width), lambda i, r, c: (b, 0, i // OWN_CAP, 0, 0)),
        pl.BlockSpec((16, width), whole),
        pl.BlockSpec((8, width), whole),
    ]
    args = [rows, counts, x, dy, u, zn, rstd, conv_point, taps, gains]
    sum_spec = pl.BlockSpec((None, width, width), lambda i, r, c: (i // OWN_CAP, 0, 0))
    out_specs = [pl.BlockSpec(seq, at_row), pl.BlockSpec((24, width), whole)]
    out_shape = [
        jax.ShapeDtypeStruct((slots, length, width), BF16),
        jax.ShapeDtypeStruct((24, width), F32),
    ]
    scratch = [
        pltpu.VMEM((length + 2 * PAD, width), F32),
        pltpu.VMEM((length + 2 * PAD, width), F32),
        pltpu.VMEM((length, width), F32),
    ]
    alias = {}
    if first_half:
        out_specs.append(sum_spec)
        out_shape.append(jax.ShapeDtypeStruct((KINDS - 2, width, width), F32))
    else:
        in_specs.append(sum_spec)
        args.append(sums)
        out_specs.append(
            pl.BlockSpec((groups, width // groups, width), lambda i, r, c: (0, 4 + i // OWN_CAP, 0))
        )
        out_shape.append(jax.ShapeDtypeStruct(packed[1].shape, BF16))
        in_specs.append(ANY_SPEC)
        alias = {len(args): 2}
        args.append(packed[1])
        scratch.append(pltpu.VMEM((width, width), F32))
    in_specs.append(ANY_SPEC)
    alias = {**alias, len(args): 0}
    args.append(dx_in)
    return pl.pallas_call(
        kernel,
        grid_spec=pltpu.PrefetchScalarGridSpec(
            num_scalar_prefetch=2,
            grid=(steps,),
            in_specs=in_specs,
            out_specs=out_specs,
            scratch_shapes=scratch,
        ),
        out_shape=out_shape,
        input_output_aliases=alias,
        compiler_params=params_of(1),
        cost_estimate=pl.CostEstimate(
            flops=3 * steps * length * width * width, transcendentals=0, bytes_accessed=50 * 2**20
        ),
        name="conv_backward",
    )(*args)


def owner_forward(b, half, tables, x, weights, small_weights, earlier):
    part = b * HALVES + half
    attn_qkv, attn_out, ffn_up, ffn_down, conv_point = weights
    taps, gains, shifts = small_weights
    norms = (gains, shifts)
    y, *kept_f = feed_forward(part, tables, x, (ffn_up, ffn_down), norms, earlier)
    y, *kept_a = attention_forward(part, tables, x, (attn_qkv, attn_out), norms, y)
    y, *kept_c = conv_forward(part, tables, x, (taps, conv_point), norms, y)
    return y, kept_f, kept_a, kept_c


def both_forward(b, tables, x, weights, small_weights):
    y, kept_a, kept_c, kept_f = [], [], [], None
    for half in range(HALVES):
        yh, kept_f, ka, kc = owner_forward(
            b, half, tables, x[half], weights, small_weights, kept_f
        )
        y.append(yh)
        kept_a.append(ka)
        kept_c.append(kc)
    return y, (kept_f, kept_a, kept_c)


def join_small(small_f, small_a, small_c):
    return jnp.concatenate(
        [
            small_c[:15],
            small_a[0:1],
            small_c[15:18],
            small_f[0:1],
            small_a[1:2],
            small_c[18:21],
            small_f[1:2],
        ]
    )


def owner_backward(b, tables, x, dy, kept, weights, small_weights, groups, wait_for):
    attn_qkv, attn_out, ffn_up, ffn_down, conv_point = weights
    taps, gains, shifts = small_weights
    kept_f, kept_a, kept_c = kept
    width = x[0].shape[-1]
    rest_rows = 7 * width // groups + SMALL_ROWS
    attn, conv = (attn_qkv, attn_out), (taps, conv_point)
    lead, other = 1, 0
    first, second = b * HALVES + lead, b * HALVES + other
    d_lead, small_a0, *sum_a = attention_backward(
        first, tables, x[lead], dy[lead], kept_a[lead], attn, gains, None, None, None
    )
    d_lead, small_c0, sum_c = conv_backward(
        first, tables, x[lead], dy[lead], kept_c[lead], conv, gains, d_lead, None, (groups,)
    )
    small_f, *dx, feed_pack = feed_backward(
        b, tables, x, dy, kept_f, (ffn_up, ffn_down), gains, d_lead, lead, groups, wait_for
    )
    dx[other], small_a1, rest_pack = attention_backward(
        second,
        tables,
        x[other],
        dy[other],
        kept_a[other],
        attn,
        gains,
        dx[other],
        sum_a,
        (groups, rest_rows),
    )
    dx[other], small_c1, rest_pack = conv_backward(
        second,
        tables,
        x[other],
        dy[other],
        kept_c[other],
        conv,
        gains,
        dx[other],
        sum_c,
        (groups, rest_pack),
    )
    small = join_small(small_f, small_a0 + small_a1, small_c0 + small_c1).astype(BF16)
    small = small.reshape(25, groups, width // groups)
    small = small.transpose(1, 0, 2)
    small = jnp.pad(small, ((0, 0), (0, SMALL_ROWS - 25), (0, width - width // groups)))
    rest_pack = lax.dynamic_update_slice(rest_pack, small, (0, rest_rows - SMALL_ROWS, 0))
    return dx, feed_pack, rest_pack


def finish_feed(b, feed, totals, up_out, down_out, shapes):
    parts = shapes[0].shape[-1] // FF_PART
    tall, width = shapes[0].shape[2], FF_PART

    def kernel(up_ref, down_ref, count_ref, *rest):
        up_to, down_to = rest[-2:]
        scale = 1.0 / count_ref[b : b + 1, KINDS - 1 : KINDS]
        up_to[...] = up_ref[...].astype(F32) * scale
        down_to[...] = down_ref[...].astype(F32) * scale

    old = [] if up_out is None else [up_out, down_out]
    return pl.pallas_call(
        kernel,
        grid=(parts,),
        in_specs=[
            pl.BlockSpec((tall, width), lambda c: (c, 0)),
            pl.BlockSpec((tall, width), lambda c: (parts + c, 0)),
            pl.BlockSpec((BLOCKS, 8), lambda c: (0, 0)),
        ]
        + [ANY_SPEC] * len(old),
        out_specs=[
            pl.BlockSpec((None, None, tall, width), lambda c: (b, 0, 0, c)),
            pl.BlockSpec((None, None, tall, width), lambda c: (b, 0, c, 0)),
        ],
        out_shape=list(shapes),
        input_output_aliases={3 + n: n for n in range(len(old))},
        compiler_params=params_of(1),
        cost_estimate=pl.CostEstimate(flops=0, transcendentals=0, bytes_accessed=8 * 2**20),
        name="finish_feed",
    )(feed, feed, totals, *old)


def finish_rest(b, rest, totals, old, shapes, wait_for):
    tall, width = shapes[1].shape[2:]

    def kernel(rest_ref, count_ref, *refs):
        qkv_to, out_to, taps_to, point_to, gain_to, shift_to = refs[-6:]
        scales = 1.0 / jnp.maximum(count_ref[b : b + 1, :], 1.0)

        def piece(n, k):
            return rest_ref[n * tall : (n + 1) * tall, :].astype(F32) * scales[:, k : k + 1]

        for n in range(3):
            qkv_to[:, n * width : (n + 1) * width] = piece(n, 0)
        out_to[...] = piece(3, 0)
        for k in range(1, KINDS - 1):
            point_to[k - 1] = piece(3 + k, k)
        small = rest_ref[7 * tall : 7 * tall + SMALL_ROWS, :].astype(F32)
        row = lax.broadcasted_iota(jnp.int32, small.shape, 0)
        which = jnp.where(row < 3, 1, jnp.where(row < 8, 2, jnp.where(row < 15, 3, 0)))
        which = jnp.where(row >= 15, row - 15, which)
        which = jnp.where(row >= 20, row - 20, which)
        scale = jnp.zeros_like(small)
        for k in range(KINDS):
            scale = jnp.where(which == k, scales[:, k : k + 1], scale)
        small = small * scale
        for r in range(15):
            taps_to[r] = small[r : r + 1, :tall]
        for r in range(KINDS):
            gain_to[r] = small[15 + r : 16 + r, :tall]
            shift_to[r] = small[20 + r : 21 + r, :tall]

    old = list(old)
    return pl.pallas_call(
        kernel,
        grid=(1,),
        in_specs=[
            pl.BlockSpec(rest.shape, lambda i: (0, 0)),
            pl.BlockSpec((BLOCKS, 8), lambda i: (0, 0)),
        ]
        + [ANY_SPEC] * (len(old) + len(wait_for)),
        out_specs=[
            pl.BlockSpec((None, None, tall, 3 * width), lambda i: (b, 0, 0, 0)),
            pl.BlockSpec((None, None, tall, width), lambda i: (b, 0, 0, 0)),
            pl.BlockSpec((None, 15, 1, tall), lambda i: (b, 0, 0, 0)),
            pl.BlockSpec((None, None, KINDS - 2, tall, width), lambda i: (b, 0, 0, 0, 0)),
            pl.BlockSpec((None, KINDS, 1, tall), lambda i: (b, 0, 0, 0)),
            pl.BlockSpec((None, KINDS, 1, tall), lambda i: (b, 0, 0, 0)),
        ],
        out_shape=list(shapes),
        input_output_aliases={2 + n: n for n in range(len(old))},
        compiler_params=params_of(1),
        cost_estimate=pl.CostEstimate(flops=0, transcendentals=0, bytes_accessed=8 * 2**20),
        name="finish_rest",
    )(rest, totals, *old, *wait_for)


def small_params(b, conv_taps, norm_gain, norm_bias):
    taps = jnp.pad(conv_taps[b, 0].astype(F32), ((0, 1), (0, 0)))
    gains = jnp.pad(norm_gain[b, 0].astype(F32), ((0, 3), (0, 0)))
    shifts = jnp.pad(norm_bias[b, 0].astype(F32), ((0, 3), (0, 0)))
    return taps, gains, shifts


def exchange(rows):
    return lax.all_to_all(rows, "op", split_axis=0, concat_axis=0, tiled=True)


def group_sum(pack):
    return lax.psum_scatter(pack, "dp", scatter_dimension=0, tiled=False)


def per_device(
    inputs,
    candidate,
    attn_qkv,
    attn_out,
    ffn_up,
    ffn_down,
    conv_taps,
    conv_point,
    norm_gain,
    norm_bias,
    cotangent,
):
    owners = lax.axis_size("op")
    groups = lax.axis_size("dp")
    seqs = inputs.shape[0]
    width = inputs.shape[-1]
    hidden = ffn_up.shape[-1]
    weights = (attn_qkv, attn_out, ffn_up, ffn_down, conv_point)
    smalls = [small_params(b, conv_taps, norm_gain, norm_bias) for b in range(BLOCKS)]
    send, relay, tags = home_tables(candidate.reshape(-1), owners, seqs)
    marks = BLOCKS * HALVES
    told = tags.reshape(owners, -1)
    told = exchange(told)
    everyone = told[:, marks:].reshape(-1)
    tables = owner_tables(told[:, :marks].reshape(-1), owners)
    both = range(HALVES)

    def start(b, half):
        return (b * HALVES + half) * owners

    me = lax.axis_index("op").astype(jnp.int32)[None]
    routed = owners < seqs
    if routed:
        route, lost = route_tables(everyone, me, owners, seqs)
    else:
        lost = jnp.zeros((1,), jnp.int32)
    lost = lax.psum(jnp.concatenate([lost, tables[1]]), "dp")
    totals = lost[1:].reshape(BLOCKS, HALVES, 8).sum(axis=1).astype(F32)

    x0 = [
        exchange(
            move_rows(send, [start(0, h)], [inputs], owners, False, "send_inputs", (lost,) * h if routed else ())
        )
        for h in both
    ]
    first = owner_forward(0, 0, tables, x0[0], weights, smalls[0], None)
    leaving = bring_rows(route, 0, [first[0]], "hop_x") if routed else None

    def on_the_way(table, sources, name):
        return bring_rows(route, table * owners, sources, name)

    def straight_there(y):
        hop0 = exchange(leaving)
        hop1 = exchange(on_the_way(1, [hop0, y[1]], "hop_x"))
        hop2 = exchange(on_the_way(2, [y[1], hop1], "hop_x"))
        return [on_the_way(3, [hop0, hop1], "land_x"), on_the_way(4, [hop2], "land_x")]

    def straight_back(dx):
        hop0 = exchange(on_the_way(5, [dx[1]], "hop_dx"))
        hop1 = exchange(on_the_way(6, [dx[0], hop0], "hop_dx"))
        hop2 = exchange(on_the_way(7, [dx[0], hop1], "hop_dx"))
        return [on_the_way(9, [hop2], "land_dx"), on_the_way(8, [hop0, hop1], "land_dx")]

    def home_there(y):
        return [
            exchange(move_rows(relay, [start(0, h)], [exchange(y[h])], owners, False, "relay_x"))
            for h in both
        ]

    def home_back(dx):
        return [
            exchange(move_rows(relay, [start(1, h)], [exchange(dx[h])], owners, False, "relay_dx"))
            for h in both
        ]

    def after_first(there, back, x0, first):
        y00, kept_f, ka0, kc0 = first
        y01, kept_f, ka1, kc1 = owner_forward(
            0, 1, tables, x0[1], weights, smalls[0], kept_f
        )
        kept0 = (kept_f, [ka0, ka1], [kc0, kc1])
        x1 = there([y00, y01])
        y1, kept1 = both_forward(1, tables, x1, weights, smalls[1])
        dy1 = [
            exchange(
                move_rows(
                    send,
                    [start(1, h)],
                    [cotangent],
                    owners,
                    False,
                    "send_cotangent",
                    (y1[1 - h],),
                )
            )
            for h in both
        ]
        dx1, feed1, rest1 = owner_backward(
            1, tables, x1, dy1, kept1, weights, smalls[1], groups, ()
        )
        feed1 = group_sum(feed1)
        rest1 = group_sum(rest1)
        dy0 = back(dx1)
        dx0, feed0, rest0 = owner_backward(
            0, tables, x0, dy0, kept0, weights, smalls[0], groups, (feed1,)
        )
        feed0 = group_sum(feed0)
        rest0 = group_sum(rest0)
        y_home = [exchange(after(y1[h], (dy0[0],))) for h in both]
        outputs = move_rows(send, [start(1, h) for h in both], y_home, seqs, True, "outputs")
        dx_home = [
            exchange(after(dx0[0], (feed0,))),
            exchange(after(dx0[1], (rest1,))),
        ]
        input_grad = move_rows(
            send, [start(0, h) for h in both], dx_home, seqs, True, "input_grad"
        )
        tall, deep = width // groups, hidden // groups
        grad = lambda *dims: jax.ShapeDtypeStruct((BLOCKS, 1) + dims, F32)
        feed_shapes = (grad(tall, hidden), grad(deep, width))
        rest_shapes = (
            grad(tall, 3 * width),
            grad(tall, width),
            jax.ShapeDtypeStruct((BLOCKS, 15, 1, tall), F32),
            grad(KINDS - 2, tall, width),
            jax.ShapeDtypeStruct((BLOCKS, KINDS, 1, tall), F32),
            jax.ShapeDtypeStruct((BLOCKS, KINDS, 1, tall), F32),
        )
        feeds = finish_feed(1, feed1, totals, None, None, feed_shapes)
        rests = finish_rest(1, rest1, totals, (), rest_shapes, ())
        feeds = finish_feed(0, feed0, totals, *feeds, feed_shapes)
        rests = finish_rest(0, rest0, totals, rests, rest_shapes, (outputs, input_grad, feeds[0]))
        qkv, out, taps, point, gain, shift = rests
        return (outputs, input_grad, qkv, out, *feeds, taps, point, gain, shift)

    def in_place(results):
        turned = [rows.transpose(0, 2, 1, 3) if n in (6, 8, 9) else rows for n, rows in enumerate(results)]
        return tuple(turned)

    if not routed:
        return in_place(after_first(home_there, home_back, x0, first))
    results = lax.cond(
        lost[0] == 0,
        lambda x0, first: after_first(straight_there, straight_back, x0, first),
        lambda x0, first: after_first(home_there, home_back, x0, first),
        x0,
        first,
    )
    return in_place(results)


def solution(mesh):
    placed = (
        P(("dp", "op"), None, None),
        P(("dp", "op"), None),
        P(None, "op", None, None),
        P(None, "op", None, None),
        P(None, "op", None, None),
        P(None, "op", None, None),
        P(None, "op", None, None),
        P(None, "op", None, None, None),
        P(None, "op", None, None),
        P(None, "op", None, None),
        P(("dp", "op"), None, None),
    )
    return jax.shard_map(
        per_device,
        mesh=mesh,
        in_specs=placed,
        out_specs=(
            P(("dp", "op"), None, None),
            P(("dp", "op"), None, None),
            P(None, "op", "dp", None),
            P(None, "op", "dp", None),
            P(None, "op", "dp", None),
            P(None, "op", "dp", None),
            P(None, "op", None, "dp"),
            P(None, "op", None, "dp", None),
            P(None, "op", None, "dp"),
            P(None, "op", None, "dp"),
        ),
        check_vma=False,
    )
```
